32 devices in a mesh: dp: 8 (over z, core), heads: 2 (over x), expert: 2 (over y).
Axes of the slice: x: 2, y: 2, z: 4, core: 2. Of those that a mesh axis runs over, the one named last changes fastest.
Arguments:
- block_in: bfloat16 [64, 197, 768], P(('dp', 'expert'), None, 'heads'), may hold values from -6 to 6
- cotangent: bfloat16 [64, 197, 768], P(('dp', 'expert'), None, 'heads'), may hold values from -8 to 8
- route_ids: int32 [64, 197, 2], P(('dp', 'expert')), may hold values from 0 to 7, all different within a row; in each aligned block of 788 rows (0 to 787, 788 to 1575, ..., all dimensions but the last counted through in order) at most 281 rows name the same one
- gain_attn: bfloat16 [768], P(('dp', 'expert')), may hold values from 0.099609375 to 1.8984375
- w_qkv: bfloat16 [768, 3, 768], P(('dp', 'expert'), None, 'heads'), may hold values from -0.21875 to 0.21875
- w_out_attn: bfloat16 [768, 768], P(('dp', 'expert'), 'heads'), may hold values from -0.875 to 0.875
- gain_moe: bfloat16 [768], P(('dp', 'expert')), may hold values from 0.099609375 to 1.8984375
- router: bfloat16 [768, 8], P(('dp', 'expert')), may hold values from -0.21875 to 0.21875
- w_in: bfloat16 [768, 8, 3072], P('dp', 'expert', 'heads'), may hold values from -0.21875 to 0.21875
- w_out: bfloat16 [768, 8, 3072], P('dp', 'expert', 'heads'), may hold values from -2.5 to 2.5
Outputs:
- block_out: bfloat16 [64, 197, 768], P(('dp', 'expert'), None, 'heads')
- grad_block_in: bfloat16 [64, 197, 768], P(('dp', 'expert'), None, 'heads')
- grad_gain_attn: float32 [768], P(('dp', 'expert'))
- grad_w_qkv: float32 [768, 3, 768], P(('dp', 'expert'), None, 'heads')
- grad_w_out_attn: float32 [768, 768], P(('dp', 'expert'), 'heads')
- grad_gain_moe: float32 [768], P(('dp', 'expert'))
- grad_router: float32 [768, 8], P(('dp', 'expert'))
- grad_w_in: float32 [768, 8, 3072], P('dp', 'expert', 'heads')
- grad_w_out: float32 [768, 8, 3072], P('dp', 'expert', 'heads')
The draws below stay inside these ranges and needn't reach their ends.
Inputs may be any that keep to these rules, and one draw needn't show every extreme that they name: `route_ids`: each token names two different experts. Within each aligned block of 788 tokens (the images of one index of dp and expert) no expert is named more than 281 times, a bound that some block reaches.
All inputs are finite; a program needn't handle non-finite values.
Results may differ from the reference program's by a relative error of at most 0.022.
Values may be sent and summed in bfloat16 or wider, within the bound.
No kernel may reach another device: no remote copies, remote signals or barrier semaphores. Data moves between devices by JAX's collectives and lax.ppermute only.
A program may use at most 192 MiB of HBM per device.

```python
import math
import jax
import jax.numpy as jnp
import numpy as np
from jax import lax

D = 768
HEADS = 12
HEAD_DIM = 64
FF = 3072
S = 197
HD = 768
EXPERTS = 8
IMAGES = 64
GROUP_TOK = 788
CAP = 281


def raised(values, stream_key, source, target, parts, factor):
    owner, partner = [(jnp.arange(values.shape[axis_at]) // (values.shape[axis_at] // parts)).reshape([-1 if axis == axis_at else 1 for axis in range(values.ndim)]) for axis_at in (source, target)]
    chosen = jax.random.permutation(stream_key, parts)[partner]
    strong = (owner == chosen) | (owner == (partner + parts // 2) % parts)
    return jnp.where(strong, factor * values, values)


def shard_levels(own_key, extent, cuts, low, top_value):
    gain, own = 1.0, jax.random.fold_in(own_key, 6)
    for position, blocks in cuts:
        steps = jnp.exp(jax.random.uniform(jax.random.fold_in(own, position), (blocks,), jnp.float32, low / len(cuts), top_value / len(cuts)))
        gain = gain * jnp.repeat(steps, extent[position] // blocks).reshape([-1 if axis == position else 1 for axis in range(len(extent))])
    return gain


def shared_out(own_key, own, number, rows, count, top, bound, lean):
    sequence = jax.random.permutation(own_key, count)
    heavy_load, usual = shares(count, rows * top, bound, lean, True), shares(count, rows * top, bound, lean, False)
    places = jnp.arange(count)

    def named(sizes, turn):
        used = int((sizes > 0).sum())
        fixed = max(1, used // 4)
        shifted = fixed + (places - fixed + turn * (used - fixed)) % max(1, count - fixed)
        return jnp.zeros((count,), jnp.int32).at[sequence[jnp.where(places < fixed, places, shifted)]].set(jnp.asarray(sizes, jnp.int32))

    sizes = jnp.where(number % 4 == 0, named(heavy_load, number // 4), named(usual, number - number // 4 - 1))
    mixed = jax.random.permutation(jax.random.fold_in(own, 3), count)
    source_of, receiver = mixed[0:count // 2 * 2:2], mixed[1:count // 2 * 2:2]
    slack = jnp.minimum(sizes[source_of] - 1, bound - sizes[receiver]) // 2
    slack = jnp.where((source_of == sequence[0]) | (receiver == sequence[0]) | (sizes[receiver] == 0), 0, jnp.maximum(slack, 0))
    shifted = jax.random.randint(jax.random.fold_in(own, 4), (count // 2,), 0, 1 << 20) % (slack + 1)
    sizes = sizes.at[source_of].add(-shifted).at[receiver].add(shifted)
    members = jnp.searchsorted(jnp.cumsum(sizes), jnp.arange(rows * top), side="right").astype(jnp.int32)
    listing = members.reshape(top, rows).T
    listing = listing[jax.random.permutation(jax.random.fold_in(own, 1), rows)]
    turn = jax.random.randint(jax.random.fold_in(own, 2), (rows, 1), 0, top)
    return jnp.take_along_axis(listing, (jnp.arange(top)[None, :] + turn) % top, axis=1)


def shares(amount, total, reach, lean, full):
    portions = [(1 << 20) // math.isqrt(standing ** lean) + 1 for standing in range(1, amount + 1)]
    largest = reach if full else min(reach, max(-(-total // amount), total * portions[0] // sum(portions)))
    least = 1 if total - largest >= amount - 1 else 0
    counts, spare = [largest] + [least] * (amount - 1), total - largest - least * (amount - 1)
    while spare > 0:
        free = [i for i in range(1, amount) if counts[i] < largest] or [i for i in range(1, amount) if counts[i] < reach]
        mass, left = sum([portions[i] for i in free]), spare
        for i in free:
            more = min(reach - counts[i], max(1, left * portions[i] // mass), spare)
            counts[i] = counts[i] + more
            spare = spare - more
    return np.array(counts)


def scatter_about(key, shape, width, reach, shards=(), held_as=jnp.bfloat16):
    result = width * jax.random.normal(key, shape, jnp.float32)
    if shards:
        result = result * shard_levels(key, shape, shards, -0.22, 0.18)
    return jnp.clip(result, -reach, reach).astype(held_as)


def gaussian_with(key, dims, width, reach, cuts, heavy, kind=jnp.bfloat16):
    values = width * jax.random.normal(key, dims, jnp.float32)
    if cuts:
        values = values * shard_levels(key, dims, cuts, -0.22, 0.18)
    return jnp.clip(raised(values, jax.random.fold_in(key, 3), *heavy), -reach, reach).astype(kind)


def setup_inputs(seed: int = 0) -> dict:
    key_of = jax.random.split(jax.random.key(seed), 11)
    block_in = scatter_about(key_of[0], (IMAGES, S, D), 1.0, 6.0, ((0, 16), (2, 2)))
    cotangent = gaussian_with(key_of[1], (IMAGES, S, D), 1.0, 8.0, ((0, 16), (2, 2)), (0, 2, 16, 2.0))
    route_ids_keys = jax.random.split(jax.random.fold_in(key_of[2], 1), IMAGES * S // GROUP_TOK)
    route_ids_turns = jax.random.permutation(jax.random.fold_in(key_of[2], 3), IMAGES * S // GROUP_TOK)
    route_ids = jax.vmap(lambda own, number: shared_out(jax.random.fold_in(key_of[2], 2), own, number, GROUP_TOK, EXPERTS, 2, CAP, 2))(route_ids_keys, route_ids_turns).reshape((IMAGES, S, 2))
    gain_attn = jnp.clip(1.0 + 0.18 * jax.random.normal(key_of[3], (D,), jnp.float32), 0.099609375, 1.8984375).astype(jnp.bfloat16)
    w_qkv = scatter_about(key_of[4], (D, 3, HD), D ** -0.5, 0.21875, ((0, 16), (2, 2)))
    w_out_attn = scatter_about(key_of[5], (D, HD), (HD // 16) ** -0.5, 0.875, ((0, 16), (1, 2)))
    gain_moe = jnp.clip(1.0 + 0.18 * jax.random.normal(key_of[6], (D,), jnp.float32), 0.099609375, 1.8984375).astype(jnp.bfloat16)
    router = scatter_about(key_of[7], (D, EXPERTS), D ** -0.5, 0.21875, ((0, 16),))
    w_in = scatter_about(key_of[8], (D, EXPERTS, FF), D ** -0.5, 0.21875, ((0, 8), (1, 2), (2, 2)))
    w_out = scatter_about(key_of[9], (D, EXPERTS, FF), (max(FF // 512, 1)) ** -0.5, 2.5, ((0, 8), (1, 2), (2, 2)))
    return dict(block_in=block_in, cotangent=cotangent, route_ids=route_ids, gain_attn=gain_attn, w_qkv=w_qkv, w_out_attn=w_out_attn, gain_moe=gain_moe, router=router, w_in=w_in, w_out=w_out)


@jax.custom_vjp
def low(v):
    return lax.optimization_barrier(v.astype(jnp.bfloat16)).astype(jnp.float32)

@jax.custom_vjp
def low_back(v):
    return v

def low_keep(v):
    return (low(v), None)

def low_pass(kept, grad):
    return (grad,)

def back_keep(v):
    return (v, None)

def back_low(kept, grad):
    return (low(grad),)
low.defvjp(low_keep, low_pass)
low_back.defvjp(back_keep, back_low)

def layer_norm(inputs, norm_gain):
    average = lax.optimization_barrier(jnp.mean(inputs, axis=-1, keepdims=True))
    centred = inputs - average
    spread = lax.optimization_barrier(jnp.mean(centred * centred, axis=-1, keepdims=True))
    return centred * lax.rsqrt(spread + 1e-06) * norm_gain

def forward(inputs, gain_attn, w_qkv, w_out_attn, gain_moe, router, w_in, w_out, route_ids):
    highest = lax.Precision.HIGHEST
    images = inputs.shape[0]
    normed_one = low(layer_norm(inputs, gain_attn))
    grouped = normed_one.reshape(images // 16, 16, S, D)

    def attend(image_block):
        projected = low(low_back(jnp.einsum('isd,dkh->iskh', image_block, w_qkv, precision=highest)))
        queries = projected[:, :, 0].reshape(16, S, HEADS, HEAD_DIM)
        keys_in = projected[:, :, 1].reshape(16, S, HEADS, HEAD_DIM)
        values_in = projected[:, :, 2].reshape(16, S, HEADS, HEAD_DIM)
        scores = low_back(jnp.einsum('iqhc,ikhc->ihqk', queries, keys_in, precision=highest) * HEAD_DIM ** (-0.5))
        weights = low(jax.nn.softmax(scores, axis=-1))
        context = low(low_back(jnp.einsum('ihqk,ikhc->iqhc', weights, values_in, precision=highest)))
        return jnp.einsum('ish,dh->isd', context.reshape(16, S, HD), w_out_attn, precision=highest)
    attended = lax.map(jax.checkpoint(attend), grouped).reshape(images, S, D)
    middle = inputs + low_back(attended)
    normed_two = low(layer_norm(middle, gain_moe))
    blocks = images * S // GROUP_TOK
    grouped_rows = normed_two.reshape(blocks, GROUP_TOK, D)
    logits = low_back(jnp.einsum('btd,de->bte', grouped_rows, router, precision=highest))
    route_probs = jax.nn.softmax(logits, axis=-1)
    choice_ids = route_ids.reshape(blocks, GROUP_TOK, 2).astype(jnp.int32)
    gate_values = jnp.take_along_axis(route_probs, choice_ids, axis=-1)
    pair_ids = choice_ids.reshape(blocks, GROUP_TOK * 2)
    one_hot = (pair_ids[:, :, None] == jnp.arange(EXPERTS, dtype=jnp.int32)[None, None, :]).astype(jnp.int32)
    earlier = (jnp.cumsum(one_hot, axis=1).astype(jnp.int32) - one_hot) * one_hot
    slot_rank = lax.optimization_barrier(jnp.sum(earlier, axis=-1)).astype(jnp.int32)
    flat_index = (pair_ids * CAP + slot_rank).astype(jnp.int32)
    block_range = jnp.arange(blocks, dtype=jnp.int32)[:, None]
    pair_values = jnp.broadcast_to(jnp.arange(GROUP_TOK * 2, dtype=jnp.int32)[None, :], (blocks, GROUP_TOK * 2))
    slot_owner = jnp.zeros((blocks, EXPERTS * CAP), jnp.int32).at[block_range, flat_index].set(pair_values)
    filled = jnp.zeros((blocks, EXPERTS * CAP), jnp.float32).at[block_range, flat_index].set(1.0)
    source_rows = (slot_owner // 2).astype(jnp.int32)
    slot_rows = jnp.take_along_axis(grouped_rows, source_rows[:, :, None], axis=1) * filled[:, :, None]
    slot_rows = low_back(slot_rows).reshape(blocks, EXPERTS, CAP, D)

    def expert_block(block_rows):
        hidden = low_back(jnp.einsum('ecd,def->ecf', block_rows, w_in, precision=highest))
        active = low(jax.nn.gelu(hidden))
        return low(low_back(jnp.einsum('ecf,def->ecd', active, w_out, precision=highest)))
    expert_result = lax.map(jax.checkpoint(expert_block), slot_rows).reshape(blocks, EXPERTS * CAP, D)
    picked = jnp.take_along_axis(expert_result, flat_index[:, :, None], axis=1).reshape(blocks, GROUP_TOK, 2, D)
    mixture = lax.optimization_barrier(jnp.sum(gate_values[..., None] * picked, axis=2))
    return middle + mixture.reshape(images, S, D)

def reference(block_in, cotangent, route_ids, gain_attn, w_qkv, w_out_attn, gain_moe, router, w_in, w_out):
    params = [array.astype(jnp.float32) for array in (block_in, gain_attn, w_qkv, w_out_attn, gain_moe, router, w_in, w_out)]

    def layer(inputs, gain_one, qkv_weight, out_weight, gain_two, router_weight, expert_in, expert_out):
        return forward(inputs, gain_one, qkv_weight, out_weight, gain_two, router_weight, expert_in, expert_out, route_ids)
    output, pullback = jax.vjp(layer, params[0], params[1], params[2], params[3], params[4], params[5], params[6], params[7])
    gradients = pullback(cotangent.astype(jnp.float32))
    return (output.astype(jnp.bfloat16), gradients[0].astype(jnp.bfloat16), gradients[1], gradients[2], gradients[3], gradients[4], gradients[5], gradients[6], gradients[7])
```

```python
import functools

import jax
import jax.numpy as jnp
from jax import lax
from jax.experimental import pallas as pl
from jax.experimental.pallas import tpu as pltpu
from jax.sharding import PartitionSpec as P

HEAD_DIM = 64
CORES = 2
EPS = 1e-06
F32 = jnp.float32
BF16 = jnp.bfloat16
VMEM_LIMIT = 56 * 1024 * 1024


def dot(a, b, ca, cb):
    return lax.dot_general(a, b, (((ca,), (cb,)), ((), ())), preferred_element_type=F32)


def params(dims):
    return pltpu.CompilerParams(
        dimension_semantics=("arbitrary",) * dims, vmem_limit_bytes=VMEM_LIMIT
    )


def norm_parts(rows):
    average = jnp.mean(rows, axis=-1, keepdims=True)
    centred = rows - average
    spread = jnp.mean(centred * centred, axis=-1, keepdims=True)
    scale = lax.rsqrt(spread + EPS)
    return centred * scale, scale


def attend_kernel(x_ref, gain_ref, wqkv_ref, wo_ref, part_ref, qkv_ref, ctx_ref):
    width = wo_ref.shape[1]
    unit, _ = norm_parts(x_ref[0].astype(F32))
    normed = (unit * gain_ref[...]).astype(BF16)
    for part in range(3):
        cols = slice(part * width, (part + 1) * width)
        qkv_ref[0, :, cols] = dot(normed, wqkv_ref[:, cols], 1, 0).astype(BF16)
    seq = x_ref.shape[1]
    lane = lax.broadcasted_iota(jnp.int32, (seq, 128), 1)
    for pair in range(width // 128):
        q, k, v = (
            qkv_ref[0, :, part * width + pair * 128 : part * width + (pair + 1) * 128]
            for part in range(3)
        )
        ctx = jnp.zeros((seq, 128), F32)
        for side in range(2):
            mine = (lane >= 64) if side else (lane < 64)
            own_k = jnp.where(mine, k, jnp.zeros_like(k))
            own_v = jnp.where(mine, v, jnp.zeros_like(v))
            scores = dot(q, own_k, 1, 1) * (HEAD_DIM**-0.5)
            powers = jnp.exp(scores - jnp.max(scores, axis=-1, keepdims=True))
            weights = powers / jnp.sum(powers, axis=-1, keepdims=True)
            ctx = ctx + dot(weights.astype(BF16), own_v, 1, 0)
        ctx_ref[0, :, pair * 128 : (pair + 1) * 128] = ctx.astype(BF16)
    part_ref[0] = dot(ctx_ref[0], wo_ref[...], 1, 1).astype(BF16)


def attend(inputs, gain, packed, width):
    images, seq, model = inputs.shape
    whole = lambda i: (i, 0, 0)
    return pl.pallas_call(
        attend_kernel,
        grid=(images,),
        in_specs=[
            pl.BlockSpec((1, seq, model), whole),
            pl.BlockSpec((1, model), lambda i: (0, 0)),
            pl.BlockSpec((model, 3 * width), lambda i: (0, 0)),
            pl.BlockSpec((model, width), lambda i: (0, 3)),
        ],
        out_specs=[
            pl.BlockSpec((1, seq, model), whole),
            pl.BlockSpec((1, seq, 3 * width), whole),
            pl.BlockSpec((1, seq, width), whole),
        ],
        out_shape=[
            jax.ShapeDtypeStruct((images, seq, model), BF16),
            jax.ShapeDtypeStruct((images, seq, 3 * width), BF16),
            jax.ShapeDtypeStruct((images, seq, width), BF16),
        ],
        compiler_params=params(1),
        cost_estimate=pl.CostEstimate(
            flops=2 * images * seq * model * width * 5,
            bytes_accessed=8 * images * seq * model,
            transcendentals=images * seq * seq * width // 64,
        ),
        name="attend",
    )(inputs, gain, packed, packed)


def attend_back_kernel(
    x_ref, gain_ref, datt_ref, qkv_ref, ctx_ref, wqkv_ref, wo_ref,
    dnorm_ref, stats_ref, dgain_ref, dwqkv_ref, dwo_ref, dproj_ref,
):
    width = wo_ref.shape[1]
    seq, model = x_ref.shape[1], x_ref.shape[2]

    @pl.when(pl.program_id(0) == 0)
    def _():
        dgain_ref[...] = jnp.zeros_like(dgain_ref)
        dwqkv_ref[...] = jnp.zeros_like(dwqkv_ref)
        dwo_ref[...] = jnp.zeros_like(dwo_ref)

    datt = datt_ref[0]
    dwo_ref[...] += dot(datt, ctx_ref[0], 0, 0)
    dctx_all = dot(datt, wo_ref[...], 1, 0).astype(BF16)
    lane = lax.broadcasted_iota(jnp.int32, (seq, 128), 1)
    for pair in range(width // 128):
        cols = slice(pair * 128, (pair + 1) * 128)
        q, k, v = (
            qkv_ref[0, :, part * width + pair * 128 : part * width + (pair + 1) * 128]
            for part in range(3)
        )
        dctx = dctx_all[:, cols]
        dq = jnp.zeros((seq, 128), F32)
        dk = jnp.zeros((seq, 128), F32)
        dv = jnp.zeros((seq, 128), F32)
        for side in range(2):
            mine = (lane >= 64) if side else (lane < 64)
            own = lambda t: jnp.where(mine, t, jnp.zeros_like(t))
            own_k, own_v = own(k), own(v)
            scores = dot(q, own_k, 1, 1) * (HEAD_DIM**-0.5)
            powers = jnp.exp(scores - jnp.max(scores, axis=-1, keepdims=True))
            weights = powers / jnp.sum(powers, axis=-1, keepdims=True)
            dweights = dot(dctx, own_v, 1, 1)
            inner = jnp.sum(dweights * weights, axis=-1, keepdims=True)
            dscores = (weights * (dweights - inner)).astype(BF16)
            dq = dq + dot(dscores, own_k, 1, 0)
            dk = dk + dot(dscores, own(q), 0, 0)
            dv = dv + dot(weights.astype(BF16), own(dctx), 0, 0)
        for part, value in enumerate((dq * HEAD_DIM**-0.5, dk * HEAD_DIM**-0.5, dv)):
            start = part * width + pair * 128
            dproj_ref[:, start : start + 128] = value.astype(BF16)
    dproj = dproj_ref[...]
    gain = gain_ref[...]
    unit, scale = norm_parts(x_ref[0].astype(F32))
    normed = (unit * gain).astype(BF16)
    dwqkv_ref[...] += dot(normed, dproj, 0, 0)
    dnormed = dot(dproj, wqkv_ref[...], 1, 1)
    dnorm_ref[0] = dnormed.astype(BF16)
    along = dnormed * unit
    dgain_ref[...] += jnp.sum(along, axis=0, keepdims=True)
    first = jnp.sum(dnormed * gain, axis=-1, keepdims=True)
    second = jnp.sum(along * gain, axis=-1, keepdims=True)
    stats_ref[0] = jnp.where(lane == 0, first, jnp.where(lane == 1, second, 0.0))


def attend_back(inputs, gain, datt, qkv, ctx, packed, width):
    images, seq, model = inputs.shape
    whole = lambda i: (i, 0, 0)
    fixed = lambda i: (0, 0)
    return pl.pallas_call(
        attend_back_kernel,
        grid=(images,),
        in_specs=[
            pl.BlockSpec((1, seq, model), whole),
            pl.BlockSpec((1, model), fixed),
            pl.BlockSpec((1, seq, model), whole),
            pl.BlockSpec((1, seq, 3 * width), whole),
            pl.BlockSpec((1, seq, width), whole),
            pl.BlockSpec((model, 3 * width), fixed),
            pl.BlockSpec((model, width), lambda i: (0, 3)),
        ],
        out_specs=[
            pl.BlockSpec((1, seq, model), whole),
            pl.BlockSpec((1, seq, 128), whole),
            pl.BlockSpec((1, model), fixed),
            pl.BlockSpec((model, 3 * width), fixed),
            pl.BlockSpec((model, width), fixed),
        ],
        out_shape=[
            jax.ShapeDtypeStruct((images, seq, model), BF16),
            jax.ShapeDtypeStruct((images, seq, 128), F32),
            jax.ShapeDtypeStruct((1, model), F32),
            jax.ShapeDtypeStruct((model, 3 * width), F32),
            jax.ShapeDtypeStruct((model, width), F32),
        ],
        scratch_shapes=[pltpu.VMEM((seq, 3 * width), BF16)],
        compiler_params=params(1),
        cost_estimate=pl.CostEstimate(
            flops=2 * images * seq * model * width * 14,
            bytes_accessed=16 * images * seq * model,
            transcendentals=images * seq * seq * width // 64,
        ),
        name="attend_back",
    )(inputs, gain, datt, qkv, ctx, packed, packed)


def expert_kernel(
    slot_ref, prob_ref, x_ref, grad_ref, win_ref, wout_ref,
    rows_ref, grows_ref, gact_ref, dhid_ref, dgate_ref, drows_ref, yrows_ref,
):
    slots = rows_ref.shape[2]
    tokens, model = x_ref.shape[1], x_ref.shape[2]
    hidden_width = win_ref.shape[3]
    at = lax.broadcasted_iota(jnp.int32, (slots, tokens), 0)
    mask = at == slot_ref[0, 0]
    pick = jnp.where(mask, 1.0, 0.0).astype(BF16)
    gate = jnp.sum(jnp.where(mask, prob_ref[0, 0], 0.0), axis=1, keepdims=True)
    rows = dot(pick, x_ref[0], 1, 0).astype(BF16)
    grows = dot(pick, grad_ref[0], 1, 0).astype(BF16)
    rows_ref[0, 0] = rows
    grows_ref[0, 0] = grows
    dgate = jnp.zeros((slots, 1), F32)
    drows = jnp.zeros((slots, model), F32)
    yrows = jnp.zeros((slots, model), F32)
    tile = 512 if hidden_width % 512 == 0 else hidden_width
    curve = 0.7978845608028654
    for start in range(0, hidden_width, tile):
        cols = slice(start, start + tile)
        win = win_ref[:, 0, :, cols].reshape(model, tile)
        wout = wout_ref[:, 0, :, cols].reshape(model, tile)
        hidden = dot(rows, win, 1, 0)
        pulled = dot(grows, wout, 1, 0)
        square = hidden * hidden
        bend = jnp.tanh(hidden * (curve + curve * 0.044715 * square))
        half = 0.5 + 0.5 * bend
        active = hidden * half
        slope = half + 0.5 * hidden * (1.0 - bend * bend) * (
            curve + 3.0 * curve * 0.044715 * square
        )
        dgate = dgate + jnp.sum(active * pulled, axis=1, keepdims=True)
        gact = (gate * active).astype(BF16)
        dhid = (gate * pulled * slope).astype(BF16)
        gact_ref[0, 0, :, cols] = gact
        dhid_ref[0, 0, :, cols] = dhid
        drows = drows + dot(dhid, win, 1, 1)
        yrows = yrows + dot(gact, wout, 1, 1)
    dgate_ref[0, 0] = dgate
    drows_ref[0, 0] = drows.astype(BF16)
    yrows_ref[0, 0] = yrows.astype(BF16)


def run_experts(slot_of, probs, tokens_all, grads_all, w_in, w_out, slots):
    blocks, local, _, tokens = slot_of.shape
    model = tokens_all.shape[2]
    depth, _, part_rows, width = w_in.shape
    pair = lambda e, b: (b, e, 0, 0)
    block = lambda e, b: (b, 0, 0)
    weight = pl.BlockSpec((depth, 1, part_rows, width), lambda e, b: (0, e, 0, 0))
    shape = lambda last, kind: jax.ShapeDtypeStruct((blocks, local, slots, last), kind)
    spec = lambda last: pl.BlockSpec((1, 1, slots, last), pair)
    return pl.pallas_call(
        expert_kernel,
        grid=(local, blocks),
        in_specs=[
            pl.BlockSpec((1, 1, 1, tokens), pair),
            pl.BlockSpec((1, 1, 1, tokens), pair),
            pl.BlockSpec((1, tokens, model), block),
            pl.BlockSpec((1, tokens, model), block),
            weight,
            weight,
        ],
        out_specs=[
            spec(model), spec(model), spec(width), spec(width), spec(1), spec(model), spec(model)
        ],
        out_shape=[
            shape(model, BF16), shape(model, BF16), shape(width, BF16), shape(width, BF16),
            shape(1, F32), shape(model, BF16), shape(model, BF16),
        ],
        compiler_params=params(2),
        cost_estimate=pl.CostEstimate(
            flops=8 * blocks * local * slots * model * width
            + 4 * blocks * local * slots * model * tokens,
            bytes_accessed=16 * blocks * local * slots * model,
            transcendentals=blocks * local * slots * width,
        ),
        name="experts",
    )(slot_of, probs, tokens_all, grads_all, w_in, w_out)


def weight_grad_kernel(rows_ref, cols_ref, out_ref):
    blocks, _, slots, model = rows_ref.shape
    depth, _, part_rows, tile = out_ref.shape
    left = rows_ref[...].reshape(blocks * slots, model)
    right = cols_ref[...].reshape(blocks * slots, tile)
    out_ref[...] = dot(left, right, 0, 0).astype(BF16).reshape(depth, 1, part_rows, tile)


def weight_grad(rows, cols, depth):
    blocks, local, slots, model = rows.shape
    width = cols.shape[3]
    tile = width // 2 if width % 256 == 0 else width
    return pl.pallas_call(
        weight_grad_kernel,
        grid=(local, width // tile),
        in_specs=[
            pl.BlockSpec((blocks, 1, slots, model), lambda e, f: (0, e, 0, 0)),
            pl.BlockSpec((blocks, 1, slots, tile), lambda e, f: (0, e, 0, f)),
        ],
        out_specs=pl.BlockSpec((depth, 1, model // depth, tile), lambda e, f: (0, e, 0, f)),
        out_shape=jax.ShapeDtypeStruct((depth, local, model // depth, width), BF16),
        compiler_params=params(2),
        cost_estimate=pl.CostEstimate(
            flops=2 * blocks * local * slots * model * width,
            bytes_accessed=2 * local * (blocks * slots * (model + width) + model * width),
            transcendentals=0,
        ),
        name="weight_grad",
    )(rows, cols)


def combine_kernel(slot_ref, rows_ref, out_ref):
    _, local, slots, model = rows_ref.shape
    tokens = out_ref.shape[1]
    at = lax.broadcasted_iota(jnp.int32, (tokens, slots), 1)
    total = jnp.zeros((tokens, model), F32)
    for e in range(local):
        pick = jnp.where(at == slot_ref[0, :, e : e + 1], 1.0, 0.0).astype(BF16)
        total = total + dot(pick, rows_ref[0, e], 1, 0)
    out_ref[0] = total.astype(BF16)


def combine_add_kernel(slot_ref, rows_ref, dlog_ref, router_ref, out_ref):
    _, local, slots, model = rows_ref.shape
    tokens = out_ref.shape[1]
    at = lax.broadcasted_iota(jnp.int32, (tokens, slots), 1)
    total = dot(dlog_ref[0], router_ref[...], 0, 1)
    for e in range(local):
        pick = jnp.where(at == slot_ref[0, :, e : e + 1], 1.0, 0.0).astype(BF16)
        total = total + dot(pick, rows_ref[0, e], 1, 0)
    out_ref[0] = total.astype(BF16)


def combine(slot_cols, rows, extra=None):
    blocks, tokens, local = slot_cols.shape
    slots, model = rows.shape[2:]
    in_specs = [
        pl.BlockSpec((1, tokens, local), lambda b: (b, 0, 0)),
        pl.BlockSpec((1, local, slots, model), lambda b: (b, 0, 0, 0)),
    ]
    args = (slot_cols, rows)
    if extra is not None:
        dlog, router = extra
        in_specs += [
            pl.BlockSpec((1,) + dlog.shape[1:], lambda b: (b, 0, 0)),
            pl.BlockSpec(router.shape, lambda b: (0, 0)),
        ]
        args += extra
    return pl.pallas_call(
        combine_kernel if extra is None else combine_add_kernel,
        grid=(blocks,),
        in_specs=in_specs,
        out_specs=pl.BlockSpec((1, tokens, model), lambda b: (b, 0, 0)),
        out_shape=jax.ShapeDtypeStruct((blocks, tokens, model), BF16),
        compiler_params=params(1),
        cost_estimate=pl.CostEstimate(
            flops=2 * blocks * local * slots * model * tokens,
            bytes_accessed=2 * blocks * model * (local * slots + tokens),
            transcendentals=0,
        ),
        name="combine",
    )(*args)


def per_device(
    block_in, cotangent, route_ids, gain_attn, w_qkv, w_out_attn, gain_moe, router, w_in, w_out
):
    n_dp, n_heads, n_exp = (lax.axis_size(name) for name in ("dp", "heads", "expert"))
    n_z = n_dp // CORES
    dp, head, exp = (lax.axis_index(name) for name in ("dp", "heads", "expert"))
    z, core = dp // CORES, dp % CORES
    images, seq, half_width = block_in.shape
    tokens = images * seq
    model = half_width * n_heads
    width = w_qkv.shape[2]
    expert_count = router.shape[1]
    group = w_in.shape[1]
    local = group // CORES
    hidden_width = w_in.shape[2]
    capacity = 20 * tokens // (7 * expert_count)
    slots = -(-capacity // 16) * 16

    def shift(value, axis, step):
        size = lax.axis_size(axis)
        return lax.ppermute(value, axis, [(i, (i + step) % size) for i in range(size)])

    def shift_z(value, step):
        pairs = [
            (a * CORES + c, ((a + step) % n_z) * CORES + c) for a in range(n_z) for c in range(CORES)
        ]
        return lax.ppermute(value, "dp", pairs)

    def swap_core(value):
        return lax.ppermute(value, "dp", [(i, i ^ 1) for i in range(n_dp)])

    def place(pieces, index, count):
        if count == 2:
            first = index == 0
            return jnp.stack(
                [jnp.where(first, pieces[0], pieces[1]), jnp.where(first, pieces[1], pieces[0])]
            )
        out = jnp.zeros((count,) + pieces[0].shape, pieces[0].dtype)
        for k, piece in enumerate(pieces):
            out = lax.dynamic_update_index_in_dim(out, piece, (index - k) % count, 0)
        return out

    def spread(value, axis):
        return [value] + [shift(value, axis, k) for k in range(1, lax.axis_size(axis))]

    def take(value, index, dim=0):
        return lax.dynamic_index_in_dim(value, index, dim, keepdims=False)

    rest = 128
    tail = jnp.concatenate(
        [router, gain_attn[:, None], gain_moe[:, None],
         jnp.zeros((router.shape[0], rest - expert_count - 2), BF16)], axis=1
    )
    own_pack = jnp.concatenate(
        [w_qkv.reshape(w_qkv.shape[0], 3 * width), w_out_attn, tail], axis=1
    )
    pack = place(spread(own_pack, "expert"), exp, n_exp)
    pack = place([pack] + [shift_z(pack, k) for k in range(1, n_z)], z, n_z)
    other_pack = swap_core(pack)
    low = core == 0
    pack = jnp.stack(
        [jnp.where(low, pack, other_pack), jnp.where(low, other_pack, pack)], axis=1
    ).reshape(model, own_pack.shape[1])
    side = pack[:, 4 * width :]
    router_all = side[:, :expert_count]
    gain_one = side[:, expert_count].astype(F32)[None, :]
    gain_two = side[:, expert_count + 1].astype(F32)[None, :]

    def full_rows(value):
        parts = place(spread(value, "heads"), head, n_heads)
        return jnp.concatenate([parts[i] for i in range(n_heads)], axis=-1)

    inputs = full_rows(block_in)

    def expert_weight(weight):
        by_core = weight.reshape(weight.shape[0], CORES, local, hidden_width).transpose(1, 2, 0, 3)
        other = swap_core(take(by_core, 1 - core))
        mine = take(by_core, core)
        piece = jnp.concatenate(
            [jnp.where(low, mine, other), jnp.where(low, other, mine)], axis=1
        )
        pieces = [piece]
        for _ in range(1, n_z):
            pieces.append(shift_z(pieces[-1], 1))
        return place(pieces, z, n_z)

    out_all = expert_weight(w_out)
    in_all = expert_weight(w_in)

    def blocks_of(value):
        along = jnp.stack(spread(value, "expert"))
        return jnp.concatenate([along, swap_core(along)])

    grad_full = full_rows(cotangent).reshape(tokens, model)
    grads_all = blocks_of(grad_full)
    ids = route_ids.reshape(tokens, 2).T
    ids_all = blocks_of(ids)
    blocks = n_exp * CORES
    first_expert = exp * group + core * local
    named = first_expert + jnp.arange(local, dtype=jnp.int32)
    chosen = jnp.any(ids_all[:, None, :, :] == named[None, :, None, None], axis=2)
    before = (
        jnp.arange(tokens)[:, None] < jnp.arange(tokens)[None, :]
    ).astype(BF16)
    rank = jnp.dot(
        chosen.astype(BF16).reshape(blocks * local, tokens), before, preferred_element_type=F32
    ).astype(jnp.int32).reshape(blocks, local, tokens)
    slot_of = jnp.where(chosen, rank, -1)
    slot_cols = slot_of.transpose(0, 2, 1)

    part, qkv, ctx = attend(inputs, gain_one, pack, width)
    part_other = shift(part, "heads", 1)
    for k in range(2, n_heads):
        part_other = part_other + shift(part, "heads", k)
    middle = (inputs.astype(F32) + (part.astype(F32) + part_other.astype(F32))).reshape(
        tokens, model
    )
    unit_two, scale_two = norm_parts(middle)
    normed_two = (unit_two * gain_two).astype(BF16)
    tokens_all = blocks_of(normed_two)

    logits = jnp.einsum("de,btd->bet", router_all, tokens_all, preferred_element_type=F32)
    probs = jax.nn.softmax(logits, axis=1)
    own_probs = lax.dynamic_slice_in_dim(probs, first_expert, local, 1)

    rows, grows, gact, dhid, dgate, drows, yrows = run_experts(
        slot_of[:, :, None, :], own_probs[:, :, None, :], tokens_all, grads_all, in_all, out_all, slots
    )

    def ring_sum(total):
        moving = take(total, (z - 1) % n_z)
        for step in range(1, n_z):
            arrived = shift_z(moving, 1)
            mine = take(total, (z - 1 - step) % n_z)
            moving = arrived.astype(F32) + mine.astype(F32)
            if step < n_z - 1:
                moving = moving.astype(BF16)
        halves = moving.reshape(local, CORES, w_in.shape[0], hidden_width)
        other = swap_core(take(halves, 1 - core, 1).astype(BF16)).astype(F32)
        mine = take(halves, core, 1)
        joined = jnp.concatenate(
            [jnp.where(low, mine, other), jnp.where(low, other, mine)], axis=0
        )
        return joined.transpose(1, 0, 2)

    grad_w_in = ring_sum(weight_grad(rows, dhid, n_z))
    grad_w_out = ring_sum(weight_grad(grows, gact, n_z))

    at = jnp.arange(slots, dtype=jnp.int32)
    dchosen = jnp.sum(
        jnp.where(slot_of[:, :, None, :] == at[None, None, :, None], dgate, 0.0), axis=2
    )
    dprobs = lax.dynamic_update_slice_in_dim(jnp.zeros_like(probs), dchosen, first_expert, 1)
    dlogits = (probs * (dprobs - jnp.sum(dprobs * probs, axis=1, keepdims=True))).astype(BF16)
    grad_router = jnp.einsum("btd,bet->de", tokens_all, dlogits, preferred_element_type=F32)

    def home(partial):
        keep, send = partial[:n_exp], partial[n_exp:]
        total = keep.astype(F32) + swap_core(send).astype(F32)
        own = total[0]
        for k in range(1, n_exp):
            own = own + shift(total[k].astype(BF16), "expert", -k).astype(F32)
        return own

    dsum = home(combine(slot_cols, drows, (dlogits, router_all))).astype(BF16)
    dsum_other = shift(dsum, "heads", 1)
    for k in range(2, n_heads):
        dsum_other = dsum_other + shift(dsum, "heads", k)
    dnormed_two = dsum.astype(F32) + dsum_other.astype(F32)
    scaled = dnormed_two * gain_two
    grad_gain_two = jnp.sum(dnormed_two * unit_two, axis=0)
    dmiddle = grad_full.astype(F32) + scale_two * (
        scaled
        - jnp.mean(scaled, axis=-1, keepdims=True)
        - unit_two * jnp.mean(scaled * unit_two, axis=-1, keepdims=True)
    )
    datt = dmiddle.astype(BF16).reshape(images, seq, model)

    yrows, datt = lax.optimization_barrier((yrows, datt))
    y_own = home(combine(slot_cols, yrows)).astype(BF16)
    y_parts = y_own.reshape(tokens, n_heads, half_width).transpose(1, 0, 2)
    y_total = take(y_parts, head).astype(F32)
    for k in range(1, n_heads):
        y_total = y_total + shift(take(y_parts, (head + k) % n_heads), "heads", k).astype(F32)
    middle_own = lax.dynamic_slice_in_dim(middle, head * half_width, half_width, 1)
    block_out = (middle_own + y_total).astype(BF16).reshape(images, seq, half_width)

    dnorm, stats, dgain_one, dw_qkv, dw_o = attend_back(
        inputs, gain_one, datt, qkv, ctx, pack, width
    )
    dn_parts = dnorm.reshape(tokens, n_heads, half_width).transpose(1, 0, 2)
    dn_own = take(dn_parts, head).astype(F32)
    sums = stats.reshape(tokens, 128)[:, :2].T
    sums_total = sums
    for k in range(1, n_heads):
        dn_own = dn_own + shift(take(dn_parts, (head + k) % n_heads), "heads", k).astype(F32)
        sums_total = sums_total + shift(sums, "heads", k)
    unit_one, scale_one = norm_parts(inputs.astype(F32).reshape(tokens, model))
    unit_own = lax.dynamic_slice_in_dim(unit_one, head * half_width, half_width, 1)
    gain_own = lax.dynamic_slice_in_dim(gain_one, head * half_width, half_width, 1)
    dmiddle_own = lax.dynamic_slice_in_dim(dmiddle, head * half_width, half_width, 1)
    grad_in = dmiddle_own + scale_one * (
        dn_own * gain_own
        - sums_total[0][:, None] / model
        - unit_own * (sums_total[1][:, None] / model)
    )
    grad_block_in = grad_in.astype(BF16).reshape(images, seq, half_width)

    dside = jnp.concatenate(
        [grad_router, dgain_one.T, grad_gain_two[:, None],
         jnp.zeros((model, rest - expert_count - 2), F32)], axis=1
    )
    dpack = jnp.concatenate(
        [dw_qkv.astype(BF16), dw_o.astype(BF16), dside.astype(BF16)], axis=1
    ).reshape(n_z, CORES, n_exp, own_pack.shape[0], own_pack.shape[1])
    dsent = swap_core(take(dpack, 1 - core, 1))
    dpack = (take(dpack, core, 1).astype(F32) + dsent.astype(F32)).astype(BF16)
    dtotal = take(dpack, exp, 1).astype(F32)
    for k in range(1, n_exp):
        dtotal = dtotal + shift(take(dpack, (exp + k) % n_exp, 1), "expert", k).astype(F32)
    dpack = dtotal.astype(BF16)
    dtotal = take(dpack, z).astype(F32)
    for k in range(1, n_z):
        dtotal = dtotal + shift_z(take(dpack, (z + k) % n_z), k).astype(F32)
    dside = dtotal[:, 4 * width :]
    over_heads = dside[:, : expert_count + 1].T
    summed = over_heads
    for k in range(1, n_heads):
        summed = summed + shift(over_heads, "heads", k)
    return (
        block_out,
        grad_block_in,
        summed[expert_count],
        dtotal[:, : 3 * width].reshape(-1, 3, width),
        dtotal[:, 3 * width : 4 * width],
        dside[:, expert_count + 1],
        summed[:expert_count].T,
        grad_w_in,
        grad_w_out,
    )


def solution(mesh):
    return jax.shard_map(
        per_device,
        mesh=mesh,
        in_specs=(
            P(("dp", "expert"), None, "heads"),
            P(("dp", "expert"), None, "heads"),
            P(("dp", "expert"), None, None),
            P(("dp", "expert")),
            P(("dp", "expert"), None, "heads"),
            P(("dp", "expert"), "heads"),
            P(("dp", "expert")),
            P(("dp", "expert"), None),
            P("dp", "expert", "heads"),
            P("dp", "expert", "heads"),
        ),
        out_specs=(
            P(("dp", "expert"), None, "heads"),
            P(("dp", "expert"), None, "heads"),
            P(("dp", "expert")),
            P(("dp", "expert"), None, "heads"),
            P(("dp", "expert"), "heads"),
            P(("dp", "expert")),
            P(("dp", "expert"), None),
            P("dp", "expert", "heads"),
            P("dp", "expert", "heads"),
        ),
        check_vma=False,
    )
```

```python
import functools

import jax
import jax.numpy as jnp
from jax import lax
from jax.experimental import pallas as pl
from jax.experimental.pallas import tpu as pltpu
from jax.sharding import PartitionSpec as P

HEAD_DIM = 64
CORES = 2
EPS = 1e-06
LOW = -1e30
F32 = jnp.float32
BF16 = jnp.bfloat16
VMEM_LIMIT = 56 * 1024 * 1024


def dot(a, b, ca, cb):
    return lax.dot_general(a, b, (((ca,), (cb,)), ((), ())), preferred_element_type=F32)


def shaped(shape, kind):
    return jax.ShapeDtypeStruct(shape, kind)


def params(dims=1):
    return pltpu.CompilerParams(
        dimension_semantics=("arbitrary",) * dims, vmem_limit_bytes=VMEM_LIMIT
    )


def cost(flops, size, powers=0):
    return pl.CostEstimate(flops=flops, bytes_accessed=size, transcendentals=powers)


def after(value, *others):
    return lax.optimization_barrier((value,) + others)[0]


def norm_parts(rows):
    average = jnp.mean(rows, axis=-1, keepdims=True)
    centred = rows - average
    spread = jnp.mean(centred * centred, axis=-1, keepdims=True)
    scale = lax.rsqrt(spread + EPS)
    return centred * scale, scale


def softmax_rows(q, own_k, real):
    scores = jnp.where(real, dot(q, own_k, 1, 1) * (HEAD_DIM**-0.5), LOW)
    powers = jnp.exp(scores - jnp.max(scores, axis=-1, keepdims=True))
    return powers / jnp.sum(powers, axis=-1, keepdims=True)


def attend_kernel(seq, x_ref, gain_ref, wqkv_ref, wo_ref, part_ref, qkv_ref, ctx_ref):
    width = wo_ref.shape[1]
    span = x_ref.shape[0]
    unit, _ = norm_parts(x_ref[...].astype(F32))
    normed = (unit * gain_ref[...]).astype(BF16)
    for part in range(3):
        cols = slice(part * width, (part + 1) * width)
        qkv_ref[:, cols] = dot(normed, wqkv_ref[:, cols], 1, 0).astype(BF16)
    lane = lax.broadcasted_iota(jnp.int32, (span, 128), 1)
    real = lax.broadcasted_iota(jnp.int32, (span, span), 1) < seq
    for pair in range(width // 128):
        q, k, v = (
            qkv_ref[:, part * width + pair * 128 : part * width + (pair + 1) * 128]
            for part in range(3)
        )
        ctx = jnp.zeros((span, 128), F32)
        for side in range(2):
            mine = (lane >= 64) if side else (lane < 64)
            own_k = jnp.where(mine, k, jnp.zeros_like(k))
            own_v = jnp.where(mine, v, jnp.zeros_like(v))
            weights = softmax_rows(q, own_k, real)
            ctx = ctx + dot(weights.astype(BF16), own_v, 1, 0)
        ctx_ref[:, pair * 128 : (pair + 1) * 128] = ctx.astype(BF16)
    part_ref[...] = dot(ctx_ref[...], wo_ref[...], 1, 1).astype(BF16)


def attend(inputs, gain, packed, width, images, seq):
    rows, model = inputs.shape
    span = rows // images
    image = lambda last: pl.BlockSpec((span, last), lambda i: (i, 0))
    return pl.pallas_call(
        functools.partial(attend_kernel, seq),
        grid=(images,),
        in_specs=[
            image(model),
            pl.BlockSpec((1, model), lambda i: (0, 0)),
            pl.BlockSpec((model, 3 * width), lambda i: (0, 0)),
            pl.BlockSpec((model, width), lambda i: (0, 3)),
        ],
        out_specs=[image(model), image(3 * width), image(width)],
        out_shape=[
            shaped((rows, model), BF16), shaped((rows, 3 * width), BF16), shaped((rows, width), BF16)
        ],
        compiler_params=params(),
        cost_estimate=cost(10 * rows * model * width, 8 * rows * model, rows * span * width // 64),
        name="attend",
    )(inputs, gain, packed, packed)


def attend_back_kernel(
    seq, gain_at,
    x_ref, gain_ref, datt_ref, qkv_ref, ctx_ref, wqkv_ref, wo_ref, side_ref,
    dnorm_ref, stats_ref, pack_ref, dproj_ref, dgain_ref, dwqkv_ref, dwo_ref,
):
    width = wo_ref.shape[1]
    span, model = x_ref.shape
    step = pl.program_id(0)

    @pl.when(step == 0)
    def _():
        dgain_ref[...] = jnp.zeros_like(dgain_ref)
        dwqkv_ref[...] = jnp.zeros_like(dwqkv_ref)
        dwo_ref[...] = jnp.zeros_like(dwo_ref)

    datt = datt_ref[...]
    dwo_ref[...] += dot(datt, ctx_ref[...], 0, 0)
    dctx_all = dot(datt, wo_ref[...], 1, 0).astype(BF16)
    lane = lax.broadcasted_iota(jnp.int32, (span, 128), 1)
    real = lax.broadcasted_iota(jnp.int32, (span, span), 1) < seq
    for pair in range(width // 128):
        q, k, v = (
            qkv_ref[:, part * width + pair * 128 : part * width + (pair + 1) * 128]
            for part in range(3)
        )
        dctx = dctx_all[:, pair * 128 : (pair + 1) * 128]
        dq = jnp.zeros((span, 128), F32)
        dk = jnp.zeros((span, 128), F32)
        dv = jnp.zeros((span, 128), F32)
        for side in range(2):
            mine = (lane >= 64) if side else (lane < 64)
            own = lambda t: jnp.where(mine, t, jnp.zeros_like(t))
            own_k, own_v = own(k), own(v)
            weights = softmax_rows(q, own_k, real)
            dweights = dot(dctx, own_v, 1, 1)
            inner = jnp.sum(dweights * weights, axis=-1, keepdims=True)
            dscores = (weights * (dweights - inner)).astype(BF16)
            dq = dq + dot(dscores, own_k, 1, 0)
            dk = dk + dot(dscores, own(q), 0, 0)
            dv = dv + dot(weights.astype(BF16), own(dctx), 0, 0)
        for part, value in enumerate((dq * HEAD_DIM**-0.5, dk * HEAD_DIM**-0.5, dv)):
            start = part * width + pair * 128
            dproj_ref[:, start : start + 128] = value.astype(BF16)
    dproj = dproj_ref[...]
    gain = gain_ref[...]
    unit, _ = norm_parts(x_ref[...].astype(F32))
    normed = (unit * gain).astype(BF16)
    dwqkv_ref[...] += dot(normed, dproj, 0, 0)
    dnormed = dot(dproj, wqkv_ref[...], 1, 1)
    halves, _, half = dnorm_ref.shape
    for h in range(halves):
        dnorm_ref[h] = dnormed[:, h * half : (h + 1) * half].astype(BF16)
    along = dnormed * unit
    dgain_ref[...] += jnp.sum(along, axis=0, keepdims=True)
    first = jnp.sum(dnormed * gain, axis=-1, keepdims=True)
    second = jnp.sum(along * gain, axis=-1, keepdims=True)
    stats_ref[...] = jnp.where(lane == 0, first, jnp.where(lane == 1, second, 0.0))

    @pl.when(step == pl.num_programs(0) - 1)
    def _():
        pack_ref[:, : 3 * width] = dwqkv_ref[...].astype(BF16)
        pack_ref[:, 3 * width : 4 * width] = dwo_ref[...].astype(BF16)
        line = lax.broadcasted_iota(jnp.int32, (128, model), 0)
        column = jnp.where(line == gain_at, dgain_ref[...], 0.0).T
        pack_ref[:, 4 * width :] = (side_ref[...] + column).astype(BF16)


def attend_back(inputs, gain, datt, qkv, ctx, packed, dside, gain_at, width, images, seq, halves):
    rows, model = inputs.shape
    span = rows // images
    image = lambda last: pl.BlockSpec((span, last), lambda i: (i, 0))
    fixed = lambda *size: pl.BlockSpec(size, lambda i: (0, 0))
    return pl.pallas_call(
        functools.partial(attend_back_kernel, seq, gain_at),
        grid=(images,),
        in_specs=[
            image(model), fixed(1, model), image(model), image(3 * width), image(width),
            fixed(model, 3 * width), pl.BlockSpec((model, width), lambda i: (0, 3)),
            fixed(model, 128),
        ],
        out_specs=[
            pl.BlockSpec((halves, span, model // halves), lambda i: (0, i, 0)),
            image(128),
            fixed(*packed.shape),
        ],
        out_shape=[
            shaped((halves, rows, model // halves), BF16),
            shaped((rows, 128), F32),
            shaped(packed.shape, BF16),
        ],
        scratch_shapes=[
            pltpu.VMEM((span, 3 * width), BF16),
            pltpu.VMEM((1, model), F32),
            pltpu.VMEM((model, 3 * width), F32),
            pltpu.VMEM((model, width), F32),
        ],
        compiler_params=params(),
        cost_estimate=cost(28 * rows * model * width, 12 * rows * model, rows * span * width // 64),
        name="attend_back",
    )(inputs, gain, datt, qkv, ctx, packed, packed, dside)


def expert_kernel(depth, blocks, place_ref, slot_ref, router_ref, *refs):
    x_refs, refs = refs[:blocks], refs[blocks:]
    grad_refs, refs = refs[:blocks], refs[blocks:]
    win_refs, refs = refs[:depth], refs[depth:]
    wout_refs, refs = refs[:depth], refs[depth:]
    (
        rows_ref, grows_ref, gact_ref, dhid_ref, dchosen_ref, drows_ref, yrows_ref, probs_ref,
        win_all, wout_all,
    ) = refs
    _, slots, model = rows_ref.shape
    tokens = x_refs[0].shape[0]
    part_rows, width = win_refs[0].shape[-2:]
    step = pl.program_id(0)

    @pl.when(step == 0)
    def _():
        for k in range(depth):
            owner = lax.rem(place_ref[0] - k + depth, depth)
            at = pl.ds(pl.multiple_of(owner * part_rows, 16), part_rows)
            win_all[at, :] = win_refs[k][...]
            wout_all[at, :] = wout_refs[k][0]

    mask = lax.broadcasted_iota(jnp.int32, (slots, tokens), 0) == slot_ref[0]
    pick = jnp.where(mask, 1.0, 0.0).astype(BF16)
    for b in range(blocks):

        @pl.when(step == b)
        def _(b=b):
            rows_ref[0] = dot(pick, x_refs[b][...], 1, 0).astype(BF16)
            grows_ref[0] = dot(pick, grad_refs[b][...], 1, 0).astype(BF16)
            logits = dot(router_ref[...], x_refs[b][...], 1, 1)
            powers = jnp.exp(logits - jnp.max(logits, axis=0, keepdims=True))
            probs_ref[0] = powers / jnp.sum(powers, axis=0, keepdims=True)

    probs = probs_ref[0]
    line = lax.broadcasted_iota(jnp.int32, probs.shape, 0)
    own = jnp.sum(jnp.where(line == place_ref[1], probs, 0.0), axis=0, keepdims=True)
    gate = jnp.sum(jnp.where(mask, own, 0.0), axis=1, keepdims=True)
    rows, grows = rows_ref[0], grows_ref[0]
    dgate = jnp.zeros((slots, 1), F32)
    drows = jnp.zeros((slots, model), F32)
    yrows = jnp.zeros((slots, model), F32)
    tile = 512 if width % 512 == 0 else width
    curve = 0.7978845608028654
    for start in range(0, width, tile):
        cols = slice(start, start + tile)
        win, wout = win_all[:, cols], wout_all[:, cols]
        hidden = dot(rows, win, 1, 0)
        pulled = dot(grows, wout, 1, 0)
        square = hidden * hidden
        bend = jnp.tanh(hidden * (curve + curve * 0.044715 * square))
        half = 0.5 + 0.5 * bend
        active = hidden * half
        slope = half + 0.5 * hidden * (1.0 - bend * bend) * (
            curve + 3.0 * curve * 0.044715 * square
        )
        dgate = dgate + jnp.sum(active * pulled, axis=1, keepdims=True)
        gact = (gate * active).astype(BF16)
        dhid = (gate * pulled * slope).astype(BF16)
        gact_ref[0, :, cols] = gact
        dhid_ref[0, :, cols] = dhid
        drows = drows + dot(dhid, win, 1, 1)
        yrows = yrows + dot(gact, wout, 1, 1)
    dchosen_ref[0] = jnp.sum(jnp.where(mask, dgate, 0.0), axis=0, keepdims=True)
    drows_ref[0] = drows.astype(BF16)
    yrows_ref[0] = yrows.astype(BF16)


def run_expert(index, place, slot_of, router_rows, xs, grads, w_in, w_out, slots):
    blocks, depth = len(xs), len(w_in)
    tokens, model = xs[0].shape
    part_rows, width = w_in[0].shape
    experts = router_rows.shape[0]
    fixed = lambda *size: pl.BlockSpec(
        size, lambda b, s: (0,) * len(size), pipeline_mode=pl.Buffered(1)
    )
    block = lambda *size: pl.BlockSpec((1,) + size, lambda b, s: (b, 0, 0))
    return pl.pallas_call(
        functools.partial(expert_kernel, depth, blocks),
        grid_spec=pltpu.PrefetchScalarGridSpec(
            num_scalar_prefetch=1,
            grid=(blocks,),
            in_specs=[block(1, tokens), fixed(experts, model)]
            + [fixed(tokens, model)] * (2 * blocks)
            + [fixed(part_rows, width)] * depth
            + [
                pl.BlockSpec(
                    (1, part_rows, width), lambda b, s: (index, 0, 0),
                    pipeline_mode=pl.Buffered(1),
                )
            ]
            * depth,
            out_specs=[
                block(slots, model), block(slots, model), block(slots, width), block(slots, width),
                block(1, tokens), block(slots, model), block(slots, model), block(experts, tokens),
            ],
            scratch_shapes=[pltpu.VMEM((model, width), BF16)] * 2,
        ),
        out_shape=[
            shaped((blocks, slots, model), BF16), shaped((blocks, slots, model), BF16),
            shaped((blocks, slots, width), BF16), shaped((blocks, slots, width), BF16),
            shaped((blocks, 1, tokens), F32), shaped((blocks, slots, model), BF16),
            shaped((blocks, slots, model), BF16), shaped((blocks, experts, tokens), F32),
        ],
        compiler_params=params(),
        cost_estimate=cost(
            8 * blocks * slots * model * width + 4 * blocks * slots * model * tokens,
            16 * blocks * slots * model,
            blocks * slots * width,
        ),
        name="expert",
    )(place, slot_of, router_rows, *xs, *grads, *w_in, *w_out)


def weight_grad_kernel(depth, place_ref, rows_ref, cols_ref, *refs):
    out_refs, total_ref = refs[:depth], refs[depth]
    blocks, slots, model = rows_ref.shape
    tile = cols_ref.shape[2]
    part_rows = model // depth
    left = rows_ref[...].reshape(blocks * slots, model)
    right = cols_ref[...].reshape(blocks * slots, tile)
    total_ref[...] = dot(left, right, 0, 0)
    for k in range(depth):
        owner = lax.rem(place_ref[0] - k + depth, depth)
        at = pl.ds(pl.multiple_of(owner * part_rows, 16), part_rows)
        out_refs[k][...] = total_ref[at, :].astype(BF16)


def weight_grad(place, rows, cols, depth):
    blocks, slots, model = rows.shape
    width = cols.shape[2]
    tile = width // 2 if width % 256 == 0 else width
    return pl.pallas_call(
        functools.partial(weight_grad_kernel, depth),
        grid_spec=pltpu.PrefetchScalarGridSpec(
            num_scalar_prefetch=1,
            grid=(width // tile,),
            in_specs=[
                pl.BlockSpec((blocks, slots, model), lambda f, s: (0, 0, 0)),
                pl.BlockSpec((blocks, slots, tile), lambda f, s: (0, 0, f)),
            ],
            out_specs=[pl.BlockSpec((model // depth, tile), lambda f, s: (0, f))] * depth,
            scratch_shapes=[pltpu.VMEM((model, tile), F32)],
        ),
        out_shape=[shaped((model // depth, width), BF16)] * depth,
        compiler_params=params(),
        cost_estimate=cost(
            2 * blocks * slots * model * width,
            2 * (blocks * slots * (model + width) + model * width),
        ),
        name="weight_grad",
    )(place, rows, cols)


def combine_kernel(local, added, slot_ref, *refs):
    rows_refs, refs = refs[:local], refs[local:]
    out_ref = refs[-1]
    tokens = out_ref.shape[-2]
    slots, model = rows_refs[0].shape[1:]
    at = lax.broadcasted_iota(jnp.int32, (tokens, slots), 1)
    total = refs[0][...].astype(F32) if added else jnp.zeros((tokens, model), F32)
    for e in range(local):
        pick = jnp.where(at == slot_ref[0, :, e : e + 1], 1.0, 0.0).astype(BF16)
        total = total + dot(pick, rows_refs[e][0], 1, 0)
    out_ref[...] = total.astype(BF16)


def combine(slot_cols, rows, b, add=None):
    _, tokens, local = slot_cols.shape
    slots, model = rows[0].shape[1:]
    whole = pl.BlockSpec((tokens, model), lambda i: (0, 0))
    return pl.pallas_call(
        functools.partial(combine_kernel, local, add is not None),
        grid=(1,),
        in_specs=[pl.BlockSpec((1, tokens, local), lambda i: (b, 0, 0))]
        + [pl.BlockSpec((1, slots, model), lambda i: (b, 0, 0))] * local
        + [whole] * (add is not None),
        out_specs=whole,
        out_shape=shaped((tokens, model), BF16),
        compiler_params=params(),
        cost_estimate=cost(
            2 * local * slots * model * tokens, 2 * model * (local * slots + 2 * tokens)
        ),
        name="combine",
    )(slot_cols, *rows, *(() if add is None else (add,)))


def combine_back_kernel(local, added, place_ref, slot_ref, *refs):
    rows_refs, refs = refs[:local], refs[local:]
    dchosen_refs, refs = refs[:local], refs[local:]
    probs_ref, router_ref, x_ref = refs[:3]
    out_ref, drouter_ref = refs[-2:]
    tokens = out_ref.shape[0]
    slots = rows_refs[0].shape[1]
    at = lax.broadcasted_iota(jnp.int32, (tokens, slots), 1)
    probs = probs_ref[0]
    line = lax.broadcasted_iota(jnp.int32, probs.shape, 0)
    dprobs = jnp.zeros_like(probs)
    for e in range(local):
        dprobs = jnp.where(line == place_ref[1] + e, dchosen_refs[e][0], dprobs)
    inner = jnp.sum(dprobs * probs, axis=0, keepdims=True)
    dlogits = (probs * (dprobs - inner)).astype(BF16)
    drouter_ref[...] = dot(dlogits, x_ref[...], 1, 0)
    total = dot(dlogits, router_ref[...], 0, 0)
    if added:
        total = total + refs[3][...].astype(F32)
    for e in range(local):
        pick = jnp.where(at == slot_ref[0, :, e : e + 1], 1.0, 0.0).astype(BF16)
        total = total + dot(pick, rows_refs[e][0], 1, 0)
    out_ref[...] = total.astype(BF16)


def combine_back(place, slot_cols, rows, dchosen, probs, router_rows, x, b, add=None):
    _, tokens, local = slot_cols.shape
    slots, model = rows[0].shape[1:]
    experts = router_rows.shape[0]
    whole = pl.BlockSpec((tokens, model), lambda i, s: (0, 0))
    block = lambda *size: pl.BlockSpec((1,) + size, lambda i, s: (b, 0, 0))
    small = pl.BlockSpec((experts, model), lambda i, s: (0, 0))
    return pl.pallas_call(
        functools.partial(combine_back_kernel, local, add is not None),
        grid_spec=pltpu.PrefetchScalarGridSpec(
            num_scalar_prefetch=1,
            grid=(1,),
            in_specs=[block(tokens, local)]
            + [block(slots, model)] * local
            + [block(1, tokens)] * local
            + [block(experts, tokens), small, whole]
            + [whole] * (add is not None),
            out_specs=[whole, small],
        ),
        out_shape=[shaped((tokens, model), BF16), shaped((experts, model), F32)],
        compiler_params=params(),
        cost_estimate=cost(
            2 * local * slots * model * tokens, 2 * model * (local * slots + 3 * tokens)
        ),
        name="combine_back",
    )(place, slot_cols, *rows, *dchosen, probs, router_rows, x, *(() if add is None else (add,)))


def per_device(
    block_in, cotangent, route_ids, gain_attn, w_qkv, w_out_attn, gain_moe, router, w_in, w_out
):
    n_dp, n_heads, n_exp = (lax.axis_size(name) for name in ("dp", "heads", "expert"))
    n_z = n_dp // CORES
    dp, head, exp = (lax.axis_index(name) for name in ("dp", "heads", "expert"))
    z, core = dp // CORES, dp % CORES
    low = core == 0
    images, seq, half_width = block_in.shape
    span = -(-seq // 16) * 16
    rows = images * span
    model = half_width * n_heads
    width = w_qkv.shape[2]
    shard = w_qkv.shape[0]
    expert_count = router.shape[1]
    group = w_in.shape[1]
    local = group // CORES
    part_rows, _, hidden_width = w_in.shape
    capacity = 20 * images * seq // (7 * expert_count)
    slots = -(-capacity // 16) * 16
    blocks = n_exp * CORES
    rest = 128

    def shift(value, axis, step):
        size = lax.axis_size(axis)
        return lax.ppermute(value, axis, [(i, (i + step) % size) for i in range(size)])

    def shift_z(value, step):
        pairs = [
            (a * CORES + c, ((a + step) % n_z) * CORES + c) for a in range(n_z) for c in range(CORES)
        ]
        return lax.ppermute(value, "dp", pairs)

    def swap_core(value):
        return lax.ppermute(value, "dp", [(i, i ^ 1) for i in range(n_dp)])

    def place_at(pieces, index, count):
        if count == 2:
            first = index == 0
            return jnp.stack(
                [jnp.where(first, pieces[0], pieces[1]), jnp.where(first, pieces[1], pieces[0])]
            )
        out = jnp.zeros((count,) + pieces[0].shape, pieces[0].dtype)
        for k, piece in enumerate(pieces):
            out = lax.dynamic_update_index_in_dim(out, piece, (index - k) % count, 0)
        return out

    def spread(value, axis):
        return [value] + [shift(value, axis, k) for k in range(1, lax.axis_size(axis))]

    def take(value, index, dim=0):
        return lax.dynamic_index_in_dim(value, index, dim, keepdims=False)

    tail = jnp.concatenate(
        [router, gain_attn[:, None], gain_moe[:, None],
         jnp.zeros((shard, rest - expert_count - 2), BF16)], axis=1
    )
    own_pack = jnp.concatenate([w_qkv.reshape(shard, 3 * width), w_out_attn, tail], axis=1)
    columns = own_pack.shape[1]
    pack_z = place_at([own_pack] + [shift_z(own_pack, k) for k in range(1, n_z)], z, n_z)
    pack = place_at(spread(pack_z, "expert"), exp, n_exp)
    other_pack = swap_core(pack)
    pack = jnp.stack([jnp.where(low, pack, other_pack), jnp.where(low, other_pack, pack)])
    pack = pack.transpose(2, 0, 1, 3, 4).reshape(model, columns)
    side = pack[:, 4 * width :].T
    router_rows = side[:expert_count]
    gain_one = side[expert_count : expert_count + 1].astype(F32)
    gain_two = side[expert_count + 1 : expert_count + 2].astype(F32)

    def full_rows(value):
        padded = jnp.pad(value, ((0, 0), (0, span - seq), (0, 0))).reshape(rows, half_width)
        parts = place_at(spread(padded, "heads"), head, n_heads)
        return jnp.concatenate([parts[i] for i in range(n_heads)], axis=-1)

    inputs = full_rows(block_in)

    def expert_shards(weight):
        by_core = weight.reshape(part_rows, CORES, local, hidden_width).transpose(1, 2, 0, 3)
        other = swap_core(take(by_core, 1 - core))
        mine = take(by_core, core)
        return jnp.concatenate(
            [jnp.where(low, mine, other), jnp.where(low, other, mine)], axis=1
        )

    def ring(piece):
        pieces = [piece]
        for _ in range(1, n_z):
            pieces.append(shift_z(pieces[-1], 1))
        return pieces

    out_pieces = ring(expert_shards(w_out))
    in_shards = expert_shards(w_in)
    in_pieces = []
    for e in range(local):
        hold = pack_z if e == 0 else out_pieces[1]
        in_pieces.append(ring(after(in_shards[e], hold)))

    def blocks_of(value, hold=()):
        along = spread(value, "expert")
        along = along[:1] + [after(part, *hold) for part in along[1:]]
        return along + [swap_core(part) for part in along]

    ids = jnp.pad(route_ids, ((0, 0), (0, span - seq), (0, 0)), constant_values=-1)
    ids_all = jnp.stack(blocks_of(ids.reshape(rows, 2).T))
    first_expert = exp * group + core * local
    named = first_expert + jnp.arange(local, dtype=jnp.int32)
    chosen = jnp.any(ids_all[:, None, :, :] == named[None, :, None, None], axis=2)
    before = (jnp.arange(rows)[:, None] < jnp.arange(rows)[None, :]).astype(BF16)
    rank = jnp.dot(
        chosen.astype(BF16).reshape(blocks * local, rows), before, preferred_element_type=F32
    ).astype(jnp.int32).reshape(blocks, local, rows)
    slot_of = jnp.where(chosen, rank, -1)
    slot_cols = slot_of.transpose(0, 2, 1)
    place = [jnp.stack([z, first_expert + e]).astype(jnp.int32) for e in range(local)]

    inputs_ready = after(inputs, out_pieces[1])
    part, qkv, ctx = attend(inputs_ready, gain_one, pack, width, images, seq)
    grad_full = full_rows(after(cotangent, pack_z))
    grads_all = blocks_of(grad_full)
    part_other = shift(part, "heads", 1)
    for k in range(2, n_heads):
        part_other = part_other + shift(part, "heads", k)
    part_other = after(part_other, out_pieces[min(2, n_z - 1)], in_pieces[0][1])
    middle = inputs.astype(F32) + (part.astype(F32) + part_other.astype(F32))
    unit_two, scale_two = norm_parts(middle)
    normed_two = (unit_two * gain_two).astype(BF16)
    tokens_all = blocks_of(
        normed_two, [pieces[min(2 - e, n_z - 1)] for e, pieces in enumerate(in_pieces[:2])]
    )

    done = []
    moving = []
    mine = []
    for e in range(local):
        shards_in = [p for p in in_pieces[e]]
        if e:
            shards_in[0] = after(shards_in[0], *[m[0] for m in moving])
        result = run_expert(
            e, place[e], slot_of[:, e : e + 1, :], router_rows, tokens_all, grads_all,
            shards_in, out_pieces, slots,
        )
        done.append(result)
        rows_e, grows_e, gact_e, dhid_e = result[:4]
        for left, right in ((grows_e, gact_e), (rows_e, dhid_e)):
            chunks = weight_grad(place[e], left, right, n_z)
            mine.append(chunks)
            moving.append([chunks[1 % n_z]])
    drows, yrows, dchosen = ([r[i] for r in done] for i in (5, 6, 4))
    probs = done[0][7]

    def back_of(b, add=None):
        return combine_back(
            place[0], slot_cols, drows, dchosen, probs, router_rows, tokens_all[b], b, add
        )

    drouter = jnp.zeros((expert_count, model), F32)
    arrived = [None] * n_exp
    for k in reversed(range(n_exp)):
        sent, more = back_of(n_exp + k)
        arrived[k] = swap_core(sent)
        drouter = drouter + more
    from_exp = []
    for k in reversed(range(n_exp)):
        total, more = back_of(k, arrived[k])
        drouter = drouter + more
        if k:
            from_exp.append(shift(total, "expert", -k))
    dsum = total.astype(F32)
    for value in from_exp:
        dsum = dsum + value.astype(F32)
    dsum = dsum.astype(BF16)

    def ring_step(number, hold):
        for r in range(len(moving)):
            came = shift_z(moving[r][-1], 1)
            own = after(mine[r][(number + 1) % n_z], hold)
            total = came.astype(F32) + own.astype(F32)
            moving[r].append(total if number == n_z - 1 else total.astype(BF16))

    ring_step(1, dsum)
    dsum_other = shift(dsum, "heads", 1)
    for k in range(2, n_heads):
        dsum_other = dsum_other + shift(dsum, "heads", k)
    dnormed_two = dsum.astype(F32) + dsum_other.astype(F32)
    scaled = dnormed_two * gain_two
    grad_gain_two = jnp.sum(dnormed_two * unit_two, axis=0)
    dmiddle = grad_full.astype(F32) + scale_two * (
        scaled
        - jnp.mean(scaled, axis=-1, keepdims=True)
        - unit_two * jnp.mean(scaled * unit_two, axis=-1, keepdims=True)
    )
    datt = dmiddle.astype(BF16)
    for number in range(2, n_z - 1):
        ring_step(number, datt)

    dside = jnp.concatenate(
        [drouter, jnp.zeros((1, model), F32), grad_gain_two[None, :],
         jnp.zeros((rest - expert_count - 2, model), F32)], axis=0
    ).T
    dnorm, stats, dpack = attend_back(
        inputs, gain_one, datt, qkv, ctx, pack, dside, expert_count, width, images, seq, n_heads
    )
    if n_z > 2:
        ring_step(n_z - 1, dpack)

    dpack = dpack.reshape(n_z, CORES, n_exp, shard, columns)
    dsent = swap_core(take(dpack, 1 - core, 1))
    dpack = (take(dpack, core, 1).astype(F32) + dsent.astype(F32)).astype(BF16)
    dtotal = take(dpack, exp, 1).astype(F32)
    for k in range(1, n_exp):
        dtotal = dtotal + shift(take(dpack, (exp + k) % n_exp, 1), "expert", k).astype(F32)
    dpack = dtotal.astype(BF16)
    dtotal = take(dpack, z).astype(F32)
    for k in range(1, n_z):
        dtotal = dtotal + shift_z(take(dpack, (z + k) % n_z), k).astype(F32)
    dside = dtotal[:, 4 * width :]
    over_heads = dside[:, : expert_count + 1].T
    summed = over_heads
    for k in range(1, n_heads):
        summed = summed + shift(over_heads, "heads", k)

    def own_half(value):
        return lax.dynamic_slice_in_dim(value, head * half_width, half_width, 1)

    def cut(value):
        return value.astype(BF16).reshape(images, span, half_width)[:, :seq]

    dn_own = take(dnorm, head).astype(F32)
    sums = stats[:, :2].T
    sums_total = sums
    for k in range(1, n_heads):
        dn_own = dn_own + shift(take(dnorm, (head + k) % n_heads), "heads", k).astype(F32)
        sums_total = sums_total + shift(sums, "heads", k)
    unit_one, scale_one = norm_parts(inputs.astype(F32))
    grad_in = own_half(dmiddle) + scale_one * (
        dn_own * own_half(gain_one)
        - sums_total[0][:, None] / model
        - own_half(unit_one) * (sums_total[1][:, None] / model)
    )

    yrows[0] = after(yrows[0], datt)
    y_came = [swap_core(combine(slot_cols, yrows, n_exp + k)) for k in range(n_exp)]
    y_own = combine(slot_cols, yrows, 0, y_came[0]).astype(F32)
    for k in range(1, n_exp):
        y_own = y_own + shift(combine(slot_cols, yrows, k, y_came[k]), "expert", -k).astype(F32)
    y_own = y_own.astype(BF16)
    y_total = own_half(y_own).astype(F32)
    for k in range(1, n_heads):
        there = (head + k) % n_heads
        part_y = lax.dynamic_slice_in_dim(y_own, there * half_width, half_width, 1)
        y_total = y_total + shift(part_y, "heads", k).astype(F32)
    block_out = own_half(middle) + y_total

    def finish(totals):
        stacked = jnp.stack(totals).reshape(local, CORES, part_rows, hidden_width)
        other = swap_core(take(stacked, 1 - core, 1).astype(BF16)).astype(F32)
        own = take(stacked, core, 1).astype(F32)
        joined = jnp.concatenate([jnp.where(low, own, other), jnp.where(low, other, own)], axis=0)
        return joined.transpose(1, 0, 2)

    return (
        cut(block_out),
        cut(grad_in),
        summed[expert_count],
        dtotal[:, : 3 * width].reshape(shard, 3, width),
        dtotal[:, 3 * width : 4 * width],
        dside[:, expert_count + 1],
        summed[:expert_count].T,
        finish([moving[2 * e + 1][-1] for e in range(local)]),
        finish([moving[2 * e][-1] for e in range(local)]),
    )


def solution(mesh):
    return jax.shard_map(
        per_device,
        mesh=mesh,
        in_specs=(
            P(("dp", "expert"), None, "heads"),
            P(("dp", "expert"), None, "heads"),
            P(("dp", "expert"), None, None),
            P(("dp", "expert")),
            P(("dp", "expert"), None, "heads"),
            P(("dp", "expert"), "heads"),
            P(("dp", "expert")),
            P(("dp", "expert"), None),
            P("dp", "expert", "heads"),
            P("dp", "expert", "heads"),
        ),
        out_specs=(
            P(("dp", "expert"), None, "heads"),
            P(("dp", "expert"), None, "heads"),
            P(("dp", "expert")),
            P(("dp", "expert"), None, "heads"),
            P(("dp", "expert"), "heads"),
            P(("dp", "expert")),
            P(("dp", "expert"), None),
            P("dp", "expert", "heads"),
            P("dp", "expert", "heads"),
        ),
        check_vma=False,
    )
```

```python
import functools

import jax
import jax.numpy as jnp
from jax import lax
from jax.experimental import pallas as pl
from jax.experimental.pallas import tpu as pltpu
from jax.sharding import PartitionSpec as P

HEAD_DIM = 64
CORES = 2
EPS = 1e-06
LOW = -1e30
F32 = jnp.float32
BF16 = jnp.bfloat16
VMEM_LIMIT = 56 * 1024 * 1024
SHARE = 64


def dot(a, b, ca, cb):
    return lax.dot_general(a, b, (((ca,), (cb,)), ((), ())), preferred_element_type=F32)


def shaped(shape, kind):
    return jax.ShapeDtypeStruct(shape, kind)


def params(dims=1):
    return pltpu.CompilerParams(
        dimension_semantics=("arbitrary",) * dims, vmem_limit_bytes=VMEM_LIMIT
    )


def cost(flops, size, powers=0):
    return pl.CostEstimate(
        flops=flops // SHARE, bytes_accessed=size // SHARE, transcendentals=powers // SHARE
    )


def after(value, *others):
    return lax.optimization_barrier((value,) + others)[0]


def norm_parts(rows):
    average = jnp.mean(rows, axis=-1, keepdims=True)
    centred = rows - average
    spread = jnp.mean(centred * centred, axis=-1, keepdims=True)
    scale = lax.rsqrt(spread + EPS)
    return centred * scale, scale


def softmax_rows(q, own_k, real):
    scores = jnp.where(real, dot(q, own_k, 1, 1) * (HEAD_DIM**-0.5), LOW)
    powers = jnp.exp(scores - jnp.max(scores, axis=-1, keepdims=True))
    return powers / jnp.sum(powers, axis=-1, keepdims=True)


def attend_kernel(seq, x_ref, gain_ref, wqkv_ref, wo_ref, part_ref, qkv_ref, ctx_ref):
    width = wo_ref.shape[1]
    span = x_ref.shape[0]
    unit, _ = norm_parts(x_ref[...].astype(F32))
    normed = (unit * gain_ref[...]).astype(BF16)
    for part in range(3):
        cols = slice(part * width, (part + 1) * width)
        qkv_ref[:, cols] = dot(normed, wqkv_ref[:, cols], 1, 0).astype(BF16)
    lane = lax.broadcasted_iota(jnp.int32, (span, 128), 1)
    real = lax.broadcasted_iota(jnp.int32, (span, span), 1) < seq
    for pair in range(width // 128):
        q, k, v = (
            qkv_ref[:, part * width + pair * 128 : part * width + (pair + 1) * 128]
            for part in range(3)
        )
        ctx = jnp.zeros((span, 128), F32)
        for side in range(2):
            mine = (lane >= 64) if side else (lane < 64)
            own_k = jnp.where(mine, k, jnp.zeros_like(k))
            own_v = jnp.where(mine, v, jnp.zeros_like(v))
            weights = softmax_rows(q, own_k, real)
            ctx = ctx + dot(weights.astype(BF16), own_v, 1, 0)
        ctx_ref[:, pair * 128 : (pair + 1) * 128] = ctx.astype(BF16)
    part_ref[...] = dot(ctx_ref[...], wo_ref[...], 1, 1).astype(BF16)


def attend(inputs, gain, packed, width, images, seq):
    rows, model = inputs.shape
    span = rows // images
    image = lambda last: pl.BlockSpec((span, last), lambda i: (i, 0))
    return pl.pallas_call(
        functools.partial(attend_kernel, seq),
        grid=(images,),
        in_specs=[
            image(model),
            pl.BlockSpec((1, model), lambda i: (0, 0)),
            pl.BlockSpec((model, 3 * width), lambda i: (0, 0)),
            pl.BlockSpec((model, width), lambda i: (0, 3)),
        ],
        out_specs=[image(model), image(3 * width), image(width)],
        out_shape=[
            shaped((rows, model), BF16), shaped((rows, 3 * width), BF16), shaped((rows, width), BF16)
        ],
        compiler_params=params(),
        cost_estimate=cost(10 * rows * model * width, 8 * rows * model, rows * span * width // 64),
        name="attend",
    )(inputs, gain, packed, packed)


def attend_back_kernel(
    seq, gain_at,
    x_ref, gain_ref, datt_ref, qkv_ref, ctx_ref, wqkv_ref, wo_ref, side_ref,
    dnorm_ref, stats_ref, pack_ref, dproj_ref, dgain_ref, dwqkv_ref, dwo_ref,
):
    width = wo_ref.shape[1]
    span, model = x_ref.shape
    step = pl.program_id(0)

    @pl.when(step == 0)
    def _():
        dgain_ref[...] = jnp.zeros_like(dgain_ref)
        dwqkv_ref[...] = jnp.zeros_like(dwqkv_ref)
        dwo_ref[...] = jnp.zeros_like(dwo_ref)

    datt = datt_ref[...]
    dwo_ref[...] += dot(datt, ctx_ref[...], 0, 0)
    dctx_all = dot(datt, wo_ref[...], 1, 0).astype(BF16)
    lane = lax.broadcasted_iota(jnp.int32, (span, 128), 1)
    real = lax.broadcasted_iota(jnp.int32, (span, span), 1) < seq
    for pair in range(width // 128):
        q, k, v = (
            qkv_ref[:, part * width + pair * 128 : part * width + (pair + 1) * 128]
            for part in range(3)
        )
        dctx = dctx_all[:, pair * 128 : (pair + 1) * 128]
        dq = jnp.zeros((span, 128), F32)
        dk = jnp.zeros((span, 128), F32)
        dv = jnp.zeros((span, 128), F32)
        for side in range(2):
            mine = (lane >= 64) if side else (lane < 64)
            own = lambda t: jnp.where(mine, t, jnp.zeros_like(t))
            own_k, own_v = own(k), own(v)
            weights = softmax_rows(q, own_k, real)
            dweights = dot(dctx, own_v, 1, 1)
            inner = jnp.sum(dweights * weights, axis=-1, keepdims=True)
            dscores = (weights * (dweights - inner)).astype(BF16)
            dq = dq + dot(dscores, own_k, 1, 0)
            dk = dk + dot(dscores, own(q), 0, 0)
            dv = dv + dot(weights.astype(BF16), own(dctx), 0, 0)
        for part, value in enumerate((dq * HEAD_DIM**-0.5, dk * HEAD_DIM**-0.5, dv)):
            start = part * width + pair * 128
            dproj_ref[:, start : start + 128] = value.astype(BF16)
    dproj = dproj_ref[...]
    gain = gain_ref[...]
    unit, _ = norm_parts(x_ref[...].astype(F32))
    normed = (unit * gain).astype(BF16)
    dwqkv_ref[...] += dot(normed, dproj, 0, 0)
    dnormed = dot(dproj, wqkv_ref[...], 1, 1)
    halves, _, half = dnorm_ref.shape
    for h in range(halves):
        dnorm_ref[h] = dnormed[:, h * half : (h + 1) * half].astype(BF16)
    along = dnormed * unit
    dgain_ref[...] += jnp.sum(along, axis=0, keepdims=True)
    first = jnp.sum(dnormed * gain, axis=-1, keepdims=True)
    second = jnp.sum(along * gain, axis=-1, keepdims=True)
    stats_ref[...] = jnp.where(lane == 0, first, jnp.where(lane == 1, second, 0.0))

    @pl.when(step == pl.num_programs(0) - 1)
    def _():
        pack_ref[:, : 3 * width] = dwqkv_ref[...].astype(BF16)
        pack_ref[:, 3 * width : 4 * width] = dwo_ref[...].astype(BF16)
        line = lax.broadcasted_iota(jnp.int32, (128, model), 0)
        column = jnp.where(line == gain_at, dgain_ref[...], 0.0).T
        pack_ref[:, 4 * width :] = (side_ref[...] + column).astype(BF16)


def attend_back(inputs, gain, datt, qkv, ctx, packed, dside, gain_at, width, images, seq, halves):
    rows, model = inputs.shape
    span = rows // images
    image = lambda last: pl.BlockSpec((span, last), lambda i: (i, 0))
    fixed = lambda *size: pl.BlockSpec(size, lambda i: (0, 0))
    return pl.pallas_call(
        functools.partial(attend_back_kernel, seq, gain_at),
        grid=(images,),
        in_specs=[
            image(model), fixed(1, model), image(model), image(3 * width), image(width),
            fixed(model, 3 * width), pl.BlockSpec((model, width), lambda i: (0, 3)),
            fixed(model, 128),
        ],
        out_specs=[
            pl.BlockSpec((halves, span, model // halves), lambda i: (0, i, 0)),
            image(128),
            fixed(*packed.shape),
        ],
        out_shape=[
            shaped((halves, rows, model // halves), BF16),
            shaped((rows, 128), F32),
            shaped(packed.shape, BF16),
        ],
        scratch_shapes=[
            pltpu.VMEM((span, 3 * width), BF16),
            pltpu.VMEM((1, model), F32),
            pltpu.VMEM((model, 3 * width), F32),
            pltpu.VMEM((model, width), F32),
        ],
        compiler_params=params(),
        cost_estimate=cost(28 * rows * model * width, 12 * rows * model, rows * span * width // 64),
        name="attend_back",
    )(inputs, gain, datt, qkv, ctx, packed, packed, dside)


def expert_kernel(depth, blocks, place_ref, slot_ref, router_ref, *refs):
    x_refs, refs = refs[:blocks], refs[blocks:]
    grad_refs, refs = refs[:blocks], refs[blocks:]
    win_refs, refs = refs[:depth], refs[depth:]
    wout_refs, refs = refs[:depth], refs[depth:]
    (
        rows_ref, grows_ref, gact_ref, dhid_ref, dchosen_ref, drows_ref, probs_ref,
        win_all, wout_all,
    ) = refs
    _, slots, model = rows_ref.shape
    tokens = x_refs[0].shape[0]
    part_rows, width = win_refs[0].shape[-2:]
    step = pl.program_id(0)

    @pl.when(step == 0)
    def _():
        for k in range(depth):
            owner = lax.rem(place_ref[0] - k + depth, depth)
            at = pl.ds(pl.multiple_of(owner * part_rows, 16), part_rows)
            win_all[at, :] = win_refs[k][...]
            wout_all[at, :] = wout_refs[k][...]

    mask = lax.broadcasted_iota(jnp.int32, (slots, tokens), 0) == slot_ref[0]
    pick = jnp.where(mask, 1.0, 0.0).astype(BF16)
    for b in range(blocks):

        @pl.when(step == b)
        def _(b=b):
            rows_ref[0] = dot(pick, x_refs[b][...], 1, 0).astype(BF16)
            grows_ref[0] = dot(pick, grad_refs[b][...], 1, 0).astype(BF16)
            logits = dot(router_ref[...], x_refs[b][...], 1, 1)
            powers = jnp.exp(logits - jnp.max(logits, axis=0, keepdims=True))
            probs_ref[0] = powers / jnp.sum(powers, axis=0, keepdims=True)

    probs = probs_ref[0]
    line = lax.broadcasted_iota(jnp.int32, probs.shape, 0)
    own = jnp.sum(jnp.where(line == place_ref[1], probs, 0.0), axis=0, keepdims=True)
    gate = jnp.sum(jnp.where(mask, own, 0.0), axis=1, keepdims=True)
    rows, grows = rows_ref[0], grows_ref[0]
    dgate = jnp.zeros((slots, 1), F32)
    drows = jnp.zeros((slots, model), F32)
    tile = 512 if width % 512 == 0 else width
    curve = 0.7978845608028654
    for start in range(0, width, tile):
        cols = slice(start, start + tile)
        win, wout = win_all[:, cols], wout_all[:, cols]
        hidden = dot(rows, win, 1, 0)
        pulled = dot(grows, wout, 1, 0)
        square = hidden * hidden
        bend = jnp.tanh(hidden * (curve + curve * 0.044715 * square))
        half = 0.5 + 0.5 * bend
        active = hidden * half
        slope = half + 0.5 * hidden * (1.0 - bend * bend) * (
            curve + 3.0 * curve * 0.044715 * square
        )
        dgate = dgate + jnp.sum(active * pulled, axis=1, keepdims=True)
        gact = (gate * active).astype(BF16)
        dhid = (gate * pulled * slope).astype(BF16)
        gact_ref[0, :, cols] = gact
        dhid_ref[0, :, cols] = dhid
        drows = drows + dot(dhid, win, 1, 1)
    dchosen_ref[0] = jnp.sum(jnp.where(mask, dgate, 0.0), axis=0, keepdims=True)
    drows_ref[0] = drows.astype(BF16)


def run_expert(place, slot_of, router_rows, xs, grads, w_in, w_out, slots):
    blocks, depth = len(xs), len(w_in)
    tokens, model = xs[0].shape
    part_rows, width = w_in[0].shape
    experts = router_rows.shape[0]
    fixed = lambda *size: pl.BlockSpec(
        size, lambda b, s: (0,) * len(size), pipeline_mode=pl.Buffered(1)
    )
    block = lambda *size: pl.BlockSpec((1,) + size, lambda b, s: (b, 0, 0))
    return pl.pallas_call(
        functools.partial(expert_kernel, depth, blocks),
        grid_spec=pltpu.PrefetchScalarGridSpec(
            num_scalar_prefetch=1,
            grid=(blocks,),
            in_specs=[block(1, tokens), fixed(experts, model)]
            + [fixed(tokens, model)] * (2 * blocks)
            + [fixed(part_rows, width)] * (2 * depth),
            out_specs=[
                block(slots, model), block(slots, model), block(slots, width), block(slots, width),
                block(1, tokens), block(slots, model), block(experts, tokens),
            ],
            scratch_shapes=[pltpu.VMEM((model, width), BF16)] * 2,
        ),
        out_shape=[
            shaped((blocks, slots, model), BF16), shaped((blocks, slots, model), BF16),
            shaped((blocks, slots, width), BF16), shaped((blocks, slots, width), BF16),
            shaped((blocks, 1, tokens), F32), shaped((blocks, slots, model), BF16),
            shaped((blocks, experts, tokens), F32),
        ],
        compiler_params=params(),
        cost_estimate=cost(
            6 * blocks * slots * model * width + 4 * blocks * slots * model * tokens,
            16 * blocks * slots * model,
            blocks * slots * width,
        ),
        name="expert",
    )(place, slot_of, router_rows, *xs, *grads, *w_in, *w_out)


def result_kernel(depth, place_ref, gact_ref, *refs):
    wout_refs, (out_ref, wout_all) = refs[:depth], refs[depth:]
    part_rows = wout_refs[0].shape[0]

    @pl.when(pl.program_id(0) == 0)
    def _():
        for k in range(depth):
            owner = lax.rem(place_ref[0] - k + depth, depth)
            at = pl.ds(pl.multiple_of(owner * part_rows, 16), part_rows)
            wout_all[at, :] = wout_refs[k][...]

    out_ref[0] = dot(gact_ref[0], wout_all[...], 1, 1).astype(BF16)


def result_rows(place, gact, w_out):
    blocks, slots, width = gact.shape
    depth, part_rows = len(w_out), w_out[0].shape[0]
    model = depth * part_rows
    block = lambda *size: pl.BlockSpec((1,) + size, lambda b, s: (b, 0, 0))
    return pl.pallas_call(
        functools.partial(result_kernel, depth),
        grid_spec=pltpu.PrefetchScalarGridSpec(
            num_scalar_prefetch=1,
            grid=(blocks,),
            in_specs=[block(slots, width)]
            + [
                pl.BlockSpec(
                    (part_rows, width), lambda b, s: (0, 0), pipeline_mode=pl.Buffered(1)
                )
            ]
            * depth,
            out_specs=block(slots, model),
            scratch_shapes=[pltpu.VMEM((model, width), BF16)],
        ),
        out_shape=shaped((blocks, slots, model), BF16),
        compiler_params=params(),
        cost_estimate=cost(
            2 * blocks * slots * model * width, 2 * blocks * slots * (model + width)
        ),
        name="result_rows",
    )(place, gact, *w_out)


def weight_grad_kernel(depth, place_ref, rows_ref, cols_ref, *refs):
    out_refs, total_ref = refs[:depth], refs[depth]
    blocks, slots, model = rows_ref.shape
    tile = cols_ref.shape[2]
    part_rows = model // depth
    left = rows_ref[...].reshape(blocks * slots, model)
    right = cols_ref[...].reshape(blocks * slots, tile)
    total_ref[...] = dot(left, right, 0, 0)
    for k in range(depth):
        owner = lax.rem(place_ref[0] - k + depth, depth)
        at = pl.ds(pl.multiple_of(owner * part_rows, 16), part_rows)
        out_refs[k][...] = total_ref[at, :].astype(BF16)


def weight_grad(place, rows, cols, depth):
    blocks, slots, model = rows.shape
    width = cols.shape[2]
    tile = width
    return pl.pallas_call(
        functools.partial(weight_grad_kernel, depth),
        grid_spec=pltpu.PrefetchScalarGridSpec(
            num_scalar_prefetch=1,
            grid=(width // tile,),
            in_specs=[
                pl.BlockSpec((blocks, slots, model), lambda f, s: (0, 0, 0)),
                pl.BlockSpec((blocks, slots, tile), lambda f, s: (0, 0, f)),
            ],
            out_specs=[pl.BlockSpec((model // depth, tile), lambda f, s: (0, f))] * depth,
            scratch_shapes=[pltpu.VMEM((model, tile), F32)],
        ),
        out_shape=[shaped((model // depth, width), BF16)] * depth,
        compiler_params=params(),
        cost_estimate=cost(
            2 * blocks * slots * model * width,
            2 * (blocks * slots * (model + width) + model * width),
        ),
        name="weight_grad",
    )(place, rows, cols)


def combine_kernel(local, added, slot_ref, *refs):
    rows_refs, refs = refs[:local], refs[local:]
    out_ref = refs[-1]
    tokens = out_ref.shape[-2]
    slots, model = rows_refs[0].shape[1:]
    at = lax.broadcasted_iota(jnp.int32, (tokens, slots), 1)
    total = refs[0][...].astype(F32) if added else jnp.zeros((tokens, model), F32)
    for e in range(local):
        pick = jnp.where(at == slot_ref[0, :, e : e + 1], 1.0, 0.0).astype(BF16)
        total = total + dot(pick, rows_refs[e][0], 1, 0)
    out_ref[...] = total.astype(BF16)


def combine(slot_cols, rows, b, add=None):
    _, tokens, local = slot_cols.shape
    slots, model = rows[0].shape[1:]
    whole = pl.BlockSpec((tokens, model), lambda i: (0, 0))
    return pl.pallas_call(
        functools.partial(combine_kernel, local, add is not None),
        grid=(1,),
        in_specs=[pl.BlockSpec((1, tokens, local), lambda i: (b, 0, 0))]
        + [pl.BlockSpec((1, slots, model), lambda i: (b, 0, 0))] * local
        + [whole] * (add is not None),
        out_specs=whole,
        out_shape=shaped((tokens, model), BF16),
        compiler_params=params(),
        cost_estimate=cost(
            2 * local * slots * model * tokens, 2 * model * (local * slots + 2 * tokens)
        ),
        name="combine",
    )(slot_cols, *rows, *(() if add is None else (add,)))


def combine_back_kernel(local, added, place_ref, slot_ref, *refs):
    rows_refs, refs = refs[:local], refs[local:]
    dchosen_refs, refs = refs[:local], refs[local:]
    probs_ref, router_ref, x_ref = refs[:3]
    out_ref, drouter_ref = refs[-2:]
    tokens = out_ref.shape[0]
    slots = rows_refs[0].shape[1]
    at = lax.broadcasted_iota(jnp.int32, (tokens, slots), 1)
    probs = probs_ref[0]
    line = lax.broadcasted_iota(jnp.int32, probs.shape, 0)
    dprobs = jnp.zeros_like(probs)
    for e in range(local):
        dprobs = jnp.where(line == place_ref[1] + e, dchosen_refs[e][0], dprobs)
    inner = jnp.sum(dprobs * probs, axis=0, keepdims=True)
    dlogits = (probs * (dprobs - inner)).astype(BF16)
    drouter_ref[...] = dot(dlogits, x_ref[...], 1, 0)
    total = dot(dlogits, router_ref[...], 0, 0)
    if added:
        total = total + refs[3][...].astype(F32)
    for e in range(local):
        pick = jnp.where(at == slot_ref[0, :, e : e + 1], 1.0, 0.0).astype(BF16)
        total = total + dot(pick, rows_refs[e][0], 1, 0)
    out_ref[...] = total.astype(BF16)


def combine_back(place, slot_cols, rows, dchosen, probs, router_rows, x, b, add=None):
    _, tokens, local = slot_cols.shape
    slots, model = rows[0].shape[1:]
    experts = router_rows.shape[0]
    whole = pl.BlockSpec((tokens, model), lambda i, s: (0, 0))
    block = lambda *size: pl.BlockSpec((1,) + size, lambda i, s: (b, 0, 0))
    small = pl.BlockSpec((experts, model), lambda i, s: (0, 0))
    return pl.pallas_call(
        functools.partial(combine_back_kernel, local, add is not None),
        grid_spec=pltpu.PrefetchScalarGridSpec(
            num_scalar_prefetch=1,
            grid=(1,),
            in_specs=[block(tokens, local)]
            + [block(slots, model)] * local
            + [block(1, tokens)] * local
            + [block(experts, tokens), small, whole]
            + [whole] * (add is not None),
            out_specs=[whole, small],
        ),
        out_shape=[shaped((tokens, model), BF16), shaped((experts, model), F32)],
        compiler_params=params(),
        cost_estimate=cost(
            2 * local * slots * model * tokens, 2 * model * (local * slots + 3 * tokens)
        ),
        name="combine_back",
    )(place, slot_cols, *rows, *dchosen, probs, router_rows, x, *(() if add is None else (add,)))


def per_device(
    block_in, cotangent, route_ids, gain_attn, w_qkv, w_out_attn, gain_moe, router, w_in, w_out
):
    n_dp, n_heads, n_exp = (lax.axis_size(name) for name in ("dp", "heads", "expert"))
    n_z = n_dp // CORES
    dp, head, exp = (lax.axis_index(name) for name in ("dp", "heads", "expert"))
    z, core = dp // CORES, dp % CORES
    low = core == 0
    images, seq, half_width = block_in.shape
    span = -(-seq // 16) * 16
    rows = images * span
    model = half_width * n_heads
    width = w_qkv.shape[2]
    shard = w_qkv.shape[0]
    expert_count = router.shape[1]
    group = w_in.shape[1]
    local = group // CORES
    part_rows, _, hidden_width = w_in.shape
    capacity = 20 * images * seq // (7 * expert_count)
    slots = -(-capacity // 16) * 16
    blocks = n_exp * CORES
    rest = 128

    def shift(value, axis, step):
        size = lax.axis_size(axis)
        return lax.ppermute(value, axis, [(i, (i + step) % size) for i in range(size)])

    def shift_z(value, step):
        pairs = [
            (a * CORES + c, ((a + step) % n_z) * CORES + c) for a in range(n_z) for c in range(CORES)
        ]
        return lax.ppermute(value, "dp", pairs)

    def swap_core(value):
        return lax.ppermute(value, "dp", [(i, i ^ 1) for i in range(n_dp)])

    def place_at(pieces, index, count):
        if count == 2:
            first = index == 0
            return jnp.stack(
                [jnp.where(first, pieces[0], pieces[1]), jnp.where(first, pieces[1], pieces[0])]
            )
        out = jnp.zeros((count,) + pieces[0].shape, pieces[0].dtype)
        for k, piece in enumerate(pieces):
            out = lax.dynamic_update_index_in_dim(out, piece, (index - k) % count, 0)
        return out

    def spread(value, axis):
        return [value] + [shift(value, axis, k) for k in range(1, lax.axis_size(axis))]

    def take(value, index, dim=0):
        return lax.dynamic_index_in_dim(value, index, dim, keepdims=False)

    def expert_shards(weight):
        by_core = weight.reshape(part_rows, CORES, local, hidden_width).transpose(1, 2, 0, 3)
        other = swap_core(take(by_core, 1 - core))
        mine = take(by_core, core)
        return jnp.concatenate(
            [jnp.where(low, mine, other), jnp.where(low, other, mine)], axis=1
        )

    ways_up = n_z // 2
    ways_down = n_z - 1 - ways_up

    def ring(piece):
        pieces = [piece] + [None] * (n_z - 1)
        for k in range(1, ways_up + 1):
            pieces[k] = shift_z(pieces[k - 1], 1)
        for k in range(1, ways_down + 1):
            pieces[n_z - k] = shift_z(pieces[(n_z - k + 1) % n_z], -1)
        return pieces

    def blocks_of(value, hold=()):
        along = spread(value, "expert")
        along = along[:1] + [after(part, *hold) for part in along[1:]]
        return along + [swap_core(part) for part in along]

    tail = jnp.concatenate(
        [router, gain_attn[:, None], gain_moe[:, None],
         jnp.zeros((shard, rest - expert_count - 2), BF16)], axis=1
    )
    own_pack = jnp.concatenate([w_qkv.reshape(shard, 3 * width), w_out_attn, tail], axis=1)
    columns = own_pack.shape[1]
    out_shards = expert_shards(w_out)
    ids = jnp.pad(route_ids, ((0, 0), (0, span - seq), (0, 0)), constant_values=-1)
    ids_all = jnp.stack(blocks_of(ids.reshape(rows, 2).T))
    pack_z = place_at(
        [own_pack] + [after(shift_z(own_pack, k), out_shards) for k in range(1, n_z)], z, n_z
    )
    pack = place_at(spread(after(pack_z, ids_all), "expert"), exp, n_exp)
    in_shards = expert_shards(w_in)
    out_pieces, in_pieces = [], []
    hold = (pack_z,)
    for e in range(local):
        out_pieces.append(ring(after(out_shards[e], *hold) if e else out_shards[e]))
        in_pieces.append(ring(after(in_shards[e], *hold)))
        hold = (out_pieces[e][1], in_pieces[e][1])
    last = local - 1

    pack = after(pack, out_pieces[0][1])
    other_pack = swap_core(pack)
    pack = jnp.stack([jnp.where(low, pack, other_pack), jnp.where(low, other_pack, pack)])
    pack = pack.transpose(2, 0, 1, 3, 4).reshape(model, columns)
    side = pack[:, 4 * width :].T
    router_rows = side[:expert_count]
    gain_one = side[expert_count : expert_count + 1].astype(F32)
    gain_two = side[expert_count + 1 : expert_count + 2].astype(F32)

    def full_rows(value):
        padded = jnp.pad(value, ((0, 0), (0, span - seq), (0, 0))).reshape(rows, half_width)
        parts = place_at(spread(padded, "heads"), head, n_heads)
        return jnp.concatenate([parts[i] for i in range(n_heads)], axis=-1)

    inputs = full_rows(block_in)

    first_expert = exp * group + core * local
    named = first_expert + jnp.arange(local, dtype=jnp.int32)
    chosen = jnp.any(ids_all[:, None, :, :] == named[None, :, None, None], axis=2)
    before = (jnp.arange(rows)[:, None] < jnp.arange(rows)[None, :]).astype(BF16)
    rank = jnp.dot(
        chosen.astype(BF16).reshape(blocks * local, rows), before, preferred_element_type=F32
    ).astype(jnp.int32).reshape(blocks, local, rows)
    slot_of = jnp.where(chosen, rank, -1)
    slot_cols = slot_of.transpose(0, 2, 1)
    place = [jnp.stack([z, first_expert + e]).astype(jnp.int32) for e in range(local)]

    grad_full = full_rows(cotangent)
    grads_all = blocks_of(grad_full)
    inputs_ready = after(inputs, out_pieces[0][-1], grad_full)
    part, qkv, ctx = attend(inputs_ready, gain_one, pack, width, images, seq)
    part_other = shift(part, "heads", 1)
    for k in range(2, n_heads):
        part_other = part_other + shift(part, "heads", k)
    part_other = after(part_other, in_pieces[0][1], in_pieces[0][-1], out_pieces[0][ways_up])
    middle = inputs.astype(F32) + (part.astype(F32) + part_other.astype(F32))
    unit_two, scale_two = norm_parts(middle)
    normed_two = (unit_two * gain_two).astype(BF16)
    tokens_all = blocks_of(
        normed_two, (in_pieces[0][ways_up], out_pieces[last][1], in_pieces[last][1])
    )

    done = []

    def begin_rings(e, *hold):
        rows_e, grows_e, gact_e, dhid_e = done[e][:4]
        rings.append(
            [
                weight_grad(place[e], after(left, *hold), right, n_z)
                for left, right in ((grows_e, gact_e), (rows_e, dhid_e))
            ]
        )

    def ring_first(e):
        return [shift_z(chunks[-ways_up % n_z], 1) for chunks in rings[e]]

    def ring_middle(e, arrived, *hold):
        ups, downs = [], []
        for upward, chunks in zip(arrived, rings[e]):
            for k in range(ways_up - 1, 0, -1):
                own = after(chunks[n_z - k], *hold)
                upward = (upward.astype(F32) + own.astype(F32)).astype(BF16)
                if k > 1:
                    upward = shift_z(upward, 1)
            downward = chunks[ways_down]
            for k in range(ways_down - 1, 0, -1):
                own = after(chunks[k], *hold)
                downward = (shift_z(downward, -1).astype(F32) + own.astype(F32)).astype(BF16)
            ups.append(upward)
            downs.append(shift_z(downward, -1))
        return ups, downs

    def ring_end(e, sums, *hold):
        out = []
        for i, chunks in enumerate(rings[e]):
            own = after(chunks[0], *hold).astype(F32)
            out.append(own + shift_z(sums[0][i], 1).astype(F32) + sums[1][i].astype(F32))
        return out

    rings = []
    for e in range(local):
        shards_in = list(in_pieces[e])
        if e:
            shards_in[0] = after(shards_in[0], *[c[0] for c in rings[-1]])
        done.append(
            run_expert(
                place[e], slot_of[:, e : e + 1, :], router_rows, tokens_all, grads_all,
                shards_in, out_pieces[e], slots,
            )
        )
        if e < local - 1:
            begin_rings(e)
    drows, dchosen = ([r[i] for r in done] for i in (5, 4))
    probs = done[0][6]

    arrived_zero = ring_first(0)
    drows[0] = after(drows[0], *arrived_zero)

    def back_of(b, add=None):
        return combine_back(
            place[0], slot_cols, drows, dchosen, probs, router_rows, tokens_all[b], b, add
        )

    drouter = jnp.zeros((expert_count, model), F32)
    arrived = [None] * n_exp
    for k in reversed(range(n_exp)):
        sent, more = back_of(n_exp + k)
        arrived[k] = swap_core(sent)
        drouter = drouter + more
    from_exp = []
    for k in reversed(range(n_exp)):
        total, more = back_of(k, arrived[k])
        drouter = drouter + more
        if k:
            from_exp.append(shift(total, "expert", -k))
            if k == 1:
                begin_rings(last, total)
                early = ring_middle(0, arrived_zero, total)
    dsum = after(total, *early[0], *early[1], *[c[0] for c in rings[last]]).astype(F32)
    for value in from_exp:
        dsum = dsum + value.astype(F32)
    dsum = dsum.astype(BF16)

    yrows = [
        result_rows(place[e], after(done[e][2], dsum), out_pieces[e]) for e in range(local)
    ]
    y_came = [swap_core(combine(slot_cols, yrows, n_exp + k)) for k in range(n_exp)]
    y_from = []
    for k in reversed(range(n_exp)):
        y_own = combine(slot_cols, yrows, k, y_came[k])
        if k:
            y_from.append(shift(y_own, "expert", -k))
    y_own = y_own.astype(F32)
    for value in y_from:
        y_own = y_own + value.astype(F32)
    y_own = y_own.astype(BF16)

    dsum_other = shift(dsum, "heads", 1)
    for k in range(2, n_heads):
        dsum_other = dsum_other + shift(dsum, "heads", k)
    ends = [ring_end(0, early, dsum)]
    arrived_last = ring_first(last)
    dsum_other = after(dsum_other, *ends[0], *arrived_last)
    dnormed_two = dsum.astype(F32) + dsum_other.astype(F32)
    scaled = dnormed_two * gain_two
    grad_gain_two = jnp.sum(dnormed_two * unit_two, axis=0)
    dmiddle = grad_full.astype(F32) + scale_two * (
        scaled
        - jnp.mean(scaled, axis=-1, keepdims=True)
        - unit_two * jnp.mean(scaled * unit_two, axis=-1, keepdims=True)
    )
    late = ring_middle(last, arrived_last, dsum_other)
    datt = after(dmiddle.astype(BF16), *late[0])

    dside = jnp.concatenate(
        [drouter, jnp.zeros((1, model), F32), grad_gain_two[None, :],
         jnp.zeros((rest - expert_count - 2, model), F32)], axis=0
    ).T
    dnorm, stats, dpack = attend_back(
        inputs, gain_one, datt, qkv, ctx, pack, dside, expert_count, width, images, seq, n_heads
    )
    dpack = after(dpack, y_own, *late[1])

    dpack = dpack.reshape(n_z, CORES, n_exp, shard, columns)
    dsent = swap_core(take(dpack, 1 - core, 1))
    dpack = (take(dpack, core, 1).astype(F32) + dsent.astype(F32)).astype(BF16)
    dtotal = take(dpack, exp, 1).astype(F32)
    for k in range(1, n_exp):
        dtotal = dtotal + shift(take(dpack, (exp + k) % n_exp, 1), "expert", k).astype(F32)
    dpack = dtotal.astype(BF16)
    ends.append(ring_end(last, late, dpack))
    dtotal = take(dpack, z).astype(F32)
    for k in range(1, n_z):
        dtotal = dtotal + shift_z(take(dpack, (z + k) % n_z), k).astype(F32)
    dside = dtotal[:, 4 * width :]
    over_heads = dside[:, : expert_count + 1].T
    summed = over_heads
    for k in range(1, n_heads):
        summed = summed + shift(over_heads, "heads", k)

    def own_half(value):
        return lax.dynamic_slice_in_dim(value, head * half_width, half_width, 1)

    def cut(value):
        return value.astype(BF16).reshape(images, span, half_width)[:, :seq]

    dn_own = take(dnorm, head).astype(F32)
    sums = stats[:, :2].T
    sums_total = sums
    for k in range(1, n_heads):
        dn_own = dn_own + shift(take(dnorm, (head + k) % n_heads), "heads", k).astype(F32)
        sums_total = sums_total + shift(sums, "heads", k)
    unit_one, scale_one = norm_parts(inputs.astype(F32))
    grad_in = own_half(dmiddle) + scale_one * (
        dn_own * own_half(gain_one)
        - sums_total[0][:, None] / model
        - own_half(unit_one) * (sums_total[1][:, None] / model)
    )

    y_total = own_half(y_own).astype(F32)
    for k in range(1, n_heads):
        there = (head + k) % n_heads
        part_y = lax.dynamic_slice_in_dim(y_own, there * half_width, half_width, 1)
        y_total = y_total + shift(part_y, "heads", k).astype(F32)
    block_out = own_half(middle) + y_total

    def finish(totals):
        stacked = jnp.stack(totals).reshape(local, CORES, part_rows, hidden_width)
        other = swap_core(take(stacked, 1 - core, 1).astype(BF16)).astype(F32)
        own = take(stacked, core, 1).astype(F32)
        joined = jnp.concatenate([jnp.where(low, own, other), jnp.where(low, other, own)], axis=0)
        return joined.transpose(1, 0, 2)

    return (
        cut(block_out),
        cut(grad_in),
        summed[expert_count],
        dtotal[:, : 3 * width].reshape(shard, 3, width),
        dtotal[:, 3 * width : 4 * width],
        dside[:, expert_count + 1],
        summed[:expert_count].T,
        finish([pair[1] for pair in ends]),
        finish([pair[0] for pair in ends]),
    )


def solution(mesh):
    return jax.shard_map(
        per_device,
        mesh=mesh,
        in_specs=(
            P(("dp", "expert"), None, "heads"),
            P(("dp", "expert"), None, "heads"),
            P(("dp", "expert"), None, None),
            P(("dp", "expert")),
            P(("dp", "expert"), None, "heads"),
            P(("dp", "expert"), "heads"),
            P(("dp", "expert")),
            P(("dp", "expert"), None),
            P("dp", "expert", "heads"),
            P("dp", "expert", "heads"),
        ),
        out_specs=(
            P(("dp", "expert"), None, "heads"),
            P(("dp", "expert"), None, "heads"),
            P(("dp", "expert")),
            P(("dp", "expert"), None, "heads"),
            P(("dp", "expert"), "heads"),
            P(("dp", "expert")),
            P(("dp", "expert"), None),
            P("dp", "expert", "heads"),
            P("dp", "expert", "heads"),
        ),
        check_vma=False,
    )
```

```python
import functools

import jax
import jax.numpy as jnp
from jax import lax
from jax.experimental import pallas as pl
from jax.experimental.pallas import tpu as pltpu
from jax.sharding import PartitionSpec as P

HEAD_DIM = 64
CORES = 2
EPS = 1e-06
LOW = -1e30
F32 = jnp.float32
BF16 = jnp.bfloat16
VMEM_LIMIT = 56 * 1024 * 1024
SHARE = 64


def dot(a, b, ca, cb):
    return lax.dot_general(a, b, (((ca,), (cb,)), ((), ())), preferred_element_type=F32)


def shaped(shape, kind):
    return jax.ShapeDtypeStruct(shape, kind)


def params(dims=1):
    return pltpu.CompilerParams(
        dimension_semantics=("arbitrary",) * dims, vmem_limit_bytes=VMEM_LIMIT
    )


def cost(flops, size, powers=0):
    return pl.CostEstimate(
        flops=flops // SHARE, bytes_accessed=size // SHARE, transcendentals=powers // SHARE
    )


def after(value, *others):
    return lax.optimization_barrier((value,) + others)[0]


def norm_parts(rows):
    average = jnp.mean(rows, axis=-1, keepdims=True)
    centred = rows - average
    spread = jnp.mean(centred * centred, axis=-1, keepdims=True)
    scale = lax.rsqrt(spread + EPS)
    return centred * scale, scale


def softmax_rows(q, own_k, real):
    scores = jnp.where(real, dot(q, own_k, 1, 1) * (HEAD_DIM**-0.5), LOW)
    powers = jnp.exp(scores - jnp.max(scores, axis=-1, keepdims=True))
    return powers / jnp.sum(powers, axis=-1, keepdims=True)


def attend_kernel(seq, x_ref, gain_ref, wqkv_ref, wo_ref, part_ref, qkv_ref, ctx_ref):
    width = wo_ref.shape[1]
    span = x_ref.shape[0]
    unit, _ = norm_parts(x_ref[...].astype(F32))
    normed = (unit * gain_ref[...]).astype(BF16)
    for part in range(3):
        cols = slice(part * width, (part + 1) * width)
        qkv_ref[:, cols] = dot(normed, wqkv_ref[:, cols], 1, 0).astype(BF16)
    lane = lax.broadcasted_iota(jnp.int32, (span, 128), 1)
    real = lax.broadcasted_iota(jnp.int32, (span, span), 1) < seq
    for pair in range(width // 128):
        q, k, v = (
            qkv_ref[:, part * width + pair * 128 : part * width + (pair + 1) * 128]
            for part in range(3)
        )
        ctx = jnp.zeros((span, 128), F32)
        for side in range(2):
            mine = (lane >= 64) if side else (lane < 64)
            own_k = jnp.where(mine, k, jnp.zeros_like(k))
            own_v = jnp.where(mine, v, jnp.zeros_like(v))
            weights = softmax_rows(q, own_k, real)
            ctx = ctx + dot(weights.astype(BF16), own_v, 1, 0)
        ctx_ref[:, pair * 128 : (pair + 1) * 128] = ctx.astype(BF16)
    part_ref[...] = dot(ctx_ref[...], wo_ref[...], 1, 1).astype(BF16)


def attend(inputs, gain, packed, width, images, seq):
    rows, model = inputs.shape
    span = rows // images
    image = lambda last: pl.BlockSpec((span, last), lambda i: (i, 0))
    return pl.pallas_call(
        functools.partial(attend_kernel, seq),
        grid=(images,),
        in_specs=[
            image(model),
            pl.BlockSpec((1, model), lambda i: (0, 0)),
            pl.BlockSpec((model, 3 * width), lambda i: (0, 0)),
            pl.BlockSpec((model, width), lambda i: (0, 3)),
        ],
        out_specs=[image(model), image(3 * width), image(width)],
        out_shape=[
            shaped((rows, model), BF16), shaped((rows, 3 * width), BF16), shaped((rows, width), BF16)
        ],
        compiler_params=params(),
        cost_estimate=cost(10 * rows * model * width, 8 * rows * model, rows * span * width // 64),
        name="attend",
    )(inputs, gain, packed, packed)


def attend_back_kernel(
    seq, gain_at,
    x_ref, gain_ref, datt_ref, qkv_ref, ctx_ref, wqkv_ref, wo_ref, side_ref,
    dnorm_ref, stats_ref, pack_ref, dproj_ref, dgain_ref, dwqkv_ref, dwo_ref,
):
    width = wo_ref.shape[1]
    span, model = x_ref.shape
    step = pl.program_id(0)

    @pl.when(step == 0)
    def _():
        dgain_ref[...] = jnp.zeros_like(dgain_ref)
        dwqkv_ref[...] = jnp.zeros_like(dwqkv_ref)
        dwo_ref[...] = jnp.zeros_like(dwo_ref)

    datt = datt_ref[...]
    dwo_ref[...] += dot(datt, ctx_ref[...], 0, 0)
    dctx_all = dot(datt, wo_ref[...], 1, 0).astype(BF16)
    lane = lax.broadcasted_iota(jnp.int32, (span, 128), 1)
    real = lax.broadcasted_iota(jnp.int32, (span, span), 1) < seq
    for pair in range(width // 128):
        q, k, v = (
            qkv_ref[:, part * width + pair * 128 : part * width + (pair + 1) * 128]
            for part in range(3)
        )
        dctx = dctx_all[:, pair * 128 : (pair + 1) * 128]
        dq = jnp.zeros((span, 128), F32)
        dk = jnp.zeros((span, 128), F32)
        dv = jnp.zeros((span, 128), F32)
        for side in range(2):
            mine = (lane >= 64) if side else (lane < 64)
            own = lambda t: jnp.where(mine, t, jnp.zeros_like(t))
            own_k, own_v = own(k), own(v)
            weights = softmax_rows(q, own_k, real)
            dweights = dot(dctx, own_v, 1, 1)
            inner = jnp.sum(dweights * weights, axis=-1, keepdims=True)
            dscores = (weights * (dweights - inner)).astype(BF16)
            dq = dq + dot(dscores, own_k, 1, 0)
            dk = dk + dot(dscores, own(q), 0, 0)
            dv = dv + dot(weights.astype(BF16), own(dctx), 0, 0)
        for part, value in enumerate((dq * HEAD_DIM**-0.5, dk * HEAD_DIM**-0.5, dv)):
            start = part * width + pair * 128
            dproj_ref[:, start : start + 128] = value.astype(BF16)
    dproj = dproj_ref[...]
    gain = gain_ref[...]
    unit, _ = norm_parts(x_ref[...].astype(F32))
    normed = (unit * gain).astype(BF16)
    dwqkv_ref[...] += dot(normed, dproj, 0, 0)
    dnormed = dot(dproj, wqkv_ref[...], 1, 1)
    halves, _, half = dnorm_ref.shape
    for h in range(halves):
        dnorm_ref[h] = dnormed[:, h * half : (h + 1) * half].astype(BF16)
    along = dnormed * unit
    dgain_ref[...] += jnp.sum(along, axis=0, keepdims=True)
    first = jnp.sum(dnormed * gain, axis=-1, keepdims=True)
    second = jnp.sum(along * gain, axis=-1, keepdims=True)
    stats_ref[...] = jnp.where(lane == 0, first, jnp.where(lane == 1, second, 0.0))

    @pl.when(step == pl.num_programs(0) - 1)
    def _():
        pack_ref[:, : 3 * width] = dwqkv_ref[...].astype(BF16)
        pack_ref[:, 3 * width : 4 * width] = dwo_ref[...].astype(BF16)
        line = lax.broadcasted_iota(jnp.int32, (128, model), 0)
        column = jnp.where(line == gain_at, dgain_ref[...], 0.0).T
        pack_ref[:, 4 * width :] = (side_ref[...] + column).astype(BF16)


def attend_back(inputs, gain, datt, qkv, ctx, packed, dside, gain_at, width, images, seq, halves):
    rows, model = inputs.shape
    span = rows // images
    image = lambda last: pl.BlockSpec((span, last), lambda i: (i, 0))
    fixed = lambda *size: pl.BlockSpec(size, lambda i: (0, 0))
    return pl.pallas_call(
        functools.partial(attend_back_kernel, seq, gain_at),
        grid=(images,),
        in_specs=[
            image(model), fixed(1, model), image(model), image(3 * width), image(width),
            fixed(model, 3 * width), pl.BlockSpec((model, width), lambda i: (0, 3)),
            fixed(model, 128),
        ],
        out_specs=[
            pl.BlockSpec((halves, span, model // halves), lambda i: (0, i, 0)),
            image(128),
            fixed(*packed.shape),
        ],
        out_shape=[
            shaped((halves, rows, model // halves), BF16),
            shaped((rows, 128), F32),
            shaped(packed.shape, BF16),
        ],
        scratch_shapes=[
            pltpu.VMEM((span, 3 * width), BF16),
            pltpu.VMEM((1, model), F32),
            pltpu.VMEM((model, 3 * width), F32),
            pltpu.VMEM((model, width), F32),
        ],
        compiler_params=params(),
        cost_estimate=cost(28 * rows * model * width, 12 * rows * model, rows * span * width // 64),
        name="attend_back",
    )(inputs, gain, datt, qkv, ctx, packed, packed, dside)


def expert_kernel(depth, blocks, place_ref, slot_ref, router_ref, *refs):
    x_refs, refs = refs[:blocks], refs[blocks:]
    grad_refs, refs = refs[:blocks], refs[blocks:]
    win_refs, refs = refs[:depth], refs[depth:]
    wout_refs, refs = refs[:depth], refs[depth:]
    (
        rows_ref, mids_ref, dchosen_ref, drows_ref, yrows_ref, probs_ref, win_all, wout_all,
    ) = refs
    slots, model = rows_ref.shape[2:]
    tokens = x_refs[0].shape[0]
    part_rows, width = win_refs[0].shape[1:]
    step = pl.program_id(0)

    @pl.when(step == 0)
    def _():
        for k in range(depth):
            owner = lax.rem(place_ref[0] - k + depth, depth)
            at = pl.ds(pl.multiple_of(owner * part_rows, 16), part_rows)
            win_all[at, :] = win_refs[k][0]
            wout_all[at, :] = wout_refs[k][0]

    mask = lax.broadcasted_iota(jnp.int32, (slots, tokens), 0) == slot_ref[0]
    pick = jnp.where(mask, 1.0, 0.0).astype(BF16)
    for b in range(blocks):

        @pl.when(step == b)
        def _(b=b):
            rows_ref[0, 0] = dot(pick, grad_refs[b][...], 1, 0).astype(BF16)
            rows_ref[1, 0] = dot(pick, x_refs[b][...], 1, 0).astype(BF16)
            logits = dot(router_ref[...], x_refs[b][...], 1, 1)
            powers = jnp.exp(logits - jnp.max(logits, axis=0, keepdims=True))
            probs_ref[0] = powers / jnp.sum(powers, axis=0, keepdims=True)

    probs = probs_ref[0]
    line = lax.broadcasted_iota(jnp.int32, probs.shape, 0)
    own = jnp.sum(jnp.where(line == place_ref[1], probs, 0.0), axis=0, keepdims=True)
    gate = jnp.sum(jnp.where(mask, own, 0.0), axis=1, keepdims=True)
    grows, rows = rows_ref[0, 0], rows_ref[1, 0]
    dgate = jnp.zeros((slots, 1), F32)
    drows = jnp.zeros((slots, model), F32)
    yrows = jnp.zeros((slots, model), F32)
    tile = 512 if width % 512 == 0 else width
    curve = 0.7978845608028654
    for start in range(0, width, tile):
        cols = slice(start, start + tile)
        win, wout = win_all[:, cols], wout_all[:, cols]
        hidden = dot(rows, win, 1, 0)
        pulled = dot(grows, wout, 1, 0)
        square = hidden * hidden
        bend = jnp.tanh(hidden * (curve + curve * 0.044715 * square))
        half = 0.5 + 0.5 * bend
        active = hidden * half
        slope = half + 0.5 * hidden * (1.0 - bend * bend) * (
            curve + 3.0 * curve * 0.044715 * square
        )
        dgate = dgate + jnp.sum(active * pulled, axis=1, keepdims=True)
        gact = (gate * active).astype(BF16)
        dhid = (gate * pulled * slope).astype(BF16)
        mids_ref[0, 0, :, cols] = gact
        mids_ref[1, 0, :, cols] = dhid
        drows = drows + dot(dhid, win, 1, 1)
        yrows = yrows + dot(gact, wout, 1, 1)
    dchosen_ref[0] = jnp.sum(jnp.where(mask, dgate, 0.0), axis=0, keepdims=True)
    drows_ref[0] = drows.astype(BF16)
    yrows_ref[0] = yrows.astype(BF16)


def run_expert(place, slot_of, router_rows, xs, grads, pieces, slots):
    blocks, depth = len(xs), len(pieces)
    tokens, model = xs[0].shape
    _, part_rows, width = pieces[0].shape
    experts = router_rows.shape[0]
    fixed = lambda *size: pl.BlockSpec(
        size, lambda b, s: (0,) * len(size), pipeline_mode=pl.Buffered(1)
    )
    block = lambda *size: pl.BlockSpec((1,) + size, lambda b, s: (b, 0, 0))
    both = lambda last: pl.BlockSpec((2, 1, slots, last), lambda b, s: (0, b, 0, 0))
    weight = lambda which: pl.BlockSpec(
        (1, part_rows, width), lambda b, s: (which, 0, 0), pipeline_mode=pl.Buffered(1)
    )
    return pl.pallas_call(
        functools.partial(expert_kernel, depth, blocks),
        grid_spec=pltpu.PrefetchScalarGridSpec(
            num_scalar_prefetch=1,
            grid=(blocks,),
            in_specs=[block(1, tokens), fixed(experts, model)]
            + [fixed(tokens, model)] * (2 * blocks)
            + [weight(1)] * depth
            + [weight(0)] * depth,
            out_specs=[
                both(model), both(width), block(1, tokens), block(slots, model),
                block(slots, model), block(experts, tokens),
            ],
            scratch_shapes=[pltpu.VMEM((model, width), BF16)] * 2,
        ),
        out_shape=[
            shaped((2, blocks, slots, model), BF16), shaped((2, blocks, slots, width), BF16),
            shaped((blocks, 1, tokens), F32), shaped((blocks, slots, model), BF16),
            shaped((blocks, slots, model), BF16), shaped((blocks, experts, tokens), F32),
        ],
        compiler_params=params(),
        cost_estimate=cost(
            8 * blocks * slots * model * width + 4 * blocks * slots * model * tokens,
            16 * blocks * slots * model,
            blocks * slots * width,
        ),
        name="expert",
    )(place, slot_of, router_rows, *xs, *grads, *pieces, *pieces)


def weight_grad_kernel(depth, place_ref, rows_ref, cols_ref, *refs):
    out_refs, total_ref = refs[:depth], refs[depth]
    _, blocks, slots, model = rows_ref.shape
    width = cols_ref.shape[3]
    part_rows = model // depth
    left = rows_ref[0].reshape(blocks * slots, model)
    right = cols_ref[0].reshape(blocks * slots, width)
    total_ref[...] = dot(left, right, 0, 0)
    for k in range(depth):
        owner = lax.rem(place_ref[0] - k + depth, depth)
        at = pl.ds(pl.multiple_of(owner * part_rows, 16), part_rows)
        out_refs[k][0] = total_ref[at, :].astype(BF16)


def weight_grad(place, rows, cols, depth):
    _, blocks, slots, model = rows.shape
    width = cols.shape[3]
    both = lambda last: pl.BlockSpec((1, blocks, slots, last), lambda i, s: (i, 0, 0, 0))
    return pl.pallas_call(
        functools.partial(weight_grad_kernel, depth),
        grid_spec=pltpu.PrefetchScalarGridSpec(
            num_scalar_prefetch=1,
            grid=(2,),
            in_specs=[both(model), both(width)],
            out_specs=[pl.BlockSpec((1, model // depth, width), lambda i, s: (i, 0, 0))] * depth,
            scratch_shapes=[pltpu.VMEM((model, width), F32)],
        ),
        out_shape=[shaped((2, model // depth, width), BF16)] * depth,
        compiler_params=params(),
        cost_estimate=cost(
            4 * blocks * slots * model * width,
            4 * (blocks * slots * (model + width) + model * width),
        ),
        name="weight_grad",
    )(place, rows, cols)


def combine_kernel(local, added, slot_ref, *refs):
    rows_refs, refs = refs[:local], refs[local:]
    out_ref = refs[-1]
    tokens = out_ref.shape[-2]
    slots, model = rows_refs[0].shape[1:]
    at = lax.broadcasted_iota(jnp.int32, (tokens, slots), 1)
    total = refs[0][...].astype(F32) if added else jnp.zeros((tokens, model), F32)
    for e in range(local):
        pick = jnp.where(at == slot_ref[0, :, e : e + 1], 1.0, 0.0).astype(BF16)
        total = total + dot(pick, rows_refs[e][0], 1, 0)
    out_ref[...] = total.astype(BF16)


def combine(slot_cols, rows, b, add=None):
    _, tokens, local = slot_cols.shape
    slots, model = rows[0].shape[1:]
    whole = pl.BlockSpec((tokens, model), lambda i: (0, 0))
    return pl.pallas_call(
        functools.partial(combine_kernel, local, add is not None),
        grid=(1,),
        in_specs=[pl.BlockSpec((1, tokens, local), lambda i: (b, 0, 0))]
        + [pl.BlockSpec((1, slots, model), lambda i: (b, 0, 0))] * local
        + [whole] * (add is not None),
        out_specs=whole,
        out_shape=shaped((tokens, model), BF16),
        compiler_params=params(),
        cost_estimate=cost(
            2 * local * slots * model * tokens, 2 * model * (local * slots + 2 * tokens)
        ),
        name="combine",
    )(slot_cols, *rows, *(() if add is None else (add,)))


def combine_back_kernel(local, added, place_ref, slot_ref, *refs):
    rows_refs, refs = refs[:local], refs[local:]
    dchosen_refs, refs = refs[:local], refs[local:]
    probs_ref, router_ref, x_ref = refs[:3]
    out_ref, drouter_ref = refs[-2:]
    tokens = out_ref.shape[0]
    slots = rows_refs[0].shape[1]
    at = lax.broadcasted_iota(jnp.int32, (tokens, slots), 1)
    probs = probs_ref[0]
    line = lax.broadcasted_iota(jnp.int32, probs.shape, 0)
    dprobs = jnp.zeros_like(probs)
    for e in range(local):
        dprobs = jnp.where(line == place_ref[1] + e, dchosen_refs[e][0], dprobs)
    inner = jnp.sum(dprobs * probs, axis=0, keepdims=True)
    dlogits = (probs * (dprobs - inner)).astype(BF16)
    drouter_ref[...] = dot(dlogits, x_ref[...], 1, 0)
    total = dot(dlogits, router_ref[...], 0, 0)
    if added:
        total = total + refs[3][...].astype(F32)
    for e in range(local):
        pick = jnp.where(at == slot_ref[0, :, e : e + 1], 1.0, 0.0).astype(BF16)
        total = total + dot(pick, rows_refs[e][0], 1, 0)
    out_ref[...] = total.astype(BF16)


def combine_back(place, slot_cols, rows, dchosen, probs, router_rows, x, b, add=None):
    _, tokens, local = slot_cols.shape
    slots, model = rows[0].shape[1:]
    experts = router_rows.shape[0]
    whole = pl.BlockSpec((tokens, model), lambda i, s: (0, 0))
    block = lambda *size: pl.BlockSpec((1,) + size, lambda i, s: (b, 0, 0))
    small = pl.BlockSpec((experts, model), lambda i, s: (0, 0))
    return pl.pallas_call(
        functools.partial(combine_back_kernel, local, add is not None),
        grid_spec=pltpu.PrefetchScalarGridSpec(
            num_scalar_prefetch=1,
            grid=(1,),
            in_specs=[block(tokens, local)]
            + [block(slots, model)] * local
            + [block(1, tokens)] * local
            + [block(experts, tokens), small, whole]
            + [whole] * (add is not None),
            out_specs=[whole, small],
        ),
        out_shape=[shaped((tokens, model), BF16), shaped((experts, model), F32)],
        compiler_params=params(),
        cost_estimate=cost(
            2 * local * slots * model * tokens, 2 * model * (local * slots + 3 * tokens)
        ),
        name="combine_back",
    )(place, slot_cols, *rows, *dchosen, probs, router_rows, x, *(() if add is None else (add,)))


def per_device(
    block_in, cotangent, route_ids, gain_attn, w_qkv, w_out_attn, gain_moe, router, w_in, w_out
):
    n_dp, n_heads, n_exp = (lax.axis_size(name) for name in ("dp", "heads", "expert"))
    n_z = n_dp // CORES
    dp, head, exp = (lax.axis_index(name) for name in ("dp", "heads", "expert"))
    z, core = dp // CORES, dp % CORES
    low = core == 0
    images, seq, half_width = block_in.shape
    span = -(-seq // 16) * 16
    rows = images * span
    model = half_width * n_heads
    width = w_qkv.shape[2]
    shard = w_qkv.shape[0]
    expert_count = router.shape[1]
    group = w_in.shape[1]
    local = group // CORES
    part_rows, _, hidden_width = w_in.shape
    capacity = 20 * images * seq // (7 * expert_count)
    slots = -(-capacity // 16) * 16
    blocks = n_exp * CORES
    rest = 128

    def shift(value, axis, step):
        size = lax.axis_size(axis)
        return lax.ppermute(value, axis, [(i, (i + step) % size) for i in range(size)])

    def shift_z(value, step):
        pairs = [
            (a * CORES + c, ((a + step) % n_z) * CORES + c) for a in range(n_z) for c in range(CORES)
        ]
        return lax.ppermute(value, "dp", pairs)

    def swap_core(value):
        return lax.ppermute(value, "dp", [(i, i ^ 1) for i in range(n_dp)])

    def place_at(pieces, index, count):
        if count == 2:
            first = index == 0
            return jnp.stack(
                [jnp.where(first, pieces[0], pieces[1]), jnp.where(first, pieces[1], pieces[0])]
            )
        out = jnp.zeros((count,) + pieces[0].shape, pieces[0].dtype)
        for k, piece in enumerate(pieces):
            out = lax.dynamic_update_index_in_dim(out, piece, (index - k) % count, 0)
        return out

    def spread(value, axis):
        return [value] + [shift(value, axis, k) for k in range(1, lax.axis_size(axis))]

    def take(value, index, dim=0):
        return lax.dynamic_index_in_dim(value, index, dim, keepdims=False)

    def expert_shards():
        both = jnp.stack([w_out, w_in]).reshape(2, part_rows, CORES, local, hidden_width)
        by_core = both.transpose(2, 3, 0, 1, 4)
        other = swap_core(take(by_core, 1 - core))
        mine = take(by_core, core)
        return jnp.concatenate(
            [jnp.where(low, mine, other), jnp.where(low, other, mine)], axis=2
        )

    ways_up = n_z // 2
    ways_down = n_z - 1 - ways_up

    def ring(piece):
        pieces = [piece] + [None] * (n_z - 1)
        for k in range(1, ways_up + 1):
            pieces[k] = shift_z(pieces[k - 1], 1)
        for k in range(1, ways_down + 1):
            pieces[n_z - k] = shift_z(pieces[(n_z - k + 1) % n_z], -1)
        return pieces

    def blocks_of(value, hold=()):
        along = spread(value, "expert")
        along = along[:1] + [after(part, *hold) for part in along[1:]]
        return along + [swap_core(part) for part in along]

    tail = jnp.concatenate(
        [router, gain_attn[:, None], gain_moe[:, None],
         jnp.zeros((shard, rest - expert_count - 2), BF16)], axis=1
    )
    own_pack = jnp.concatenate([w_qkv.reshape(shard, 3 * width), w_out_attn, tail], axis=1)
    columns = own_pack.shape[1]
    shards = expert_shards()
    ids = jnp.pad(route_ids, ((0, 0), (0, span - seq), (0, 0)), constant_values=-1)
    ids_all = jnp.stack(blocks_of(ids.reshape(rows, 2).T))
    pack_z = place_at(
        [own_pack] + [after(shift_z(own_pack, k), shards) for k in range(1, n_z)], z, n_z
    )
    pack = place_at(spread(after(pack_z, ids_all), "expert"), exp, n_exp)
    pieces = []
    for e in range(local):
        pieces.append(ring(after(shards[e], pieces[-1][1]) if e else shards[e]))
    last = local - 1

    other_pack = swap_core(pack)
    pack = jnp.stack([jnp.where(low, pack, other_pack), jnp.where(low, other_pack, pack)])
    pack = pack.transpose(2, 0, 1, 3, 4).reshape(model, columns)
    side = pack[:, 4 * width :].T
    router_rows = side[:expert_count]
    gain_one = side[expert_count : expert_count + 1].astype(F32)
    gain_two = side[expert_count + 1 : expert_count + 2].astype(F32)

    def full_rows(value):
        padded = jnp.pad(value, ((0, 0), (0, span - seq), (0, 0))).reshape(rows, half_width)
        parts = place_at(spread(padded, "heads"), head, n_heads)
        return jnp.concatenate([parts[i] for i in range(n_heads)], axis=-1)

    inputs = full_rows(block_in)

    first_expert = exp * group + core * local
    named = first_expert + jnp.arange(local, dtype=jnp.int32)
    chosen = jnp.any(ids_all[:, None, :, :] == named[None, :, None, None], axis=2)
    before = (jnp.arange(rows)[:, None] < jnp.arange(rows)[None, :]).astype(BF16)
    rank = jnp.dot(
        chosen.astype(BF16).reshape(blocks * local, rows), before, preferred_element_type=F32
    ).astype(jnp.int32).reshape(blocks, local, rows)
    slot_of = jnp.where(chosen, rank, -1)
    slot_cols = slot_of.transpose(0, 2, 1)
    place = [jnp.stack([z, first_expert + e]).astype(jnp.int32) for e in range(local)]

    grad_full = full_rows(cotangent)
    grads_all = blocks_of(grad_full)
    inputs_ready = after(inputs, pieces[0][1], grad_full)
    part, qkv, ctx = attend(inputs_ready, gain_one, pack, width, images, seq)
    part = after(part, pieces[0][-1])
    part_other = shift(part, "heads", 1)
    for k in range(2, n_heads):
        part_other = part_other + shift(part, "heads", k)
    part_other = after(part_other, pieces[0][ways_up])
    middle = inputs.astype(F32) + (part.astype(F32) + part_other.astype(F32))
    unit_two, scale_two = norm_parts(middle)
    normed_two = (unit_two * gain_two).astype(BF16)
    tokens_all = blocks_of(normed_two, (pieces[last][1],))

    done = []

    def begin_rings(e, *hold):
        rows_e, mids_e = done[e][:2]
        rings.append(weight_grad(place[e], after(rows_e, *hold), mids_e, n_z))

    def ring_first(e):
        return shift_z(rings[e][-ways_up % n_z], 1)

    def ring_down(e):
        chunks = rings[e]
        downward = chunks[ways_down]
        for k in range(ways_down - 1, 0, -1):
            downward = (shift_z(downward, -1).astype(F32) + chunks[k].astype(F32)).astype(BF16)
        return shift_z(downward, -1)

    def ring_middle(e, upward, *hold):
        chunks = rings[e]
        for k in range(ways_up - 1, 0, -1):
            own = after(chunks[n_z - k], *hold)
            upward = (upward.astype(F32) + own.astype(F32)).astype(BF16)
            if k > 1:
                upward = shift_z(upward, 1)
        return upward

    def ring_end(e, upward, downward, *hold):
        own = after(rings[e][0], *hold).astype(F32)
        return own + shift_z(upward, 1).astype(F32) + downward.astype(F32)

    rings = []
    for e in range(local):
        here = list(pieces[e])
        if e:
            here[0] = after(here[0], rings[-1][0])
        done.append(
            run_expert(
                place[e], slot_of[:, e : e + 1, :], router_rows, tokens_all, grads_all, here, slots
            )
        )
        if e < local - 1:
            begin_rings(e)
    drows, yrows, dchosen = ([r[i] for r in done] for i in (3, 4, 2))
    probs = done[0][5]

    arrived_zero, down_zero = ring_first(0), ring_down(0)
    drows[0] = after(drows[0], arrived_zero, down_zero)

    def back_of(b, add=None):
        return combine_back(
            place[0], slot_cols, drows, dchosen, probs, router_rows, tokens_all[b], b, add
        )

    drouter = jnp.zeros((expert_count, model), F32)
    arrived = [None] * n_exp
    for k in reversed(range(n_exp)):
        sent, more = back_of(n_exp + k)
        arrived[k] = swap_core(sent)
        drouter = drouter + more
    from_exp = []
    for k in reversed(range(n_exp)):
        total, more = back_of(k, arrived[k])
        drouter = drouter + more
        if k:
            from_exp.append(shift(total, "expert", -k))
            if k == 1:
                begin_rings(last, total)
                early = ring_middle(0, arrived_zero, total)
    dsum = after(total, early, rings[last][0]).astype(F32)
    for value in from_exp:
        dsum = dsum + value.astype(F32)
    dsum = dsum.astype(BF16)

    dsum_other = shift(dsum, "heads", 1)
    for k in range(2, n_heads):
        dsum_other = dsum_other + shift(dsum, "heads", k)
    ends = [ring_end(0, early, down_zero, dsum)]
    yrows[0] = after(yrows[0], ends[0])
    y_came = [swap_core(combine(slot_cols, yrows, n_exp + k)) for k in range(n_exp)]
    y_from = []
    for k in reversed(range(n_exp)):
        y_own = combine(slot_cols, yrows, k, y_came[k])
        if k:
            y_from.append(shift(y_own, "expert", -k))
    y_own = y_own.astype(F32)
    for value in y_from:
        y_own = y_own + value.astype(F32)
    y_own = y_own.astype(BF16)

    arrived_last, down_last = ring_first(last), ring_down(last)
    dsum_other = after(dsum_other, ends[0], arrived_last)
    dnormed_two = dsum.astype(F32) + dsum_other.astype(F32)
    scaled = dnormed_two * gain_two
    grad_gain_two = jnp.sum(dnormed_two * unit_two, axis=0)
    dmiddle = grad_full.astype(F32) + scale_two * (
        scaled
        - jnp.mean(scaled, axis=-1, keepdims=True)
        - unit_two * jnp.mean(scaled * unit_two, axis=-1, keepdims=True)
    )
    late = ring_middle(last, arrived_last, dsum_other)
    datt = after(dmiddle.astype(BF16), late)

    dside = jnp.concatenate(
        [drouter, jnp.zeros((1, model), F32), grad_gain_two[None, :],
         jnp.zeros((rest - expert_count - 2, model), F32)], axis=0
    ).T
    dnorm, stats, dpack = attend_back(
        inputs, gain_one, datt, qkv, ctx, pack, dside, expert_count, width, images, seq, n_heads
    )
    dpack = after(dpack, y_own, down_last)

    dpack = dpack.reshape(n_z, CORES, n_exp, shard, columns)
    dsent = swap_core(take(dpack, 1 - core, 1))
    dpack = (take(dpack, core, 1).astype(F32) + dsent.astype(F32)).astype(BF16)
    dtotal = take(dpack, exp, 1).astype(F32)
    for k in range(1, n_exp):
        dtotal = dtotal + shift(take(dpack, (exp + k) % n_exp, 1), "expert", k).astype(F32)
    dpack = dtotal.astype(BF16)
    ends.append(ring_end(last, late, down_last, dpack))
    dtotal = take(dpack, z).astype(F32)
    for k in range(1, n_z):
        dtotal = dtotal + shift_z(take(dpack, (z + k) % n_z), k).astype(F32)
    dside = dtotal[:, 4 * width :]
    over_heads = dside[:, : expert_count + 1].T
    summed = over_heads
    for k in range(1, n_heads):
        summed = summed + shift(over_heads, "heads", k)

    def own_half(value):
        return lax.dynamic_slice_in_dim(value, head * half_width, half_width, 1)

    def cut(value):
        return value.astype(BF16).reshape(images, span, half_width)[:, :seq]

    dn_own = take(dnorm, head).astype(F32)
    sums = stats[:, :2].T
    sums_total = sums
    for k in range(1, n_heads):
        dn_own = dn_own + shift(take(dnorm, (head + k) % n_heads), "heads", k).astype(F32)
        sums_total = sums_total + shift(sums, "heads", k)
    unit_one, scale_one = norm_parts(inputs.astype(F32))
    grad_in = own_half(dmiddle) + scale_one * (
        dn_own * own_half(gain_one)
        - sums_total[0][:, None] / model
        - own_half(unit_one) * (sums_total[1][:, None] / model)
    )

    y_total = own_half(y_own).astype(F32)
    for k in range(1, n_heads):
        there = (head + k) % n_heads
        part_y = lax.dynamic_slice_in_dim(y_own, there * half_width, half_width, 1)
        y_total = y_total + shift(part_y, "heads", k).astype(F32)
    block_out = own_half(middle) + y_total

    stacked = jnp.stack(ends).reshape(local, 2, CORES, part_rows, hidden_width)
    other = swap_core(take(stacked, 1 - core, 2).astype(BF16)).astype(F32)
    own = take(stacked, core, 2)
    joined = jnp.concatenate([jnp.where(low, own, other), jnp.where(low, other, own)], axis=0)
    grads = joined.transpose(1, 2, 0, 3)

    return (
        cut(block_out),
        cut(grad_in),
        summed[expert_count],
        dtotal[:, : 3 * width].reshape(shard, 3, width),
        dtotal[:, 3 * width : 4 * width],
        dside[:, expert_count + 1],
        summed[:expert_count].T,
        grads[1],
        grads[0],
    )


def solution(mesh):
    return jax.shard_map(
        per_device,
        mesh=mesh,
        in_specs=(
            P(("dp", "expert"), None, "heads"),
            P(("dp", "expert"), None, "heads"),
            P(("dp", "expert"), None, None),
            P(("dp", "expert")),
            P(("dp", "expert"), None, "heads"),
            P(("dp", "expert"), "heads"),
            P(("dp", "expert")),
            P(("dp", "expert"), None),
            P("dp", "expert", "heads"),
            P("dp", "expert", "heads"),
        ),
        out_specs=(
            P(("dp", "expert"), None, "heads"),
            P(("dp", "expert"), None, "heads"),
            P(("dp", "expert")),
            P(("dp", "expert"), None, "heads"),
            P(("dp", "expert"), "heads"),
            P(("dp", "expert")),
            P(("dp", "expert"), None),
            P("dp", "expert", "heads"),
            P("dp", "expert", "heads"),
        ),
        check_vma=False,
    )
```

```python
import functools

import jax
import jax.numpy as jnp
from jax import lax
from jax.experimental import pallas as pl
from jax.experimental.pallas import tpu as pltpu
from jax.sharding import PartitionSpec as P

HEAD_DIM = 64
CORES = 2
EPS = 1e-06
LOW = -1e30
F32 = jnp.float32
BF16 = jnp.bfloat16
VMEM_LIMIT = 56 * 1024 * 1024
SHARE = 64
PARTS = 2


def dot(a, b, ca, cb):
    return lax.dot_general(a, b, (((ca,), (cb,)), ((), ())), preferred_element_type=F32)


def shaped(shape, kind):
    return jax.ShapeDtypeStruct(shape, kind)


def params(dims=1):
    return pltpu.CompilerParams(
        dimension_semantics=("arbitrary",) * dims, vmem_limit_bytes=VMEM_LIMIT
    )


def cost(flops, size, powers=0):
    return pl.CostEstimate(
        flops=flops // SHARE, bytes_accessed=size // SHARE, transcendentals=powers // SHARE
    )


def after(value, *others):
    return lax.optimization_barrier((value,) + others)[0]


def norm_parts(rows):
    average = jnp.mean(rows, axis=-1, keepdims=True)
    centred = rows - average
    spread = jnp.mean(centred * centred, axis=-1, keepdims=True)
    scale = lax.rsqrt(spread + EPS)
    return centred * scale, scale


def softmax_rows(q, own_k, real):
    scores = jnp.where(real, dot(q, own_k, 1, 1) * (HEAD_DIM**-0.5), LOW)
    powers = jnp.exp(scores - jnp.max(scores, axis=-1, keepdims=True))
    return powers / jnp.sum(powers, axis=-1, keepdims=True)


def attend_kernel(seq, x_ref, gain_ref, wqkv_ref, wo_ref, part_ref, qkv_ref, ctx_ref):
    width = wo_ref.shape[1]
    span = x_ref.shape[0]
    unit, _ = norm_parts(x_ref[...].astype(F32))
    normed = (unit * gain_ref[...]).astype(BF16)
    for part in range(3):
        cols = slice(part * width, (part + 1) * width)
        qkv_ref[:, cols] = dot(normed, wqkv_ref[:, cols], 1, 0).astype(BF16)
    lane = lax.broadcasted_iota(jnp.int32, (span, 128), 1)
    real = lax.broadcasted_iota(jnp.int32, (span, span), 1) < seq
    for pair in range(width // 128):
        q, k, v = (
            qkv_ref[:, part * width + pair * 128 : part * width + (pair + 1) * 128]
            for part in range(3)
        )
        ctx = jnp.zeros((span, 128), F32)
        for side in range(2):
            mine = (lane >= 64) if side else (lane < 64)
            own_k = jnp.where(mine, k, jnp.zeros_like(k))
            own_v = jnp.where(mine, v, jnp.zeros_like(v))
            weights = softmax_rows(q, own_k, real)
            ctx = ctx + dot(weights.astype(BF16), own_v, 1, 0)
        ctx_ref[:, pair * 128 : (pair + 1) * 128] = ctx.astype(BF16)
    part_ref[...] = dot(ctx_ref[...], wo_ref[...], 1, 1).astype(BF16)


def attend(inputs, gain, packed, width, images, seq):
    rows, model = inputs.shape
    span = rows // images
    image = lambda last: pl.BlockSpec((span, last), lambda i: (i, 0))
    return pl.pallas_call(
        functools.partial(attend_kernel, seq),
        grid=(images,),
        in_specs=[
            image(model),
            pl.BlockSpec((1, model), lambda i: (0, 0)),
            pl.BlockSpec((model, 3 * width), lambda i: (0, 0)),
            pl.BlockSpec((model, width), lambda i: (0, 3)),
        ],
        out_specs=[image(model), image(3 * width), image(width)],
        out_shape=[
            shaped((rows, model), BF16), shaped((rows, 3 * width), BF16), shaped((rows, width), BF16)
        ],
        compiler_params=params(),
        cost_estimate=cost(10 * rows * model * width, 8 * rows * model, rows * span * width // 64),
        name="attend",
    )(inputs, gain, packed, packed)


def attend_back_kernel(
    seq, gain_at,
    x_ref, gain_ref, datt_ref, qkv_ref, ctx_ref, wqkv_ref, wo_ref, side_ref,
    dnorm_ref, stats_ref, pack_ref, dproj_ref, dgain_ref, dwqkv_ref, dwo_ref,
):
    width = wo_ref.shape[1]
    span, model = x_ref.shape
    step = pl.program_id(0)

    @pl.when(step == 0)
    def _():
        dgain_ref[...] = jnp.zeros_like(dgain_ref)
        dwqkv_ref[...] = jnp.zeros_like(dwqkv_ref)
        dwo_ref[...] = jnp.zeros_like(dwo_ref)

    datt = datt_ref[...]
    dwo_ref[...] += dot(datt, ctx_ref[...], 0, 0)
    dctx_all = dot(datt, wo_ref[...], 1, 0).astype(BF16)
    lane = lax.broadcasted_iota(jnp.int32, (span, 128), 1)
    real = lax.broadcasted_iota(jnp.int32, (span, span), 1) < seq
    for pair in range(width // 128):
        q, k, v = (
            qkv_ref[:, part * width + pair * 128 : part * width + (pair + 1) * 128]
            for part in range(3)
        )
        dctx = dctx_all[:, pair * 128 : (pair + 1) * 128]
        dq = jnp.zeros((span, 128), F32)
        dk = jnp.zeros((span, 128), F32)
        dv = jnp.zeros((span, 128), F32)
        for side in range(2):
            mine = (lane >= 64) if side else (lane < 64)
            own = lambda t: jnp.where(mine, t, jnp.zeros_like(t))
            own_k, own_v = own(k), own(v)
            weights = softmax_rows(q, own_k, real)
            dweights = dot(dctx, own_v, 1, 1)
            inner = jnp.sum(dweights * weights, axis=-1, keepdims=True)
            dscores = (weights * (dweights - inner)).astype(BF16)
            dq = dq + dot(dscores, own_k, 1, 0)
            dk = dk + dot(dscores, own(q), 0, 0)
            dv = dv + dot(weights.astype(BF16), own(dctx), 0, 0)
        for part, value in enumerate((dq * HEAD_DIM**-0.5, dk * HEAD_DIM**-0.5, dv)):
            start = part * width + pair * 128
            dproj_ref[:, start : start + 128] = value.astype(BF16)
    dproj = dproj_ref[...]
    gain = gain_ref[...]
    unit, _ = norm_parts(x_ref[...].astype(F32))
    normed = (unit * gain).astype(BF16)
    dwqkv_ref[...] += dot(normed, dproj, 0, 0)
    dnormed = dot(dproj, wqkv_ref[...], 1, 1)
    halves, _, half = dnorm_ref.shape
    for h in range(halves):
        dnorm_ref[h] = dnormed[:, h * half : (h + 1) * half].astype(BF16)
    along = dnormed * unit
    dgain_ref[...] += jnp.sum(along, axis=0, keepdims=True)
    first = jnp.sum(dnormed * gain, axis=-1, keepdims=True)
    second = jnp.sum(along * gain, axis=-1, keepdims=True)
    stats_ref[...] = jnp.where(lane == 0, first, jnp.where(lane == 1, second, 0.0))

    @pl.when(step == pl.num_programs(0) - 1)
    def _():
        pack_ref[:, : 3 * width] = dwqkv_ref[...].astype(BF16)
        pack_ref[:, 3 * width : 4 * width] = dwo_ref[...].astype(BF16)
        line = lax.broadcasted_iota(jnp.int32, (128, model), 0)
        column = jnp.where(line == gain_at, dgain_ref[...], 0.0).T
        pack_ref[:, 4 * width :] = (side_ref[...] + column).astype(BF16)


def attend_back(inputs, gain, datt, qkv, ctx, packed, dside, gain_at, width, images, seq, halves):
    rows, model = inputs.shape
    span = rows // images
    image = lambda last: pl.BlockSpec((span, last), lambda i: (i, 0))
    fixed = lambda *size: pl.BlockSpec(size, lambda i: (0, 0))
    return pl.pallas_call(
        functools.partial(attend_back_kernel, seq, gain_at),
        grid=(images,),
        in_specs=[
            image(model), fixed(1, model), image(model), image(3 * width), image(width),
            fixed(model, 3 * width), pl.BlockSpec((model, width), lambda i: (0, 3)),
            fixed(model, 128),
        ],
        out_specs=[
            pl.BlockSpec((halves, span, model // halves), lambda i: (0, i, 0)),
            image(128),
            fixed(*packed.shape),
        ],
        out_shape=[
            shaped((halves, rows, model // halves), BF16),
            shaped((rows, 128), F32),
            shaped(packed.shape, BF16),
        ],
        scratch_shapes=[
            pltpu.VMEM((span, 3 * width), BF16),
            pltpu.VMEM((1, model), F32),
            pltpu.VMEM((model, 3 * width), F32),
            pltpu.VMEM((model, width), F32),
        ],
        compiler_params=params(),
        cost_estimate=cost(28 * rows * model * width, 12 * rows * model, rows * span * width // 64),
        name="attend_back",
    )(inputs, gain, datt, qkv, ctx, packed, packed, dside)


def expert_kernel(depth, blocks, place_ref, slot_ref, router_ref, *refs):
    x_refs, refs = refs[:blocks], refs[blocks:]
    grad_refs, refs = refs[:blocks], refs[blocks:]
    win_refs, refs = refs[:depth], refs[depth:]
    wout_refs, refs = refs[:depth], refs[depth:]
    (
        rows_ref, mids_ref, dchosen_ref, drows_ref, yrows_ref, probs_ref, win_all, wout_all,
    ) = refs
    slots, model = rows_ref.shape[2:]
    tokens = x_refs[0].shape[0]
    part_rows, width = win_refs[0].shape[1:]
    step = pl.program_id(0)

    @pl.when(step == 0)
    def _():
        for k in range(depth):
            owner = lax.rem(place_ref[0] - k + depth, depth)
            at = pl.ds(pl.multiple_of(owner * part_rows, 16), part_rows)
            win_all[at, :] = win_refs[k][0]
            wout_all[at, :] = wout_refs[k][0]

    mask = lax.broadcasted_iota(jnp.int32, (slots, tokens), 0) == slot_ref[0]
    pick = jnp.where(mask, 1.0, 0.0).astype(BF16)
    for b in range(blocks):

        @pl.when(step == b)
        def _(b=b):
            rows_ref[0, 0] = dot(pick, grad_refs[b][...], 1, 0).astype(BF16)
            rows_ref[1, 0] = dot(pick, x_refs[b][...], 1, 0).astype(BF16)
            logits = dot(router_ref[...], x_refs[b][...], 1, 1)
            powers = jnp.exp(logits - jnp.max(logits, axis=0, keepdims=True))
            probs_ref[0] = powers / jnp.sum(powers, axis=0, keepdims=True)

    probs = probs_ref[0]
    line = lax.broadcasted_iota(jnp.int32, probs.shape, 0)
    own = jnp.sum(jnp.where(line == place_ref[1], probs, 0.0), axis=0, keepdims=True)
    gate = jnp.sum(jnp.where(mask, own, 0.0), axis=1, keepdims=True)
    grows, rows = rows_ref[0, 0], rows_ref[1, 0]
    dgate = jnp.zeros((slots, 1), F32)
    drows = jnp.zeros((slots, model), F32)
    yrows = jnp.zeros((slots, model), F32)
    tile = 512 if width % 512 == 0 else width
    curve = 0.7978845608028654

    def products(start):
        cols = slice(start, start + tile)
        return dot(rows, win_all[:, cols], 1, 0), dot(grows, wout_all[:, cols], 1, 0)

    ahead = products(0)
    for start in range(0, width, tile):
        cols = slice(start, start + tile)
        hidden, pulled = ahead
        if start + tile < width:
            ahead = products(start + tile)
        square = hidden * hidden
        bend = jnp.tanh(hidden * (curve + curve * 0.044715 * square))
        half = 0.5 + 0.5 * bend
        active = hidden * half
        slope = half + 0.5 * hidden * (1.0 - bend * bend) * (
            curve + 3.0 * curve * 0.044715 * square
        )
        dgate = dgate + jnp.sum(active * pulled, axis=1, keepdims=True)
        gact = (gate * active).astype(BF16)
        dhid = (gate * pulled * slope).astype(BF16)
        mids_ref[0, 0, :, cols] = gact
        mids_ref[1, 0, :, cols] = dhid
        drows = drows + dot(dhid, win_all[:, cols], 1, 1)
        yrows = yrows + dot(gact, wout_all[:, cols], 1, 1)
    dchosen_ref[0] = jnp.sum(jnp.where(mask, dgate, 0.0), axis=0, keepdims=True)
    drows_ref[0] = drows.astype(BF16)
    yrows_ref[0] = yrows.astype(BF16)


def run_expert(place, slot_of, router_rows, xs, grads, pieces, slots):
    blocks, depth = len(xs), len(pieces)
    tokens, model = xs[0].shape
    _, part_rows, width = pieces[0].shape
    experts = router_rows.shape[0]
    fixed = lambda *size: pl.BlockSpec(
        size, lambda b, s: (0,) * len(size), pipeline_mode=pl.Buffered(1)
    )
    block = lambda *size: pl.BlockSpec((1,) + size, lambda b, s: (b, 0, 0))
    both = lambda last: pl.BlockSpec((2, 1, slots, last), lambda b, s: (0, b, 0, 0))
    weight = lambda which: pl.BlockSpec(
        (1, part_rows, width), lambda b, s: (which, 0, 0), pipeline_mode=pl.Buffered(1)
    )
    return pl.pallas_call(
        functools.partial(expert_kernel, depth, blocks),
        grid_spec=pltpu.PrefetchScalarGridSpec(
            num_scalar_prefetch=1,
            grid=(blocks,),
            in_specs=[block(1, tokens), fixed(experts, model)]
            + [fixed(tokens, model)] * (2 * blocks)
            + [weight(1)] * depth
            + [weight(0)] * depth,
            out_specs=[
                both(model), both(width), block(1, tokens), block(slots, model),
                block(slots, model), block(experts, tokens),
            ],
            scratch_shapes=[pltpu.VMEM((model, width), BF16)] * 2,
        ),
        out_shape=[
            shaped((2, blocks, slots, model), BF16), shaped((2, blocks, slots, width), BF16),
            shaped((blocks, 1, tokens), F32), shaped((blocks, slots, model), BF16),
            shaped((blocks, slots, model), BF16), shaped((blocks, experts, tokens), F32),
        ],
        compiler_params=params(),
        cost_estimate=cost(
            8 * blocks * slots * model * width + 4 * blocks * slots * model * tokens,
            16 * blocks * slots * model,
            blocks * slots * width,
        ),
        name="expert",
    )(place, slot_of, router_rows, *xs, *grads, *pieces, *pieces)


def weight_grad_kernel(depth, place_ref, rows_ref, cols_ref, *refs):
    out_refs, total_ref = refs[:depth], refs[depth]
    _, blocks, slots, model = rows_ref.shape
    width = cols_ref.shape[3]
    part_rows = model // depth
    left = rows_ref[0].reshape(blocks * slots, model)
    right = cols_ref[0].reshape(blocks * slots, width)
    total_ref[...] = dot(left, right, 0, 0)
    for k in range(depth):
        owner = lax.rem(place_ref[0] - k + depth, depth)
        at = pl.ds(pl.multiple_of(owner * part_rows, 16), part_rows)
        out_refs[k][0] = total_ref[at, :].astype(BF16)


def weight_grad(place, rows, cols, depth):
    _, blocks, slots, model = rows.shape
    width = cols.shape[3]
    both = lambda last: pl.BlockSpec((1, blocks, slots, last), lambda i, s: (i, 0, 0, 0))
    return pl.pallas_call(
        functools.partial(weight_grad_kernel, depth),
        grid_spec=pltpu.PrefetchScalarGridSpec(
            num_scalar_prefetch=1,
            grid=(2,),
            in_specs=[both(model), both(width)],
            out_specs=[pl.BlockSpec((1, model // depth, width), lambda i, s: (i, 0, 0))] * depth,
            scratch_shapes=[pltpu.VMEM((model, width), F32)],
        ),
        out_shape=[shaped((2, model // depth, width), BF16)] * depth,
        compiler_params=params(),
        cost_estimate=cost(
            4 * blocks * slots * model * width,
            4 * (blocks * slots * (model + width) + model * width),
        ),
        name="weight_grad",
    )(place, rows, cols)


def combine_kernel(local, added, slot_ref, *refs):
    rows_refs, refs = refs[:local], refs[local:]
    out_ref = refs[-1]
    tokens = out_ref.shape[-2]
    slots, model = rows_refs[0].shape[1:]
    at = lax.broadcasted_iota(jnp.int32, (tokens, slots), 1)
    total = refs[0][...].astype(F32) if added else jnp.zeros((tokens, model), F32)
    for e in range(local):
        pick = jnp.where(at == slot_ref[0, :, e : e + 1], 1.0, 0.0).astype(BF16)
        total = total + dot(pick, rows_refs[e][0], 1, 0)
    out_ref[...] = total.astype(BF16)


def combine(slot_cols, rows, b, add=None):
    _, tokens, local = slot_cols.shape
    slots, model = rows[0].shape[1:]
    whole = pl.BlockSpec((tokens, model), lambda i: (0, 0))
    return pl.pallas_call(
        functools.partial(combine_kernel, local, add is not None),
        grid=(1,),
        in_specs=[pl.BlockSpec((1, tokens, local), lambda i: (b, 0, 0))]
        + [pl.BlockSpec((1, slots, model), lambda i: (b, 0, 0))] * local
        + [whole] * (add is not None),
        out_specs=whole,
        out_shape=shaped((tokens, model), BF16),
        compiler_params=params(),
        cost_estimate=cost(
            2 * local * slots * model * tokens, 2 * model * (local * slots + 2 * tokens)
        ),
        name="combine",
    )(slot_cols, *rows, *(() if add is None else (add,)))


def combine_back_kernel(local, added, place_ref, slot_ref, *refs):
    rows_refs, refs = refs[:local], refs[local:]
    dchosen_refs, refs = refs[:local], refs[local:]
    probs_ref, router_ref, x_ref = refs[:3]
    out_refs, drouter_ref = refs[-1 - PARTS : -1], refs[-1]
    tokens = out_refs[0].shape[0]
    slots = rows_refs[0].shape[1]
    at = lax.broadcasted_iota(jnp.int32, (tokens, slots), 1)
    probs = probs_ref[0]
    line = lax.broadcasted_iota(jnp.int32, probs.shape, 0)
    dprobs = jnp.zeros_like(probs)
    for e in range(local):
        dprobs = jnp.where(line == place_ref[1] + e, dchosen_refs[e][0], dprobs)
    inner = jnp.sum(dprobs * probs, axis=0, keepdims=True)
    dlogits = (probs * (dprobs - inner)).astype(BF16)
    drouter_ref[...] = dot(dlogits, x_ref[...], 1, 0)
    total = dot(dlogits, router_ref[...], 0, 0)
    for e in range(local):
        pick = jnp.where(at == slot_ref[0, :, e : e + 1], 1.0, 0.0).astype(BF16)
        total = total + dot(pick, rows_refs[e][0], 1, 0)
    part = out_refs[0].shape[1]
    for p in range(PARTS):
        piece = total[:, p * part : (p + 1) * part]
        if added:
            piece = piece + refs[3 + p][...].astype(F32)
        out_refs[p][...] = piece.astype(BF16)


def combine_back(place, slot_cols, rows, dchosen, probs, router_rows, x, b, add=None):
    _, tokens, local = slot_cols.shape
    slots, model = rows[0].shape[1:]
    experts = router_rows.shape[0]
    whole = pl.BlockSpec((tokens, model), lambda i, s: (0, 0))
    part = pl.BlockSpec((tokens, model // PARTS), lambda i, s: (0, 0))
    block = lambda *size: pl.BlockSpec((1,) + size, lambda i, s: (b, 0, 0))
    small = pl.BlockSpec((experts, model), lambda i, s: (0, 0))
    return pl.pallas_call(
        functools.partial(combine_back_kernel, local, add is not None),
        grid_spec=pltpu.PrefetchScalarGridSpec(
            num_scalar_prefetch=1,
            grid=(1,),
            in_specs=[block(tokens, local)]
            + [block(slots, model)] * local
            + [block(1, tokens)] * local
            + [block(experts, tokens), small, whole]
            + [part] * (PARTS * (add is not None)),
            out_specs=[part] * PARTS + [small],
        ),
        out_shape=[shaped((tokens, model // PARTS), BF16)] * PARTS
        + [shaped((experts, model), F32)],
        compiler_params=params(),
        cost_estimate=cost(
            2 * local * slots * model * tokens, 2 * model * (local * slots + 3 * tokens)
        ),
        name="combine_back",
    )(place, slot_cols, *rows, *dchosen, probs, router_rows, x, *(() if add is None else add))


def per_device(
    block_in, cotangent, route_ids, gain_attn, w_qkv, w_out_attn, gain_moe, router, w_in, w_out
):
    n_dp, n_heads, n_exp = (lax.axis_size(name) for name in ("dp", "heads", "expert"))
    n_z = n_dp // CORES
    dp, head, exp = (lax.axis_index(name) for name in ("dp", "heads", "expert"))
    z, core = dp // CORES, dp % CORES
    low = core == 0
    images, seq, half_width = block_in.shape
    span = -(-seq // 16) * 16
    rows = images * span
    model = half_width * n_heads
    width = w_qkv.shape[2]
    shard = w_qkv.shape[0]
    expert_count = router.shape[1]
    group = w_in.shape[1]
    local = group // CORES
    part_rows, _, hidden_width = w_in.shape
    capacity = 20 * images * seq // (7 * expert_count)
    slots = -(-capacity // 16) * 16
    blocks = n_exp * CORES
    rest = 128

    def shift(value, axis, step):
        size = lax.axis_size(axis)
        return lax.ppermute(value, axis, [(i, (i + step) % size) for i in range(size)])

    def shift_z(value, step):
        pairs = [
            (a * CORES + c, ((a + step) % n_z) * CORES + c) for a in range(n_z) for c in range(CORES)
        ]
        return lax.ppermute(value, "dp", pairs)

    def swap_core(value):
        return lax.ppermute(value, "dp", [(i, i ^ 1) for i in range(n_dp)])

    def place_at(pieces, index, count):
        if count == 2:
            first = index == 0
            return jnp.stack(
                [jnp.where(first, pieces[0], pieces[1]), jnp.where(first, pieces[1], pieces[0])]
            )
        out = jnp.zeros((count,) + pieces[0].shape, pieces[0].dtype)
        for k, piece in enumerate(pieces):
            out = lax.dynamic_update_index_in_dim(out, piece, (index - k) % count, 0)
        return out

    def spread(value, axis):
        return [value] + [shift(value, axis, k) for k in range(1, lax.axis_size(axis))]

    def take(value, index, dim=0):
        return lax.dynamic_index_in_dim(value, index, dim, keepdims=False)

    def expert_shards():
        both = jnp.stack([w_out, w_in]).reshape(2, part_rows, CORES, local, hidden_width)
        by_core = both.transpose(2, 3, 0, 1, 4)
        other = swap_core(take(by_core, 1 - core))
        mine = take(by_core, core)
        return jnp.concatenate(
            [jnp.where(low, mine, other), jnp.where(low, other, mine)], axis=2
        )

    ways_up = n_z // 2
    ways_down = n_z - 1 - ways_up

    def ring(piece):
        pieces = [piece] + [None] * (n_z - 1)
        for k in range(1, ways_up + 1):
            pieces[k] = shift_z(pieces[k - 1], 1)
        for k in range(1, ways_down + 1):
            pieces[n_z - k] = shift_z(pieces[(n_z - k + 1) % n_z], -1)
        return pieces

    def blocks_of(value, hold=()):
        along = spread(value, "expert")
        along = along[:1] + [after(part, *hold) for part in along[1:]]
        return along + [swap_core(part) for part in along]

    def full_rows(value):
        padded = jnp.pad(value, ((0, 0), (0, span - seq), (0, 0))).reshape(rows, half_width)
        parts = place_at(spread(padded, "heads"), head, n_heads)
        return jnp.concatenate([parts[i] for i in range(n_heads)], axis=-1)

    inputs = full_rows(block_in)
    grad_full = full_rows(cotangent)

    tail = jnp.concatenate(
        [router, gain_attn[:, None], gain_moe[:, None],
         jnp.zeros((shard, rest - expert_count - 2), BF16)], axis=1
    )
    own_pack = jnp.concatenate([w_qkv.reshape(shard, 3 * width), w_out_attn, tail], axis=1)
    columns = own_pack.shape[1]
    shards = expert_shards()
    ids = jnp.pad(route_ids, ((0, 0), (0, span - seq), (0, 0)), constant_values=-1)
    ids_all = jnp.stack(blocks_of(ids.reshape(rows, 2).T))
    pack_z = place_at(
        [own_pack] + [after(shift_z(own_pack, k), shards, inputs) for k in range(1, n_z)], z, n_z
    )
    pack = place_at(spread(after(pack_z, ids_all), "expert"), exp, n_exp)
    pieces = []
    for e in range(local):
        pieces.append(ring(after(shards[e], pieces[-1][1]) if e else shards[e]))
    last = local - 1

    pack = after(pack, pieces[0][1])
    other_pack = after(swap_core(pack), grad_full)
    pack = jnp.stack([jnp.where(low, pack, other_pack), jnp.where(low, other_pack, pack)])
    pack = pack.transpose(2, 0, 1, 3, 4).reshape(model, columns)
    side = pack[:, 4 * width :].T
    router_rows = side[:expert_count]
    gain_one = side[expert_count : expert_count + 1].astype(F32)
    gain_two = side[expert_count + 1 : expert_count + 2].astype(F32)

    first_expert = exp * group + core * local
    named = first_expert + jnp.arange(local, dtype=jnp.int32)
    chosen = jnp.any(ids_all[:, None, :, :] == named[None, :, None, None], axis=2)
    before = (jnp.arange(rows)[:, None] < jnp.arange(rows)[None, :]).astype(BF16)
    rank = jnp.dot(
        chosen.astype(BF16).reshape(blocks * local, rows), before, preferred_element_type=F32
    ).astype(jnp.int32).reshape(blocks, local, rows)
    slot_of = jnp.where(chosen, rank, -1)
    slot_cols = slot_of.transpose(0, 2, 1)
    slot_rows = [slot_of[:, e : e + 1, :] for e in range(local)]
    place = [jnp.stack([z, first_expert + e]).astype(jnp.int32) for e in range(local)]

    grads_all = blocks_of(grad_full)
    inputs_ready = inputs
    part, qkv, ctx = attend(inputs_ready, gain_one, pack, width, images, seq)
    part = after(part, pieces[0][-1])
    part_other = shift(part, "heads", 1)
    for k in range(2, n_heads):
        part_other = part_other + shift(part, "heads", k)
    part_other = after(part_other, pieces[0][ways_up], slot_cols, *slot_rows)
    middle = inputs.astype(F32) + (part.astype(F32) + part_other.astype(F32))
    unit_two, scale_two = norm_parts(middle)
    normed_two = (unit_two * gain_two).astype(BF16)
    tokens_all = blocks_of(normed_two, (pieces[last][1],))

    done = []

    def begin_rings(e, *hold):
        rows_e, mids_e = done[e][:2]
        rings.append(weight_grad(place[e], after(rows_e, *hold), mids_e, n_z))

    def ring_first(e):
        return shift_z(rings[e][-ways_up % n_z], 1)

    def ring_down(e):
        chunks = rings[e]
        downward = chunks[ways_down]
        for k in range(ways_down - 1, 0, -1):
            downward = (shift_z(downward, -1).astype(F32) + chunks[k].astype(F32)).astype(BF16)
        return shift_z(downward, -1)

    def ring_middle(e, upward, *hold):
        chunks = rings[e]
        for k in range(ways_up - 1, 0, -1):
            own = after(chunks[n_z - k], *hold)
            upward = (upward.astype(F32) + own.astype(F32)).astype(BF16)
            if k > 1:
                upward = shift_z(upward, 1)
        return upward

    def ring_end(e, upward, downward, *hold):
        own = after(rings[e][0], *hold).astype(F32)
        return own + shift_z(upward, 1).astype(F32) + downward.astype(F32)

    rings = []
    for e in range(local):
        here = list(pieces[e])
        if e:
            here[0] = after(here[0], rings[-1][0])
        done.append(
            run_expert(
                place[e], slot_rows[e], router_rows, tokens_all, grads_all, here, slots
            )
        )
        if e < local - 1:
            begin_rings(e)
    drows, yrows, dchosen = ([r[i] for r in done] for i in (3, 4, 2))
    probs = done[0][5]

    begin_rings(last)
    arrived_zero, down_zero = ring_first(0), ring_down(0)
    early = ring_middle(0, arrived_zero)
    arrived_last, down_last = ring_first(last), ring_down(last)
    drows[0] = after(drows[0], early, down_zero, rings[last][0])

    def back_of(b, add=None):
        *parts, more = combine_back(
            place[0], slot_cols, drows, dchosen, probs, router_rows, tokens_all[b], b, add
        )
        return parts, more

    drouter = jnp.zeros((expert_count, model), F32)
    arrived = [None] * n_exp
    for k in reversed(range(n_exp)):
        sent, more = back_of(n_exp + k)
        arrived[k] = [swap_core(part) for part in sent]
        drouter = drouter + more
    from_exp = []
    for k in reversed(range(n_exp)):
        total, more = back_of(k, arrived[k])
        drouter = drouter + more
        if k:
            from_exp.append([shift(part, "expert", -k) for part in total])
    ends = [ring_end(0, early, down_zero)]
    dsum, dsum_other = [], []
    for p in range(PARTS):
        value = (after(total[p], ends[0]) if p == 0 else total[p]).astype(F32)
        for came in from_exp:
            value = value + came[p].astype(F32)
        dsum.append(value.astype(BF16))
        other = shift(dsum[p], "heads", 1)
        for k in range(2, n_heads):
            other = other + shift(dsum[p], "heads", k)
        dsum_other.append(other)
    dsum_other[-1] = after(dsum_other[-1], arrived_last)

    yrows[0] = after(yrows[0], dsum[-1])
    y_came = [swap_core(combine(slot_cols, yrows, n_exp + k)) for k in range(n_exp)]
    y_from = [
        shift(combine(slot_cols, yrows, k, after(y_came[k], dsum_other[-1])), "expert", -k)
        for k in range(1, n_exp)
    ]
    dnormed_two = jnp.concatenate(
        [own.astype(F32) + other.astype(F32) for own, other in zip(dsum, dsum_other)], axis=1
    )
    scaled = dnormed_two * gain_two
    grad_gain_two = jnp.sum(dnormed_two * unit_two, axis=0)
    dmiddle = grad_full.astype(F32) + scale_two * (
        scaled
        - jnp.mean(scaled, axis=-1, keepdims=True)
        - unit_two * jnp.mean(scaled * unit_two, axis=-1, keepdims=True)
    )
    late = ring_middle(last, arrived_last, dsum_other[-1])
    datt = after(dmiddle.astype(BF16), late, *y_came)

    dside = jnp.concatenate(
        [drouter, jnp.zeros((1, model), F32), grad_gain_two[None, :],
         jnp.zeros((rest - expert_count - 2, model), F32)], axis=0
    ).T
    dnorm, stats, dpack = attend_back(
        inputs, gain_one, datt, qkv, ctx, pack, dside, expert_count, width, images, seq, n_heads
    )
    dpack = after(dpack, *y_from, down_last)
    y_own = combine(slot_cols, yrows, 0, after(y_came[0], dpack)).astype(F32)
    for value in y_from:
        y_own = y_own + value.astype(F32)
    y_own = y_own.astype(BF16)

    dpack = dpack.reshape(n_z, CORES, n_exp, shard, columns)
    dsent = swap_core(take(dpack, 1 - core, 1))
    dpack = (take(dpack, core, 1).astype(F32) + dsent.astype(F32)).astype(BF16)
    dtotal = take(dpack, exp, 1).astype(F32)
    for k in range(1, n_exp):
        dtotal = dtotal + shift(take(dpack, (exp + k) % n_exp, 1), "expert", k).astype(F32)
    dpack = dtotal.astype(BF16)
    ends.append(ring_end(last, late, down_last, dpack))
    dtotal = take(dpack, z).astype(F32)
    for k in range(1, n_z):
        dtotal = dtotal + shift_z(take(dpack, (z + k) % n_z), k).astype(F32)
    dside = dtotal[:, 4 * width :]
    over_heads = dside[:, : expert_count + 1].T
    summed = over_heads
    for k in range(1, n_heads):
        summed = summed + shift(over_heads, "heads", k)

    def own_half(value):
        return lax.dynamic_slice_in_dim(value, head * half_width, half_width, 1)

    def cut(value):
        return value.astype(BF16).reshape(images, span, half_width)[:, :seq]

    dn_own = take(dnorm, head).astype(F32)
    sums = stats[:, :2].T
    sums_total = sums
    for k in range(1, n_heads):
        came = shift(take(dnorm, (head + k) % n_heads), "heads", k)
        dn_own = dn_own + after(came, dtotal).astype(F32)
        sums_total = sums_total + after(shift(sums, "heads", k), dtotal)
    unit_one, scale_one = norm_parts(inputs.astype(F32))
    grad_in = own_half(dmiddle) + scale_one * (
        dn_own * own_half(gain_one)
        - sums_total[0][:, None] / model
        - own_half(unit_one) * (sums_total[1][:, None] / model)
    )

    y_total = own_half(y_own).astype(F32)
    for k in range(1, n_heads):
        there = (head + k) % n_heads
        part_y = lax.dynamic_slice_in_dim(y_own, there * half_width, half_width, 1)
        y_total = y_total + after(shift(part_y, "heads", k), dtotal).astype(F32)
    block_out = own_half(middle) + y_total

    stacked = jnp.stack(ends).reshape(local, 2, CORES, part_rows, hidden_width)
    other = swap_core(take(stacked, 1 - core, 2).astype(BF16)).astype(F32)
    own = take(stacked, core, 2)
    joined = jnp.concatenate([jnp.where(low, own, other), jnp.where(low, other, own)], axis=0)
    grads = joined.transpose(1, 2, 0, 3)

    return (
        cut(block_out),
        cut(grad_in),
        summed[expert_count],
        dtotal[:, : 3 * width].reshape(shard, 3, width),
        dtotal[:, 3 * width : 4 * width],
        dside[:, expert_count + 1],
        summed[:expert_count].T,
        grads[1],
        grads[0],
    )


def solution(mesh):
    return jax.shard_map(
        per_device,
        mesh=mesh,
        in_specs=(
            P(("dp", "expert"), None, "heads"),
            P(("dp", "expert"), None, "heads"),
            P(("dp", "expert"), None, None),
            P(("dp", "expert")),
            P(("dp", "expert"), None, "heads"),
            P(("dp", "expert"), "heads"),
            P(("dp", "expert")),
            P(("dp", "expert"), None),
            P("dp", "expert", "heads"),
            P("dp", "expert", "heads"),
        ),
        out_specs=(
            P(("dp", "expert"), None, "heads"),
            P(("dp", "expert"), None, "heads"),
            P(("dp", "expert")),
            P(("dp", "expert"), None, "heads"),
            P(("dp", "expert"), "heads"),
            P(("dp", "expert")),
            P(("dp", "expert"), None),
            P("dp", "expert", "heads"),
            P("dp", "expert", "heads"),
        ),
        check_vma=False,
    )
```

```python
import functools

import jax
import jax.numpy as jnp
from jax import lax
from jax.experimental import pallas as pl
from jax.experimental.pallas import tpu as pltpu
from jax.sharding import PartitionSpec as P

HEAD_DIM = 64
CORES = 2
EPS = 1e-06
LOW = -1e30
F32 = jnp.float32
BF16 = jnp.bfloat16
VMEM_LIMIT = 56 * 1024 * 1024
SHARE = 64
PARTS = 2


def dot(a, b, ca, cb):
    return lax.dot_general(a, b, (((ca,), (cb,)), ((), ())), preferred_element_type=F32)


def shaped(shape, kind):
    return jax.ShapeDtypeStruct(shape, kind)


def params(dims=1):
    return pltpu.CompilerParams(
        dimension_semantics=("arbitrary",) * dims, vmem_limit_bytes=VMEM_LIMIT
    )


def cost(flops, size, powers=0):
    return pl.CostEstimate(
        flops=flops // SHARE, bytes_accessed=size // SHARE, transcendentals=powers // SHARE
    )


def after(value, *others):
    return lax.optimization_barrier((value,) + others)[0]


def norm_parts(rows):
    average = jnp.mean(rows, axis=-1, keepdims=True)
    centred = rows - average
    spread = jnp.mean(centred * centred, axis=-1, keepdims=True)
    scale = lax.rsqrt(spread + EPS)
    return centred * scale, scale


def softmax_rows(q, own_k, real):
    scores = jnp.where(real, dot(q, own_k, 1, 1) * (HEAD_DIM**-0.5), LOW)
    powers = jnp.exp(scores - jnp.max(scores, axis=-1, keepdims=True))
    return powers / jnp.sum(powers, axis=-1, keepdims=True)


def attend_kernel(
    seq, gain_at, x_ref, side_ref, wqkv_ref, wo_ref, part_ref, qkv_ref, ctx_ref, gain_ref
):
    width = wo_ref.shape[1]
    span = x_ref.shape[0]

    @pl.when(pl.program_id(0) == 0)
    def _():
        gain_ref[...] = side_ref[...].astype(F32).T[gain_at : gain_at + 1, :]

    unit, _ = norm_parts(x_ref[...].astype(F32))
    normed = (unit * gain_ref[...]).astype(BF16)
    for part in range(3):
        cols = slice(part * width, (part + 1) * width)
        qkv_ref[:, cols] = dot(normed, wqkv_ref[:, cols], 1, 0).astype(BF16)
    lane = lax.broadcasted_iota(jnp.int32, (span, 128), 1)
    real = lax.broadcasted_iota(jnp.int32, (span, span), 1) < seq
    for pair in range(width // 128):
        q, k, v = (
            qkv_ref[:, part * width + pair * 128 : part * width + (pair + 1) * 128]
            for part in range(3)
        )
        ctx = jnp.zeros((span, 128), F32)
        for side in range(2):
            mine = (lane >= 64) if side else (lane < 64)
            own_k = jnp.where(mine, k, jnp.zeros_like(k))
            own_v = jnp.where(mine, v, jnp.zeros_like(v))
            weights = softmax_rows(q, own_k, real)
            ctx = ctx + dot(weights.astype(BF16), own_v, 1, 0)
        ctx_ref[:, pair * 128 : (pair + 1) * 128] = ctx.astype(BF16)
    part_ref[...] = dot(ctx_ref[...], wo_ref[...], 1, 1).astype(BF16)


def attend(inputs, gain_at, packed, width, images, seq):
    rows, model = inputs.shape
    span = rows // images
    image = lambda last: pl.BlockSpec((span, last), lambda i: (i, 0))
    return pl.pallas_call(
        functools.partial(attend_kernel, seq, gain_at),
        grid=(images,),
        in_specs=[
            image(model),
            pl.BlockSpec((model, 128), lambda i: (0, 4 * width // 128)),
            pl.BlockSpec((model, 3 * width), lambda i: (0, 0)),
            pl.BlockSpec((model, width), lambda i: (0, 3)),
        ],
        out_specs=[image(model), image(3 * width), image(width)],
        scratch_shapes=[pltpu.VMEM((1, model), F32)],
        out_shape=[
            shaped((rows, model), BF16), shaped((rows, 3 * width), BF16), shaped((rows, width), BF16)
        ],
        compiler_params=params(),
        cost_estimate=cost(10 * rows * model * width, 8 * rows * model, rows * span * width // 64),
        name="attend",
    )(inputs, packed, packed, packed)


def attend_back_kernel(
    seq, gain_at,
    x_ref, gain_ref, datt_ref, qkv_ref, ctx_ref, wqkv_ref, wo_ref, side_ref,
    dnorm_ref, stats_ref, pack_ref, dproj_ref, dgain_ref, dwqkv_ref, dwo_ref,
):
    width = wo_ref.shape[1]
    span, model = x_ref.shape
    step = pl.program_id(0)

    @pl.when(step == 0)
    def _():
        dgain_ref[...] = jnp.zeros_like(dgain_ref)
        dwqkv_ref[...] = jnp.zeros_like(dwqkv_ref)
        dwo_ref[...] = jnp.zeros_like(dwo_ref)

    datt = datt_ref[...]
    dwo_ref[...] += dot(datt, ctx_ref[...], 0, 0)
    dctx_all = dot(datt, wo_ref[...], 1, 0).astype(BF16)
    lane = lax.broadcasted_iota(jnp.int32, (span, 128), 1)
    real = lax.broadcasted_iota(jnp.int32, (span, span), 1) < seq
    for pair in range(width // 128):
        q, k, v = (
            qkv_ref[:, part * width + pair * 128 : part * width + (pair + 1) * 128]
            for part in range(3)
        )
        dctx = dctx_all[:, pair * 128 : (pair + 1) * 128]
        dq = jnp.zeros((span, 128), F32)
        dk = jnp.zeros((span, 128), F32)
        dv = jnp.zeros((span, 128), F32)
        for side in range(2):
            mine = (lane >= 64) if side else (lane < 64)
            own = lambda t: jnp.where(mine, t, jnp.zeros_like(t))
            own_k, own_v = own(k), own(v)
            weights = softmax_rows(q, own_k, real)
            dweights = dot(dctx, own_v, 1, 1)
            inner = jnp.sum(dweights * weights, axis=-1, keepdims=True)
            dscores = (weights * (dweights - inner)).astype(BF16)
            dq = dq + dot(dscores, own_k, 1, 0)
            dk = dk + dot(dscores, own(q), 0, 0)
            dv = dv + dot(weights.astype(BF16), own(dctx), 0, 0)
        for part, value in enumerate((dq * HEAD_DIM**-0.5, dk * HEAD_DIM**-0.5, dv)):
            start = part * width + pair * 128
            dproj_ref[:, start : start + 128] = value.astype(BF16)
    dproj = dproj_ref[...]
    gain = gain_ref[...]
    unit, _ = norm_parts(x_ref[...].astype(F32))
    normed = (unit * gain).astype(BF16)
    dwqkv_ref[...] += dot(normed, dproj, 0, 0)
    dnormed = dot(dproj, wqkv_ref[...], 1, 1)
    halves, _, half = dnorm_ref.shape
    for h in range(halves):
        dnorm_ref[h] = dnormed[:, h * half : (h + 1) * half].astype(BF16)
    along = dnormed * unit
    dgain_ref[...] += jnp.sum(along, axis=0, keepdims=True)
    first = jnp.sum(dnormed * gain, axis=-1, keepdims=True)
    second = jnp.sum(along * gain, axis=-1, keepdims=True)
    stats_ref[...] = jnp.where(lane == 0, first, jnp.where(lane == 1, second, 0.0))

    @pl.when(step == pl.num_programs(0) - 1)
    def _():
        pack_ref[:, : 3 * width] = dwqkv_ref[...].astype(BF16)
        pack_ref[:, 3 * width : 4 * width] = dwo_ref[...].astype(BF16)
        line = lax.broadcasted_iota(jnp.int32, (128, model), 0)
        column = jnp.where(line == gain_at, dgain_ref[...], 0.0).T
        pack_ref[:, 4 * width :] = (side_ref[...] + column).astype(BF16)


def attend_back(inputs, gain, datt, qkv, ctx, packed, dside, gain_at, width, images, seq, halves):
    rows, model = inputs.shape
    span = rows // images
    image = lambda last: pl.BlockSpec((span, last), lambda i: (i, 0))
    fixed = lambda *size: pl.BlockSpec(size, lambda i: (0, 0))
    return pl.pallas_call(
        functools.partial(attend_back_kernel, seq, gain_at),
        grid=(images,),
        in_specs=[
            image(model), fixed(1, model), image(model), image(3 * width), image(width),
            fixed(model, 3 * width), pl.BlockSpec((model, width), lambda i: (0, 3)),
            fixed(model, 128),
        ],
        out_specs=[
            pl.BlockSpec((halves, span, model // halves), lambda i: (0, i, 0)),
            image(128),
            fixed(*packed.shape),
        ],
        out_shape=[
            shaped((halves, rows, model // halves), BF16),
            shaped((rows, 128), F32),
            shaped(packed.shape, BF16),
        ],
        scratch_shapes=[
            pltpu.VMEM((span, 3 * width), BF16),
            pltpu.VMEM((1, model), F32),
            pltpu.VMEM((model, 3 * width), F32),
            pltpu.VMEM((model, width), F32),
        ],
        compiler_params=params(),
        cost_estimate=cost(28 * rows * model * width, 12 * rows * model, rows * span * width // 64),
        name="attend_back",
    )(inputs, gain, datt, qkv, ctx, packed, packed, dside)


def expert_kernel(index, depth, blocks, place_ref, slot_ref, router_ref, *refs):
    x_refs, refs = refs[:blocks], refs[blocks:]
    grad_refs, refs = refs[:blocks], refs[blocks:]
    win_refs, refs = refs[:depth], refs[depth:]
    wout_refs, refs = refs[:depth], refs[depth:]
    (
        rows_ref, mids_ref, dchosen_ref, drows_ref, yrows_ref, probs_ref, win_all, wout_all,
    ) = refs
    slots, model = rows_ref.shape[2:]
    tokens = x_refs[0].shape[0]
    part_rows, width = win_refs[0].shape[1:]
    step = pl.program_id(0)

    @pl.when(step == 0)
    def _():
        for k in range(depth):
            owner = lax.rem(place_ref[0] - k + depth, depth)
            at = pl.ds(pl.multiple_of(owner * part_rows, 16), part_rows)
            win_all[at, :] = win_refs[k][0]
            wout_all[at, :] = wout_refs[k][0]

    mask = lax.broadcasted_iota(jnp.int32, (slots, tokens), 0) == slot_ref[0, index : index + 1, :]
    pick = jnp.where(mask, 1.0, 0.0).astype(BF16)
    for b in range(blocks):

        @pl.when(step == b)
        def _(b=b):
            rows_ref[0, 0] = dot(pick, grad_refs[b][...], 1, 0).astype(BF16)
            rows_ref[1, 0] = dot(pick, x_refs[b][...], 1, 0).astype(BF16)
            logits = dot(router_ref[...], x_refs[b][...], 1, 1)
            powers = jnp.exp(logits - jnp.max(logits, axis=0, keepdims=True))
            probs_ref[0] = powers / jnp.sum(powers, axis=0, keepdims=True)

    probs = probs_ref[0]
    line = lax.broadcasted_iota(jnp.int32, probs.shape, 0)
    own = jnp.sum(jnp.where(line == place_ref[1], probs, 0.0), axis=0, keepdims=True)
    gate = jnp.sum(jnp.where(mask, own, 0.0), axis=1, keepdims=True)
    grows, rows = rows_ref[0, 0], rows_ref[1, 0]
    dgate = jnp.zeros((slots, 1), F32)
    drows = jnp.zeros((slots, model), F32)
    yrows = jnp.zeros((slots, model), F32)
    tile = 512 if width % 512 == 0 else width
    curve = 0.7978845608028654

    def products(start):
        cols = slice(start, start + tile)
        return dot(rows, win_all[:, cols], 1, 0), dot(grows, wout_all[:, cols], 1, 0)

    ahead = products(0)
    for start in range(0, width, tile):
        cols = slice(start, start + tile)
        hidden, pulled = ahead
        if start + tile < width:
            ahead = products(start + tile)
        square = hidden * hidden
        bend = jnp.tanh(hidden * (curve + curve * 0.044715 * square))
        half = 0.5 + 0.5 * bend
        active = hidden * half
        slope = half + 0.5 * hidden * (1.0 - bend * bend) * (
            curve + 3.0 * curve * 0.044715 * square
        )
        dgate = dgate + jnp.sum(active * pulled, axis=1, keepdims=True)
        gact = (gate * active).astype(BF16)
        dhid = (gate * pulled * slope).astype(BF16)
        mids_ref[0, 0, :, cols] = gact
        mids_ref[1, 0, :, cols] = dhid
        drows = drows + dot(dhid, win_all[:, cols], 1, 1)
        yrows = yrows + dot(gact, wout_all[:, cols], 1, 1)
    dchosen_ref[0] = jnp.sum(jnp.where(mask, dgate, 0.0), axis=0, keepdims=True)
    drows_ref[0] = drows.astype(BF16)
    yrows_ref[0] = yrows.astype(BF16)


def run_expert(index, place, slot_of, router_rows, xs, grads, pieces, slots):
    blocks, depth = len(xs), len(pieces)
    tokens, model = xs[0].shape
    _, part_rows, width = pieces[0].shape
    experts = router_rows.shape[0]
    fixed = lambda *size: pl.BlockSpec(
        size, lambda b, s: (0,) * len(size), pipeline_mode=pl.Buffered(1)
    )
    block = lambda *size: pl.BlockSpec((1,) + size, lambda b, s: (b, 0, 0))
    both = lambda last: pl.BlockSpec((2, 1, slots, last), lambda b, s: (0, b, 0, 0))
    weight = lambda which: pl.BlockSpec(
        (1, part_rows, width), lambda b, s: (which, 0, 0), pipeline_mode=pl.Buffered(1)
    )
    return pl.pallas_call(
        functools.partial(expert_kernel, index, depth, blocks),
        grid_spec=pltpu.PrefetchScalarGridSpec(
            num_scalar_prefetch=1,
            grid=(blocks,),
            in_specs=[block(slot_of.shape[1], tokens), fixed(experts, model)]
            + [fixed(tokens, model)] * (2 * blocks)
            + [weight(1)] * depth
            + [weight(0)] * depth,
            out_specs=[
                both(model), both(width), block(1, tokens), block(slots, model),
                block(slots, model), block(experts, tokens),
            ],
            scratch_shapes=[pltpu.VMEM((model, width), BF16)] * 2,
        ),
        out_shape=[
            shaped((2, blocks, slots, model), BF16), shaped((2, blocks, slots, width), BF16),
            shaped((blocks, 1, tokens), F32), shaped((blocks, slots, model), BF16),
            shaped((blocks, slots, model), BF16), shaped((blocks, experts, tokens), F32),
        ],
        compiler_params=params(),
        cost_estimate=cost(
            8 * blocks * slots * model * width + 4 * blocks * slots * model * tokens,
            16 * blocks * slots * model,
            blocks * slots * width,
        ),
        name="expert",
    )(place, slot_of, router_rows, *xs, *grads, *pieces, *pieces)


def weight_grad_kernel(depth, place_ref, rows_ref, cols_ref, *refs):
    out_refs, total_ref = refs[:depth], refs[depth]
    _, blocks, slots, model = rows_ref.shape
    width = cols_ref.shape[3]
    part_rows = model // depth
    left = rows_ref[0].reshape(blocks * slots, model)
    right = cols_ref[0].reshape(blocks * slots, width)
    total_ref[...] = dot(left, right, 0, 0)
    for k in range(depth):
        owner = lax.rem(place_ref[0] - k + depth, depth)
        at = pl.ds(pl.multiple_of(owner * part_rows, 16), part_rows)
        out_refs[k][0] = total_ref[at, :].astype(BF16)


def weight_grad(place, rows, cols, depth):
    _, blocks, slots, model = rows.shape
    width = cols.shape[3]
    both = lambda last: pl.BlockSpec((1, blocks, slots, last), lambda i, s: (i, 0, 0, 0))
    return pl.pallas_call(
        functools.partial(weight_grad_kernel, depth),
        grid_spec=pltpu.PrefetchScalarGridSpec(
            num_scalar_prefetch=1,
            grid=(2,),
            in_specs=[both(model), both(width)],
            out_specs=[pl.BlockSpec((1, model // depth, width), lambda i, s: (i, 0, 0))] * depth,
            scratch_shapes=[pltpu.VMEM((model, width), F32)],
        ),
        out_shape=[shaped((2, model // depth, width), BF16)] * depth,
        compiler_params=params(),
        cost_estimate=cost(
            4 * blocks * slots * model * width,
            4 * (blocks * slots * (model + width) + model * width),
        ),
        name="weight_grad",
    )(place, rows, cols)


def gathered(local, slot_ref, rows_refs, all_ref):
    slots, tokens = rows_refs[0].shape[1], slot_ref.shape[1]
    at = lax.broadcasted_iota(jnp.int32, (tokens, local * slots), 1)
    mask = at == slot_ref[0, :, 0:1]
    all_ref[0:slots, :] = rows_refs[0][0]
    for e in range(1, local):
        mask = mask | (at == slot_ref[0, :, e : e + 1])
        all_ref[e * slots : (e + 1) * slots, :] = rows_refs[e][0]
    return dot(jnp.where(mask, 1.0, 0.0).astype(BF16), all_ref[...], 1, 0)


def combine_kernel(local, added, slot_ref, *refs):
    rows_refs, refs = refs[:local], refs[local:]
    out_ref, all_ref = refs[-2:]
    total = gathered(local, slot_ref, rows_refs, all_ref)
    if added:
        total = total + refs[0][...].astype(F32)
    out_ref[...] = total.astype(BF16)


def combine(slot_cols, rows, b, add=None):
    _, tokens, local = slot_cols.shape
    slots, model = rows[0].shape[1:]
    whole = pl.BlockSpec((tokens, model), lambda i: (0, 0))
    return pl.pallas_call(
        functools.partial(combine_kernel, local, add is not None),
        grid=(1,),
        in_specs=[pl.BlockSpec((1, tokens, local), lambda i: (b, 0, 0))]
        + [pl.BlockSpec((1, slots, model), lambda i: (b, 0, 0))] * local
        + [whole] * (add is not None),
        out_specs=whole,
        out_shape=shaped((tokens, model), BF16),
        scratch_shapes=[pltpu.VMEM((local * slots, model), BF16)],
        compiler_params=params(),
        cost_estimate=cost(
            2 * local * slots * model * tokens, 2 * model * (local * slots + 2 * tokens)
        ),
        name="combine",
    )(slot_cols, *rows, *(() if add is None else (add,)))


def combine_back_kernel(local, added, place_ref, slot_ref, *refs):
    rows_refs, refs = refs[:local], refs[local:]
    dchosen_refs, refs = refs[:local], refs[local:]
    probs_ref, router_ref, x_ref = refs[:3]
    out_refs, (drouter_ref, all_ref) = refs[-2 - PARTS : -2], refs[-2:]
    probs = probs_ref[0]
    line = lax.broadcasted_iota(jnp.int32, probs.shape, 0)
    dprobs = jnp.zeros_like(probs)
    for e in range(local):
        dprobs = jnp.where(line == place_ref[1] + e, dchosen_refs[e][0], dprobs)
    inner = jnp.sum(dprobs * probs, axis=0, keepdims=True)
    dlogits = (probs * (dprobs - inner)).astype(BF16)
    drouter_ref[...] = dot(dlogits, x_ref[...], 1, 0)
    total = gathered(local, slot_ref, rows_refs, all_ref) + dot(dlogits, router_ref[...], 0, 0)
    part = out_refs[0].shape[1]
    for p in range(PARTS):
        piece = total[:, p * part : (p + 1) * part]
        if added:
            piece = piece + refs[3 + p][...].astype(F32)
        out_refs[p][...] = piece.astype(BF16)


def combine_back(place, slot_cols, rows, dchosen, probs, router_rows, x, b, add=None):
    _, tokens, local = slot_cols.shape
    slots, model = rows[0].shape[1:]
    experts = router_rows.shape[0]
    whole = pl.BlockSpec((tokens, model), lambda i, s: (0, 0))
    part = pl.BlockSpec((tokens, model // PARTS), lambda i, s: (0, 0))
    block = lambda *size: pl.BlockSpec((1,) + size, lambda i, s: (b, 0, 0))
    small = pl.BlockSpec((experts, model), lambda i, s: (0, 0))
    return pl.pallas_call(
        functools.partial(combine_back_kernel, local, add is not None),
        grid_spec=pltpu.PrefetchScalarGridSpec(
            num_scalar_prefetch=1,
            grid=(1,),
            in_specs=[block(tokens, local)]
            + [block(slots, model)] * local
            + [block(1, tokens)] * local
            + [block(experts, tokens), small, whole]
            + [part] * (PARTS * (add is not None)),
            out_specs=[part] * PARTS + [small],
            scratch_shapes=[pltpu.VMEM((local * slots, model), BF16)],
        ),
        out_shape=[shaped((tokens, model // PARTS), BF16)] * PARTS
        + [shaped((experts, model), F32)],
        compiler_params=params(),
        cost_estimate=cost(
            2 * local * slots * model * tokens, 2 * model * (local * slots + 3 * tokens)
        ),
        name="combine_back",
    )(place, slot_cols, *rows, *dchosen, probs, router_rows, x, *(() if add is None else add))


def per_device(
    block_in, cotangent, route_ids, gain_attn, w_qkv, w_out_attn, gain_moe, router, w_in, w_out
):
    n_dp, n_heads, n_exp = (lax.axis_size(name) for name in ("dp", "heads", "expert"))
    n_z = n_dp // CORES
    dp, head, exp = (lax.axis_index(name) for name in ("dp", "heads", "expert"))
    z, core = dp // CORES, dp % CORES
    low = core == 0
    images, seq, half_width = block_in.shape
    span = -(-seq // 16) * 16
    rows = images * span
    model = half_width * n_heads
    width = w_qkv.shape[2]
    shard = w_qkv.shape[0]
    expert_count = router.shape[1]
    group = w_in.shape[1]
    local = group // CORES
    part_rows, _, hidden_width = w_in.shape
    capacity = 20 * images * seq // (7 * expert_count)
    slots = -(-capacity // 16) * 16
    blocks = n_exp * CORES
    rest = 128

    def shift(value, axis, step):
        size = lax.axis_size(axis)
        return lax.ppermute(value, axis, [(i, (i + step) % size) for i in range(size)])

    def shift_z(value, step):
        pairs = [
            (a * CORES + c, ((a + step) % n_z) * CORES + c) for a in range(n_z) for c in range(CORES)
        ]
        return lax.ppermute(value, "dp", pairs)

    def swap_core(value):
        return lax.ppermute(value, "dp", [(i, i ^ 1) for i in range(n_dp)])

    def place_at(pieces, index, count):
        if count == 2:
            first = index == 0
            return jnp.stack(
                [jnp.where(first, pieces[0], pieces[1]), jnp.where(first, pieces[1], pieces[0])]
            )
        out = jnp.zeros((count,) + pieces[0].shape, pieces[0].dtype)
        for k, piece in enumerate(pieces):
            out = lax.dynamic_update_index_in_dim(out, piece, (index - k) % count, 0)
        return out

    def spread(value, axis):
        return [value] + [shift(value, axis, k) for k in range(1, lax.axis_size(axis))]

    def take(value, index, dim=0):
        return lax.dynamic_index_in_dim(value, index, dim, keepdims=False)

    def expert_shards():
        both = jnp.stack([w_out, w_in]).reshape(2, part_rows, CORES, local, hidden_width)
        by_core = both.transpose(2, 3, 0, 1, 4)
        other = swap_core(take(by_core, 1 - core))
        mine = take(by_core, core)
        return jnp.concatenate(
            [jnp.where(low, mine, other), jnp.where(low, other, mine)], axis=2
        )

    ways_up = n_z // 2
    ways_down = n_z - 1 - ways_up

    def ring(piece):
        pieces = [piece] + [None] * (n_z - 1)
        for k in range(1, ways_up + 1):
            pieces[k] = shift_z(pieces[k - 1], 1)
        for k in range(1, ways_down + 1):
            pieces[n_z - k] = shift_z(pieces[(n_z - k + 1) % n_z], -1)
        return pieces

    def blocks_of(value, hold=()):
        along = spread(value, "expert")
        along = along[:1] + [after(part, *hold) for part in along[1:]]
        return along + [swap_core(part) for part in along]

    def full_rows(value):
        padded = jnp.pad(value, ((0, 0), (0, span - seq), (0, 0))).reshape(rows, half_width)
        parts = place_at(spread(padded, "heads"), head, n_heads)
        return jnp.concatenate([parts[i] for i in range(n_heads)], axis=-1)

    inputs = full_rows(block_in)
    grad_full = full_rows(cotangent)

    tail = jnp.concatenate(
        [router, gain_attn[:, None], gain_moe[:, None],
         jnp.zeros((shard, rest - expert_count - 2), BF16)], axis=1
    )
    own_pack = jnp.concatenate([w_qkv.reshape(shard, 3 * width), w_out_attn, tail], axis=1)
    columns = own_pack.shape[1]
    shards = expert_shards()
    ids = jnp.pad(route_ids, ((0, 0), (0, span - seq), (0, 0)), constant_values=-1)
    ids_all = jnp.stack(blocks_of(ids.reshape(rows, 2).T))
    pack_z = place_at(
        [own_pack] + [after(shift_z(own_pack, k), shards, inputs, grad_full) for k in range(1, n_z)], z, n_z
    )
    pack = place_at(spread(after(pack_z, ids_all), "expert"), exp, n_exp)
    pieces = []
    for e in range(local):
        pieces.append(ring(after(shards[e], pieces[-1][1]) if e else shards[e]))
    last = local - 1

    pack = after(pack, pieces[0][1])
    other_pack = swap_core(pack)
    pack = jnp.stack([jnp.where(low, pack, other_pack), jnp.where(low, other_pack, pack)])
    pack = pack.transpose(2, 0, 1, 3, 4).reshape(model, columns)
    side = pack[:, 4 * width :].T
    router_rows = side[:expert_count]
    gain_one = side[expert_count : expert_count + 1].astype(F32)
    gain_two = side[expert_count + 1 : expert_count + 2].astype(F32)

    first_expert = exp * group + core * local
    named = first_expert + jnp.arange(local, dtype=jnp.int32)
    chosen = jnp.any(ids_all[:, None, :, :] == named[None, :, None, None], axis=2)
    before = (jnp.arange(rows)[:, None] < jnp.arange(rows)[None, :]).astype(BF16)
    rank = jnp.dot(
        chosen.astype(BF16).reshape(blocks * local, rows), before, preferred_element_type=F32
    ).astype(jnp.int32).reshape(blocks, local, rows)
    slot_of = jnp.where(chosen, rank, -1)
    spread_slots = slot_of + slots * jnp.arange(local, dtype=jnp.int32)[None, :, None]
    slot_cols = jnp.where(chosen, spread_slots, -1).transpose(0, 2, 1)
    place = [jnp.stack([z, first_expert + e]).astype(jnp.int32) for e in range(local)]

    grads_all = blocks_of(grad_full)
    inputs_ready = inputs
    part, qkv, ctx = attend(inputs_ready, expert_count, pack, width, images, seq)
    part = after(part, pieces[0][-1])
    part_other = shift(part, "heads", 1)
    for k in range(2, n_heads):
        part_other = part_other + shift(part, "heads", k)
    part_other = after(part_other, pieces[0][ways_up], slot_cols)
    middle = inputs.astype(F32) + (part.astype(F32) + part_other.astype(F32))
    unit_two, scale_two = norm_parts(middle)
    normed_two = (unit_two * gain_two).astype(BF16)
    tokens_all = blocks_of(normed_two, (pieces[last][1],))

    done = []

    def begin_rings(e, *hold):
        rows_e, mids_e = done[e][:2]
        rings.append(weight_grad(place[e], after(rows_e, *hold), mids_e, n_z))

    def ring_first(e):
        return shift_z(rings[e][-ways_up % n_z], 1)

    def ring_down(e):
        chunks = rings[e]
        downward = chunks[ways_down]
        for k in range(ways_down - 1, 0, -1):
            downward = (shift_z(downward, -1).astype(F32) + chunks[k].astype(F32)).astype(BF16)
        return shift_z(downward, -1)

    def ring_middle(e, upward, *hold):
        chunks = rings[e]
        for k in range(ways_up - 1, 0, -1):
            own = after(chunks[n_z - k], *hold)
            upward = (upward.astype(F32) + own.astype(F32)).astype(BF16)
            if k > 1:
                upward = shift_z(upward, 1)
        return upward

    def ring_end(e, upward, downward, *hold):
        own = after(rings[e][0], *hold).astype(F32)
        return own + shift_z(upward, 1).astype(F32) + downward.astype(F32)

    rings = []
    for e in range(local):
        here = list(pieces[e])
        if e:
            here[0] = after(here[0], rings[-1][0])
        done.append(
            run_expert(
                e, place[e], slot_of, router_rows, tokens_all, grads_all, here, slots
            )
        )
        if e < local - 1:
            begin_rings(e)
    drows, yrows, dchosen = ([r[i] for r in done] for i in (3, 4, 2))
    probs = done[0][5]

    begin_rings(last)
    arrived_zero, down_zero = ring_first(0), ring_down(0)
    early = ring_middle(0, arrived_zero, rings[last][0])
    arrived_last, down_last = ring_first(last), ring_down(last)
    drows[0] = after(drows[0], early, down_zero, rings[last][0])

    def back_of(b, add=None):
        *parts, more = combine_back(
            place[0], slot_cols, drows, dchosen, probs, router_rows, tokens_all[b], b, add
        )
        return parts, more

    drouter = jnp.zeros((expert_count, model), F32)
    arrived = [None] * n_exp
    for k in reversed(range(n_exp)):
        sent, more = back_of(n_exp + k)
        arrived[k] = [swap_core(part) for part in sent]
        drouter = drouter + more
    from_exp = []
    for k in reversed(range(n_exp)):
        total, more = back_of(k, arrived[k])
        drouter = drouter + more
        if k:
            from_exp.append([shift(part, "expert", -k) for part in total])
    ends = [ring_end(0, early, down_zero)]
    dsum, dsum_other = [], []
    for p in range(PARTS):
        value = (after(total[p], ends[0]) if p == 0 else total[p]).astype(F32)
        for came in from_exp:
            value = value + came[p].astype(F32)
        dsum.append(value.astype(BF16))
        other = shift(dsum[p], "heads", 1)
        for k in range(2, n_heads):
            other = other + shift(dsum[p], "heads", k)
        dsum_other.append(other)
    dsum_other[-1] = after(dsum_other[-1], arrived_last)

    yrows[0] = after(yrows[0], dsum[-1])
    y_came = [swap_core(combine(slot_cols, yrows, n_exp + k)) for k in range(n_exp)]
    y_from = [
        shift(combine(slot_cols, yrows, k, after(y_came[k], dsum_other[-1])), "expert", -k)
        for k in range(1, n_exp)
    ]
    dnormed_two = jnp.concatenate(
        [own.astype(F32) + other.astype(F32) for own, other in zip(dsum, dsum_other)], axis=1
    )
    scaled = dnormed_two * gain_two
    grad_gain_two = jnp.sum(dnormed_two * unit_two, axis=0)
    dmiddle = grad_full.astype(F32) + scale_two * (
        scaled
        - jnp.mean(scaled, axis=-1, keepdims=True)
        - unit_two * jnp.mean(scaled * unit_two, axis=-1, keepdims=True)
    )
    late = ring_middle(last, arrived_last, dsum_other[-1])
    datt = after(dmiddle.astype(BF16), late, *y_came)

    dside = jnp.concatenate(
        [drouter, jnp.zeros((1, model), F32), grad_gain_two[None, :],
         jnp.zeros((rest - expert_count - 2, model), F32)], axis=0
    ).T
    dnorm, stats, dpack = attend_back(
        inputs, gain_one, datt, qkv, ctx, pack, dside, expert_count, width, images, seq, n_heads
    )
    dpack = after(dpack, *y_from, down_last)
    y_own = combine(slot_cols, yrows, 0, after(y_came[0], dpack)).astype(F32)
    for value in y_from:
        y_own = y_own + value.astype(F32)
    y_own = y_own.astype(BF16)

    dpack = dpack.reshape(n_z, CORES, n_exp, shard, columns)
    ends.append(ring_end(last, late, down_last))
    dsent = after(swap_core(take(dpack, 1 - core, 1)), ends[last])
    dpack = (take(dpack, core, 1).astype(F32) + dsent.astype(F32)).astype(BF16)
    dtotal = take(dpack, exp, 1).astype(F32)
    for k in range(1, n_exp):
        dtotal = dtotal + shift(take(dpack, (exp + k) % n_exp, 1), "expert", k).astype(F32)
    dpack = dtotal.astype(BF16)
    dtotal = take(dpack, z).astype(F32)
    for k in range(1, n_z):
        dtotal = dtotal + shift_z(take(dpack, (z + k) % n_z), k).astype(F32)
    dside = dtotal[:, 4 * width :]
    over_heads = dside[:, : expert_count + 1].T
    summed = over_heads
    for k in range(1, n_heads):
        summed = summed + shift(over_heads, "heads", k)

    def own_half(value):
        return lax.dynamic_slice_in_dim(value, head * half_width, half_width, 1)

    def cut(value):
        return value.astype(BF16).reshape(images, span, half_width)[:, :seq]

    dn_own = take(dnorm, head).astype(F32)
    sums = stats[:, :2].T
    sums_total = sums
    for k in range(1, n_heads):
        came = shift(take(dnorm, (head + k) % n_heads), "heads", k)
        dn_own = dn_own + after(came, dtotal).astype(F32)
        sums_total = sums_total + after(shift(sums, "heads", k), dtotal)
    unit_one, scale_one = norm_parts(inputs.astype(F32))
    grad_in = own_half(dmiddle) + scale_one * (
        dn_own * own_half(gain_one)
        - sums_total[0][:, None] / model
        - own_half(unit_one) * (sums_total[1][:, None] / model)
    )

    y_total = own_half(y_own).astype(F32)
    for k in range(1, n_heads):
        there = (head + k) % n_heads
        part_y = lax.dynamic_slice_in_dim(y_own, there * half_width, half_width, 1)
        y_total = y_total + after(shift(part_y, "heads", k), dtotal).astype(F32)
    block_out = own_half(middle) + y_total

    stacked = jnp.stack(ends).reshape(local, 2, CORES, part_rows, hidden_width)
    other = swap_core(take(stacked, 1 - core, 2).astype(BF16)).astype(F32)
    own = take(stacked, core, 2)
    joined = jnp.concatenate([jnp.where(low, own, other), jnp.where(low, other, own)], axis=0)
    grads = joined.transpose(1, 2, 0, 3)

    return (
        cut(block_out),
        cut(grad_in),
        summed[expert_count],
        dtotal[:, : 3 * width].reshape(shard, 3, width),
        dtotal[:, 3 * width : 4 * width],
        dside[:, expert_count + 1],
        summed[:expert_count].T,
        grads[1],
        grads[0],
    )


def solution(mesh):
    return jax.shard_map(
        per_device,
        mesh=mesh,
        in_specs=(
            P(("dp", "expert"), None, "heads"),
            P(("dp", "expert"), None, "heads"),
            P(("dp", "expert"), None, None),
            P(("dp", "expert")),
            P(("dp", "expert"), None, "heads"),
            P(("dp", "expert"), "heads"),
            P(("dp", "expert")),
            P(("dp", "expert"), None),
            P("dp", "expert", "heads"),
            P("dp", "expert", "heads"),
        ),
        out_specs=(
            P(("dp", "expert"), None, "heads"),
            P(("dp", "expert"), None, "heads"),
            P(("dp", "expert")),
            P(("dp", "expert"), None, "heads"),
            P(("dp", "expert"), "heads"),
            P(("dp", "expert")),
            P(("dp", "expert"), None),
            P("dp", "expert", "heads"),
            P("dp", "expert", "heads"),
        ),
        check_vma=False,
    )
```

```python
import functools

import jax
import jax.numpy as jnp
from jax import lax
from jax.experimental import pallas as pl
from jax.experimental.pallas import tpu as pltpu
from jax.sharding import PartitionSpec as P

HEAD_DIM = 64
CORES = 2
EPS = 1e-06
LOW = -1e30
F32 = jnp.float32
BF16 = jnp.bfloat16
VMEM_LIMIT = 56 * 1024 * 1024
SHARE = 64
PARTS = 2


def dot(a, b, ca, cb):
    return lax.dot_general(a, b, (((ca,), (cb,)), ((), ())), preferred_element_type=F32)


def shaped(shape, kind):
    return jax.ShapeDtypeStruct(shape, kind)


def params(dims=1):
    return pltpu.CompilerParams(
        dimension_semantics=("arbitrary",) * dims, vmem_limit_bytes=VMEM_LIMIT
    )


def cost(flops, size, powers=0):
    return pl.CostEstimate(
        flops=flops // SHARE, bytes_accessed=size // SHARE, transcendentals=powers // SHARE
    )


def after(value, *others):
    return lax.optimization_barrier((value,) + others)[0]


def norm_parts(rows):
    average = jnp.mean(rows, axis=-1, keepdims=True)
    centred = rows - average
    spread = jnp.mean(centred * centred, axis=-1, keepdims=True)
    scale = lax.rsqrt(spread + EPS)
    return centred * scale, scale


def softmax_rows(q, own_k, real):
    scores = jnp.where(real, dot(q, own_k, 1, 1) * (HEAD_DIM**-0.5), LOW)
    powers = jnp.exp(scores - jnp.max(scores, axis=-1, keepdims=True))
    return powers / jnp.sum(powers, axis=-1, keepdims=True)


def attend_kernel(
    seq, gain_at, x_ref, side_ref, wqkv_ref, wo_ref, part_ref, qkv_ref, ctx_ref, gain_ref
):
    width = wo_ref.shape[1]
    span = x_ref.shape[0]

    @pl.when(pl.program_id(0) == 0)
    def _():
        gain_ref[...] = side_ref[...].astype(F32).T[gain_at : gain_at + 1, :]

    unit, _ = norm_parts(x_ref[...].astype(F32))
    normed = (unit * gain_ref[...]).astype(BF16)
    for part in range(3):
        cols = slice(part * width, (part + 1) * width)
        qkv_ref[:, cols] = dot(normed, wqkv_ref[:, cols], 1, 0).astype(BF16)
    lane = lax.broadcasted_iota(jnp.int32, (span, 128), 1)
    real = lax.broadcasted_iota(jnp.int32, (span, span), 1) < seq
    for pair in range(width // 128):
        q, k, v = (
            qkv_ref[:, part * width + pair * 128 : part * width + (pair + 1) * 128]
            for part in range(3)
        )
        ctx = jnp.zeros((span, 128), F32)
        for side in range(2):
            mine = (lane >= 64) if side else (lane < 64)
            own_k = jnp.where(mine, k, jnp.zeros_like(k))
            own_v = jnp.where(mine, v, jnp.zeros_like(v))
            weights = softmax_rows(q, own_k, real)
            ctx = ctx + dot(weights.astype(BF16), own_v, 1, 0)
        ctx_ref[:, pair * 128 : (pair + 1) * 128] = ctx.astype(BF16)
    part_ref[...] = dot(ctx_ref[...], wo_ref[...], 1, 1).astype(BF16)


def attend(inputs, gain_at, packed, width, images, seq):
    rows, model = inputs.shape
    span = rows // images
    image = lambda last: pl.BlockSpec((span, last), lambda i: (i, 0))
    return pl.pallas_call(
        functools.partial(attend_kernel, seq, gain_at),
        grid=(images,),
        in_specs=[
            image(model),
            pl.BlockSpec((model, 128), lambda i: (0, 4 * width // 128)),
            pl.BlockSpec((model, 3 * width), lambda i: (0, 0)),
            pl.BlockSpec((model, width), lambda i: (0, 3)),
        ],
        out_specs=[image(model), image(3 * width), image(width)],
        scratch_shapes=[pltpu.VMEM((1, model), F32)],
        out_shape=[
            shaped((rows, model), BF16), shaped((rows, 3 * width), BF16), shaped((rows, width), BF16)
        ],
        compiler_params=params(),
        cost_estimate=cost(10 * rows * model * width, 8 * rows * model, rows * span * width // 64),
        name="attend",
    )(inputs, packed, packed, packed)


def attend_back_kernel(
    seq, gain_at, depth,
    core_ref, x_ref, gain_ref, datt_ref, qkv_ref, ctx_ref, wqkv_ref, wo_ref, side_ref,
    dnorm_ref, stats_ref, keep_ref, send_ref, dproj_ref, dgain_ref, dwqkv_ref, dwo_ref, dside_ref,
):
    width = wo_ref.shape[1]
    span, model = x_ref.shape
    step = pl.program_id(0)

    @pl.when(step == 0)
    def _():
        dgain_ref[...] = jnp.zeros_like(dgain_ref)
        dwqkv_ref[...] = jnp.zeros_like(dwqkv_ref)
        dwo_ref[...] = jnp.zeros_like(dwo_ref)

    datt = datt_ref[...]
    dwo_ref[...] += dot(datt, ctx_ref[...], 0, 0)
    dctx_all = dot(datt, wo_ref[...], 1, 0).astype(BF16)
    lane = lax.broadcasted_iota(jnp.int32, (span, 128), 1)
    real = lax.broadcasted_iota(jnp.int32, (span, span), 1) < seq
    for pair in range(width // 128):
        q, k, v = (
            qkv_ref[:, part * width + pair * 128 : part * width + (pair + 1) * 128]
            for part in range(3)
        )
        dctx = dctx_all[:, pair * 128 : (pair + 1) * 128]
        dq = jnp.zeros((span, 128), F32)
        dk = jnp.zeros((span, 128), F32)
        dv = jnp.zeros((span, 128), F32)
        for side in range(2):
            mine = (lane >= 64) if side else (lane < 64)
            own = lambda t: jnp.where(mine, t, jnp.zeros_like(t))
            own_k, own_v = own(k), own(v)
            weights = softmax_rows(q, own_k, real)
            dweights = dot(dctx, own_v, 1, 1)
            inner = jnp.sum(dweights * weights, axis=-1, keepdims=True)
            dscores = (weights * (dweights - inner)).astype(BF16)
            dq = dq + dot(dscores, own_k, 1, 0)
            dk = dk + dot(dscores, own(q), 0, 0)
            dv = dv + dot(weights.astype(BF16), own(dctx), 0, 0)
        for part, value in enumerate((dq * HEAD_DIM**-0.5, dk * HEAD_DIM**-0.5, dv)):
            start = part * width + pair * 128
            dproj_ref[:, start : start + 128] = value.astype(BF16)
    dproj = dproj_ref[...]
    gain = gain_ref[...]
    unit, _ = norm_parts(x_ref[...].astype(F32))
    normed = (unit * gain).astype(BF16)
    dwqkv_ref[...] += dot(normed, dproj, 0, 0)
    dnormed = dot(dproj, wqkv_ref[...], 1, 1)
    halves, _, half = dnorm_ref.shape
    for h in range(halves):
        dnorm_ref[h] = dnormed[:, h * half : (h + 1) * half].astype(BF16)
    along = dnormed * unit
    dgain_ref[...] += jnp.sum(along, axis=0, keepdims=True)
    first = jnp.sum(dnormed * gain, axis=-1, keepdims=True)
    second = jnp.sum(along * gain, axis=-1, keepdims=True)
    stats_ref[...] = jnp.where(lane == 0, first, jnp.where(lane == 1, second, 0.0))

    @pl.when(step == pl.num_programs(0) - 1)
    def _():
        line = lax.broadcasted_iota(jnp.int32, (128, model), 0)
        dside_ref[...] = side_ref[...] + jnp.where(line == gain_at, dgain_ref[...], 0.0).T
        part = model // (depth * CORES)
        for out_ref, which in ((keep_ref, core_ref[0]), (send_ref, 1 - core_ref[0])):
            for z in range(depth):
                rows = pl.ds(pl.multiple_of((z * CORES + which) * part, 16), part)
                here = slice(z * part, (z + 1) * part)
                out_ref[here, : 3 * width] = dwqkv_ref[rows, :].astype(BF16)
                out_ref[here, 3 * width : 4 * width] = dwo_ref[rows, :].astype(BF16)
                out_ref[here, 4 * width :] = dside_ref[rows, :].astype(BF16)


def attend_back(inputs, gain, datt, qkv, ctx, packed, dside, gain_at, width, images, seq, halves, core, depth):
    rows, model = inputs.shape
    span = rows // images
    image = lambda last: pl.BlockSpec((span, last), lambda i, s: (i, 0))
    fixed = lambda *size: pl.BlockSpec(size, lambda i, s: (0, 0))
    return pl.pallas_call(
        functools.partial(attend_back_kernel, seq, gain_at, depth),
        grid_spec=pltpu.PrefetchScalarGridSpec(
            num_scalar_prefetch=1,
            grid=(images,),
            in_specs=[
            image(model), fixed(1, model), image(model), image(3 * width), image(width),
            fixed(model, 3 * width), pl.BlockSpec((model, width), lambda i, s: (0, 3)),
            fixed(model, 128),
        ],
        out_specs=[
            pl.BlockSpec((halves, span, model // halves), lambda i, s: (0, i, 0)),
            image(128),
            fixed(model // CORES, packed.shape[1]),
            fixed(model // CORES, packed.shape[1]),
        ],
        scratch_shapes=[
            pltpu.VMEM((span, 3 * width), BF16),
            pltpu.VMEM((1, model), F32),
            pltpu.VMEM((model, 3 * width), F32),
            pltpu.VMEM((model, width), F32),
            pltpu.VMEM((model, 128), F32),
        ],
        ),
        out_shape=[
            shaped((halves, rows, model // halves), BF16),
            shaped((rows, 128), F32),
            shaped((model // CORES, packed.shape[1]), BF16),
            shaped((model // CORES, packed.shape[1]), BF16),
        ],
        compiler_params=params(),
        cost_estimate=cost(28 * rows * model * width, 12 * rows * model, rows * span * width // 64),
        name="attend_back",
    )(core, inputs, gain, datt, qkv, ctx, packed, packed, dside)


def slot_kernel(slots, place_ref, ids_ref, rows_ref, cols_ref):
    local, tokens = rows_ref.shape[1:]
    ids = ids_ref[0]
    line = lax.broadcasted_iota(jnp.int32, (8, tokens), 0)
    chosen = jnp.zeros((8, tokens), F32)
    for e in range(local):
        named = jnp.max(jnp.where(ids == place_ref[1] + e, 1.0, 0.0), axis=0, keepdims=True)
        chosen = jnp.where(line == e, named, chosen)
    first = lax.broadcasted_iota(jnp.int32, (tokens, tokens), 0)
    second = lax.broadcasted_iota(jnp.int32, (tokens, tokens), 1)
    before = jnp.where(first < second, 1.0, 0.0).astype(BF16)
    same = jnp.where(first == second, 1.0, 0.0).astype(BF16)
    marks = chosen.astype(BF16)
    rank = dot(marks, before, 1, 0)
    rows_ref[0] = jnp.where(chosen > 0.5, rank, -1.0)[:local].astype(jnp.int32)
    column = lax.broadcasted_iota(jnp.int32, (tokens, 8), 1).astype(F32) * slots
    found = jnp.where(dot(same, marks, 1, 1) > 0.5, dot(before, marks, 0, 1) + column, -1.0)
    cols_ref[0] = found[:, :local].astype(jnp.int32)


def find_slots(place, ids, local, slots):
    blocks, _, tokens = ids.shape
    block = lambda *size: pl.BlockSpec((1,) + size, lambda b, s: (b, 0, 0))
    return pl.pallas_call(
        functools.partial(slot_kernel, slots),
        grid_spec=pltpu.PrefetchScalarGridSpec(
            num_scalar_prefetch=1,
            grid=(blocks,),
            in_specs=[block(2, tokens)],
            out_specs=[block(local, tokens), block(tokens, local)],
        ),
        out_shape=[
            shaped((blocks, local, tokens), jnp.int32), shaped((blocks, tokens, local), jnp.int32)
        ],
        compiler_params=params(),
        cost_estimate=cost(64 * blocks * tokens * tokens, 64 * blocks * tokens),
        name="find_slots",
    )(place, ids)


def expert_kernel(index, depth, blocks, place_ref, slot_ref, router_ref, *refs):
    x_refs, refs = refs[:blocks], refs[blocks:]
    grad_refs, refs = refs[:blocks], refs[blocks:]
    win_refs, refs = refs[:depth], refs[depth:]
    wout_refs, refs = refs[:depth], refs[depth:]
    (
        rows_ref, mids_ref, dchosen_ref, drows_ref, yrows_ref, probs_ref, win_all, wout_all,
    ) = refs
    slots, model = rows_ref.shape[2:]
    tokens = x_refs[0].shape[0]
    part_rows, width = win_refs[0].shape[1:]
    step = pl.program_id(0)

    @pl.when(step == 0)
    def _():
        for k in range(depth):
            owner = lax.rem(place_ref[0] - k + depth, depth)
            at = pl.ds(pl.multiple_of(owner * part_rows, 16), part_rows)
            win_all[at, :] = win_refs[k][0]
            wout_all[at, :] = wout_refs[k][0]

    mask = lax.broadcasted_iota(jnp.int32, (slots, tokens), 0) == slot_ref[0, index : index + 1, :]
    pick = jnp.where(mask, 1.0, 0.0).astype(BF16)
    for b in range(blocks):

        @pl.when(step == b)
        def _(b=b):
            rows_ref[0, 0] = dot(pick, grad_refs[b][...], 1, 0).astype(BF16)
            rows_ref[1, 0] = dot(pick, x_refs[b][...], 1, 0).astype(BF16)
            logits = dot(router_ref[...], x_refs[b][...], 1, 1)
            powers = jnp.exp(logits - jnp.max(logits, axis=0, keepdims=True))
            probs_ref[0] = powers / jnp.sum(powers, axis=0, keepdims=True)

    probs = probs_ref[0]
    line = lax.broadcasted_iota(jnp.int32, probs.shape, 0)
    own = jnp.sum(jnp.where(line == place_ref[1], probs, 0.0), axis=0, keepdims=True)
    gate = jnp.sum(jnp.where(mask, own, 0.0), axis=1, keepdims=True)
    grows, rows = rows_ref[0, 0], rows_ref[1, 0]
    dgate = jnp.zeros((slots, 1), F32)
    drows = jnp.zeros((slots, model), F32)
    yrows = jnp.zeros((slots, model), F32)
    tile = 512 if width % 512 == 0 else width
    curve = 0.7978845608028654

    def products(start):
        cols = slice(start, start + tile)
        return dot(rows, win_all[:, cols], 1, 0), dot(grows, wout_all[:, cols], 1, 0)

    ahead = products(0)
    for start in range(0, width, tile):
        cols = slice(start, start + tile)
        hidden, pulled = ahead
        if start + tile < width:
            ahead = products(start + tile)
        square = hidden * hidden
        bend = jnp.tanh(hidden * (curve + curve * 0.044715 * square))
        half = 0.5 + 0.5 * bend
        active = hidden * half
        slope = half + 0.5 * hidden * (1.0 - bend * bend) * (
            curve + 3.0 * curve * 0.044715 * square
        )
        dgate = dgate + jnp.sum(active * pulled, axis=1, keepdims=True)
        gact = (gate * active).astype(BF16)
        dhid = (gate * pulled * slope).astype(BF16)
        mids_ref[0, 0, :, cols] = gact
        mids_ref[1, 0, :, cols] = dhid
        drows = drows + dot(dhid, win_all[:, cols], 1, 1)
        yrows = yrows + dot(gact, wout_all[:, cols], 1, 1)
    dchosen_ref[0] = jnp.sum(jnp.where(mask, dgate, 0.0), axis=0, keepdims=True)
    drows_ref[0] = drows.astype(BF16)
    yrows_ref[0] = yrows.astype(BF16)


def run_expert(index, place, slot_of, router_rows, xs, grads, pieces, slots):
    blocks, depth = len(xs), len(pieces)
    tokens, model = xs[0].shape
    _, part_rows, width = pieces[0].shape
    experts = router_rows.shape[0]
    fixed = lambda *size: pl.BlockSpec(
        size, lambda b, s: (0,) * len(size), pipeline_mode=pl.Buffered(1)
    )
    block = lambda *size: pl.BlockSpec((1,) + size, lambda b, s: (b, 0, 0))
    both = lambda last: pl.BlockSpec((2, 1, slots, last), lambda b, s: (0, b, 0, 0))
    weight = lambda which: pl.BlockSpec(
        (1, part_rows, width), lambda b, s: (which, 0, 0), pipeline_mode=pl.Buffered(1)
    )
    return pl.pallas_call(
        functools.partial(expert_kernel, index, depth, blocks),
        grid_spec=pltpu.PrefetchScalarGridSpec(
            num_scalar_prefetch=1,
            grid=(blocks,),
            in_specs=[block(slot_of.shape[1], tokens), fixed(experts, model)]
            + [fixed(tokens, model)] * (2 * blocks)
            + [weight(1)] * depth
            + [weight(0)] * depth,
            out_specs=[
                both(model), both(width), block(1, tokens), block(slots, model),
                block(slots, model), block(experts, tokens),
            ],
            scratch_shapes=[pltpu.VMEM((model, width), BF16)] * 2,
        ),
        out_shape=[
            shaped((2, blocks, slots, model), BF16), shaped((2, blocks, slots, width), BF16),
            shaped((blocks, 1, tokens), F32), shaped((blocks, slots, model), BF16),
            shaped((blocks, slots, model), BF16), shaped((blocks, experts, tokens), F32),
        ],
        compiler_params=params(),
        cost_estimate=cost(
            8 * blocks * slots * model * width + 4 * blocks * slots * model * tokens,
            16 * blocks * slots * model,
            blocks * slots * width,
        ),
        name="expert",
    )(place, slot_of, router_rows, *xs, *grads, *pieces, *pieces)


def weight_grad_kernel(depth, place_ref, rows_ref, cols_ref, *refs):
    out_refs, total_ref = refs[:depth], refs[depth]
    _, blocks, slots, model = rows_ref.shape
    width = cols_ref.shape[3]
    part_rows = model // depth
    left = rows_ref[0].reshape(blocks * slots, model)
    right = cols_ref[0].reshape(blocks * slots, width)
    total_ref[...] = dot(left, right, 0, 0)
    for k in range(depth):
        owner = lax.rem(place_ref[0] - k + depth, depth)
        at = pl.ds(pl.multiple_of(owner * part_rows, 16), part_rows)
        out_refs[k][0] = total_ref[at, :].astype(BF16)


def weight_grad(place, rows, cols, depth):
    _, blocks, slots, model = rows.shape
    width = cols.shape[3]
    both = lambda last: pl.BlockSpec((1, blocks, slots, last), lambda i, s: (i, 0, 0, 0))
    return pl.pallas_call(
        functools.partial(weight_grad_kernel, depth),
        grid_spec=pltpu.PrefetchScalarGridSpec(
            num_scalar_prefetch=1,
            grid=(2,),
            in_specs=[both(model), both(width)],
            out_specs=[pl.BlockSpec((1, model // depth, width), lambda i, s: (i, 0, 0))] * depth,
            scratch_shapes=[pltpu.VMEM((model, width), F32)],
        ),
        out_shape=[shaped((2, model // depth, width), BF16)] * depth,
        compiler_params=params(),
        cost_estimate=cost(
            4 * blocks * slots * model * width,
            4 * (blocks * slots * (model + width) + model * width),
        ),
        name="weight_grad",
    )(place, rows, cols)


def gathered(local, slot_ref, rows_refs, all_ref):
    slots, tokens = rows_refs[0].shape[1], slot_ref.shape[1]
    at = lax.broadcasted_iota(jnp.int32, (tokens, local * slots), 1)
    mask = at == slot_ref[0, :, 0:1]
    all_ref[0:slots, :] = rows_refs[0][0]
    for e in range(1, local):
        mask = mask | (at == slot_ref[0, :, e : e + 1])
        all_ref[e * slots : (e + 1) * slots, :] = rows_refs[e][0]
    return dot(jnp.where(mask, 1.0, 0.0).astype(BF16), all_ref[...], 1, 0)


def combine_kernel(local, added, slot_ref, *refs):
    rows_refs, refs = refs[:local], refs[local:]
    out_ref, all_ref = refs[-2:]
    total = gathered(local, slot_ref, rows_refs, all_ref)
    if added:
        total = total + refs[0][...].astype(F32)
    out_ref[...] = total.astype(BF16)


def combine(slot_cols, rows, b, add=None):
    _, tokens, local = slot_cols.shape
    slots, model = rows[0].shape[1:]
    whole = pl.BlockSpec((tokens, model), lambda i: (0, 0))
    return pl.pallas_call(
        functools.partial(combine_kernel, local, add is not None),
        grid=(1,),
        in_specs=[pl.BlockSpec((1, tokens, local), lambda i: (b, 0, 0))]
        + [pl.BlockSpec((1, slots, model), lambda i: (b, 0, 0))] * local
        + [whole] * (add is not None),
        out_specs=whole,
        out_shape=shaped((tokens, model), BF16),
        scratch_shapes=[pltpu.VMEM((local * slots, model), BF16)],
        compiler_params=params(),
        cost_estimate=cost(
            2 * local * slots * model * tokens, 2 * model * (local * slots + 2 * tokens)
        ),
        name="combine",
    )(slot_cols, *rows, *(() if add is None else (add,)))


def combine_back_kernel(local, added, place_ref, slot_ref, *refs):
    rows_refs, refs = refs[:local], refs[local:]
    dchosen_refs, refs = refs[:local], refs[local:]
    probs_ref, router_ref, x_ref = refs[:3]
    out_refs, (drouter_ref, all_ref) = refs[-2 - PARTS : -2], refs[-2:]
    probs = probs_ref[0]
    line = lax.broadcasted_iota(jnp.int32, probs.shape, 0)
    dprobs = jnp.zeros_like(probs)
    for e in range(local):
        dprobs = jnp.where(line == place_ref[1] + e, dchosen_refs[e][0], dprobs)
    inner = jnp.sum(dprobs * probs, axis=0, keepdims=True)
    dlogits = (probs * (dprobs - inner)).astype(BF16)
    drouter_ref[...] = dot(dlogits, x_ref[...], 1, 0)
    total = gathered(local, slot_ref, rows_refs, all_ref) + dot(dlogits, router_ref[...], 0, 0)
    part = out_refs[0].shape[1]
    for p in range(PARTS):
        piece = total[:, p * part : (p + 1) * part]
        if added:
            piece = piece + refs[3 + p][...].astype(F32)
        out_refs[p][...] = piece.astype(BF16)


def combine_back(place, slot_cols, rows, dchosen, probs, router_rows, x, b, add=None):
    _, tokens, local = slot_cols.shape
    slots, model = rows[0].shape[1:]
    experts = router_rows.shape[0]
    whole = pl.BlockSpec((tokens, model), lambda i, s: (0, 0))
    part = pl.BlockSpec((tokens, model // PARTS), lambda i, s: (0, 0))
    block = lambda *size: pl.BlockSpec((1,) + size, lambda i, s: (b, 0, 0))
    small = pl.BlockSpec((experts, model), lambda i, s: (0, 0))
    return pl.pallas_call(
        functools.partial(combine_back_kernel, local, add is not None),
        grid_spec=pltpu.PrefetchScalarGridSpec(
            num_scalar_prefetch=1,
            grid=(1,),
            in_specs=[block(tokens, local)]
            + [block(slots, model)] * local
            + [block(1, tokens)] * local
            + [block(experts, tokens), small, whole]
            + [part] * (PARTS * (add is not None)),
            out_specs=[part] * PARTS + [small],
            scratch_shapes=[pltpu.VMEM((local * slots, model), BF16)],
        ),
        out_shape=[shaped((tokens, model // PARTS), BF16)] * PARTS
        + [shaped((experts, model), F32)],
        compiler_params=params(),
        cost_estimate=cost(
            2 * local * slots * model * tokens, 2 * model * (local * slots + 3 * tokens)
        ),
        name="combine_back",
    )(place, slot_cols, *rows, *dchosen, probs, router_rows, x, *(() if add is None else add))


def per_device(
    block_in, cotangent, route_ids, gain_attn, w_qkv, w_out_attn, gain_moe, router, w_in, w_out
):
    n_dp, n_heads, n_exp = (lax.axis_size(name) for name in ("dp", "heads", "expert"))
    n_z = n_dp // CORES
    dp, head, exp = (lax.axis_index(name) for name in ("dp", "heads", "expert"))
    z, core = dp // CORES, dp % CORES
    low = core == 0
    images, seq, half_width = block_in.shape
    span = -(-seq // 16) * 16
    rows = images * span
    model = half_width * n_heads
    width = w_qkv.shape[2]
    shard = w_qkv.shape[0]
    expert_count = router.shape[1]
    group = w_in.shape[1]
    local = group // CORES
    part_rows, _, hidden_width = w_in.shape
    capacity = 20 * images * seq // (7 * expert_count)
    slots = -(-capacity // 16) * 16
    blocks = n_exp * CORES
    rest = 128

    def shift(value, axis, step):
        size = lax.axis_size(axis)
        return lax.ppermute(value, axis, [(i, (i + step) % size) for i in range(size)])

    def shift_z(value, step):
        pairs = [
            (a * CORES + c, ((a + step) % n_z) * CORES + c) for a in range(n_z) for c in range(CORES)
        ]
        return lax.ppermute(value, "dp", pairs)

    def swap_core(value):
        return lax.ppermute(value, "dp", [(i, i ^ 1) for i in range(n_dp)])

    def place_at(pieces, index, count):
        if count == 2:
            first = index == 0
            return jnp.stack(
                [jnp.where(first, pieces[0], pieces[1]), jnp.where(first, pieces[1], pieces[0])]
            )
        out = jnp.zeros((count,) + pieces[0].shape, pieces[0].dtype)
        for k, piece in enumerate(pieces):
            out = lax.dynamic_update_index_in_dim(out, piece, (index - k) % count, 0)
        return out

    def spread(value, axis):
        return [value] + [shift(value, axis, k) for k in range(1, lax.axis_size(axis))]

    def take(value, index, dim=0):
        return lax.dynamic_index_in_dim(value, index, dim, keepdims=False)

    def expert_shards():
        both = jnp.stack([w_out, w_in]).reshape(2, part_rows, CORES, local, hidden_width)
        by_core = both.transpose(2, 3, 0, 1, 4)
        other = swap_core(take(by_core, 1 - core))
        mine = take(by_core, core)
        return jnp.concatenate(
            [jnp.where(low, mine, other), jnp.where(low, other, mine)], axis=2
        )

    ways_up = n_z // 2
    ways_down = n_z - 1 - ways_up

    def ring(piece):
        pieces = [piece] + [None] * (n_z - 1)
        for k in range(1, ways_up + 1):
            pieces[k] = shift_z(pieces[k - 1], 1)
        for k in range(1, ways_down + 1):
            pieces[n_z - k] = shift_z(pieces[(n_z - k + 1) % n_z], -1)
        return pieces

    def blocks_of(value, hold=()):
        along = spread(value, "expert")
        along = along[:1] + [after(part, *hold) for part in along[1:]]
        return along + [swap_core(part) for part in along]

    def full_rows(value):
        padded = jnp.pad(value, ((0, 0), (0, span - seq), (0, 0))).reshape(rows, half_width)
        parts = place_at(spread(padded, "heads"), head, n_heads)
        return jnp.concatenate([parts[i] for i in range(n_heads)], axis=-1)

    inputs = full_rows(block_in)
    grad_full = full_rows(cotangent)

    tail = jnp.concatenate(
        [router, gain_attn[:, None], gain_moe[:, None],
         jnp.zeros((shard, rest - expert_count - 2), BF16)], axis=1
    )
    own_pack = jnp.concatenate([w_qkv.reshape(shard, 3 * width), w_out_attn, tail], axis=1)
    columns = own_pack.shape[1]
    shards = expert_shards()
    ids = jnp.pad(route_ids, ((0, 0), (0, span - seq), (0, 0)), constant_values=-1)
    ids_all = jnp.stack(blocks_of(ids.reshape(rows, 2).T))
    pack_z = place_at(
        [own_pack] + [after(shift_z(own_pack, k), shards) for k in range(1, n_z)], z, n_z
    )
    pack = place_at(spread(after(pack_z, ids_all), "expert"), exp, n_exp)
    pieces = []
    for e in range(local):
        pieces.append(ring(after(shards[e], pieces[-1][1]) if e else shards[e]))
    last = local - 1

    pack = after(pack, pieces[0][1], inputs, grad_full)
    other_pack = swap_core(pack)
    pack = jnp.stack([jnp.where(low, pack, other_pack), jnp.where(low, other_pack, pack)])
    pack = pack.transpose(2, 0, 1, 3, 4).reshape(model, columns)
    side = pack[:, 4 * width :].T
    router_rows = side[:expert_count]
    gain_one = side[expert_count : expert_count + 1].astype(F32)
    gain_two = side[expert_count + 1 : expert_count + 2].astype(F32)

    first_expert = exp * group + core * local
    place = [jnp.stack([z, first_expert + e]).astype(jnp.int32) for e in range(local)]
    slot_of, slot_cols = find_slots(place[0], ids_all, local, slots)

    grads_all = blocks_of(grad_full)
    inputs_ready = inputs
    part, qkv, ctx = attend(inputs_ready, expert_count, pack, width, images, seq)
    part = after(part, pieces[0][-1])
    part_other = shift(part, "heads", 1)
    for k in range(2, n_heads):
        part_other = part_other + shift(part, "heads", k)
    part_other = after(part_other, pieces[0][ways_up], slot_cols)
    middle = inputs.astype(F32) + (part.astype(F32) + part_other.astype(F32))
    unit_two, scale_two = norm_parts(middle)
    normed_two = (unit_two * gain_two).astype(BF16)
    tokens_all = blocks_of(normed_two, (pieces[last][1],))

    done = []

    def begin_rings(e, *hold):
        rows_e, mids_e = done[e][:2]
        rings.append(weight_grad(place[e], after(rows_e, *hold), mids_e, n_z))

    def ring_first(e):
        return shift_z(rings[e][-ways_up % n_z], 1)

    def ring_down(e):
        chunks = rings[e]
        downward = chunks[ways_down]
        for k in range(ways_down - 1, 0, -1):
            downward = (shift_z(downward, -1).astype(F32) + chunks[k].astype(F32)).astype(BF16)
        return shift_z(downward, -1)

    def ring_middle(e, upward, *hold):
        chunks = rings[e]
        for k in range(ways_up - 1, 0, -1):
            own = after(chunks[n_z - k], *hold)
            upward = (upward.astype(F32) + own.astype(F32)).astype(BF16)
            if k > 1:
                upward = shift_z(upward, 1)
        return upward

    def ring_end(e, upward, downward, *hold):
        own = after(rings[e][0], *hold).astype(F32)
        return own + shift_z(upward, 1).astype(F32) + downward.astype(F32)

    rings = []
    for e in range(local):
        here = list(pieces[e])
        if e:
            here[0] = after(here[0], rings[-1][0])
        done.append(
            run_expert(
                e, place[e], slot_of, router_rows, tokens_all, grads_all, here, slots
            )
        )
        if e < local - 1:
            begin_rings(e)
    drows, yrows, dchosen = ([r[i] for r in done] for i in (3, 4, 2))
    probs = done[0][5]

    begin_rings(last)
    arrived_zero, down_zero = ring_first(0), ring_down(0)
    early = ring_middle(0, arrived_zero, rings[last][0])
    arrived_last, down_last = ring_first(last), ring_down(last)
    drows[0] = after(drows[0], early, down_zero, rings[last][0])

    def back_of(b, add=None):
        *parts, more = combine_back(
            place[0], slot_cols, drows, dchosen, probs, router_rows, tokens_all[b], b, add
        )
        return parts, more

    drouter = jnp.zeros((expert_count, model), F32)
    arrived = [None] * n_exp
    for k in reversed(range(n_exp)):
        sent, more = back_of(n_exp + k)
        arrived[k] = [swap_core(part) for part in sent]
        drouter = drouter + more
    from_exp = []
    for k in reversed(range(n_exp)):
        if k < n_exp - 1:
            arrived[k][0] = after(arrived[k][0], total[0])
        total, more = back_of(k, arrived[k])
        drouter = drouter + more
        if k:
            from_exp.append([shift(part, "expert", -k) for part in total])
    ends = [ring_end(0, early, down_zero)]
    dsum, dsum_other = [], []
    for p in range(PARTS):
        value = (after(total[p], ends[0]) if p == 0 else total[p]).astype(F32)
        for came in from_exp:
            value = value + came[p].astype(F32)
        dsum.append(value.astype(BF16))
        other = shift(dsum[p], "heads", 1)
        for k in range(2, n_heads):
            other = other + shift(dsum[p], "heads", k)
        dsum_other.append(other)
    dsum_other[-1] = after(dsum_other[-1], arrived_last)

    yrows[0] = after(yrows[0], dsum[0])
    y_came = [swap_core(combine(slot_cols, yrows, n_exp + k)) for k in range(n_exp)]
    y_from = [
        shift(combine(slot_cols, yrows, k, after(y_came[k], dsum[-1])), "expert", -k)
        for k in range(1, n_exp)
    ]
    dnormed_two = jnp.concatenate(
        [own.astype(F32) + other.astype(F32) for own, other in zip(dsum, dsum_other)], axis=1
    )
    scaled = dnormed_two * gain_two
    grad_gain_two = jnp.sum(dnormed_two * unit_two, axis=0)
    dmiddle = grad_full.astype(F32) + scale_two * (
        scaled
        - jnp.mean(scaled, axis=-1, keepdims=True)
        - unit_two * jnp.mean(scaled * unit_two, axis=-1, keepdims=True)
    )
    late = ring_middle(last, arrived_last, dsum_other[-1])
    datt = after(dmiddle.astype(BF16), late, *y_came)

    dside = jnp.concatenate(
        [drouter, jnp.zeros((1, model), F32), grad_gain_two[None, :],
         jnp.zeros((rest - expert_count - 2, model), F32)], axis=0
    ).T
    dnorm, stats, dkeep, dsend = attend_back(
        inputs, gain_one, datt, qkv, ctx, pack, dside, expert_count, width, images, seq, n_heads,
        core.astype(jnp.int32)[None], n_z,
    )
    dsend = after(dsend, *y_from, down_last)

    dcame = swap_core(dsend)
    dpack = (dkeep.astype(F32) + dcame.astype(F32)).astype(BF16)
    dpack = dpack.reshape(n_z, n_exp, shard, columns)
    y_own = combine(slot_cols, yrows, 0, after(y_came[0], dcame)).astype(F32)
    for value in y_from:
        y_own = y_own + value.astype(F32)
    y_own = y_own.astype(BF16)

    ends.append(ring_end(last, late, down_last, dsend))
    dtotal = take(dpack, exp, 1).astype(F32)
    for k in range(1, n_exp):
        came = shift(take(dpack, (exp + k) % n_exp, 1), "expert", k)
        dtotal = dtotal + after(came, ends[last]).astype(F32)
    dpack = dtotal.astype(BF16)
    dtotal = take(dpack, z).astype(F32)
    for k in range(1, n_z):
        dtotal = dtotal + shift_z(take(dpack, (z + k) % n_z), k).astype(F32)
    dside = dtotal[:, 4 * width :]
    over_heads = dside[:, : expert_count + 1].T
    summed = over_heads
    for k in range(1, n_heads):
        summed = summed + shift(over_heads, "heads", k)

    def own_half(value):
        return lax.dynamic_slice_in_dim(value, head * half_width, half_width, 1)

    def cut(value):
        return value.astype(BF16).reshape(images, span, half_width)[:, :seq]

    dnorm, stats = lax.optimization_barrier((dnorm, stats, dcame))[:2]
    dn_own = take(dnorm, head).astype(F32)
    sums = stats[:, :2].T
    sums_total = sums
    for k in range(1, n_heads):
        came = shift(take(dnorm, (head + k) % n_heads), "heads", k)
        dn_own = dn_own + after(came, dtotal).astype(F32)
        sums_total = sums_total + after(shift(sums, "heads", k), dtotal)
    unit_one, scale_one = norm_parts(inputs.astype(F32))
    grad_in = own_half(dmiddle) + scale_one * (
        dn_own * own_half(gain_one)
        - sums_total[0][:, None] / model
        - own_half(unit_one) * (sums_total[1][:, None] / model)
    )

    y_total = own_half(y_own).astype(F32)
    for k in range(1, n_heads):
        there = (head + k) % n_heads
        part_y = lax.dynamic_slice_in_dim(y_own, there * half_width, half_width, 1)
        y_total = y_total + after(shift(part_y, "heads", k), dtotal).astype(F32)
    block_out = own_half(middle) + y_total

    stacked = jnp.stack(ends).reshape(local, 2, CORES, part_rows, hidden_width)
    other = swap_core(take(stacked, 1 - core, 2).astype(BF16)).astype(F32)
    own = take(stacked, core, 2)
    joined = jnp.concatenate([jnp.where(low, own, other), jnp.where(low, other, own)], axis=0)
    grads = joined.transpose(1, 2, 0, 3)

    return (
        cut(block_out),
        cut(grad_in),
        summed[expert_count],
        dtotal[:, : 3 * width].reshape(shard, 3, width),
        dtotal[:, 3 * width : 4 * width],
        dside[:, expert_count + 1],
        summed[:expert_count].T,
        grads[1],
        grads[0],
    )


def solution(mesh):
    return jax.shard_map(
        per_device,
        mesh=mesh,
        in_specs=(
            P(("dp", "expert"), None, "heads"),
            P(("dp", "expert"), None, "heads"),
            P(("dp", "expert"), None, None),
            P(("dp", "expert")),
            P(("dp", "expert"), None, "heads"),
            P(("dp", "expert"), "heads"),
            P(("dp", "expert")),
            P(("dp", "expert"), None),
            P("dp", "expert", "heads"),
            P("dp", "expert", "heads"),
        ),
        out_specs=(
            P(("dp", "expert"), None, "heads"),
            P(("dp", "expert"), None, "heads"),
            P(("dp", "expert")),
            P(("dp", "expert"), None, "heads"),
            P(("dp", "expert"), "heads"),
            P(("dp", "expert")),
            P(("dp", "expert"), None),
            P("dp", "expert", "heads"),
            P("dp", "expert", "heads"),
        ),
        check_vma=False,
    )
```

```python
import functools

import jax
import jax.numpy as jnp
from jax import lax
from jax.experimental import pallas as pl
from jax.experimental.pallas import tpu as pltpu
from jax.sharding import PartitionSpec as P

HEAD_DIM = 64
CORES = 2
EPS = 1e-06
LOW = -1e30
F32 = jnp.float32
BF16 = jnp.bfloat16
VMEM_LIMIT = 56 * 1024 * 1024
SHARE = 64
PARTS = 2


def dot(a, b, ca, cb):
    return lax.dot_general(a, b, (((ca,), (cb,)), ((), ())), preferred_element_type=F32)


def shaped(shape, kind):
    return jax.ShapeDtypeStruct(shape, kind)


def params(dims=1):
    return pltpu.CompilerParams(
        dimension_semantics=("arbitrary",) * dims, vmem_limit_bytes=VMEM_LIMIT
    )


def cost(flops, size, powers=0):
    return pl.CostEstimate(
        flops=flops // SHARE, bytes_accessed=size // SHARE, transcendentals=powers // SHARE
    )


def after(value, *others):
    return lax.optimization_barrier((value,) + others)[0]


def norm_parts(rows):
    average = jnp.mean(rows, axis=-1, keepdims=True)
    centred = rows - average
    spread = jnp.mean(centred * centred, axis=-1, keepdims=True)
    scale = lax.rsqrt(spread + EPS)
    return centred * scale, scale


def softmax_rows(q, own_k, real):
    scores = jnp.where(real, dot(q, own_k, 1, 1) * (HEAD_DIM**-0.5), LOW)
    powers = jnp.exp(scores - jnp.max(scores, axis=-1, keepdims=True))
    return powers / jnp.sum(powers, axis=-1, keepdims=True)


def attend_kernel(
    seq, gain_at, x_ref, side_ref, wqkv_ref, wo_ref, part_ref, qkv_ref, ctx_ref, gain_ref
):
    width = wo_ref.shape[1]
    span = x_ref.shape[0]

    @pl.when(pl.program_id(0) == 0)
    def _():
        gain_ref[...] = side_ref[...].astype(F32).T[gain_at : gain_at + 1, :]

    unit, _ = norm_parts(x_ref[...].astype(F32))
    normed = (unit * gain_ref[...]).astype(BF16)
    for part in range(3):
        cols = slice(part * width, (part + 1) * width)
        qkv_ref[:, cols] = dot(normed, wqkv_ref[:, cols], 1, 0).astype(BF16)
    lane = lax.broadcasted_iota(jnp.int32, (span, 128), 1)
    real = lax.broadcasted_iota(jnp.int32, (span, span), 1) < seq
    for pair in range(width // 128):
        q, k, v = (
            qkv_ref[:, part * width + pair * 128 : part * width + (pair + 1) * 128]
            for part in range(3)
        )
        ctx = jnp.zeros((span, 128), F32)
        for side in range(2):
            mine = (lane >= 64) if side else (lane < 64)
            own_k = jnp.where(mine, k, jnp.zeros_like(k))
            own_v = jnp.where(mine, v, jnp.zeros_like(v))
            weights = softmax_rows(q, own_k, real)
            ctx = ctx + dot(weights.astype(BF16), own_v, 1, 0)
        ctx_ref[:, pair * 128 : (pair + 1) * 128] = ctx.astype(BF16)
    part_ref[...] = dot(ctx_ref[...], wo_ref[...], 1, 1).astype(BF16)


def attend(inputs, gain_at, packed, width, images, seq):
    rows, model = inputs.shape
    span = rows // images
    image = lambda last: pl.BlockSpec((span, last), lambda i: (i, 0))
    return pl.pallas_call(
        functools.partial(attend_kernel, seq, gain_at),
        grid=(images,),
        in_specs=[
            image(model),
            pl.BlockSpec((model, 128), lambda i: (0, 4 * width // 128)),
            pl.BlockSpec((model, 3 * width), lambda i: (0, 0)),
            pl.BlockSpec((model, width), lambda i: (0, 3)),
        ],
        out_specs=[image(model), image(3 * width), image(width)],
        scratch_shapes=[pltpu.VMEM((1, model), F32)],
        out_shape=[
            shaped((rows, model), BF16), shaped((rows, 3 * width), BF16), shaped((rows, width), BF16)
        ],
        compiler_params=params(),
        cost_estimate=cost(10 * rows * model * width, 8 * rows * model, rows * span * width // 64),
        name="attend",
    )(inputs, packed, packed, packed)


def attend_back_kernel(
    seq, gain_at, depth,
    core_ref, x_ref, gain_ref, datt_ref, qkv_ref, ctx_ref, wqkv_ref, wo_ref, side_ref,
    dnorm_ref, stats_ref, keep_ref, send_ref, dproj_ref, dgain_ref, dwqkv_ref, dwo_ref, dside_ref,
):
    width = wo_ref.shape[1]
    span, model = x_ref.shape
    step = pl.program_id(0)

    @pl.when(step == 0)
    def _():
        dgain_ref[...] = jnp.zeros_like(dgain_ref)
        dwqkv_ref[...] = jnp.zeros_like(dwqkv_ref)
        dwo_ref[...] = jnp.zeros_like(dwo_ref)

    datt = datt_ref[...]
    dwo_ref[...] += dot(datt, ctx_ref[...], 0, 0)
    dctx_all = dot(datt, wo_ref[...], 1, 0).astype(BF16)
    lane = lax.broadcasted_iota(jnp.int32, (span, 128), 1)
    real = lax.broadcasted_iota(jnp.int32, (span, span), 1) < seq
    for pair in range(width // 128):
        q, k, v = (
            qkv_ref[:, part * width + pair * 128 : part * width + (pair + 1) * 128]
            for part in range(3)
        )
        dctx = dctx_all[:, pair * 128 : (pair + 1) * 128]
        dq = jnp.zeros((span, 128), F32)
        dk = jnp.zeros((span, 128), F32)
        dv = jnp.zeros((span, 128), F32)
        for side in range(2):
            mine = (lane >= 64) if side else (lane < 64)
            own = lambda t: jnp.where(mine, t, jnp.zeros_like(t))
            own_k, own_v = own(k), own(v)
            weights = softmax_rows(q, own_k, real)
            dweights = dot(dctx, own_v, 1, 1)
            inner = jnp.sum(dweights * weights, axis=-1, keepdims=True)
            dscores = (weights * (dweights - inner)).astype(BF16)
            dq = dq + dot(dscores, own_k, 1, 0)
            dk = dk + dot(dscores, own(q), 0, 0)
            dv = dv + dot(weights.astype(BF16), own(dctx), 0, 0)
        for part, value in enumerate((dq * HEAD_DIM**-0.5, dk * HEAD_DIM**-0.5, dv)):
            start = part * width + pair * 128
            dproj_ref[:, start : start + 128] = value.astype(BF16)
    dproj = dproj_ref[...]
    gain = gain_ref[...]
    unit, _ = norm_parts(x_ref[...].astype(F32))
    normed = (unit * gain).astype(BF16)
    dwqkv_ref[...] += dot(normed, dproj, 0, 0)
    dnormed = dot(dproj, wqkv_ref[...], 1, 1)
    halves, _, half = dnorm_ref.shape
    for h in range(halves):
        dnorm_ref[h] = dnormed[:, h * half : (h + 1) * half].astype(BF16)
    along = dnormed * unit
    dgain_ref[...] += jnp.sum(along, axis=0, keepdims=True)
    first = jnp.sum(dnormed * gain, axis=-1, keepdims=True)
    second = jnp.sum(along * gain, axis=-1, keepdims=True)
    stats_ref[...] = jnp.where(lane == 0, first, jnp.where(lane == 1, second, 0.0))

    @pl.when(step == pl.num_programs(0) - 1)
    def _():
        line = lax.broadcasted_iota(jnp.int32, (128, model), 0)
        dside_ref[...] = side_ref[...] + jnp.where(line == gain_at, dgain_ref[...], 0.0).T
        part = model // (depth * CORES)
        for out_ref, which in ((keep_ref, core_ref[0]), (send_ref, 1 - core_ref[0])):
            for z in range(depth):
                rows = pl.ds(pl.multiple_of((z * CORES + which) * part, 16), part)
                here = slice(z * part, (z + 1) * part)
                out_ref[here, : 3 * width] = dwqkv_ref[rows, :].astype(BF16)
                out_ref[here, 3 * width : 4 * width] = dwo_ref[rows, :].astype(BF16)
                out_ref[here, 4 * width :] = dside_ref[rows, :].astype(BF16)


def attend_back(inputs, gain, datt, qkv, ctx, packed, dside, gain_at, width, images, seq, halves, core, depth):
    rows, model = inputs.shape
    span = rows // images
    image = lambda last: pl.BlockSpec((span, last), lambda i, s: (i, 0))
    fixed = lambda *size: pl.BlockSpec(size, lambda i, s: (0, 0))
    return pl.pallas_call(
        functools.partial(attend_back_kernel, seq, gain_at, depth),
        grid_spec=pltpu.PrefetchScalarGridSpec(
            num_scalar_prefetch=1,
            grid=(images,),
            in_specs=[
            image(model), fixed(1, model), image(model), image(3 * width), image(width),
            fixed(model, 3 * width), pl.BlockSpec((model, width), lambda i, s: (0, 3)),
            fixed(model, 128),
        ],
        out_specs=[
            pl.BlockSpec((halves, span, model // halves), lambda i, s: (0, i, 0)),
            image(128),
            fixed(model // CORES, packed.shape[1]),
            fixed(model // CORES, packed.shape[1]),
        ],
        scratch_shapes=[
            pltpu.VMEM((span, 3 * width), BF16),
            pltpu.VMEM((1, model), F32),
            pltpu.VMEM((model, 3 * width), F32),
            pltpu.VMEM((model, width), F32),
            pltpu.VMEM((model, 128), F32),
        ],
        ),
        out_shape=[
            shaped((halves, rows, model // halves), BF16),
            shaped((rows, 128), F32),
            shaped((model // CORES, packed.shape[1]), BF16),
            shaped((model // CORES, packed.shape[1]), BF16),
        ],
        compiler_params=params(),
        cost_estimate=cost(28 * rows * model * width, 12 * rows * model, rows * span * width // 64),
        name="attend_back",
    )(core, inputs, gain, datt, qkv, ctx, packed, packed, dside)


def slot_kernel(slots, place_ref, ids_ref, rows_ref, cols_ref):
    local, tokens = rows_ref.shape[1:]
    ids = ids_ref[0]
    line = lax.broadcasted_iota(jnp.int32, (8, tokens), 0)
    chosen = jnp.zeros((8, tokens), F32)
    for e in range(local):
        named = jnp.max(jnp.where(ids == place_ref[1] + e, 1.0, 0.0), axis=0, keepdims=True)
        chosen = jnp.where(line == e, named, chosen)
    first = lax.broadcasted_iota(jnp.int32, (tokens, tokens), 0)
    second = lax.broadcasted_iota(jnp.int32, (tokens, tokens), 1)
    before = jnp.where(first < second, 1.0, 0.0).astype(BF16)
    same = jnp.where(first == second, 1.0, 0.0).astype(BF16)
    marks = chosen.astype(BF16)
    rank = dot(marks, before, 1, 0)
    rows_ref[0] = jnp.where(chosen > 0.5, rank, -1.0)[:local].astype(jnp.int32)
    column = lax.broadcasted_iota(jnp.int32, (tokens, 8), 1).astype(F32) * slots
    found = jnp.where(dot(same, marks, 1, 1) > 0.5, dot(before, marks, 0, 1) + column, -1.0)
    cols_ref[0] = found[:, :local].astype(jnp.int32)


def find_slots(place, ids, local, slots):
    blocks, _, tokens = ids.shape
    block = lambda *size: pl.BlockSpec((1,) + size, lambda b, s: (b, 0, 0))
    return pl.pallas_call(
        functools.partial(slot_kernel, slots),
        grid_spec=pltpu.PrefetchScalarGridSpec(
            num_scalar_prefetch=1,
            grid=(blocks,),
            in_specs=[block(2, tokens)],
            out_specs=[block(local, tokens), block(tokens, local)],
        ),
        out_shape=[
            shaped((blocks, local, tokens), jnp.int32), shaped((blocks, tokens, local), jnp.int32)
        ],
        compiler_params=params(),
        cost_estimate=cost(64 * blocks * tokens * tokens, 64 * blocks * tokens),
        name="find_slots",
    )(place, ids)


def expert_kernel(index, depth, blocks, place_ref, slot_ref, router_ref, *refs):
    x_refs, refs = refs[:blocks], refs[blocks:]
    grad_refs, refs = refs[:blocks], refs[blocks:]
    win_refs, refs = refs[:depth], refs[depth:]
    wout_refs, refs = refs[:depth], refs[depth:]
    (
        rows_ref, mids_ref, dchosen_ref, drows_ref, yrows_ref, probs_ref, win_all, wout_all,
    ) = refs
    slots, model = rows_ref.shape[2:]
    tokens = x_refs[0].shape[0]
    part_rows, width = win_refs[0].shape[1:]
    step = pl.program_id(0)

    @pl.when(step == 0)
    def _():
        for k in range(depth):
            owner = lax.rem(place_ref[0] - k + depth, depth)
            at = pl.ds(pl.multiple_of(owner * part_rows, 16), part_rows)
            win_all[at, :] = win_refs[k][0]
            wout_all[at, :] = wout_refs[k][0]

    mask = lax.broadcasted_iota(jnp.int32, (slots, tokens), 0) == slot_ref[0, index : index + 1, :]
    pick = jnp.where(mask, 1.0, 0.0).astype(BF16)
    for b in range(blocks):

        @pl.when(step == b)
        def _(b=b):
            rows_ref[0, 0] = dot(pick, grad_refs[b][...], 1, 0).astype(BF16)
            rows_ref[1, 0] = dot(pick, x_refs[b][...], 1, 0).astype(BF16)
            logits = dot(router_ref[...], x_refs[b][...], 1, 1)
            powers = jnp.exp(logits - jnp.max(logits, axis=0, keepdims=True))
            probs_ref[0] = powers / jnp.sum(powers, axis=0, keepdims=True)

    probs = probs_ref[0]
    line = lax.broadcasted_iota(jnp.int32, probs.shape, 0)
    own = jnp.sum(jnp.where(line == place_ref[1], probs, 0.0), axis=0, keepdims=True)
    gate = jnp.sum(jnp.where(mask, own, 0.0), axis=1, keepdims=True)
    grows, rows = rows_ref[0, 0], rows_ref[1, 0]
    dgate = jnp.zeros((slots, 1), F32)
    drows = jnp.zeros((slots, model), F32)
    yrows = jnp.zeros((slots, model), F32)
    tile = 512 if width % 512 == 0 else width
    curve = 0.7978845608028654

    def products(start):
        cols = slice(start, start + tile)
        return dot(rows, win_all[:, cols], 1, 0), dot(grows, wout_all[:, cols], 1, 0)

    ahead = products(0)
    for start in range(0, width, tile):
        cols = slice(start, start + tile)
        hidden, pulled = ahead
        if start + tile < width:
            ahead = products(start + tile)
        square = hidden * hidden
        bend = jnp.tanh(hidden * (curve + curve * 0.044715 * square))
        half = 0.5 + 0.5 * bend
        active = hidden * half
        slope = half + 0.5 * hidden * (1.0 - bend * bend) * (
            curve + 3.0 * curve * 0.044715 * square
        )
        dgate = dgate + jnp.sum(active * pulled, axis=1, keepdims=True)
        gact = (gate * active).astype(BF16)
        dhid = (gate * pulled * slope).astype(BF16)
        mids_ref[0, 0, :, cols] = gact
        mids_ref[1, 0, :, cols] = dhid
        drows = drows + dot(dhid, win_all[:, cols], 1, 1)
        yrows = yrows + dot(gact, wout_all[:, cols], 1, 1)
    dchosen_ref[0] = jnp.sum(jnp.where(mask, dgate, 0.0), axis=0, keepdims=True)
    drows_ref[0] = drows.astype(BF16)
    yrows_ref[0] = yrows.astype(BF16)


def run_expert(index, place, slot_of, router_rows, xs, grads, pieces, slots):
    blocks, depth = len(xs), len(pieces)
    tokens, model = xs[0].shape
    _, part_rows, width = pieces[0].shape
    experts = router_rows.shape[0]
    fixed = lambda *size: pl.BlockSpec(
        size, lambda b, s: (0,) * len(size), pipeline_mode=pl.Buffered(1)
    )
    block = lambda *size: pl.BlockSpec((1,) + size, lambda b, s: (b, 0, 0))
    both = lambda last: pl.BlockSpec((2, 1, slots, last), lambda b, s: (0, b, 0, 0))
    weight = lambda which: pl.BlockSpec(
        (1, part_rows, width), lambda b, s: (which, 0, 0), pipeline_mode=pl.Buffered(1)
    )
    return pl.pallas_call(
        functools.partial(expert_kernel, index, depth, blocks),
        grid_spec=pltpu.PrefetchScalarGridSpec(
            num_scalar_prefetch=1,
            grid=(blocks,),
            in_specs=[block(slot_of.shape[1], tokens), fixed(experts, model)]
            + [fixed(tokens, model)] * (2 * blocks)
            + [weight(1)] * depth
            + [weight(0)] * depth,
            out_specs=[
                both(model), both(width), block(1, tokens), block(slots, model),
                block(slots, model), block(experts, tokens),
            ],
            scratch_shapes=[pltpu.VMEM((model, width), BF16)] * 2,
        ),
        out_shape=[
            shaped((2, blocks, slots, model), BF16), shaped((2, blocks, slots, width), BF16),
            shaped((blocks, 1, tokens), F32), shaped((blocks, slots, model), BF16),
            shaped((blocks, slots, model), BF16), shaped((blocks, experts, tokens), F32),
        ],
        compiler_params=params(),
        cost_estimate=cost(
            8 * blocks * slots * model * width + 4 * blocks * slots * model * tokens,
            16 * blocks * slots * model,
            blocks * slots * width,
        ),
        name="expert",
    )(place, slot_of, router_rows, *xs, *grads, *pieces, *pieces)


def weight_grad_kernel(depth, place_ref, rows_ref, cols_ref, *refs):
    out_refs, total_ref = refs[:depth], refs[depth]
    _, blocks, slots, model = rows_ref.shape
    width = cols_ref.shape[3]
    part_rows = model // depth
    left = rows_ref[0].reshape(blocks * slots, model)
    right = cols_ref[0].reshape(blocks * slots, width)
    total_ref[...] = dot(left, right, 0, 0)
    for k in range(depth):
        owner = lax.rem(place_ref[0] - k + depth, depth)
        at = pl.ds(pl.multiple_of(owner * part_rows, 16), part_rows)
        out_refs[k][0] = total_ref[at, :].astype(BF16)


def weight_grad(place, rows, cols, depth):
    _, blocks, slots, model = rows.shape
    width = cols.shape[3]
    both = lambda last: pl.BlockSpec((1, blocks, slots, last), lambda i, s: (i, 0, 0, 0))
    return pl.pallas_call(
        functools.partial(weight_grad_kernel, depth),
        grid_spec=pltpu.PrefetchScalarGridSpec(
            num_scalar_prefetch=1,
            grid=(2,),
            in_specs=[both(model), both(width)],
            out_specs=[pl.BlockSpec((1, model // depth, width), lambda i, s: (i, 0, 0))] * depth,
            scratch_shapes=[pltpu.VMEM((model, width), F32)],
        ),
        out_shape=[shaped((2, model // depth, width), BF16)] * depth,
        compiler_params=params(),
        cost_estimate=cost(
            4 * blocks * slots * model * width,
            4 * (blocks * slots * (model + width) + model * width),
        ),
        name="weight_grad",
    )(place, rows, cols)


def gathered(local, slot_ref, rows_refs, all_ref):
    slots, tokens = rows_refs[0].shape[1], slot_ref.shape[1]
    at = lax.broadcasted_iota(jnp.int32, (tokens, local * slots), 1)
    mask = at == slot_ref[0, :, 0:1]
    all_ref[0:slots, :] = rows_refs[0][0]
    for e in range(1, local):
        mask = mask | (at == slot_ref[0, :, e : e + 1])
        all_ref[e * slots : (e + 1) * slots, :] = rows_refs[e][0]
    return dot(jnp.where(mask, 1.0, 0.0).astype(BF16), all_ref[...], 1, 0)


def combine_kernel(local, added, slot_ref, *refs):
    rows_refs, refs = refs[:local], refs[local:]
    out_ref, all_ref = refs[-2:]
    total = gathered(local, slot_ref, rows_refs, all_ref)
    if added:
        total = total + refs[0][...].astype(F32)
    out_ref[...] = total.astype(BF16)


def combine(slot_cols, rows, b, add=None):
    _, tokens, local = slot_cols.shape
    slots, model = rows[0].shape[1:]
    whole = pl.BlockSpec((tokens, model), lambda i: (0, 0))
    return pl.pallas_call(
        functools.partial(combine_kernel, local, add is not None),
        grid=(1,),
        in_specs=[pl.BlockSpec((1, tokens, local), lambda i: (b, 0, 0))]
        + [pl.BlockSpec((1, slots, model), lambda i: (b, 0, 0))] * local
        + [whole] * (add is not None),
        out_specs=whole,
        out_shape=shaped((tokens, model), BF16),
        scratch_shapes=[pltpu.VMEM((local * slots, model), BF16)],
        compiler_params=params(),
        cost_estimate=cost(
            2 * local * slots * model * tokens, 2 * model * (local * slots + 2 * tokens)
        ),
        name="combine",
    )(slot_cols, *rows, *(() if add is None else (add,)))


def combine_back_kernel(local, added, place_ref, slot_ref, *refs):
    rows_refs, refs = refs[:local], refs[local:]
    dchosen_refs, refs = refs[:local], refs[local:]
    probs_ref, router_ref, x_ref = refs[:3]
    out_refs, (drouter_ref, all_ref) = refs[-2 - PARTS : -2], refs[-2:]
    probs = probs_ref[0]
    line = lax.broadcasted_iota(jnp.int32, probs.shape, 0)
    dprobs = jnp.zeros_like(probs)
    for e in range(local):
        dprobs = jnp.where(line == place_ref[1] + e, dchosen_refs[e][0], dprobs)
    inner = jnp.sum(dprobs * probs, axis=0, keepdims=True)
    dlogits = (probs * (dprobs - inner)).astype(BF16)
    drouter_ref[...] = dot(dlogits, x_ref[...], 1, 0)
    total = gathered(local, slot_ref, rows_refs, all_ref) + dot(dlogits, router_ref[...], 0, 0)
    part = out_refs[0].shape[1]
    for p in range(PARTS):
        piece = total[:, p * part : (p + 1) * part]
        if added:
            piece = piece + refs[3 + p][...].astype(F32)
        out_refs[p][...] = piece.astype(BF16)


def combine_back(place, slot_cols, rows, dchosen, probs, router_rows, x, b, add=None):
    _, tokens, local = slot_cols.shape
    slots, model = rows[0].shape[1:]
    experts = router_rows.shape[0]
    whole = pl.BlockSpec((tokens, model), lambda i, s: (0, 0))
    part = pl.BlockSpec((tokens, model // PARTS), lambda i, s: (0, 0))
    block = lambda *size: pl.BlockSpec((1,) + size, lambda i, s: (b, 0, 0))
    small = pl.BlockSpec((experts, model), lambda i, s: (0, 0))
    return pl.pallas_call(
        functools.partial(combine_back_kernel, local, add is not None),
        grid_spec=pltpu.PrefetchScalarGridSpec(
            num_scalar_prefetch=1,
            grid=(1,),
            in_specs=[block(tokens, local)]
            + [block(slots, model)] * local
            + [block(1, tokens)] * local
            + [block(experts, tokens), small, whole]
            + [part] * (PARTS * (add is not None)),
            out_specs=[part] * PARTS + [small],
            scratch_shapes=[pltpu.VMEM((local * slots, model), BF16)],
        ),
        out_shape=[shaped((tokens, model // PARTS), BF16)] * PARTS
        + [shaped((experts, model), F32)],
        compiler_params=params(),
        cost_estimate=cost(
            2 * local * slots * model * tokens, 2 * model * (local * slots + 3 * tokens)
        ),
        name="combine_back",
    )(place, slot_cols, *rows, *dchosen, probs, router_rows, x, *(() if add is None else add))


def per_device(
    block_in, cotangent, route_ids, gain_attn, w_qkv, w_out_attn, gain_moe, router, w_in, w_out
):
    n_dp, n_heads, n_exp = (lax.axis_size(name) for name in ("dp", "heads", "expert"))
    n_z = n_dp // CORES
    dp, head, exp = (lax.axis_index(name) for name in ("dp", "heads", "expert"))
    z, core = dp // CORES, dp % CORES
    low = core == 0
    images, seq, half_width = block_in.shape
    span = -(-seq // 16) * 16
    rows = images * span
    model = half_width * n_heads
    width = w_qkv.shape[2]
    shard = w_qkv.shape[0]
    expert_count = router.shape[1]
    group = w_in.shape[1]
    local = group // CORES
    part_rows, _, hidden_width = w_in.shape
    capacity = 20 * images * seq // (7 * expert_count)
    slots = -(-capacity // 16) * 16
    blocks = n_exp * CORES
    rest = 128

    def shift(value, axis, step):
        size = lax.axis_size(axis)
        return lax.ppermute(value, axis, [(i, (i + step) % size) for i in range(size)])

    def shift_z(value, step):
        pairs = [
            (a * CORES + c, ((a + step) % n_z) * CORES + c) for a in range(n_z) for c in range(CORES)
        ]
        return lax.ppermute(value, "dp", pairs)

    def swap_core(value):
        return lax.ppermute(value, "dp", [(i, i ^ 1) for i in range(n_dp)])

    def place_at(pieces, index, count):
        if count == 2:
            first = index == 0
            return jnp.stack(
                [jnp.where(first, pieces[0], pieces[1]), jnp.where(first, pieces[1], pieces[0])]
            )
        out = jnp.zeros((count,) + pieces[0].shape, pieces[0].dtype)
        for k, piece in enumerate(pieces):
            out = lax.dynamic_update_index_in_dim(out, piece, (index - k) % count, 0)
        return out

    def spread(value, axis):
        return [value] + [shift(value, axis, k) for k in range(1, lax.axis_size(axis))]

    def take(value, index, dim=0):
        return lax.dynamic_index_in_dim(value, index, dim, keepdims=False)

    def expert_shards():
        both = jnp.stack([w_out, w_in]).reshape(2, part_rows, CORES, local, hidden_width)
        by_core = both.transpose(2, 3, 0, 1, 4)
        other = swap_core(take(by_core, 1 - core))
        mine = take(by_core, core)
        return jnp.concatenate(
            [jnp.where(low, mine, other), jnp.where(low, other, mine)], axis=2
        )

    ways_up = n_z // 2
    ways_down = n_z - 1 - ways_up

    def ring(piece):
        pieces = [piece] + [None] * (n_z - 1)
        for k in range(1, ways_up + 1):
            pieces[k] = shift_z(pieces[k - 1], 1)
        for k in range(1, ways_down + 1):
            pieces[n_z - k] = shift_z(pieces[(n_z - k + 1) % n_z], -1)
        return pieces

    def blocks_of(value, hold=()):
        along = spread(value, "expert")
        if hold:
            along[0] = after(along[0], *hold)
        return along + [swap_core(part) for part in along]

    def full_rows(value):
        padded = jnp.pad(value, ((0, 0), (0, span - seq), (0, 0))).reshape(rows, half_width)
        parts = place_at(spread(padded, "heads"), head, n_heads)
        return jnp.concatenate([parts[i] for i in range(n_heads)], axis=-1)

    inputs = full_rows(block_in)
    grad_full = full_rows(cotangent)

    tail = jnp.concatenate(
        [router, gain_attn[:, None], gain_moe[:, None],
         jnp.zeros((shard, rest - expert_count - 2), BF16)], axis=1
    )
    own_pack = jnp.concatenate([w_qkv.reshape(shard, 3 * width), w_out_attn, tail], axis=1)
    columns = own_pack.shape[1]
    shards = expert_shards()
    ids = jnp.pad(route_ids, ((0, 0), (0, span - seq), (0, 0)), constant_values=-1)
    ids_all = jnp.stack(blocks_of(ids.reshape(rows, 2).T))
    pack_z = place_at(
        [own_pack] + [after(shift_z(own_pack, k), shards) for k in range(1, n_z)], z, n_z
    )
    pieces = []
    for e in range(local):
        pieces.append(ring(after(shards[e], pieces[-1][1]) if e else shards[e]))
    last = local - 1
    pack = place_at(spread(after(pack_z, ids_all), "expert"), exp, n_exp)

    pack = after(pack, pieces[0][1], inputs, grad_full)
    other_pack = swap_core(pack)
    pack = jnp.stack([jnp.where(low, pack, other_pack), jnp.where(low, other_pack, pack)])
    pack = pack.transpose(2, 0, 1, 3, 4).reshape(model, columns)
    side = pack[:, 4 * width :].T
    router_rows = side[:expert_count]
    gain_one = side[expert_count : expert_count + 1].astype(F32)
    gain_two = side[expert_count + 1 : expert_count + 2].astype(F32)

    first_expert = exp * group + core * local
    place = [jnp.stack([z, first_expert + e]).astype(jnp.int32) for e in range(local)]
    slot_of, slot_cols = find_slots(place[0], ids_all, local, slots)

    grads_all = blocks_of(grad_full)
    inputs_ready = inputs
    part, qkv, ctx = attend(inputs_ready, expert_count, pack, width, images, seq)
    part = after(part, pieces[0][-1])
    part_other = shift(part, "heads", 1)
    for k in range(2, n_heads):
        part_other = part_other + shift(part, "heads", k)
    part_other = after(part_other, pieces[0][ways_up], slot_cols)
    middle = inputs.astype(F32) + (part.astype(F32) + part_other.astype(F32))
    unit_two, scale_two = norm_parts(middle)
    normed_two = (unit_two * gain_two).astype(BF16)
    tokens_all = blocks_of(normed_two, (pieces[last][1],))

    done = []

    def begin_rings(e, *hold):
        rows_e, mids_e = done[e][:2]
        rings.append(weight_grad(place[e], after(rows_e, *hold), mids_e, n_z))

    def ring_first(e):
        return shift_z(rings[e][-ways_up % n_z], 1)

    def ring_down(e):
        chunks = rings[e]
        downward = chunks[ways_down]
        for k in range(ways_down - 1, 0, -1):
            downward = (shift_z(downward, -1).astype(F32) + chunks[k].astype(F32)).astype(BF16)
        return shift_z(downward, -1)

    def ring_middle(e, upward, *hold):
        chunks = rings[e]
        for k in range(ways_up - 1, 0, -1):
            own = after(chunks[n_z - k], *hold)
            upward = (upward.astype(F32) + own.astype(F32)).astype(BF16)
            if k > 1:
                upward = shift_z(upward, 1)
        return upward

    def ring_end(e, upward, downward, *hold):
        own = after(rings[e][0], *hold).astype(F32)
        return own + shift_z(upward, 1).astype(F32) + downward.astype(F32)

    rings = []
    for e in range(local):
        here = list(pieces[e])
        if e:
            here[0] = after(here[0], rings[-1][0])
        done.append(
            run_expert(
                e, place[e], slot_of, router_rows, tokens_all, grads_all, here, slots
            )
        )
        if e < local - 1:
            begin_rings(e)
    drows, yrows, dchosen = ([r[i] for r in done] for i in (3, 4, 2))
    probs = done[0][5]

    arrived_zero, down_zero = ring_first(0), ring_down(0)
    drows[0] = after(drows[0], arrived_zero)

    def back_of(b, add=None):
        *parts, more = combine_back(
            place[0], slot_cols, drows, dchosen, probs, router_rows, tokens_all[b], b, add
        )
        return parts, more

    drouter = jnp.zeros((expert_count, model), F32)
    arrived = [None] * n_exp
    for k in reversed(range(n_exp)):
        sent, more = back_of(n_exp + k)
        arrived[k] = [swap_core(part) for part in sent]
        drouter = drouter + more
    from_exp = []
    for k in reversed(range(n_exp)):
        arrived[k][0] = after(arrived[k][0], total[0] if k < n_exp - 1 else down_zero)
        total, more = back_of(k, arrived[k])
        drouter = drouter + more
        if k:
            from_exp.append([shift(part, "expert", -k) for part in total])
        if k == 1:
            begin_rings(last, total[0])
            early = ring_middle(0, arrived_zero, total[0])
    arrived_last, down_last = ring_first(last), ring_down(last)
    ends = [ring_end(0, early, down_zero)]
    dsum, dsum_other = [], []
    for p in range(PARTS):
        value = (after(total[p], rings[last][0]) if p else total[p]).astype(F32)
        for came in from_exp:
            value = value + came[p].astype(F32)
        dsum.append(value.astype(BF16))
        other = shift(dsum[p], "heads", 1)
        for k in range(2, n_heads):
            other = other + shift(dsum[p], "heads", k)
        dsum_other.append(other)
    dsum_other[0] = after(dsum_other[0], ends[0])

    yrows[0] = after(yrows[0], dsum[0])
    y_came = [swap_core(combine(slot_cols, yrows, n_exp + k)) for k in range(n_exp)]
    y_from = [
        shift(combine(slot_cols, yrows, k, after(y_came[k], dsum[-1])), "expert", -k)
        for k in range(1, n_exp)
    ]
    dnormed_two = jnp.concatenate(
        [own.astype(F32) + other.astype(F32) for own, other in zip(dsum, dsum_other)], axis=1
    )
    scaled = dnormed_two * gain_two
    grad_gain_two = jnp.sum(dnormed_two * unit_two, axis=0)
    dmiddle = grad_full.astype(F32) + scale_two * (
        scaled
        - jnp.mean(scaled, axis=-1, keepdims=True)
        - unit_two * jnp.mean(scaled * unit_two, axis=-1, keepdims=True)
    )
    late = ring_middle(last, arrived_last, dsum_other[-1])
    datt = after(dmiddle.astype(BF16), late, *y_came)

    dside = jnp.concatenate(
        [drouter, jnp.zeros((1, model), F32), grad_gain_two[None, :],
         jnp.zeros((rest - expert_count - 2, model), F32)], axis=0
    ).T
    dnorm, stats, dkeep, dsend = attend_back(
        inputs, gain_one, datt, qkv, ctx, pack, dside, expert_count, width, images, seq, n_heads,
        core.astype(jnp.int32)[None], n_z,
    )
    dsend = after(dsend, *y_from, down_last)

    dcame = swap_core(dsend)
    dpack = (dkeep.astype(F32) + dcame.astype(F32)).astype(BF16)
    dpack = dpack.reshape(n_z, n_exp, shard, columns)
    y_own = combine(slot_cols, yrows, 0, after(y_came[0], dcame)).astype(F32)
    for value in y_from:
        y_own = y_own + value.astype(F32)
    y_own = y_own.astype(BF16)

    ends.append(ring_end(last, late, down_last, dcame))
    dtotal = take(dpack, exp, 1).astype(F32)
    for k in range(1, n_exp):
        came = shift(take(dpack, (exp + k) % n_exp, 1), "expert", k)
        dtotal = dtotal + after(came, ends[last]).astype(F32)
    dpack = dtotal.astype(BF16)
    dtotal = take(dpack, z).astype(F32)
    for k in range(1, n_z):
        dtotal = dtotal + shift_z(take(dpack, (z + k) % n_z), k).astype(F32)
    dside = dtotal[:, 4 * width :]
    over_heads = dside[:, : expert_count + 1].T
    summed = over_heads
    for k in range(1, n_heads):
        summed = summed + shift(over_heads, "heads", k)

    def own_half(value):
        return lax.dynamic_slice_in_dim(value, head * half_width, half_width, 1)

    def cut(value):
        return value.astype(BF16).reshape(images, span, half_width)[:, :seq]

    dnorm, stats = lax.optimization_barrier((dnorm, stats, dcame))[:2]
    dn_own = take(dnorm, head).astype(F32)
    sums = stats[:, :2].T
    sums_total = sums
    for k in range(1, n_heads):
        came = shift(take(dnorm, (head + k) % n_heads), "heads", k)
        dn_own = dn_own + after(came, dtotal).astype(F32)
        sums_total = sums_total + after(shift(sums, "heads", k), dtotal)
    unit_one, scale_one = norm_parts(inputs.astype(F32))
    grad_in = own_half(dmiddle) + scale_one * (
        dn_own * own_half(gain_one)
        - sums_total[0][:, None] / model
        - own_half(unit_one) * (sums_total[1][:, None] / model)
    )

    y_total = own_half(y_own).astype(F32)
    for k in range(1, n_heads):
        there = (head + k) % n_heads
        part_y = lax.dynamic_slice_in_dim(y_own, there * half_width, half_width, 1)
        y_total = y_total + after(shift(part_y, "heads", k), dtotal).astype(F32)
    block_out = own_half(middle) + y_total

    stacked = jnp.stack(ends).reshape(local, 2, CORES, part_rows, hidden_width)
    other = swap_core(take(stacked, 1 - core, 2).astype(BF16)).astype(F32)
    own = take(stacked, core, 2)
    joined = jnp.concatenate([jnp.where(low, own, other), jnp.where(low, other, own)], axis=0)
    grads = joined.transpose(1, 2, 0, 3)

    return (
        cut(block_out),
        cut(grad_in),
        summed[expert_count],
        dtotal[:, : 3 * width].reshape(shard, 3, width),
        dtotal[:, 3 * width : 4 * width],
        dside[:, expert_count + 1],
        summed[:expert_count].T,
        grads[1],
        grads[0],
    )


def solution(mesh):
    return jax.shard_map(
        per_device,
        mesh=mesh,
        in_specs=(
            P(("dp", "expert"), None, "heads"),
            P(("dp", "expert"), None, "heads"),
            P(("dp", "expert"), None, None),
            P(("dp", "expert")),
            P(("dp", "expert"), None, "heads"),
            P(("dp", "expert"), "heads"),
            P(("dp", "expert")),
            P(("dp", "expert"), None),
            P("dp", "expert", "heads"),
            P("dp", "expert", "heads"),
        ),
        out_specs=(
            P(("dp", "expert"), None, "heads"),
            P(("dp", "expert"), None, "heads"),
            P(("dp", "expert")),
            P(("dp", "expert"), None, "heads"),
            P(("dp", "expert"), "heads"),
            P(("dp", "expert")),
            P(("dp", "expert"), None),
            P("dp", "expert", "heads"),
            P("dp", "expert", "heads"),
        ),
        check_vma=False,
    )
```

```python
import functools

import jax
import jax.numpy as jnp
from jax import lax
from jax.experimental import pallas as pl
from jax.experimental.pallas import tpu as pltpu
from jax.sharding import PartitionSpec as P

HEAD_DIM = 64
CORES = 2
EPS = 1e-06
LOW = -1e30
F32 = jnp.float32
BF16 = jnp.bfloat16
VMEM_LIMIT = 56 * 1024 * 1024
SHARE = 64
PARTS = 2


def dot(a, b, ca, cb):
    return lax.dot_general(a, b, (((ca,), (cb,)), ((), ())), preferred_element_type=F32)


def shaped(shape, kind):
    return jax.ShapeDtypeStruct(shape, kind)


def params(dims=1):
    return pltpu.CompilerParams(
        dimension_semantics=("arbitrary",) * dims, vmem_limit_bytes=VMEM_LIMIT
    )


def cost(flops, size, powers=0):
    return pl.CostEstimate(
        flops=flops // SHARE, bytes_accessed=size // SHARE, transcendentals=powers // SHARE
    )


def after(value, *others):
    return lax.optimization_barrier((value,) + others)[0]


def norm_parts(rows):
    average = jnp.mean(rows, axis=-1, keepdims=True)
    centred = rows - average
    spread = jnp.mean(centred * centred, axis=-1, keepdims=True)
    scale = lax.rsqrt(spread + EPS)
    return centred * scale, scale


def softmax_rows(q, own_k, real):
    scores = jnp.where(real, dot(q, own_k, 1, 1) * (HEAD_DIM**-0.5), LOW)
    powers = jnp.exp(scores - jnp.max(scores, axis=-1, keepdims=True))
    return powers / jnp.sum(powers, axis=-1, keepdims=True)


def attend_kernel(
    seq, gain_at, x_ref, side_ref, wqkv_ref, wo_ref, part_ref, qkv_ref, ctx_ref, gain_ref
):
    width = wo_ref.shape[1]
    span = x_ref.shape[0]

    @pl.when(pl.program_id(0) == 0)
    def _():
        gain_ref[...] = side_ref[...].astype(F32).T[gain_at : gain_at + 1, :]

    unit, _ = norm_parts(x_ref[...].astype(F32))
    normed = (unit * gain_ref[...]).astype(BF16)
    for part in range(3):
        cols = slice(part * width, (part + 1) * width)
        qkv_ref[:, cols] = dot(normed, wqkv_ref[:, cols], 1, 0).astype(BF16)
    lane = lax.broadcasted_iota(jnp.int32, (span, 128), 1)
    real = lax.broadcasted_iota(jnp.int32, (span, span), 1) < seq
    for pair in range(width // 128):
        q, k, v = (
            qkv_ref[:, part * width + pair * 128 : part * width + (pair + 1) * 128]
            for part in range(3)
        )
        ctx = jnp.zeros((span, 128), F32)
        for side in range(2):
            mine = (lane >= 64) if side else (lane < 64)
            own_k = jnp.where(mine, k, jnp.zeros_like(k))
            own_v = jnp.where(mine, v, jnp.zeros_like(v))
            weights = softmax_rows(q, own_k, real)
            ctx = ctx + dot(weights.astype(BF16), own_v, 1, 0)
        ctx_ref[:, pair * 128 : (pair + 1) * 128] = ctx.astype(BF16)
    part_ref[...] = dot(ctx_ref[...], wo_ref[...], 1, 1).astype(BF16)


def attend(inputs, gain_at, packed, width, images, seq):
    rows, model = inputs.shape
    span = rows // images
    image = lambda last: pl.BlockSpec((span, last), lambda i: (i, 0))
    return pl.pallas_call(
        functools.partial(attend_kernel, seq, gain_at),
        grid=(images,),
        in_specs=[
            image(model),
            pl.BlockSpec((model, 128), lambda i: (0, 4 * width // 128)),
            pl.BlockSpec((model, 3 * width), lambda i: (0, 0)),
            pl.BlockSpec((model, width), lambda i: (0, 3)),
        ],
        out_specs=[image(model), image(3 * width), image(width)],
        scratch_shapes=[pltpu.VMEM((1, model), F32)],
        out_shape=[
            shaped((rows, model), BF16), shaped((rows, 3 * width), BF16), shaped((rows, width), BF16)
        ],
        compiler_params=params(),
        cost_estimate=cost(10 * rows * model * width, 8 * rows * model, rows * span * width // 64),
        name="attend",
    )(inputs, packed, packed, packed)


def attend_back_kernel(
    seq, gain_at, depth,
    core_ref, x_ref, gain_ref, datt_ref, qkv_ref, ctx_ref, wqkv_ref, wo_ref, side_ref,
    dnorm_ref, stats_ref, keep_ref, send_ref, dproj_ref, dgain_ref, dwqkv_ref, dwo_ref, dside_ref,
):
    width = wo_ref.shape[1]
    span, model = x_ref.shape
    step = pl.program_id(0)

    @pl.when(step == 0)
    def _():
        dgain_ref[...] = jnp.zeros_like(dgain_ref)
        dwqkv_ref[...] = jnp.zeros_like(dwqkv_ref)
        dwo_ref[...] = jnp.zeros_like(dwo_ref)

    datt = datt_ref[...]
    dwo_ref[...] += dot(datt, ctx_ref[...], 0, 0)
    dctx_all = dot(datt, wo_ref[...], 1, 0).astype(BF16)
    lane = lax.broadcasted_iota(jnp.int32, (span, 128), 1)
    real = lax.broadcasted_iota(jnp.int32, (span, span), 1) < seq
    for pair in range(width // 128):
        q, k, v = (
            qkv_ref[:, part * width + pair * 128 : part * width + (pair + 1) * 128]
            for part in range(3)
        )
        dctx = dctx_all[:, pair * 128 : (pair + 1) * 128]
        dq = jnp.zeros((span, 128), F32)
        dk = jnp.zeros((span, 128), F32)
        dv = jnp.zeros((span, 128), F32)
        for side in range(2):
            mine = (lane >= 64) if side else (lane < 64)
            own = lambda t: jnp.where(mine, t, jnp.zeros_like(t))
            own_k, own_v = own(k), own(v)
            weights = softmax_rows(q, own_k, real)
            dweights = dot(dctx, own_v, 1, 1)
            inner = jnp.sum(dweights * weights, axis=-1, keepdims=True)
            dscores = (weights * (dweights - inner)).astype(BF16)
            dq = dq + dot(dscores, own_k, 1, 0)
            dk = dk + dot(dscores, own(q), 0, 0)
            dv = dv + dot(weights.astype(BF16), own(dctx), 0, 0)
        for part, value in enumerate((dq * HEAD_DIM**-0.5, dk * HEAD_DIM**-0.5, dv)):
            start = part * width + pair * 128
            dproj_ref[:, start : start + 128] = value.astype(BF16)
    dproj = dproj_ref[...]
    gain = gain_ref[...]
    unit, _ = norm_parts(x_ref[...].astype(F32))
    normed = (unit * gain).astype(BF16)
    dwqkv_ref[...] += dot(normed, dproj, 0, 0)
    dnormed = dot(dproj, wqkv_ref[...], 1, 1)
    halves, _, half = dnorm_ref.shape
    for h in range(halves):
        dnorm_ref[h] = dnormed[:, h * half : (h + 1) * half].astype(BF16)
    along = dnormed * unit
    dgain_ref[...] += jnp.sum(along, axis=0, keepdims=True)
    first = jnp.sum(dnormed * gain, axis=-1, keepdims=True)
    second = jnp.sum(along * gain, axis=-1, keepdims=True)
    stats_ref[...] = jnp.where(lane == 0, first, jnp.where(lane == 1, second, 0.0))

    @pl.when(step == pl.num_programs(0) - 1)
    def _():
        line = lax.broadcasted_iota(jnp.int32, (128, model), 0)
        dside_ref[...] = side_ref[...] + jnp.where(line == gain_at, dgain_ref[...], 0.0).T
        part = model // (depth * CORES)
        for out_ref, which in ((keep_ref, core_ref[0]), (send_ref, 1 - core_ref[0])):
            for z in range(depth):
                rows = pl.ds(pl.multiple_of((z * CORES + which) * part, 16), part)
                here = slice(z * part, (z + 1) * part)
                out_ref[here, : 3 * width] = dwqkv_ref[rows, :].astype(BF16)
                out_ref[here, 3 * width : 4 * width] = dwo_ref[rows, :].astype(BF16)
                out_ref[here, 4 * width :] = dside_ref[rows, :].astype(BF16)


def attend_back(inputs, gain, datt, qkv, ctx, packed, dside, gain_at, width, images, seq, halves, core, depth):
    rows, model = inputs.shape
    span = rows // images
    image = lambda last: pl.BlockSpec((span, last), lambda i, s: (i, 0))
    fixed = lambda *size: pl.BlockSpec(size, lambda i, s: (0, 0))
    return pl.pallas_call(
        functools.partial(attend_back_kernel, seq, gain_at, depth),
        grid_spec=pltpu.PrefetchScalarGridSpec(
            num_scalar_prefetch=1,
            grid=(images,),
            in_specs=[
            image(model), fixed(1, model), image(model), image(3 * width), image(width),
            fixed(model, 3 * width), pl.BlockSpec((model, width), lambda i, s: (0, 3)),
            fixed(model, 128),
        ],
        out_specs=[
            pl.BlockSpec((halves, span, model // halves), lambda i, s: (0, i, 0)),
            image(128),
            fixed(model // CORES, packed.shape[1]),
            fixed(model // CORES, packed.shape[1]),
        ],
        scratch_shapes=[
            pltpu.VMEM((span, 3 * width), BF16),
            pltpu.VMEM((1, model), F32),
            pltpu.VMEM((model, 3 * width), F32),
            pltpu.VMEM((model, width), F32),
            pltpu.VMEM((model, 128), F32),
        ],
        ),
        out_shape=[
            shaped((halves, rows, model // halves), BF16),
            shaped((rows, 128), F32),
            shaped((model // CORES, packed.shape[1]), BF16),
            shaped((model // CORES, packed.shape[1]), BF16),
        ],
        compiler_params=params(),
        cost_estimate=cost(28 * rows * model * width, 12 * rows * model, rows * span * width // 64),
        name="attend_back",
    )(core, inputs, gain, datt, qkv, ctx, packed, packed, dside)


def slot_kernel(slots, place_ref, ids_ref, rows_ref, cols_ref):
    local, tokens = rows_ref.shape[1:]
    ids = ids_ref[0]
    line = lax.broadcasted_iota(jnp.int32, (8, tokens), 0)
    chosen = jnp.zeros((8, tokens), F32)
    for e in range(local):
        named = jnp.max(jnp.where(ids == place_ref[1] + e, 1.0, 0.0), axis=0, keepdims=True)
        chosen = jnp.where(line == e, named, chosen)
    first = lax.broadcasted_iota(jnp.int32, (tokens, tokens), 0)
    second = lax.broadcasted_iota(jnp.int32, (tokens, tokens), 1)
    before = jnp.where(first < second, 1.0, 0.0).astype(BF16)
    same = jnp.where(first == second, 1.0, 0.0).astype(BF16)
    marks = chosen.astype(BF16)
    rank = dot(marks, before, 1, 0)
    rows_ref[0] = jnp.where(chosen > 0.5, rank, -1.0)[:local].astype(jnp.int32)
    column = lax.broadcasted_iota(jnp.int32, (tokens, 8), 1).astype(F32) * slots
    found = jnp.where(dot(same, marks, 1, 1) > 0.5, dot(before, marks, 0, 1) + column, -1.0)
    cols_ref[0] = found[:, :local].astype(jnp.int32)


def find_slots(place, ids, local, slots):
    blocks, _, tokens = ids.shape
    block = lambda *size: pl.BlockSpec((1,) + size, lambda b, s: (b, 0, 0))
    return pl.pallas_call(
        functools.partial(slot_kernel, slots),
        grid_spec=pltpu.PrefetchScalarGridSpec(
            num_scalar_prefetch=1,
            grid=(blocks,),
            in_specs=[block(2, tokens)],
            out_specs=[block(local, tokens), block(tokens, local)],
        ),
        out_shape=[
            shaped((blocks, local, tokens), jnp.int32), shaped((blocks, tokens, local), jnp.int32)
        ],
        compiler_params=params(),
        cost_estimate=cost(64 * blocks * tokens * tokens, 64 * blocks * tokens),
        name="find_slots",
    )(place, ids)


def expert_kernel(index, depth, blocks, place_ref, slot_ref, router_ref, *refs):
    x_refs, refs = refs[:blocks], refs[blocks:]
    grad_refs, refs = refs[:blocks], refs[blocks:]
    win_refs, refs = refs[:depth], refs[depth:]
    wout_refs, refs = refs[:depth], refs[depth:]
    (
        rows_ref, mids_ref, dchosen_ref, drows_ref, yrows_ref, probs_ref, win_all, wout_all,
    ) = refs
    slots, model = rows_ref.shape[2:]
    tokens = x_refs[0].shape[0]
    part_rows, width = win_refs[0].shape[1:]
    step = pl.program_id(0)

    @pl.when(step == 0)
    def _():
        for k in range(depth):
            owner = lax.rem(place_ref[0] - k + depth, depth)
            at = pl.ds(pl.multiple_of(owner * part_rows, 16), part_rows)
            win_all[at, :] = win_refs[k][0]
            wout_all[at, :] = wout_refs[k][0]

    mask = lax.broadcasted_iota(jnp.int32, (slots, tokens), 0) == slot_ref[0, index : index + 1, :]
    pick = jnp.where(mask, 1.0, 0.0).astype(BF16)
    for b in range(blocks):

        @pl.when(step == b)
        def _(b=b):
            rows_ref[0, 0] = dot(pick, grad_refs[b][...], 1, 0).astype(BF16)
            rows_ref[1, 0] = dot(pick, x_refs[b][...], 1, 0).astype(BF16)
            logits = dot(router_ref[...], x_refs[b][...], 1, 1)
            powers = jnp.exp(logits - jnp.max(logits, axis=0, keepdims=True))
            probs_ref[0] = powers / jnp.sum(powers, axis=0, keepdims=True)

    probs = probs_ref[0]
    line = lax.broadcasted_iota(jnp.int32, probs.shape, 0)
    own = jnp.sum(jnp.where(line == place_ref[1], probs, 0.0), axis=0, keepdims=True)
    gate = jnp.sum(jnp.where(mask, own, 0.0), axis=1, keepdims=True)
    grows, rows = rows_ref[0, 0], rows_ref[1, 0]
    dgate = jnp.zeros((slots, 1), F32)
    drows = jnp.zeros((slots, model), F32)
    yrows = jnp.zeros((slots, model), F32)
    tile = 512 if width % 512 == 0 else width
    curve = 0.7978845608028654

    def products(start):
        cols = slice(start, start + tile)
        return dot(rows, win_all[:, cols], 1, 0), dot(grows, wout_all[:, cols], 1, 0)

    ahead = products(0)
    for start in range(0, width, tile):
        cols = slice(start, start + tile)
        hidden, pulled = ahead
        if start + tile < width:
            ahead = products(start + tile)
        square = hidden * hidden
        bend = jnp.tanh(hidden * (curve + curve * 0.044715 * square))
        half = 0.5 + 0.5 * bend
        active = hidden * half
        slope = half + 0.5 * hidden * (1.0 - bend * bend) * (
            curve + 3.0 * curve * 0.044715 * square
        )
        dgate = dgate + jnp.sum(active * pulled, axis=1, keepdims=True)
        gact = (gate * active).astype(BF16)
        dhid = (gate * pulled * slope).astype(BF16)
        mids_ref[0, 0, :, cols] = gact
        mids_ref[1, 0, :, cols] = dhid
        drows = drows + dot(dhid, win_all[:, cols], 1, 1)
        yrows = yrows + dot(gact, wout_all[:, cols], 1, 1)
    dchosen_ref[0] = jnp.sum(jnp.where(mask, dgate, 0.0), axis=0, keepdims=True)
    drows_ref[0] = drows.astype(BF16)
    yrows_ref[0] = yrows.astype(BF16)


def run_expert(index, place, slot_of, router_rows, xs, grads, pieces, slots):
    blocks, depth = len(xs), len(pieces)
    tokens, model = xs[0].shape
    _, part_rows, width = pieces[0].shape
    experts = router_rows.shape[0]
    fixed = lambda *size: pl.BlockSpec(
        size, lambda b, s: (0,) * len(size), pipeline_mode=pl.Buffered(1)
    )
    block = lambda *size: pl.BlockSpec((1,) + size, lambda b, s: (b, 0, 0))
    both = lambda last: pl.BlockSpec((2, 1, slots, last), lambda b, s: (0, b, 0, 0))
    weight = lambda which: pl.BlockSpec(
        (1, part_rows, width), lambda b, s: (which, 0, 0), pipeline_mode=pl.Buffered(1)
    )
    return pl.pallas_call(
        functools.partial(expert_kernel, index, depth, blocks),
        grid_spec=pltpu.PrefetchScalarGridSpec(
            num_scalar_prefetch=1,
            grid=(blocks,),
            in_specs=[block(slot_of.shape[1], tokens), fixed(experts, model)]
            + [fixed(tokens, model)] * (2 * blocks)
            + [weight(1)] * depth
            + [weight(0)] * depth,
            out_specs=[
                both(model), both(width), block(1, tokens), block(slots, model),
                block(slots, model), block(experts, tokens),
            ],
            scratch_shapes=[pltpu.VMEM((model, width), BF16)] * 2,
        ),
        out_shape=[
            shaped((2, blocks, slots, model), BF16), shaped((2, blocks, slots, width), BF16),
            shaped((blocks, 1, tokens), F32), shaped((blocks, slots, model), BF16),
            shaped((blocks, slots, model), BF16), shaped((blocks, experts, tokens), F32),
        ],
        compiler_params=params(),
        cost_estimate=cost(
            8 * blocks * slots * model * width + 4 * blocks * slots * model * tokens,
            16 * blocks * slots * model,
            blocks * slots * width,
        ),
        name="expert",
    )(place, slot_of, router_rows, *xs, *grads, *pieces, *pieces)


def weight_grad_kernel(depth, place_ref, rows_ref, cols_ref, *refs):
    out_refs, total_ref = refs[:depth], refs[depth]
    _, blocks, slots, model = rows_ref.shape
    width = cols_ref.shape[3]
    part_rows = model // depth
    left = rows_ref[0].reshape(blocks * slots, model)
    right = cols_ref[0].reshape(blocks * slots, width)
    total_ref[...] = dot(left, right, 0, 0)
    for k in range(depth):
        owner = lax.rem(place_ref[0] - k + depth, depth)
        at = pl.ds(pl.multiple_of(owner * part_rows, 16), part_rows)
        out_refs[k][0] = total_ref[at, :].astype(BF16)


def weight_grad(place, rows, cols, depth):
    _, blocks, slots, model = rows.shape
    width = cols.shape[3]
    both = lambda last: pl.BlockSpec((1, blocks, slots, last), lambda i, s: (i, 0, 0, 0))
    return pl.pallas_call(
        functools.partial(weight_grad_kernel, depth),
        grid_spec=pltpu.PrefetchScalarGridSpec(
            num_scalar_prefetch=1,
            grid=(2,),
            in_specs=[both(model), both(width)],
            out_specs=[pl.BlockSpec((1, model // depth, width), lambda i, s: (i, 0, 0))] * depth,
            scratch_shapes=[pltpu.VMEM((model, width), F32)],
        ),
        out_shape=[shaped((2, model // depth, width), BF16)] * depth,
        compiler_params=params(),
        cost_estimate=cost(
            4 * blocks * slots * model * width,
            4 * (blocks * slots * (model + width) + model * width),
        ),
        name="weight_grad",
    )(place, rows, cols)


def gathered(local, slot_ref, rows_refs, all_ref):
    slots, tokens = rows_refs[0].shape[1], slot_ref.shape[1]
    at = lax.broadcasted_iota(jnp.int32, (tokens, local * slots), 1)
    mask = at == slot_ref[0, :, 0:1]
    all_ref[0:slots, :] = rows_refs[0][0]
    for e in range(1, local):
        mask = mask | (at == slot_ref[0, :, e : e + 1])
        all_ref[e * slots : (e + 1) * slots, :] = rows_refs[e][0]
    return dot(jnp.where(mask, 1.0, 0.0).astype(BF16), all_ref[...], 1, 0)


def combine_kernel(local, added, slot_ref, *refs):
    rows_refs, refs = refs[:local], refs[local:]
    out_ref, all_ref = refs[-2:]
    total = gathered(local, slot_ref, rows_refs, all_ref)
    if added:
        total = total + refs[0][...].astype(F32)
    out_ref[...] = total.astype(BF16)


def combine(slot_cols, rows, b, add=None):
    _, tokens, local = slot_cols.shape
    slots, model = rows[0].shape[1:]
    whole = pl.BlockSpec((tokens, model), lambda i: (0, 0))
    return pl.pallas_call(
        functools.partial(combine_kernel, local, add is not None),
        grid=(1,),
        in_specs=[pl.BlockSpec((1, tokens, local), lambda i: (b, 0, 0))]
        + [pl.BlockSpec((1, slots, model), lambda i: (b, 0, 0))] * local
        + [whole] * (add is not None),
        out_specs=whole,
        out_shape=shaped((tokens, model), BF16),
        scratch_shapes=[pltpu.VMEM((local * slots, model), BF16)],
        compiler_params=params(),
        cost_estimate=cost(
            2 * local * slots * model * tokens, 2 * model * (local * slots + 2 * tokens)
        ),
        name="combine",
    )(slot_cols, *rows, *(() if add is None else (add,)))


def combine_back_kernel(local, added, place_ref, slot_ref, *refs):
    rows_refs, refs = refs[:local], refs[local:]
    dchosen_refs, refs = refs[:local], refs[local:]
    probs_ref, router_ref, x_ref = refs[:3]
    out_refs, (drouter_ref, all_ref) = refs[-2 - PARTS : -2], refs[-2:]
    probs = probs_ref[0]
    line = lax.broadcasted_iota(jnp.int32, probs.shape, 0)
    dprobs = jnp.zeros_like(probs)
    for e in range(local):
        dprobs = jnp.where(line == place_ref[1] + e, dchosen_refs[e][0], dprobs)
    inner = jnp.sum(dprobs * probs, axis=0, keepdims=True)
    dlogits = (probs * (dprobs - inner)).astype(BF16)
    drouter_ref[...] = dot(dlogits, x_ref[...], 1, 0)
    total = gathered(local, slot_ref, rows_refs, all_ref) + dot(dlogits, router_ref[...], 0, 0)
    part = out_refs[0].shape[1]
    for p in range(PARTS):
        piece = total[:, p * part : (p + 1) * part]
        if added:
            piece = piece + refs[3 + p][...].astype(F32)
        out_refs[p][...] = piece.astype(BF16)


def combine_back(place, slot_cols, rows, dchosen, probs, router_rows, x, b, add=None):
    _, tokens, local = slot_cols.shape
    slots, model = rows[0].shape[1:]
    experts = router_rows.shape[0]
    whole = pl.BlockSpec((tokens, model), lambda i, s: (0, 0))
    part = pl.BlockSpec((tokens, model // PARTS), lambda i, s: (0, 0))
    block = lambda *size: pl.BlockSpec((1,) + size, lambda i, s: (b, 0, 0))
    small = pl.BlockSpec((experts, model), lambda i, s: (0, 0))
    return pl.pallas_call(
        functools.partial(combine_back_kernel, local, add is not None),
        grid_spec=pltpu.PrefetchScalarGridSpec(
            num_scalar_prefetch=1,
            grid=(1,),
            in_specs=[block(tokens, local)]
            + [block(slots, model)] * local
            + [block(1, tokens)] * local
            + [block(experts, tokens), small, whole]
            + [part] * (PARTS * (add is not None)),
            out_specs=[part] * PARTS + [small],
            scratch_shapes=[pltpu.VMEM((local * slots, model), BF16)],
        ),
        out_shape=[shaped((tokens, model // PARTS), BF16)] * PARTS
        + [shaped((experts, model), F32)],
        compiler_params=params(),
        cost_estimate=cost(
            2 * local * slots * model * tokens, 2 * model * (local * slots + 3 * tokens)
        ),
        name="combine_back",
    )(place, slot_cols, *rows, *dchosen, probs, router_rows, x, *(() if add is None else add))


def per_device(
    block_in, cotangent, route_ids, gain_attn, w_qkv, w_out_attn, gain_moe, router, w_in, w_out
):
    n_dp, n_heads, n_exp = (lax.axis_size(name) for name in ("dp", "heads", "expert"))
    n_z = n_dp // CORES
    dp, head, exp = (lax.axis_index(name) for name in ("dp", "heads", "expert"))
    z, core = dp // CORES, dp % CORES
    low = core == 0
    images, seq, half_width = block_in.shape
    span = -(-seq // 16) * 16
    rows = images * span
    model = half_width * n_heads
    width = w_qkv.shape[2]
    shard = w_qkv.shape[0]
    expert_count = router.shape[1]
    group = w_in.shape[1]
    local = group // CORES
    part_rows, _, hidden_width = w_in.shape
    capacity = 20 * images * seq // (7 * expert_count)
    slots = -(-capacity // 16) * 16
    blocks = n_exp * CORES
    rest = 128

    def shift(value, axis, step):
        size = lax.axis_size(axis)
        return lax.ppermute(value, axis, [(i, (i + step) % size) for i in range(size)])

    def shift_z(value, step):
        pairs = [
            (a * CORES + c, ((a + step) % n_z) * CORES + c) for a in range(n_z) for c in range(CORES)
        ]
        return lax.ppermute(value, "dp", pairs)

    def swap_core(value):
        return lax.ppermute(value, "dp", [(i, i ^ 1) for i in range(n_dp)])

    def place_at(pieces, index, count):
        if count == 2:
            first = index == 0
            return jnp.stack(
                [jnp.where(first, pieces[0], pieces[1]), jnp.where(first, pieces[1], pieces[0])]
            )
        out = jnp.zeros((count,) + pieces[0].shape, pieces[0].dtype)
        for k, piece in enumerate(pieces):
            out = lax.dynamic_update_index_in_dim(out, piece, (index - k) % count, 0)
        return out

    def spread(value, axis):
        return [value] + [shift(value, axis, k) for k in range(1, lax.axis_size(axis))]

    def take(value, index, dim=0):
        return lax.dynamic_index_in_dim(value, index, dim, keepdims=False)

    def expert_shards():
        both = jnp.stack([w_out, w_in]).reshape(2, part_rows, CORES, local, hidden_width)
        by_core = both.transpose(2, 3, 0, 1, 4)
        other = swap_core(take(by_core, 1 - core))
        mine = take(by_core, core)
        return jnp.concatenate(
            [jnp.where(low, mine, other), jnp.where(low, other, mine)], axis=2
        )

    ways_up = n_z // 2
    ways_down = n_z - 1 - ways_up

    def ring(piece):
        pieces = [piece] + [None] * (n_z - 1)
        for k in range(1, ways_up + 1):
            pieces[k] = shift_z(pieces[k - 1], 1)
        for k in range(1, ways_down + 1):
            pieces[n_z - k] = shift_z(pieces[(n_z - k + 1) % n_z], -1)
        return pieces

    def blocks_of(value, hold=()):
        along = spread(value, "expert")
        if hold:
            along[0] = after(along[0], *hold)
        return along + [swap_core(part) for part in along]

    def full_rows(value):
        padded = jnp.pad(value, ((0, 0), (0, span - seq), (0, 0))).reshape(rows, half_width)
        parts = place_at(spread(padded, "heads"), head, n_heads)
        return jnp.concatenate([parts[i] for i in range(n_heads)], axis=-1)

    inputs = full_rows(block_in)
    grad_full = full_rows(cotangent)

    tail = jnp.concatenate(
        [router, gain_attn[:, None], gain_moe[:, None],
         jnp.zeros((shard, rest - expert_count - 2), BF16)], axis=1
    )
    own_pack = jnp.concatenate([w_qkv.reshape(shard, 3 * width), w_out_attn, tail], axis=1)
    columns = own_pack.shape[1]
    shards = expert_shards()
    ids = jnp.pad(route_ids, ((0, 0), (0, span - seq), (0, 0)), constant_values=-1)
    ids_all = jnp.stack(blocks_of(ids.reshape(rows, 2).T))
    pack_z = place_at(
        [own_pack] + [after(shift_z(own_pack, k), shards) for k in range(1, n_z)], z, n_z
    )
    pieces = []
    for e in range(local):
        pieces.append(ring(after(shards[e], pieces[-1][1]) if e else shards[e]))
    last = local - 1
    pack = place_at(spread(after(pack_z, ids_all), "expert"), exp, n_exp)

    pack = after(pack, pieces[0][1], inputs, grad_full)
    other_pack = swap_core(pack)
    pack = jnp.stack([jnp.where(low, pack, other_pack), jnp.where(low, other_pack, pack)])
    pack = pack.transpose(2, 0, 1, 3, 4).reshape(model, columns)
    side = pack[:, 4 * width :].T
    router_rows = side[:expert_count]
    gain_one = side[expert_count : expert_count + 1].astype(F32)
    gain_two = side[expert_count + 1 : expert_count + 2].astype(F32)

    first_expert = exp * group + core * local
    place = [jnp.stack([z, first_expert + e]).astype(jnp.int32) for e in range(local)]
    slot_of, slot_cols = find_slots(place[0], ids_all, local, slots)

    grads_all = blocks_of(grad_full)
    inputs_ready = inputs
    part, qkv, ctx = attend(inputs_ready, expert_count, pack, width, images, seq)
    part = after(part, pieces[0][-1])
    part_other = shift(part, "heads", 1)
    for k in range(2, n_heads):
        part_other = part_other + shift(part, "heads", k)
    part_other = after(part_other, pieces[0][ways_up], slot_cols)
    middle = inputs.astype(F32) + (part.astype(F32) + part_other.astype(F32))
    unit_two, scale_two = norm_parts(middle)
    normed_two = (unit_two * gain_two).astype(BF16)
    tokens_all = blocks_of(normed_two, (pieces[last][1],))

    done = []

    def begin_rings(e, *hold):
        rows_e, mids_e = done[e][:2]
        rings.append(weight_grad(place[e], after(rows_e, *hold), mids_e, n_z))

    def ring_first(e):
        return shift_z(rings[e][-ways_up % n_z], 1)

    def ring_down(e, *hold):
        chunks = rings[e]
        downward = after(chunks[ways_down], *hold)
        for k in range(ways_down - 1, 0, -1):
            downward = (shift_z(downward, -1).astype(F32) + chunks[k].astype(F32)).astype(BF16)
        return shift_z(downward, -1)

    def ring_middle(e, upward, *hold):
        chunks = rings[e]
        for k in range(ways_up - 1, 0, -1):
            own = after(chunks[n_z - k], *hold)
            upward = (upward.astype(F32) + own.astype(F32)).astype(BF16)
            if k > 1:
                upward = shift_z(upward, 1)
        return upward

    def ring_end(e, upward, downward, *hold):
        own = after(rings[e][0], *hold).astype(F32)
        return own + shift_z(upward, 1).astype(F32) + downward.astype(F32)

    rings = []
    for e in range(local):
        here = list(pieces[e])
        if e:
            here[0] = after(here[0], rings[-1][0])
        done.append(
            run_expert(
                e, place[e], slot_of, router_rows, tokens_all, grads_all, here, slots
            )
        )
        if e < local - 1:
            begin_rings(e)
    drows, yrows, dchosen = ([r[i] for r in done] for i in (3, 4, 2))
    probs = done[0][5]

    arrived_zero, down_zero = ring_first(0), ring_down(0)
    drows[0] = after(drows[0], arrived_zero)

    def back_of(b, add=None):
        *parts, more = combine_back(
            place[0], slot_cols, drows, dchosen, probs, router_rows, tokens_all[b], b, add
        )
        return parts, more

    drouter = jnp.zeros((expert_count, model), F32)
    arrived = [None] * n_exp
    for k in reversed(range(n_exp)):
        sent, more = back_of(n_exp + k)
        arrived[k] = [swap_core(part) for part in sent]
        drouter = drouter + more
    from_exp = []
    for k in reversed(range(n_exp)):
        arrived[k][0] = after(arrived[k][0], total[0] if k < n_exp - 1 else down_zero)
        total, more = back_of(k, arrived[k])
        drouter = drouter + more
        if k:
            from_exp.append([shift(part, "expert", -k) for part in total])
        if k == 1:
            early = ring_middle(0, arrived_zero, total[0])
    ends = [ring_end(0, early, down_zero)]
    dsum, dsum_other = [], []
    for p in range(PARTS):
        if p == 1:
            begin_rings(last, dsum[0])
        value = (after(total[p], rings[last][0]) if p else total[p]).astype(F32)
        for came in from_exp:
            value = value + came[p].astype(F32)
        dsum.append(value.astype(BF16))
        other = shift(dsum[p], "heads", 1)
        for k in range(2, n_heads):
            other = other + shift(dsum[p], "heads", k)
        dsum_other.append(other)
    arrived_last, down_last = ring_first(last), ring_down(last)
    dsum_other[0] = after(dsum_other[0], ends[0])

    yrows[0] = after(yrows[0], dsum[0])
    y_came = [swap_core(combine(slot_cols, yrows, n_exp + k)) for k in range(n_exp)]
    y_from = [
        shift(combine(slot_cols, yrows, k, after(y_came[k], dsum[-1])), "expert", -k)
        for k in range(1, n_exp)
    ]
    dnormed_two = jnp.concatenate(
        [own.astype(F32) + other.astype(F32) for own, other in zip(dsum, dsum_other)], axis=1
    )
    scaled = dnormed_two * gain_two
    grad_gain_two = jnp.sum(dnormed_two * unit_two, axis=0)
    dmiddle = grad_full.astype(F32) + scale_two * (
        scaled
        - jnp.mean(scaled, axis=-1, keepdims=True)
        - unit_two * jnp.mean(scaled * unit_two, axis=-1, keepdims=True)
    )
    late = ring_middle(last, arrived_last, dsum_other[-1])
    datt = after(dmiddle.astype(BF16), *y_came)

    dside = jnp.concatenate(
        [drouter, jnp.zeros((1, model), F32), grad_gain_two[None, :],
         jnp.zeros((rest - expert_count - 2, model), F32)], axis=0
    ).T
    dnorm, stats, dkeep, dsend = attend_back(
        inputs, gain_one, datt, qkv, ctx, pack, dside, expert_count, width, images, seq, n_heads,
        core.astype(jnp.int32)[None], n_z,
    )
    dsend = after(dsend, *y_from, down_last)

    dcame = swap_core(dsend)
    dpack = (dkeep.astype(F32) + dcame.astype(F32)).astype(BF16)
    dpack = dpack.reshape(n_z, n_exp, shard, columns)
    y_own = combine(slot_cols, yrows, 0, after(y_came[0], dcame)).astype(F32)
    for value in y_from:
        y_own = y_own + value.astype(F32)
    y_own = y_own.astype(BF16)

    dtotal = take(dpack, exp, 1).astype(F32)
    for k in range(1, n_exp):
        came = shift(take(dpack, (exp + k) % n_exp, 1), "expert", k)
        dtotal = dtotal + came.astype(F32)
    dpack = dtotal.astype(BF16)

    came = [shift_z(take(dpack, (z + k) % n_z), k) for k in range(1, n_z)]
    dtotal = take(dpack, z).astype(F32)
    for value in came:
        dtotal = dtotal + value.astype(F32)

    ends.append(ring_end(last, late, down_last, came[0]))
    stacked = jnp.stack(ends).reshape(local, 2, CORES, part_rows, hidden_width)
    other = swap_core(take(stacked, 1 - core, 2).astype(BF16)).astype(F32)
    own = take(stacked, core, 2)
    joined = jnp.concatenate([jnp.where(low, own, other), jnp.where(low, other, own)], axis=0)
    grads = joined.transpose(1, 2, 0, 3)
    dside = dtotal[:, 4 * width :]
    over_heads = dside[:, : expert_count + 1].T
    summed = over_heads
    for k in range(1, n_heads):
        summed = summed + shift(over_heads, "heads", k)

    def own_half(value):
        return lax.dynamic_slice_in_dim(value, head * half_width, half_width, 1)

    def cut(value):
        return value.astype(BF16).reshape(images, span, half_width)[:, :seq]

    dnorm, stats = lax.optimization_barrier((dnorm, stats, dcame))[:2]
    dn_own = take(dnorm, head).astype(F32)
    sums = stats[:, :2].T
    sums_total = sums
    for k in range(1, n_heads):
        came = shift(take(dnorm, (head + k) % n_heads), "heads", k)
        dn_own = dn_own + after(came, dpack).astype(F32)
        sums_total = sums_total + after(shift(sums, "heads", k), dpack)
    unit_one, scale_one = norm_parts(inputs.astype(F32))
    grad_in = own_half(dmiddle) + scale_one * (
        dn_own * own_half(gain_one)
        - sums_total[0][:, None] / model
        - own_half(unit_one) * (sums_total[1][:, None] / model)
    )

    y_total = own_half(y_own).astype(F32)
    for k in range(1, n_heads):
        there = (head + k) % n_heads
        part_y = lax.dynamic_slice_in_dim(y_own, there * half_width, half_width, 1)
        y_total = y_total + after(shift(part_y, "heads", k), dpack).astype(F32)
    block_out = own_half(middle) + y_total

    return (
        cut(block_out),
        cut(grad_in),
        summed[expert_count],
        dtotal[:, : 3 * width].reshape(shard, 3, width),
        dtotal[:, 3 * width : 4 * width],
        dside[:, expert_count + 1],
        summed[:expert_count].T,
        grads[1],
        grads[0],
    )


def solution(mesh):
    return jax.shard_map(
        per_device,
        mesh=mesh,
        in_specs=(
            P(("dp", "expert"), None, "heads"),
            P(("dp", "expert"), None, "heads"),
            P(("dp", "expert"), None, None),
            P(("dp", "expert")),
            P(("dp", "expert"), None, "heads"),
            P(("dp", "expert"), "heads"),
            P(("dp", "expert")),
            P(("dp", "expert"), None),
            P("dp", "expert", "heads"),
            P("dp", "expert", "heads"),
        ),
        out_specs=(
            P(("dp", "expert"), None, "heads"),
            P(("dp", "expert"), None, "heads"),
            P(("dp", "expert")),
            P(("dp", "expert"), None, "heads"),
            P(("dp", "expert"), "heads"),
            P(("dp", "expert")),
            P(("dp", "expert"), None),
            P("dp", "expert", "heads"),
            P("dp", "expert", "heads"),
        ),
        check_vma=False,
    )
```

```python
import functools

import jax
import jax.numpy as jnp
from jax import lax
from jax.experimental import pallas as pl
from jax.experimental.pallas import tpu as pltpu
from jax.sharding import PartitionSpec as P

HEAD_DIM = 64
CORES = 2
EPS = 1e-06
LOW = -1e30
F32 = jnp.float32
BF16 = jnp.bfloat16
VMEM_LIMIT = 56 * 1024 * 1024
SHARE = 64
PARTS = 2


def dot(a, b, ca, cb):
    return lax.dot_general(a, b, (((ca,), (cb,)), ((), ())), preferred_element_type=F32)


def shaped(shape, kind):
    return jax.ShapeDtypeStruct(shape, kind)


def params(dims=1):
    return pltpu.CompilerParams(
        dimension_semantics=("arbitrary",) * dims, vmem_limit_bytes=VMEM_LIMIT
    )


def cost(flops, size, powers=0):
    return pl.CostEstimate(
        flops=flops // SHARE, bytes_accessed=size // SHARE, transcendentals=powers // SHARE
    )


def after(value, *others):
    return lax.optimization_barrier((value,) + others)[0]


def norm_parts(rows):
    average = jnp.mean(rows, axis=-1, keepdims=True)
    centred = rows - average
    spread = jnp.mean(centred * centred, axis=-1, keepdims=True)
    scale = lax.rsqrt(spread + EPS)
    return centred * scale, scale


def softmax_rows(q, own_k, real):
    scores = jnp.where(real, dot(q, own_k, 1, 1) * (HEAD_DIM**-0.5), LOW)
    powers = jnp.exp(scores - jnp.max(scores, axis=-1, keepdims=True))
    return powers / jnp.sum(powers, axis=-1, keepdims=True)


def attend_kernel(
    seq, gain_at, x_ref, side_ref, wqkv_ref, wo_ref, part_ref, qkv_ref, ctx_ref, gain_ref
):
    width = wo_ref.shape[1]
    span = x_ref.shape[0]

    @pl.when(pl.program_id(0) == 0)
    def _():
        gain_ref[...] = side_ref[...].astype(F32).T[gain_at : gain_at + 1, :]

    unit, _ = norm_parts(x_ref[...].astype(F32))
    normed = (unit * gain_ref[...]).astype(BF16)
    for part in range(3):
        cols = slice(part * width, (part + 1) * width)
        qkv_ref[:, cols] = dot(normed, wqkv_ref[:, cols], 1, 0).astype(BF16)
    lane = lax.broadcasted_iota(jnp.int32, (span, 128), 1)
    real = lax.broadcasted_iota(jnp.int32, (span, span), 1) < seq
    for pair in range(width // 128):
        q, k, v = (
            qkv_ref[:, part * width + pair * 128 : part * width + (pair + 1) * 128]
            for part in range(3)
        )
        ctx = jnp.zeros((span, 128), F32)
        for side in range(2):
            mine = (lane >= 64) if side else (lane < 64)
            own_k = jnp.where(mine, k, jnp.zeros_like(k))
            own_v = jnp.where(mine, v, jnp.zeros_like(v))
            weights = softmax_rows(q, own_k, real)
            ctx = ctx + dot(weights.astype(BF16), own_v, 1, 0)
        ctx_ref[:, pair * 128 : (pair + 1) * 128] = ctx.astype(BF16)
    part_ref[...] = dot(ctx_ref[...], wo_ref[...], 1, 1).astype(BF16)


def attend(inputs, gain_at, packed, width, images, seq):
    rows, model = inputs.shape
    span = rows // images
    image = lambda last: pl.BlockSpec((span, last), lambda i: (i, 0))
    return pl.pallas_call(
        functools.partial(attend_kernel, seq, gain_at),
        grid=(images,),
        in_specs=[
            image(model),
            pl.BlockSpec((model, 128), lambda i: (0, 4 * width // 128)),
            pl.BlockSpec((model, 3 * width), lambda i: (0, 0)),
            pl.BlockSpec((model, width), lambda i: (0, 3)),
        ],
        out_specs=[image(model), image(3 * width), image(width)],
        scratch_shapes=[pltpu.VMEM((1, model), F32)],
        out_shape=[
            shaped((rows, model), BF16), shaped((rows, 3 * width), BF16), shaped((rows, width), BF16)
        ],
        compiler_params=params(),
        cost_estimate=cost(10 * rows * model * width, 8 * rows * model, rows * span * width // 64),
        name="attend",
    )(inputs, packed, packed, packed)


def attend_back_kernel(
    seq, gain_at, depth,
    core_ref, x_ref, gain_ref, datt_ref, qkv_ref, ctx_ref, wqkv_ref, wo_ref, side_ref,
    dnorm_ref, stats_ref, keep_ref, send_ref, dproj_ref, dgain_ref, dwqkv_ref, dwo_ref, dside_ref,
):
    width = wo_ref.shape[1]
    span, model = x_ref.shape
    step = pl.program_id(0)

    @pl.when(step == 0)
    def _():
        dgain_ref[...] = jnp.zeros_like(dgain_ref)
        dwqkv_ref[...] = jnp.zeros_like(dwqkv_ref)
        dwo_ref[...] = jnp.zeros_like(dwo_ref)

    datt = datt_ref[...]
    dwo_ref[...] += dot(datt, ctx_ref[...], 0, 0)
    dctx_all = dot(datt, wo_ref[...], 1, 0).astype(BF16)
    lane = lax.broadcasted_iota(jnp.int32, (span, 128), 1)
    real = lax.broadcasted_iota(jnp.int32, (span, span), 1) < seq
    for pair in range(width // 128):
        q, k, v = (
            qkv_ref[:, part * width + pair * 128 : part * width + (pair + 1) * 128]
            for part in range(3)
        )
        dctx = dctx_all[:, pair * 128 : (pair + 1) * 128]
        dq = jnp.zeros((span, 128), F32)
        dk = jnp.zeros((span, 128), F32)
        dv = jnp.zeros((span, 128), F32)
        for side in range(2):
            mine = (lane >= 64) if side else (lane < 64)
            own = lambda t: jnp.where(mine, t, jnp.zeros_like(t))
            own_k, own_v = own(k), own(v)
            weights = softmax_rows(q, own_k, real)
            dweights = dot(dctx, own_v, 1, 1)
            inner = jnp.sum(dweights * weights, axis=-1, keepdims=True)
            dscores = (weights * (dweights - inner)).astype(BF16)
            dq = dq + dot(dscores, own_k, 1, 0)
            dk = dk + dot(dscores, own(q), 0, 0)
            dv = dv + dot(weights.astype(BF16), own(dctx), 0, 0)
        for part, value in enumerate((dq * HEAD_DIM**-0.5, dk * HEAD_DIM**-0.5, dv)):
            start = part * width + pair * 128
            dproj_ref[:, start : start + 128] = value.astype(BF16)
    dproj = dproj_ref[...]
    gain = gain_ref[...]
    unit, _ = norm_parts(x_ref[...].astype(F32))
    normed = (unit * gain).astype(BF16)
    dwqkv_ref[...] += dot(normed, dproj, 0, 0)
    dnormed = dot(dproj, wqkv_ref[...], 1, 1)
    halves, _, half = dnorm_ref.shape
    for h in range(halves):
        dnorm_ref[h] = dnormed[:, h * half : (h + 1) * half].astype(BF16)
    along = dnormed * unit
    dgain_ref[...] += jnp.sum(along, axis=0, keepdims=True)
    first = jnp.sum(dnormed * gain, axis=-1, keepdims=True)
    second = jnp.sum(along * gain, axis=-1, keepdims=True)
    stats_ref[...] = jnp.where(lane == 0, first, jnp.where(lane == 1, second, 0.0))

    @pl.when(step == pl.num_programs(0) - 1)
    def _():
        line = lax.broadcasted_iota(jnp.int32, (128, model), 0)
        dside_ref[...] = side_ref[...] + jnp.where(line == gain_at, dgain_ref[...], 0.0).T
        part = model // (depth * CORES)
        for out_ref, which in ((keep_ref, core_ref[0]), (send_ref, 1 - core_ref[0])):
            for z in range(depth):
                rows = pl.ds(pl.multiple_of((z * CORES + which) * part, 16), part)
                here = slice(z * part, (z + 1) * part)
                out_ref[here, : 3 * width] = dwqkv_ref[rows, :].astype(BF16)
                out_ref[here, 3 * width : 4 * width] = dwo_ref[rows, :].astype(BF16)
                out_ref[here, 4 * width :] = dside_ref[rows, :].astype(BF16)


def attend_back(inputs, gain, datt, qkv, ctx, packed, dside, gain_at, width, images, seq, halves, core, depth):
    rows, model = inputs.shape
    span = rows // images
    image = lambda last: pl.BlockSpec((span, last), lambda i, s: (i, 0))
    fixed = lambda *size: pl.BlockSpec(size, lambda i, s: (0, 0))
    return pl.pallas_call(
        functools.partial(attend_back_kernel, seq, gain_at, depth),
        grid_spec=pltpu.PrefetchScalarGridSpec(
            num_scalar_prefetch=1,
            grid=(images,),
            in_specs=[
            image(model), fixed(1, model), image(model), image(3 * width), image(width),
            fixed(model, 3 * width), pl.BlockSpec((model, width), lambda i, s: (0, 3)),
            fixed(model, 128),
        ],
        out_specs=[
            pl.BlockSpec((halves, span, model // halves), lambda i, s: (0, i, 0)),
            image(128),
            fixed(model // CORES, packed.shape[1]),
            fixed(model // CORES, packed.shape[1]),
        ],
        scratch_shapes=[
            pltpu.VMEM((span, 3 * width), BF16),
            pltpu.VMEM((1, model), F32),
            pltpu.VMEM((model, 3 * width), F32),
            pltpu.VMEM((model, width), F32),
            pltpu.VMEM((model, 128), F32),
        ],
        ),
        out_shape=[
            shaped((halves, rows, model // halves), BF16),
            shaped((rows, 128), F32),
            shaped((model // CORES, packed.shape[1]), BF16),
            shaped((model // CORES, packed.shape[1]), BF16),
        ],
        compiler_params=params(),
        cost_estimate=cost(28 * rows * model * width, 12 * rows * model, rows * span * width // 64),
        name="attend_back",
    )(core, inputs, gain, datt, qkv, ctx, packed, packed, dside)


def slot_kernel(slots, place_ref, ids_ref, rows_ref, cols_ref):
    local, tokens = rows_ref.shape[1:]
    ids = ids_ref[0]
    line = lax.broadcasted_iota(jnp.int32, (8, tokens), 0)
    chosen = jnp.zeros((8, tokens), F32)
    for e in range(local):
        named = jnp.max(jnp.where(ids == place_ref[1] + e, 1.0, 0.0), axis=0, keepdims=True)
        chosen = jnp.where(line == e, named, chosen)
    first = lax.broadcasted_iota(jnp.int32, (tokens, tokens), 0)
    second = lax.broadcasted_iota(jnp.int32, (tokens, tokens), 1)
    before = jnp.where(first < second, 1.0, 0.0).astype(BF16)
    same = jnp.where(first == second, 1.0, 0.0).astype(BF16)
    marks = chosen.astype(BF16)
    rank = dot(marks, before, 1, 0)
    rows_ref[0] = jnp.where(chosen > 0.5, rank, -1.0)[:local].astype(jnp.int32)
    column = lax.broadcasted_iota(jnp.int32, (tokens, 8), 1).astype(F32) * slots
    found = jnp.where(dot(same, marks, 1, 1) > 0.5, dot(before, marks, 0, 1) + column, -1.0)
    cols_ref[0] = found[:, :local].astype(jnp.int32)


def find_slots(place, ids, local, slots):
    blocks, _, tokens = ids.shape
    block = lambda *size: pl.BlockSpec((1,) + size, lambda b, s: (b, 0, 0))
    return pl.pallas_call(
        functools.partial(slot_kernel, slots),
        grid_spec=pltpu.PrefetchScalarGridSpec(
            num_scalar_prefetch=1,
            grid=(blocks,),
            in_specs=[block(2, tokens)],
            out_specs=[block(local, tokens), block(tokens, local)],
        ),
        out_shape=[
            shaped((blocks, local, tokens), jnp.int32), shaped((blocks, tokens, local), jnp.int32)
        ],
        compiler_params=params(),
        cost_estimate=cost(64 * blocks * tokens * tokens, 64 * blocks * tokens),
        name="find_slots",
    )(place, ids)


def expert_kernel(index, depth, blocks, place_ref, slot_ref, router_ref, *refs):
    x_refs, refs = refs[:blocks], refs[blocks:]
    grad_refs, refs = refs[:blocks], refs[blocks:]
    win_refs, refs = refs[:depth], refs[depth:]
    wout_refs, refs = refs[:depth], refs[depth:]
    (
        rows_ref, mids_ref, dchosen_ref, drows_ref, yrows_ref, probs_ref, win_all, wout_all,
    ) = refs
    slots, model = rows_ref.shape[2:]
    tokens = x_refs[0].shape[0]
    part_rows, width = win_refs[0].shape[1:]
    step = pl.program_id(0)

    @pl.when(step == 0)
    def _():
        for k in range(depth):
            owner = lax.rem(place_ref[0] - k + depth, depth)
            at = pl.ds(pl.multiple_of(owner * part_rows, 16), part_rows)
            win_all[at, :] = win_refs[k][0]
            wout_all[at, :] = wout_refs[k][0]

    mask = lax.broadcasted_iota(jnp.int32, (slots, tokens), 0) == slot_ref[0, index : index + 1, :]
    pick = jnp.where(mask, 1.0, 0.0).astype(BF16)
    for b in range(blocks):

        @pl.when(step == b)
        def _(b=b):
            rows_ref[0, 0] = dot(pick, grad_refs[b][...], 1, 0).astype(BF16)
            rows_ref[1, 0] = dot(pick, x_refs[b][...], 1, 0).astype(BF16)
            logits = dot(router_ref[...], x_refs[b][...], 1, 1)
            powers = jnp.exp(logits - jnp.max(logits, axis=0, keepdims=True))
            probs_ref[0] = powers / jnp.sum(powers, axis=0, keepdims=True)

    probs = probs_ref[0]
    line = lax.broadcasted_iota(jnp.int32, probs.shape, 0)
    own = jnp.sum(jnp.where(line == place_ref[1], probs, 0.0), axis=0, keepdims=True)
    gate = jnp.sum(jnp.where(mask, own, 0.0), axis=1, keepdims=True)
    grows, rows = rows_ref[0, 0], rows_ref[1, 0]
    dgate = jnp.zeros((slots, 1), F32)
    drows = jnp.zeros((slots, model), F32)
    yrows = jnp.zeros((slots, model), F32)
    tile = 512 if width % 512 == 0 else width
    curve = 0.7978845608028654

    def products(start):
        cols = slice(start, start + tile)
        return dot(rows, win_all[:, cols], 1, 0), dot(grows, wout_all[:, cols], 1, 0)

    ahead = products(0)
    for start in range(0, width, tile):
        cols = slice(start, start + tile)
        hidden, pulled = ahead
        if start + tile < width:
            ahead = products(start + tile)
        square = hidden * hidden
        bend = jnp.tanh(hidden * (curve + curve * 0.044715 * square))
        half = 0.5 + 0.5 * bend
        active = hidden * half
        slope = half + 0.5 * hidden * (1.0 - bend * bend) * (
            curve + 3.0 * curve * 0.044715 * square
        )
        dgate = dgate + jnp.sum(active * pulled, axis=1, keepdims=True)
        gact = (gate * active).astype(BF16)
        dhid = (gate * pulled * slope).astype(BF16)
        mids_ref[0, 0, :, cols] = gact
        mids_ref[1, 0, :, cols] = dhid
        drows = drows + dot(dhid, win_all[:, cols], 1, 1)
        yrows = yrows + dot(gact, wout_all[:, cols], 1, 1)
    dchosen_ref[0] = jnp.sum(jnp.where(mask, dgate, 0.0), axis=0, keepdims=True)
    drows_ref[0] = drows.astype(BF16)
    yrows_ref[0] = yrows.astype(BF16)


def run_expert(index, place, slot_of, router_rows, xs, grads, pieces, slots):
    blocks, depth = len(xs), len(pieces)
    tokens, model = xs[0].shape
    _, part_rows, width = pieces[0].shape
    experts = router_rows.shape[0]
    fixed = lambda *size: pl.BlockSpec(
        size, lambda b, s: (0,) * len(size), pipeline_mode=pl.Buffered(1)
    )
    block = lambda *size: pl.BlockSpec((1,) + size, lambda b, s: (b, 0, 0))
    both = lambda last: pl.BlockSpec((2, 1, slots, last), lambda b, s: (0, b, 0, 0))
    weight = lambda which: pl.BlockSpec(
        (1, part_rows, width), lambda b, s: (which, 0, 0), pipeline_mode=pl.Buffered(1)
    )
    return pl.pallas_call(
        functools.partial(expert_kernel, index, depth, blocks),
        grid_spec=pltpu.PrefetchScalarGridSpec(
            num_scalar_prefetch=1,
            grid=(blocks,),
            in_specs=[block(slot_of.shape[1], tokens), fixed(experts, model)]
            + [fixed(tokens, model)] * (2 * blocks)
            + [weight(1)] * depth
            + [weight(0)] * depth,
            out_specs=[
                both(model), both(width), block(1, tokens), block(slots, model),
                block(slots, model), block(experts, tokens),
            ],
            scratch_shapes=[pltpu.VMEM((model, width), BF16)] * 2,
        ),
        out_shape=[
            shaped((2, blocks, slots, model), BF16), shaped((2, blocks, slots, width), BF16),
            shaped((blocks, 1, tokens), F32), shaped((blocks, slots, model), BF16),
            shaped((blocks, slots, model), BF16), shaped((blocks, experts, tokens), F32),
        ],
        compiler_params=params(),
        cost_estimate=cost(
            8 * blocks * slots * model * width + 4 * blocks * slots * model * tokens,
            16 * blocks * slots * model,
            blocks * slots * width,
        ),
        name="expert",
    )(place, slot_of, router_rows, *xs, *grads, *pieces, *pieces)


def weight_grad_kernel(depth, place_ref, rows_ref, cols_ref, *refs):
    out_refs, total_ref = refs[:depth], refs[depth]
    _, blocks, slots, model = rows_ref.shape
    width = cols_ref.shape[3]
    part_rows = model // depth
    left = rows_ref[0].reshape(blocks * slots, model)
    right = cols_ref[0].reshape(blocks * slots, width)
    total_ref[...] = dot(left, right, 0, 0)
    for k in range(depth):
        owner = lax.rem(place_ref[0] - k + depth, depth)
        at = pl.ds(pl.multiple_of(owner * part_rows, 16), part_rows)
        out_refs[k][0] = total_ref[at, :].astype(BF16)


def weight_grad(place, rows, cols, depth):
    _, blocks, slots, model = rows.shape
    width = cols.shape[3]
    both = lambda last: pl.BlockSpec((1, blocks, slots, last), lambda i, s: (i, 0, 0, 0))
    return pl.pallas_call(
        functools.partial(weight_grad_kernel, depth),
        grid_spec=pltpu.PrefetchScalarGridSpec(
            num_scalar_prefetch=1,
            grid=(2,),
            in_specs=[both(model), both(width)],
            out_specs=[pl.BlockSpec((1, model // depth, width), lambda i, s: (i, 0, 0))] * depth,
            scratch_shapes=[pltpu.VMEM((model, width), F32)],
        ),
        out_shape=[shaped((2, model // depth, width), BF16)] * depth,
        compiler_params=params(),
        cost_estimate=cost(
            4 * blocks * slots * model * width,
            4 * (blocks * slots * (model + width) + model * width),
        ),
        name="weight_grad",
    )(place, rows, cols)


def gathered(local, slot_ref, rows_refs, all_ref):
    slots, tokens = rows_refs[0].shape[1], slot_ref.shape[1]
    at = lax.broadcasted_iota(jnp.int32, (tokens, local * slots), 1)
    mask = at == slot_ref[0, :, 0:1]
    all_ref[0:slots, :] = rows_refs[0][0]
    for e in range(1, local):
        mask = mask | (at == slot_ref[0, :, e : e + 1])
        all_ref[e * slots : (e + 1) * slots, :] = rows_refs[e][0]
    return dot(jnp.where(mask, 1.0, 0.0).astype(BF16), all_ref[...], 1, 0)


def combine_kernel(local, added, slot_ref, *refs):
    rows_refs, refs = refs[:local], refs[local:]
    out_ref, all_ref = refs[-2:]
    total = gathered(local, slot_ref, rows_refs, all_ref)
    if added:
        total = total + refs[0][...].astype(F32)
    out_ref[...] = total.astype(BF16)


def combine(slot_cols, rows, b, add=None):
    _, tokens, local = slot_cols.shape
    slots, model = rows[0].shape[1:]
    whole = pl.BlockSpec((tokens, model), lambda i: (0, 0))
    return pl.pallas_call(
        functools.partial(combine_kernel, local, add is not None),
        grid=(1,),
        in_specs=[pl.BlockSpec((1, tokens, local), lambda i: (b, 0, 0))]
        + [pl.BlockSpec((1, slots, model), lambda i: (b, 0, 0))] * local
        + [whole] * (add is not None),
        out_specs=whole,
        out_shape=shaped((tokens, model), BF16),
        scratch_shapes=[pltpu.VMEM((local * slots, model), BF16)],
        compiler_params=params(),
        cost_estimate=cost(
            2 * local * slots * model * tokens, 2 * model * (local * slots + 2 * tokens)
        ),
        name="combine",
    )(slot_cols, *rows, *(() if add is None else (add,)))


def combine_back_kernel(local, added, place_ref, slot_ref, *refs):
    rows_refs, refs = refs[:local], refs[local:]
    dchosen_refs, refs = refs[:local], refs[local:]
    probs_ref, router_ref, x_ref = refs[:3]
    out_refs, (drouter_ref, all_ref) = refs[-2 - PARTS : -2], refs[-2:]
    probs = probs_ref[0]
    line = lax.broadcasted_iota(jnp.int32, probs.shape, 0)
    dprobs = jnp.zeros_like(probs)
    for e in range(local):
        dprobs = jnp.where(line == place_ref[1] + e, dchosen_refs[e][0], dprobs)
    inner = jnp.sum(dprobs * probs, axis=0, keepdims=True)
    dlogits = (probs * (dprobs - inner)).astype(BF16)
    drouter_ref[...] = dot(dlogits, x_ref[...], 1, 0)
    total = gathered(local, slot_ref, rows_refs, all_ref) + dot(dlogits, router_ref[...], 0, 0)
    part = out_refs[0].shape[1]
    for p in range(PARTS):
        piece = total[:, p * part : (p + 1) * part]
        if added:
            piece = piece + refs[3 + p][...].astype(F32)
        out_refs[p][...] = piece.astype(BF16)


def combine_back(place, slot_cols, rows, dchosen, probs, router_rows, x, b, add=None):
    _, tokens, local = slot_cols.shape
    slots, model = rows[0].shape[1:]
    experts = router_rows.shape[0]
    whole = pl.BlockSpec((tokens, model), lambda i, s: (0, 0))
    part = pl.BlockSpec((tokens, model // PARTS), lambda i, s: (0, 0))
    block = lambda *size: pl.BlockSpec((1,) + size, lambda i, s: (b, 0, 0))
    small = pl.BlockSpec((experts, model), lambda i, s: (0, 0))
    return pl.pallas_call(
        functools.partial(combine_back_kernel, local, add is not None),
        grid_spec=pltpu.PrefetchScalarGridSpec(
            num_scalar_prefetch=1,
            grid=(1,),
            in_specs=[block(tokens, local)]
            + [block(slots, model)] * local
            + [block(1, tokens)] * local
            + [block(experts, tokens), small, whole]
            + [part] * (PARTS * (add is not None)),
            out_specs=[part] * PARTS + [small],
            scratch_shapes=[pltpu.VMEM((local * slots, model), BF16)],
        ),
        out_shape=[shaped((tokens, model // PARTS), BF16)] * PARTS
        + [shaped((experts, model), F32)],
        compiler_params=params(),
        cost_estimate=cost(
            2 * local * slots * model * tokens, 2 * model * (local * slots + 3 * tokens)
        ),
        name="combine_back",
    )(place, slot_cols, *rows, *dchosen, probs, router_rows, x, *(() if add is None else add))


def per_device(
    block_in, cotangent, route_ids, gain_attn, w_qkv, w_out_attn, gain_moe, router, w_in, w_out
):
    n_dp, n_heads, n_exp = (lax.axis_size(name) for name in ("dp", "heads", "expert"))
    n_z = n_dp // CORES
    dp, head, exp = (lax.axis_index(name) for name in ("dp", "heads", "expert"))
    z, core = dp // CORES, dp % CORES
    low = core == 0
    images, seq, half_width = block_in.shape
    span = -(-seq // 16) * 16
    rows = images * span
    model = half_width * n_heads
    width = w_qkv.shape[2]
    shard = w_qkv.shape[0]
    expert_count = router.shape[1]
    group = w_in.shape[1]
    local = group // CORES
    part_rows, _, hidden_width = w_in.shape
    capacity = 20 * images * seq // (7 * expert_count)
    slots = -(-capacity // 16) * 16
    blocks = n_exp * CORES
    rest = 128

    def shift(value, axis, step):
        size = lax.axis_size(axis)
        return lax.ppermute(value, axis, [(i, (i + step) % size) for i in range(size)])

    def shift_z(value, step):
        pairs = [
            (a * CORES + c, ((a + step) % n_z) * CORES + c) for a in range(n_z) for c in range(CORES)
        ]
        return lax.ppermute(value, "dp", pairs)

    def swap_core(value):
        return lax.ppermute(value, "dp", [(i, i ^ 1) for i in range(n_dp)])

    def place_at(pieces, index, count):
        if count == 2:
            first = index == 0
            return jnp.stack(
                [jnp.where(first, pieces[0], pieces[1]), jnp.where(first, pieces[1], pieces[0])]
            )
        out = jnp.zeros((count,) + pieces[0].shape, pieces[0].dtype)
        for k, piece in enumerate(pieces):
            out = lax.dynamic_update_index_in_dim(out, piece, (index - k) % count, 0)
        return out

    def spread(value, axis):
        return [value] + [shift(value, axis, k) for k in range(1, lax.axis_size(axis))]

    def take(value, index, dim=0):
        return lax.dynamic_index_in_dim(value, index, dim, keepdims=False)

    def expert_shards():
        both = jnp.stack([w_out, w_in]).reshape(2, part_rows, CORES, local, hidden_width)
        by_core = both.transpose(2, 3, 0, 1, 4)
        other = swap_core(take(by_core, 1 - core))
        mine = take(by_core, core)
        return jnp.concatenate(
            [jnp.where(low, mine, other), jnp.where(low, other, mine)], axis=2
        )

    ways_up = n_z // 2
    ways_down = n_z - 1 - ways_up

    def ring(piece):
        pieces = [piece] + [None] * (n_z - 1)
        for k in range(1, ways_up + 1):
            pieces[k] = shift_z(pieces[k - 1], 1)
        for k in range(1, ways_down + 1):
            pieces[n_z - k] = shift_z(pieces[(n_z - k + 1) % n_z], -1)
        return pieces

    def blocks_of(value, hold=()):
        along = spread(value, "expert")
        if hold:
            along[0] = after(along[0], *hold)
        return along + [swap_core(part) for part in along]

    def full_rows(value):
        padded = jnp.pad(value, ((0, 0), (0, span - seq), (0, 0))).reshape(rows, half_width)
        parts = place_at(spread(padded, "heads"), head, n_heads)
        return jnp.concatenate([parts[i] for i in range(n_heads)], axis=-1)

    inputs = full_rows(block_in)
    grad_full = full_rows(cotangent)

    tail = jnp.concatenate(
        [router, gain_attn[:, None], gain_moe[:, None],
         jnp.zeros((shard, rest - expert_count - 2), BF16)], axis=1
    )
    own_pack = jnp.concatenate([w_qkv.reshape(shard, 3 * width), w_out_attn, tail], axis=1)
    columns = own_pack.shape[1]
    shards = expert_shards()
    ids = jnp.pad(route_ids, ((0, 0), (0, span - seq), (0, 0)), constant_values=-1)
    ids_all = jnp.stack(blocks_of(ids.reshape(rows, 2).T))
    pack_z = place_at(
        [own_pack] + [after(shift_z(own_pack, k), shards) for k in range(1, n_z)], z, n_z
    )
    pieces = []
    for e in range(local):
        pieces.append(ring(after(shards[e], pieces[-1][1]) if e else shards[e]))
    last = local - 1
    pack = place_at(spread(after(pack_z, ids_all), "expert"), exp, n_exp)

    pack = after(pack, pieces[0][1], inputs, grad_full)
    other_pack = swap_core(pack)
    pack = jnp.stack([jnp.where(low, pack, other_pack), jnp.where(low, other_pack, pack)])
    pack = pack.transpose(2, 0, 1, 3, 4).reshape(model, columns)
    side = pack[:, 4 * width :].T
    router_rows = side[:expert_count]
    gain_one = side[expert_count : expert_count + 1].astype(F32)
    gain_two = side[expert_count + 1 : expert_count + 2].astype(F32)

    first_expert = exp * group + core * local
    place = [jnp.stack([z, first_expert + e]).astype(jnp.int32) for e in range(local)]
    slot_of, slot_cols = find_slots(place[0], ids_all, local, slots)

    grads_all = blocks_of(grad_full)
    inputs_ready = inputs
    part, qkv, ctx = attend(inputs_ready, expert_count, pack, width, images, seq)
    part = after(part, pieces[0][-1])
    part_other = shift(part, "heads", 1)
    for k in range(2, n_heads):
        part_other = part_other + shift(part, "heads", k)
    part_other = after(part_other, pieces[0][ways_up], slot_cols)
    middle = inputs.astype(F32) + (part.astype(F32) + part_other.astype(F32))
    unit_two, scale_two = norm_parts(middle)
    normed_two = (unit_two * gain_two).astype(BF16)
    tokens_all = blocks_of(normed_two, (pieces[last][1],))

    done = []

    def begin_rings(e, *hold):
        rows_e, mids_e = done[e][:2]
        rings.append(weight_grad(place[e], after(rows_e, *hold), mids_e, n_z))

    def ring_first(e):
        return shift_z(rings[e][-ways_up % n_z], 1)

    def ring_down(e, *hold):
        chunks = rings[e]
        downward = after(chunks[ways_down], *hold)
        for k in range(ways_down - 1, 0, -1):
            downward = (shift_z(downward, -1).astype(F32) + chunks[k].astype(F32)).astype(BF16)
        return shift_z(downward, -1)

    def ring_middle(e, upward, *hold):
        chunks = rings[e]
        for k in range(ways_up - 1, 0, -1):
            own = after(chunks[n_z - k], *hold)
            upward = (upward.astype(F32) + own.astype(F32)).astype(BF16)
            if k > 1:
                upward = shift_z(upward, 1)
        return upward

    def ring_end(e, upward, downward, *hold):
        own = after(rings[e][0], *hold).astype(F32)
        return own + shift_z(upward, 1).astype(F32) + downward.astype(F32)

    rings = []
    for e in range(local):
        here = list(pieces[e])
        if e:
            here[0] = after(here[0], rings[-1][0])
        done.append(
            run_expert(
                e, place[e], slot_of, router_rows, tokens_all, grads_all, here, slots
            )
        )
        if e < local - 1:
            begin_rings(e)
    drows, yrows, dchosen = ([r[i] for r in done] for i in (3, 4, 2))
    probs = done[0][5]

    arrived_zero, down_zero = ring_first(0), ring_down(0)
    drows[0] = after(drows[0], arrived_zero)

    def back_of(b, add=None):
        *parts, more = combine_back(
            place[0], slot_cols, drows, dchosen, probs, router_rows, tokens_all[b], b, add
        )
        return parts, more

    drouter = jnp.zeros((expert_count, model), F32)
    arrived = [None] * n_exp
    for k in reversed(range(n_exp)):
        sent, more = back_of(n_exp + k)
        arrived[k] = [swap_core(part) for part in sent]
        drouter = drouter + more
    from_exp = []
    for k in reversed(range(n_exp)):
        arrived[k][0] = after(arrived[k][0], total[0] if k < n_exp - 1 else down_zero)
        total, more = back_of(k, arrived[k])
        drouter = drouter + more
        if k:
            from_exp.append([shift(part, "expert", -k) for part in total])
        if k == 1:
            early = ring_middle(0, arrived_zero, total[0])
    ends = [ring_end(0, early, down_zero)]
    dsum, dsum_other = [], []
    for p in range(PARTS):
        if p == 1:
            begin_rings(last, dsum[0])
        value = (after(total[p], rings[last][0]) if p else total[p]).astype(F32)
        for came in from_exp:
            value = value + came[p].astype(F32)
        dsum.append(value.astype(BF16))
        other = shift(dsum[p], "heads", 1)
        for k in range(2, n_heads):
            other = other + shift(dsum[p], "heads", k)
        dsum_other.append(other)
    arrived_last, down_last = ring_first(last), ring_down(last)
    dsum_other[0] = after(dsum_other[0], ends[0])

    yrows[0] = after(yrows[0], dsum_other[0])
    y_came = [swap_core(combine(slot_cols, yrows, n_exp + k)) for k in range(n_exp)]
    y_from = [
        shift(combine(slot_cols, yrows, k, after(y_came[k], dsum[-1])), "expert", -k)
        for k in range(1, n_exp)
    ]
    dnormed_two = jnp.concatenate(
        [own.astype(F32) + other.astype(F32) for own, other in zip(dsum, dsum_other)], axis=1
    )
    scaled = dnormed_two * gain_two
    grad_gain_two = jnp.sum(dnormed_two * unit_two, axis=0)
    dmiddle = grad_full.astype(F32) + scale_two * (
        scaled
        - jnp.mean(scaled, axis=-1, keepdims=True)
        - unit_two * jnp.mean(scaled * unit_two, axis=-1, keepdims=True)
    )
    late = ring_middle(last, arrived_last, dsum_other[-1])
    datt = after(dmiddle.astype(BF16), *y_came)

    dside = jnp.concatenate(
        [drouter, jnp.zeros((1, model), F32), grad_gain_two[None, :],
         jnp.zeros((rest - expert_count - 2, model), F32)], axis=0
    ).T
    dnorm, stats, dkeep, dsend = attend_back(
        inputs, gain_one, datt, qkv, ctx, pack, dside, expert_count, width, images, seq, n_heads,
        core.astype(jnp.int32)[None], n_z,
    )
    dsend = after(dsend, *y_from, down_last)

    dcame = swap_core(dsend)
    dpack = (dkeep.astype(F32) + dcame.astype(F32)).astype(BF16)
    dpack = dpack.reshape(n_z, n_exp, shard, columns)
    y_own = combine(slot_cols, yrows, 0, after(y_came[0], dcame)).astype(F32)
    for value in y_from:
        y_own = y_own + value.astype(F32)
    y_own = y_own.astype(BF16)

    dtotal = take(dpack, exp, 1).astype(F32)
    for k in range(1, n_exp):
        came = shift(take(dpack, (exp + k) % n_exp, 1), "expert", k)
        dtotal = dtotal + came.astype(F32)
    dpack = dtotal.astype(BF16)

    came = [shift_z(take(dpack, (z + k) % n_z), k) for k in range(1, n_z)]
    dtotal = take(dpack, z).astype(F32)
    for value in came:
        dtotal = dtotal + value.astype(F32)

    ends.append(ring_end(last, late, down_last, dpack))
    stacked = jnp.stack(ends).reshape(local, 2, CORES, part_rows, hidden_width)
    other = swap_core(take(stacked, 1 - core, 2).astype(BF16)).astype(F32)
    own = take(stacked, core, 2)
    joined = jnp.concatenate([jnp.where(low, own, other), jnp.where(low, other, own)], axis=0)
    grads = joined.transpose(1, 2, 0, 3)
    dside = dtotal[:, 4 * width :]
    over_heads = dside[:, : expert_count + 1].T
    grad_w_out, grad_w_in, over_heads = lax.optimization_barrier((grads[0], grads[1], over_heads))
    summed = over_heads
    for k in range(1, n_heads):
        summed = summed + shift(over_heads, "heads", k)

    def own_half(value):
        return lax.dynamic_slice_in_dim(value, head * half_width, half_width, 1)

    def cut(value):
        return value.astype(BF16).reshape(images, span, half_width)[:, :seq]

    dnorm, stats = lax.optimization_barrier((dnorm, stats, dcame))[:2]
    dn_own = take(dnorm, head).astype(F32)
    sums = stats[:, :2].T
    sums_total = sums
    for k in range(1, n_heads):
        there = shift(take(dnorm, (head + k) % n_heads), "heads", k)
        dn_own = dn_own + after(there, came[0]).astype(F32)
        sums_total = sums_total + after(shift(sums, "heads", k), came[0])
    unit_one, scale_one = norm_parts(inputs.astype(F32))
    grad_in = own_half(dmiddle) + scale_one * (
        dn_own * own_half(gain_one)
        - sums_total[0][:, None] / model
        - own_half(unit_one) * (sums_total[1][:, None] / model)
    )

    y_total = own_half(y_own).astype(F32)
    for k in range(1, n_heads):
        there = (head + k) % n_heads
        part_y = lax.dynamic_slice_in_dim(y_own, there * half_width, half_width, 1)
        y_total = y_total + after(shift(part_y, "heads", k), came[0]).astype(F32)
    block_out = own_half(middle) + y_total

    return (
        cut(block_out),
        cut(grad_in),
        summed[expert_count],
        dtotal[:, : 3 * width].reshape(shard, 3, width),
        dtotal[:, 3 * width : 4 * width],
        dside[:, expert_count + 1],
        summed[:expert_count].T,
        grad_w_in,
        grad_w_out,
    )


def solution(mesh):
    return jax.shard_map(
        per_device,
        mesh=mesh,
        in_specs=(
            P(("dp", "expert"), None, "heads"),
            P(("dp", "expert"), None, "heads"),
            P(("dp", "expert"), None, None),
            P(("dp", "expert")),
            P(("dp", "expert"), None, "heads"),
            P(("dp", "expert"), "heads"),
            P(("dp", "expert")),
            P(("dp", "expert"), None),
            P("dp", "expert", "heads"),
            P("dp", "expert", "heads"),
        ),
        out_specs=(
            P(("dp", "expert"), None, "heads"),
            P(("dp", "expert"), None, "heads"),
            P(("dp", "expert")),
            P(("dp", "expert"), None, "heads"),
            P(("dp", "expert"), "heads"),
            P(("dp", "expert")),
            P(("dp", "expert"), None),
            P("dp", "expert", "heads"),
            P("dp", "expert", "heads"),
        ),
        check_vma=False,
    )
```

```python
import functools

import jax
import jax.numpy as jnp
from jax import lax
from jax.experimental import pallas as pl
from jax.experimental.pallas import tpu as pltpu
from jax.sharding import PartitionSpec as P

HEAD_DIM = 64
CORES = 2
EPS = 1e-06
LOW = -1e30
F32 = jnp.float32
BF16 = jnp.bfloat16
VMEM_LIMIT = 56 * 1024 * 1024
SHARE = 64
PARTS = 2


def dot(a, b, ca, cb):
    return lax.dot_general(a, b, (((ca,), (cb,)), ((), ())), preferred_element_type=F32)


def shaped(shape, kind):
    return jax.ShapeDtypeStruct(shape, kind)


def params(dims=1):
    return pltpu.CompilerParams(
        dimension_semantics=("arbitrary",) * dims, vmem_limit_bytes=VMEM_LIMIT
    )


def cost(flops, size, powers=0):
    return pl.CostEstimate(
        flops=flops // SHARE, bytes_accessed=size // SHARE, transcendentals=powers // SHARE
    )


def after(value, *others):
    return lax.optimization_barrier((value,) + others)[0]


def norm_parts(rows):
    average = jnp.mean(rows, axis=-1, keepdims=True)
    centred = rows - average
    spread = jnp.mean(centred * centred, axis=-1, keepdims=True)
    scale = lax.rsqrt(spread + EPS)
    return centred * scale, scale


def softmax_rows(q, own_k, real):
    scores = jnp.where(real, dot(q, own_k, 1, 1) * (HEAD_DIM**-0.5), LOW)
    powers = jnp.exp(scores - jnp.max(scores, axis=-1, keepdims=True))
    return powers / jnp.sum(powers, axis=-1, keepdims=True)


def attend_kernel(
    seq, gain_at, x_ref, side_ref, wqkv_ref, wo_ref, part_ref, qkv_ref, ctx_ref, gain_ref
):
    width = wo_ref.shape[1]
    span = x_ref.shape[0]

    @pl.when(pl.program_id(0) == 0)
    def _():
        gain_ref[...] = side_ref[...].astype(F32).T[gain_at : gain_at + 1, :]

    unit, _ = norm_parts(x_ref[...].astype(F32))
    normed = (unit * gain_ref[...]).astype(BF16)
    for part in range(3):
        cols = slice(part * width, (part + 1) * width)
        qkv_ref[:, cols] = dot(normed, wqkv_ref[:, cols], 1, 0).astype(BF16)
    lane = lax.broadcasted_iota(jnp.int32, (span, 128), 1)
    real = lax.broadcasted_iota(jnp.int32, (span, span), 1) < seq
    for pair in range(width // 128):
        q, k, v = (
            qkv_ref[:, part * width + pair * 128 : part * width + (pair + 1) * 128]
            for part in range(3)
        )
        ctx = jnp.zeros((span, 128), F32)
        for side in range(2):
            mine = (lane >= 64) if side else (lane < 64)
            own_k = jnp.where(mine, k, jnp.zeros_like(k))
            own_v = jnp.where(mine, v, jnp.zeros_like(v))
            weights = softmax_rows(q, own_k, real)
            ctx = ctx + dot(weights.astype(BF16), own_v, 1, 0)
        ctx_ref[:, pair * 128 : (pair + 1) * 128] = ctx.astype(BF16)
    part_ref[...] = dot(ctx_ref[...], wo_ref[...], 1, 1).astype(BF16)


def attend(inputs, gain_at, packed, width, images, seq):
    rows, model = inputs.shape
    span = rows // images
    image = lambda last: pl.BlockSpec((span, last), lambda i: (i, 0))
    return pl.pallas_call(
        functools.partial(attend_kernel, seq, gain_at),
        grid=(images,),
        in_specs=[
            image(model),
            pl.BlockSpec((model, 128), lambda i: (0, 4 * width // 128)),
            pl.BlockSpec((model, 3 * width), lambda i: (0, 0)),
            pl.BlockSpec((model, width), lambda i: (0, 3)),
        ],
        out_specs=[image(model), image(3 * width), image(width)],
        scratch_shapes=[pltpu.VMEM((1, model), F32)],
        out_shape=[
            shaped((rows, model), BF16), shaped((rows, 3 * width), BF16), shaped((rows, width), BF16)
        ],
        compiler_params=params(),
        cost_estimate=cost(10 * rows * model * width, 8 * rows * model, rows * span * width // 64),
        name="attend",
    )(inputs, packed, packed, packed)


def attend_back_kernel(
    seq, gain_at, depth,
    core_ref, x_ref, gain_ref, datt_ref, qkv_ref, ctx_ref, wqkv_ref, wo_ref, side_ref,
    dnorm_ref, stats_ref, keep_ref, send_ref, dproj_ref, dgain_ref, dwqkv_ref, dwo_ref, dside_ref,
):
    width = wo_ref.shape[1]
    span, model = x_ref.shape
    step = pl.program_id(0)

    @pl.when(step == 0)
    def _():
        dgain_ref[...] = jnp.zeros_like(dgain_ref)
        dwqkv_ref[...] = jnp.zeros_like(dwqkv_ref)
        dwo_ref[...] = jnp.zeros_like(dwo_ref)

    datt = datt_ref[...]
    dwo_ref[...] += dot(datt, ctx_ref[...], 0, 0)
    dctx_all = dot(datt, wo_ref[...], 1, 0).astype(BF16)
    lane = lax.broadcasted_iota(jnp.int32, (span, 128), 1)
    real = lax.broadcasted_iota(jnp.int32, (span, span), 1) < seq
    for pair in range(width // 128):
        q, k, v = (
            qkv_ref[:, part * width + pair * 128 : part * width + (pair + 1) * 128]
            for part in range(3)
        )
        dctx = dctx_all[:, pair * 128 : (pair + 1) * 128]
        dq = jnp.zeros((span, 128), F32)
        dk = jnp.zeros((span, 128), F32)
        dv = jnp.zeros((span, 128), F32)
        for side in range(2):
            mine = (lane >= 64) if side else (lane < 64)
            own = lambda t: jnp.where(mine, t, jnp.zeros_like(t))
            own_k, own_v = own(k), own(v)
            weights = softmax_rows(q, own_k, real)
            dweights = dot(dctx, own_v, 1, 1)
            inner = jnp.sum(dweights * weights, axis=-1, keepdims=True)
            dscores = (weights * (dweights - inner)).astype(BF16)
            dq = dq + dot(dscores, own_k, 1, 0)
            dk = dk + dot(dscores, own(q), 0, 0)
            dv = dv + dot(weights.astype(BF16), own(dctx), 0, 0)
        for part, value in enumerate((dq * HEAD_DIM**-0.5, dk * HEAD_DIM**-0.5, dv)):
            start = part * width + pair * 128
            dproj_ref[:, start : start + 128] = value.astype(BF16)
    dproj = dproj_ref[...]
    gain = gain_ref[...]
    unit, _ = norm_parts(x_ref[...].astype(F32))
    normed = (unit * gain).astype(BF16)
    dwqkv_ref[...] += dot(normed, dproj, 0, 0)
    dnormed = dot(dproj, wqkv_ref[...], 1, 1)
    halves, _, half = dnorm_ref.shape
    for h in range(halves):
        dnorm_ref[h] = dnormed[:, h * half : (h + 1) * half].astype(BF16)
    along = dnormed * unit
    dgain_ref[...] += jnp.sum(along, axis=0, keepdims=True)
    first = jnp.sum(dnormed * gain, axis=-1, keepdims=True)
    second = jnp.sum(along * gain, axis=-1, keepdims=True)
    stats_ref[...] = jnp.where(lane == 0, first, jnp.where(lane == 1, second, 0.0))

    @pl.when(step == pl.num_programs(0) - 1)
    def _():
        line = lax.broadcasted_iota(jnp.int32, (128, model), 0)
        dside_ref[...] = side_ref[...] + jnp.where(line == gain_at, dgain_ref[...], 0.0).T
        part = model // (depth * CORES)
        for out_ref, which in ((keep_ref, core_ref[0]), (send_ref, 1 - core_ref[0])):
            for z in range(depth):
                rows = pl.ds(pl.multiple_of((z * CORES + which) * part, 16), part)
                here = slice(z * part, (z + 1) * part)
                out_ref[here, : 3 * width] = dwqkv_ref[rows, :].astype(BF16)
                out_ref[here, 3 * width : 4 * width] = dwo_ref[rows, :].astype(BF16)
                out_ref[here, 4 * width :] = dside_ref[rows, :].astype(BF16)


def attend_back(inputs, gain, datt, qkv, ctx, packed, dside, gain_at, width, images, seq, halves, core, depth):
    rows, model = inputs.shape
    span = rows // images
    image = lambda last: pl.BlockSpec((span, last), lambda i, s: (i, 0))
    fixed = lambda *size: pl.BlockSpec(size, lambda i, s: (0, 0))
    return pl.pallas_call(
        functools.partial(attend_back_kernel, seq, gain_at, depth),
        grid_spec=pltpu.PrefetchScalarGridSpec(
            num_scalar_prefetch=1,
            grid=(images,),
            in_specs=[
            image(model), fixed(1, model), image(model), image(3 * width), image(width),
            fixed(model, 3 * width), pl.BlockSpec((model, width), lambda i, s: (0, 3)),
            fixed(model, 128),
        ],
        out_specs=[
            pl.BlockSpec((halves, span, model // halves), lambda i, s: (0, i, 0)),
            image(128),
            fixed(model // CORES, packed.shape[1]),
            fixed(model // CORES, packed.shape[1]),
        ],
        scratch_shapes=[
            pltpu.VMEM((span, 3 * width), BF16),
            pltpu.VMEM((1, model), F32),
            pltpu.VMEM((model, 3 * width), F32),
            pltpu.VMEM((model, width), F32),
            pltpu.VMEM((model, 128), F32),
        ],
        ),
        out_shape=[
            shaped((halves, rows, model // halves), BF16),
            shaped((rows, 128), F32),
            shaped((model // CORES, packed.shape[1]), BF16),
            shaped((model // CORES, packed.shape[1]), BF16),
        ],
        compiler_params=params(),
        cost_estimate=cost(28 * rows * model * width, 12 * rows * model, rows * span * width // 64),
        name="attend_back",
    )(core, inputs, gain, datt, qkv, ctx, packed, packed, dside)


def slot_kernel(slots, place_ref, ids_ref, rows_ref, cols_ref):
    local, tokens = rows_ref.shape[1:]
    ids = ids_ref[0]
    line = lax.broadcasted_iota(jnp.int32, (8, tokens), 0)
    chosen = jnp.zeros((8, tokens), F32)
    for e in range(local):
        named = jnp.max(jnp.where(ids == place_ref[1] + e, 1.0, 0.0), axis=0, keepdims=True)
        chosen = jnp.where(line == e, named, chosen)
    first = lax.broadcasted_iota(jnp.int32, (tokens, tokens), 0)
    second = lax.broadcasted_iota(jnp.int32, (tokens, tokens), 1)
    before = jnp.where(first < second, 1.0, 0.0).astype(BF16)
    same = jnp.where(first == second, 1.0, 0.0).astype(BF16)
    marks = chosen.astype(BF16)
    rank = dot(marks, before, 1, 0)
    rows_ref[0] = jnp.where(chosen > 0.5, rank, -1.0)[:local].astype(jnp.int32)
    column = lax.broadcasted_iota(jnp.int32, (tokens, 8), 1).astype(F32) * slots
    found = jnp.where(dot(same, marks, 1, 1) > 0.5, dot(before, marks, 0, 1) + column, -1.0)
    cols_ref[0] = found[:, :local].astype(jnp.int32)


def find_slots(place, ids, local, slots):
    blocks, _, tokens = ids.shape
    block = lambda *size: pl.BlockSpec((1,) + size, lambda b, s: (b, 0, 0))
    return pl.pallas_call(
        functools.partial(slot_kernel, slots),
        grid_spec=pltpu.PrefetchScalarGridSpec(
            num_scalar_prefetch=1,
            grid=(blocks,),
            in_specs=[block(2, tokens)],
            out_specs=[block(local, tokens), block(tokens, local)],
        ),
        out_shape=[
            shaped((blocks, local, tokens), jnp.int32), shaped((blocks, tokens, local), jnp.int32)
        ],
        compiler_params=params(),
        cost_estimate=cost(64 * blocks * tokens * tokens, 64 * blocks * tokens),
        name="find_slots",
    )(place, ids)


def expert_kernel(index, depth, blocks, place_ref, slot_ref, router_ref, *refs):
    x_refs, refs = refs[:blocks], refs[blocks:]
    grad_refs, refs = refs[:blocks], refs[blocks:]
    win_refs, refs = refs[:depth], refs[depth:]
    wout_refs, refs = refs[:depth], refs[depth:]
    (
        rows_ref, mids_ref, dchosen_ref, drows_ref, yrows_ref, probs_ref, win_all, wout_all,
    ) = refs
    slots, model = rows_ref.shape[2:]
    tokens = x_refs[0].shape[0]
    part_rows, width = win_refs[0].shape[1:]
    step = pl.program_id(0)

    @pl.when(step == 0)
    def _():
        for k in range(depth):
            owner = lax.rem(place_ref[0] - k + depth, depth)
            at = pl.ds(pl.multiple_of(owner * part_rows, 16), part_rows)
            win_all[at, :] = win_refs[k][0]
            wout_all[at, :] = wout_refs[k][0]

    mask = lax.broadcasted_iota(jnp.int32, (slots, tokens), 0) == slot_ref[0, index : index + 1, :]
    pick = jnp.where(mask, 1.0, 0.0).astype(BF16)
    for b in range(blocks):

        @pl.when(step == b)
        def _(b=b):
            rows_ref[0, 0] = dot(pick, grad_refs[b][...], 1, 0).astype(BF16)
            rows_ref[1, 0] = dot(pick, x_refs[b][...], 1, 0).astype(BF16)
            logits = dot(router_ref[...], x_refs[b][...], 1, 1)
            powers = jnp.exp(logits - jnp.max(logits, axis=0, keepdims=True))
            probs_ref[0] = powers / jnp.sum(powers, axis=0, keepdims=True)

    probs = probs_ref[0]
    line = lax.broadcasted_iota(jnp.int32, probs.shape, 0)
    own = jnp.sum(jnp.where(line == place_ref[1], probs, 0.0), axis=0, keepdims=True)
    gate = jnp.sum(jnp.where(mask, own, 0.0), axis=1, keepdims=True)
    grows, rows = rows_ref[0, 0], rows_ref[1, 0]
    dgate = jnp.zeros((slots, 1), F32)
    drows = jnp.zeros((slots, model), F32)
    yrows = jnp.zeros((slots, model), F32)
    tile = 512 if width % 512 == 0 else width
    curve = 0.7978845608028654

    def products(start):
        cols = slice(start, start + tile)
        return dot(rows, win_all[:, cols], 1, 0), dot(grows, wout_all[:, cols], 1, 0)

    ahead = products(0)
    for start in range(0, width, tile):
        cols = slice(start, start + tile)
        hidden, pulled = ahead
        if start + tile < width:
            ahead = products(start + tile)
        square = hidden * hidden
        bend = jnp.tanh(hidden * (curve + curve * 0.044715 * square))
        half = 0.5 + 0.5 * bend
        active = hidden * half
        slope = half + 0.5 * hidden * (1.0 - bend * bend) * (
            curve + 3.0 * curve * 0.044715 * square
        )
        dgate = dgate + jnp.sum(active * pulled, axis=1, keepdims=True)
        gact = (gate * active).astype(BF16)
        dhid = (gate * pulled * slope).astype(BF16)
        mids_ref[0, 0, :, cols] = gact
        mids_ref[1, 0, :, cols] = dhid
        drows = drows + dot(dhid, win_all[:, cols], 1, 1)
        yrows = yrows + dot(gact, wout_all[:, cols], 1, 1)
    dchosen_ref[0] = jnp.sum(jnp.where(mask, dgate, 0.0), axis=0, keepdims=True)
    drows_ref[0] = drows.astype(BF16)
    yrows_ref[0] = yrows.astype(BF16)


def run_expert(index, place, slot_of, router_rows, xs, grads, pieces, slots):
    blocks, depth = len(xs), len(pieces)
    tokens, model = xs[0].shape
    _, part_rows, width = pieces[0].shape
    experts = router_rows.shape[0]
    fixed = lambda *size: pl.BlockSpec(
        size, lambda b, s: (0,) * len(size), pipeline_mode=pl.Buffered(1)
    )
    block = lambda *size: pl.BlockSpec((1,) + size, lambda b, s: (b, 0, 0))
    both = lambda last: pl.BlockSpec((2, 1, slots, last), lambda b, s: (0, b, 0, 0))
    weight = lambda which: pl.BlockSpec(
        (1, part_rows, width), lambda b, s: (which, 0, 0), pipeline_mode=pl.Buffered(1)
    )
    return pl.pallas_call(
        functools.partial(expert_kernel, index, depth, blocks),
        grid_spec=pltpu.PrefetchScalarGridSpec(
            num_scalar_prefetch=1,
            grid=(blocks,),
            in_specs=[block(slot_of.shape[1], tokens), fixed(experts, model)]
            + [fixed(tokens, model)] * (2 * blocks)
            + [weight(1)] * depth
            + [weight(0)] * depth,
            out_specs=[
                both(model), both(width), block(1, tokens), block(slots, model),
                block(slots, model), block(experts, tokens),
            ],
            scratch_shapes=[pltpu.VMEM((model, width), BF16)] * 2,
        ),
        out_shape=[
            shaped((2, blocks, slots, model), BF16), shaped((2, blocks, slots, width), BF16),
            shaped((blocks, 1, tokens), F32), shaped((blocks, slots, model), BF16),
            shaped((blocks, slots, model), BF16), shaped((blocks, experts, tokens), F32),
        ],
        compiler_params=params(),
        cost_estimate=cost(
            8 * blocks * slots * model * width + 4 * blocks * slots * model * tokens,
            16 * blocks * slots * model,
            blocks * slots * width,
        ),
        name="expert",
    )(place, slot_of, router_rows, *xs, *grads, *pieces, *pieces)


def weight_grad_kernel(depth, place_ref, rows_ref, cols_ref, *refs):
    out_refs, total_ref = refs[:depth], refs[depth]
    _, blocks, slots, model = rows_ref.shape
    width = cols_ref.shape[3]
    part_rows = model // depth
    left = rows_ref[0].reshape(blocks * slots, model)
    right = cols_ref[0].reshape(blocks * slots, width)
    total_ref[...] = dot(left, right, 0, 0)
    for k in range(depth):
        owner = lax.rem(place_ref[0] - k + depth, depth)
        at = pl.ds(pl.multiple_of(owner * part_rows, 16), part_rows)
        out_refs[k][0] = total_ref[at, :].astype(BF16)


def weight_grad(place, rows, cols, depth):
    _, blocks, slots, model = rows.shape
    width = cols.shape[3]
    both = lambda last: pl.BlockSpec((1, blocks, slots, last), lambda i, s: (i, 0, 0, 0))
    return pl.pallas_call(
        functools.partial(weight_grad_kernel, depth),
        grid_spec=pltpu.PrefetchScalarGridSpec(
            num_scalar_prefetch=1,
            grid=(2,),
            in_specs=[both(model), both(width)],
            out_specs=[pl.BlockSpec((1, model // depth, width), lambda i, s: (i, 0, 0))] * depth,
            scratch_shapes=[pltpu.VMEM((model, width), F32)],
        ),
        out_shape=[shaped((2, model // depth, width), BF16)] * depth,
        compiler_params=params(),
        cost_estimate=cost(
            4 * blocks * slots * model * width,
            4 * (blocks * slots * (model + width) + model * width),
        ),
        name="weight_grad",
    )(place, rows, cols)


def gathered(local, slot_ref, rows_refs, all_ref):
    slots, tokens = rows_refs[0].shape[1], slot_ref.shape[1]
    at = lax.broadcasted_iota(jnp.int32, (tokens, local * slots), 1)
    mask = at == slot_ref[0, :, 0:1]
    all_ref[0:slots, :] = rows_refs[0][0]
    for e in range(1, local):
        mask = mask | (at == slot_ref[0, :, e : e + 1])
        all_ref[e * slots : (e + 1) * slots, :] = rows_refs[e][0]
    return dot(jnp.where(mask, 1.0, 0.0).astype(BF16), all_ref[...], 1, 0)


def combine_kernel(local, added, slot_ref, *refs):
    rows_refs, refs = refs[:local], refs[local:]
    out_ref, all_ref = refs[-2:]
    total = gathered(local, slot_ref, rows_refs, all_ref)
    if added:
        total = total + refs[0][...].astype(F32)
    out_ref[...] = total.astype(BF16)


def combine(slot_cols, rows, b, add=None):
    _, tokens, local = slot_cols.shape
    slots, model = rows[0].shape[1:]
    whole = pl.BlockSpec((tokens, model), lambda i: (0, 0))
    return pl.pallas_call(
        functools.partial(combine_kernel, local, add is not None),
        grid=(1,),
        in_specs=[pl.BlockSpec((1, tokens, local), lambda i: (b, 0, 0))]
        + [pl.BlockSpec((1, slots, model), lambda i: (b, 0, 0))] * local
        + [whole] * (add is not None),
        out_specs=whole,
        out_shape=shaped((tokens, model), BF16),
        scratch_shapes=[pltpu.VMEM((local * slots, model), BF16)],
        compiler_params=params(),
        cost_estimate=cost(
            2 * local * slots * model * tokens, 2 * model * (local * slots + 2 * tokens)
        ),
        name="combine",
    )(slot_cols, *rows, *(() if add is None else (add,)))


def combine_back_kernel(local, added, place_ref, slot_ref, *refs):
    rows_refs, refs = refs[:local], refs[local:]
    dchosen_refs, refs = refs[:local], refs[local:]
    probs_ref, router_ref, x_ref = refs[:3]
    out_refs, (drouter_ref, all_ref) = refs[-2 - PARTS : -2], refs[-2:]
    probs = probs_ref[0]
    line = lax.broadcasted_iota(jnp.int32, probs.shape, 0)
    dprobs = jnp.zeros_like(probs)
    for e in range(local):
        dprobs = jnp.where(line == place_ref[1] + e, dchosen_refs[e][0], dprobs)
    inner = jnp.sum(dprobs * probs, axis=0, keepdims=True)
    dlogits = (probs * (dprobs - inner)).astype(BF16)
    drouter_ref[...] = dot(dlogits, x_ref[...], 1, 0)
    total = gathered(local, slot_ref, rows_refs, all_ref) + dot(dlogits, router_ref[...], 0, 0)
    part = out_refs[0].shape[1]
    for p in range(PARTS):
        piece = total[:, p * part : (p + 1) * part]
        if added:
            piece = piece + refs[3 + p][...].astype(F32)
        out_refs[p][...] = piece.astype(BF16)


def combine_back(place, slot_cols, rows, dchosen, probs, router_rows, x, b, add=None):
    _, tokens, local = slot_cols.shape
    slots, model = rows[0].shape[1:]
    experts = router_rows.shape[0]
    whole = pl.BlockSpec((tokens, model), lambda i, s: (0, 0))
    part = pl.BlockSpec((tokens, model // PARTS), lambda i, s: (0, 0))
    block = lambda *size: pl.BlockSpec((1,) + size, lambda i, s: (b, 0, 0))
    small = pl.BlockSpec((experts, model), lambda i, s: (0, 0))
    return pl.pallas_call(
        functools.partial(combine_back_kernel, local, add is not None),
        grid_spec=pltpu.PrefetchScalarGridSpec(
            num_scalar_prefetch=1,
            grid=(1,),
            in_specs=[block(tokens, local)]
            + [block(slots, model)] * local
            + [block(1, tokens)] * local
            + [block(experts, tokens), small, whole]
            + [part] * (PARTS * (add is not None)),
            out_specs=[part] * PARTS + [small],
            scratch_shapes=[pltpu.VMEM((local * slots, model), BF16)],
        ),
        out_shape=[shaped((tokens, model // PARTS), BF16)] * PARTS
        + [shaped((experts, model), F32)],
        compiler_params=params(),
        cost_estimate=cost(
            2 * local * slots * model * tokens, 2 * model * (local * slots + 3 * tokens)
        ),
        name="combine_back",
    )(place, slot_cols, *rows, *dchosen, probs, router_rows, x, *(() if add is None else add))


def per_device(
    block_in, cotangent, route_ids, gain_attn, w_qkv, w_out_attn, gain_moe, router, w_in, w_out
):
    n_dp, n_heads, n_exp = (lax.axis_size(name) for name in ("dp", "heads", "expert"))
    n_z = n_dp // CORES
    dp, head, exp = (lax.axis_index(name) for name in ("dp", "heads", "expert"))
    z, core = dp // CORES, dp % CORES
    low = core == 0
    images, seq, half_width = block_in.shape
    span = -(-seq // 16) * 16
    rows = images * span
    model = half_width * n_heads
    width = w_qkv.shape[2]
    shard = w_qkv.shape[0]
    expert_count = router.shape[1]
    group = w_in.shape[1]
    local = group // CORES
    part_rows, _, hidden_width = w_in.shape
    capacity = 20 * images * seq // (7 * expert_count)
    slots = -(-capacity // 16) * 16
    blocks = n_exp * CORES
    rest = 128

    def shift(value, axis, step):
        size = lax.axis_size(axis)
        return lax.ppermute(value, axis, [(i, (i + step) % size) for i in range(size)])

    def shift_z(value, step):
        pairs = [
            (a * CORES + c, ((a + step) % n_z) * CORES + c) for a in range(n_z) for c in range(CORES)
        ]
        return lax.ppermute(value, "dp", pairs)

    def swap_core(value):
        return lax.ppermute(value, "dp", [(i, i ^ 1) for i in range(n_dp)])

    def place_at(pieces, index, count):
        if count == 2:
            first = index == 0
            return jnp.stack(
                [jnp.where(first, pieces[0], pieces[1]), jnp.where(first, pieces[1], pieces[0])]
            )
        out = jnp.zeros((count,) + pieces[0].shape, pieces[0].dtype)
        for k, piece in enumerate(pieces):
            out = lax.dynamic_update_index_in_dim(out, piece, (index - k) % count, 0)
        return out

    def spread(value, axis):
        return [value] + [shift(value, axis, k) for k in range(1, lax.axis_size(axis))]

    def take(value, index, dim=0):
        return lax.dynamic_index_in_dim(value, index, dim, keepdims=False)

    def expert_shards():
        both = jnp.stack([w_out, w_in]).reshape(2, part_rows, CORES, local, hidden_width)
        by_core = both.transpose(2, 3, 0, 1, 4)
        other = swap_core(take(by_core, 1 - core))
        mine = take(by_core, core)
        return jnp.concatenate(
            [jnp.where(low, mine, other), jnp.where(low, other, mine)], axis=2
        )

    ways_up = n_z // 2
    ways_down = n_z - 1 - ways_up

    def ring(piece):
        pieces = [piece] + [None] * (n_z - 1)
        for k in range(1, ways_up + 1):
            pieces[k] = shift_z(pieces[k - 1], 1)
        for k in range(1, ways_down + 1):
            pieces[n_z - k] = shift_z(pieces[(n_z - k + 1) % n_z], -1)
        return pieces

    def blocks_of(value, hold=()):
        along = spread(value, "expert")
        if hold:
            along[0] = after(along[0], *hold)
        return along + [swap_core(part) for part in along]

    def full_rows(value):
        padded = jnp.pad(value, ((0, 0), (0, span - seq), (0, 0))).reshape(rows, half_width)
        parts = place_at(spread(padded, "heads"), head, n_heads)
        return jnp.concatenate([parts[i] for i in range(n_heads)], axis=-1)

    inputs = full_rows(block_in)
    grad_full = full_rows(cotangent)

    tail = jnp.concatenate(
        [router, gain_attn[:, None], gain_moe[:, None],
         jnp.zeros((shard, rest - expert_count - 2), BF16)], axis=1
    )
    own_pack = jnp.concatenate([w_qkv.reshape(shard, 3 * width), w_out_attn, tail], axis=1)
    columns = own_pack.shape[1]
    shards = expert_shards()
    ids = jnp.pad(route_ids, ((0, 0), (0, span - seq), (0, 0)), constant_values=-1)
    ids_all = jnp.stack(blocks_of(ids.reshape(rows, 2).T))
    pack_z = place_at(
        [own_pack] + [after(shift_z(own_pack, k), shards) for k in range(1, n_z)], z, n_z
    )
    pieces = []
    for e in range(local):
        pieces.append(ring(after(shards[e], pieces[-1][1]) if e else shards[e]))
    last = local - 1
    pack = place_at(spread(after(pack_z, ids_all), "expert"), exp, n_exp)

    pack = after(pack, pieces[0][1], inputs, grad_full)
    other_pack = swap_core(pack)
    pack = jnp.stack([jnp.where(low, pack, other_pack), jnp.where(low, other_pack, pack)])
    pack = pack.transpose(2, 0, 1, 3, 4).reshape(model, columns)
    side = pack[:, 4 * width :].T
    router_rows = side[:expert_count]
    gain_one = side[expert_count : expert_count + 1].astype(F32)
    gain_two = side[expert_count + 1 : expert_count + 2].astype(F32)

    first_expert = exp * group + core * local
    place = [jnp.stack([z, first_expert + e]).astype(jnp.int32) for e in range(local)]
    slot_of, slot_cols = find_slots(place[0], ids_all, local, slots)

    grads_all = blocks_of(grad_full)
    inputs_ready = inputs
    part, qkv, ctx = attend(inputs_ready, expert_count, pack, width, images, seq)
    part = after(part, pieces[0][-1])
    part_other = shift(part, "heads", 1)
    for k in range(2, n_heads):
        part_other = part_other + shift(part, "heads", k)
    part_other = after(part_other, pieces[0][ways_up], slot_cols)
    middle = inputs.astype(F32) + (part.astype(F32) + part_other.astype(F32))
    unit_two, scale_two = norm_parts(middle)
    normed_two = (unit_two * gain_two).astype(BF16)
    tokens_all = blocks_of(normed_two, (pieces[last][1],))

    done = []

    def begin_rings(e, *hold):
        rows_e, mids_e = done[e][:2]
        rings.append(weight_grad(place[e], after(rows_e, *hold), mids_e, n_z))

    def ring_first(e):
        return shift_z(rings[e][-ways_up % n_z], 1)

    def ring_down(e, *hold):
        chunks = rings[e]
        downward = after(chunks[ways_down], *hold)
        for k in range(ways_down - 1, 0, -1):
            downward = (shift_z(downward, -1).astype(F32) + chunks[k].astype(F32)).astype(BF16)
        return shift_z(downward, -1)

    def ring_middle(e, upward, *hold):
        chunks = rings[e]
        for k in range(ways_up - 1, 0, -1):
            own = after(chunks[n_z - k], *hold)
            upward = (upward.astype(F32) + own.astype(F32)).astype(BF16)
            if k > 1:
                upward = shift_z(upward, 1)
        return upward

    def ring_end(e, upward, downward, *hold):
        own = after(rings[e][0], *hold).astype(F32)
        return own + shift_z(upward, 1).astype(F32) + downward.astype(F32)

    rings = []
    for e in range(local):
        here = list(pieces[e])
        if e:
            here[0] = after(here[0], rings[-1][0])
        done.append(
            run_expert(
                e, place[e], slot_of, router_rows, tokens_all, grads_all, here, slots
            )
        )
        if e < local - 1:
            begin_rings(e)
    drows, yrows, dchosen = ([r[i] for r in done] for i in (3, 4, 2))
    probs = done[0][5]

    arrived_zero, down_zero = ring_first(0), ring_down(0)
    drows[0] = after(drows[0], arrived_zero)

    def back_of(b, add=None):
        *parts, more = combine_back(
            place[0], slot_cols, drows, dchosen, probs, router_rows, tokens_all[b], b, add
        )
        return parts, more

    drouter = jnp.zeros((expert_count, model), F32)
    arrived = [None] * n_exp
    for k in reversed(range(n_exp)):
        sent, more = back_of(n_exp + k)
        arrived[k] = [swap_core(part) for part in sent]
        drouter = drouter + more
    from_exp = []
    for k in reversed(range(n_exp)):
        arrived[k][0] = after(arrived[k][0], total[0] if k < n_exp - 1 else down_zero)
        total, more = back_of(k, arrived[k])
        drouter = drouter + more
        if k:
            from_exp.append([shift(part, "expert", -k) for part in total])
        if k == 1:
            early = ring_middle(0, arrived_zero, total[0])
    ends = [ring_end(0, early, down_zero)]
    dsum, dsum_other = [], []
    for p in range(PARTS):
        if p == 1:
            begin_rings(last, dsum[0])
        value = (after(total[p], rings[last][0]) if p else total[p]).astype(F32)
        for came in from_exp:
            value = value + came[p].astype(F32)
        dsum.append(value.astype(BF16))
        other = shift(dsum[p], "heads", 1)
        for k in range(2, n_heads):
            other = other + shift(dsum[p], "heads", k)
        dsum_other.append(other)
    arrived_last, down_last = ring_first(last), ring_down(last)
    dsum_other[0] = after(dsum_other[0], ends[0])

    yrows[0] = after(yrows[0], dsum[0])
    y_came = [swap_core(combine(slot_cols, yrows, n_exp + k)) for k in range(n_exp)]
    y_from = [
        shift(combine(slot_cols, yrows, k, after(y_came[k], dsum[-1])), "expert", -k)
        for k in range(1, n_exp)
    ]
    dnormed_two = jnp.concatenate(
        [own.astype(F32) + other.astype(F32) for own, other in zip(dsum, dsum_other)], axis=1
    )
    scaled = dnormed_two * gain_two
    grad_gain_two = jnp.sum(dnormed_two * unit_two, axis=0)
    dmiddle = grad_full.astype(F32) + scale_two * (
        scaled
        - jnp.mean(scaled, axis=-1, keepdims=True)
        - unit_two * jnp.mean(scaled * unit_two, axis=-1, keepdims=True)
    )
    late = ring_middle(last, arrived_last, dsum_other[-1])
    datt = after(dmiddle.astype(BF16), *y_came)

    dside = jnp.concatenate(
        [drouter, jnp.zeros((1, model), F32), grad_gain_two[None, :],
         jnp.zeros((rest - expert_count - 2, model), F32)], axis=0
    ).T
    dnorm, stats, dkeep, dsend = attend_back(
        inputs, gain_one, datt, qkv, ctx, pack, dside, expert_count, width, images, seq, n_heads,
        core.astype(jnp.int32)[None], n_z,
    )
    dsend = after(dsend, *y_from, down_last)

    dcame = swap_core(dsend)
    dpack = (dkeep.astype(F32) + dcame.astype(F32)).astype(BF16)
    dpack = dpack.reshape(n_z, n_exp, shard, columns)
    y_own = combine(slot_cols, yrows, 0, after(y_came[0], dcame)).astype(F32)
    for value in y_from:
        y_own = y_own + value.astype(F32)
    y_own = y_own.astype(BF16)

    dtotal = take(dpack, exp, 1).astype(F32)
    for k in range(1, n_exp):
        came = shift(take(dpack, (exp + k) % n_exp, 1), "expert", k)
        dtotal = dtotal + came.astype(F32)
    dpack = dtotal.astype(BF16)

    came = [shift_z(take(dpack, (z + k) % n_z), k) for k in range(1, n_z)]
    dtotal = take(dpack, z).astype(F32)
    for value in came:
        dtotal = dtotal + value.astype(F32)

    ends.append(ring_end(last, late, down_last, dpack))
    stacked = jnp.stack(ends).reshape(local, 2, CORES, part_rows, hidden_width)
    other = swap_core(take(stacked, 1 - core, 2).astype(BF16)).astype(F32)
    own = take(stacked, core, 2)
    joined = jnp.concatenate([jnp.where(low, own, other), jnp.where(low, other, own)], axis=0)
    grads = joined.transpose(1, 2, 0, 3)
    dside = dtotal[:, 4 * width :]
    over_heads = dside[:, : expert_count + 1].T
    grad_w_out, grad_w_in, over_heads = lax.optimization_barrier((grads[0], grads[1], over_heads))
    summed = over_heads
    for k in range(1, n_heads):
        summed = summed + shift(over_heads, "heads", k)

    def own_half(value):
        return lax.dynamic_slice_in_dim(value, head * half_width, half_width, 1)

    def cut(value):
        return value.astype(BF16).reshape(images, span, half_width)[:, :seq]

    dnorm, stats = lax.optimization_barrier((dnorm, stats, dcame))[:2]
    dn_own = take(dnorm, head).astype(F32)
    sums = stats[:, :2].T
    sums_total = sums
    for k in range(1, n_heads):
        there = shift(take(dnorm, (head + k) % n_heads), "heads", k)
        dn_own = dn_own + after(there, came[0]).astype(F32)
        sums_total = sums_total + after(shift(sums, "heads", k), came[0])
    unit_one, scale_one = norm_parts(inputs.astype(F32))
    grad_in = own_half(dmiddle) + scale_one * (
        dn_own * own_half(gain_one)
        - sums_total[0][:, None] / model
        - own_half(unit_one) * (sums_total[1][:, None] / model)
    )

    y_total = own_half(y_own).astype(F32)
    for k in range(1, n_heads):
        there = (head + k) % n_heads
        part_y = lax.dynamic_slice_in_dim(y_own, there * half_width, half_width, 1)
        y_total = y_total + after(shift(part_y, "heads", k), came[0]).astype(F32)
    block_out = own_half(middle) + y_total

    return (
        cut(block_out),
        cut(grad_in),
        summed[expert_count],
        dtotal[:, : 3 * width].reshape(shard, 3, width),
        dtotal[:, 3 * width : 4 * width],
        dside[:, expert_count + 1],
        summed[:expert_count].T,
        grad_w_in,
        grad_w_out,
    )


def solution(mesh):
    return jax.shard_map(
        per_device,
        mesh=mesh,
        in_specs=(
            P(("dp", "expert"), None, "heads"),
            P(("dp", "expert"), None, "heads"),
            P(("dp", "expert"), None, None),
            P(("dp", "expert")),
            P(("dp", "expert"), None, "heads"),
            P(("dp", "expert"), "heads"),
            P(("dp", "expert")),
            P(("dp", "expert"), None),
            P("dp", "expert", "heads"),
            P("dp", "expert", "heads"),
        ),
        out_specs=(
            P(("dp", "expert"), None, "heads"),
            P(("dp", "expert"), None, "heads"),
            P(("dp", "expert")),
            P(("dp", "expert"), None, "heads"),
            P(("dp", "expert"), "heads"),
            P(("dp", "expert")),
            P(("dp", "expert"), None),
            P("dp", "expert", "heads"),
            P("dp", "expert", "heads"),
        ),
        check_vma=False,
    )
```

```python
import functools

import jax
import jax.numpy as jnp
from jax import lax
from jax.experimental import pallas as pl
from jax.experimental.pallas import tpu as pltpu
from jax.sharding import PartitionSpec as P

HEAD_DIM = 64
CORES = 2
EPS = 1e-06
LOW = -1e30
F32 = jnp.float32
BF16 = jnp.bfloat16
VMEM_LIMIT = 56 * 1024 * 1024
SHARE = 64
PARTS = 2


def dot(a, b, ca, cb):
    return lax.dot_general(a, b, (((ca,), (cb,)), ((), ())), preferred_element_type=F32)


def shaped(shape, kind):
    return jax.ShapeDtypeStruct(shape, kind)


def params(dims=1):
    return pltpu.CompilerParams(
        dimension_semantics=("arbitrary",) * dims, vmem_limit_bytes=VMEM_LIMIT
    )


def cost(flops, size, powers=0):
    return pl.CostEstimate(
        flops=flops // SHARE, bytes_accessed=size // SHARE, transcendentals=powers // SHARE
    )


def after(value, *others):
    return lax.optimization_barrier((value,) + others)[0]


def norm_parts(rows):
    average = jnp.mean(rows, axis=-1, keepdims=True)
    centred = rows - average
    spread = jnp.mean(centred * centred, axis=-1, keepdims=True)
    scale = lax.rsqrt(spread + EPS)
    return centred * scale, scale


def softmax_rows(q, own_k, real):
    scores = jnp.where(real, dot(q, own_k, 1, 1) * (HEAD_DIM**-0.5), LOW)
    powers = jnp.exp(scores - jnp.max(scores, axis=-1, keepdims=True))
    return powers / jnp.sum(powers, axis=-1, keepdims=True)


def attend_kernel(
    seq, gain_at, x_ref, side_ref, wqkv_ref, wo_ref, part_ref, qkv_ref, ctx_ref, gain_ref
):
    width = wo_ref.shape[1]
    span = x_ref.shape[0]

    @pl.when(pl.program_id(0) == 0)
    def _():
        gain_ref[...] = side_ref[...].astype(F32).T[gain_at : gain_at + 1, :]

    unit, _ = norm_parts(x_ref[...].astype(F32))
    normed = (unit * gain_ref[...]).astype(BF16)
    for part in range(3):
        cols = slice(part * width, (part + 1) * width)
        qkv_ref[:, cols] = dot(normed, wqkv_ref[:, cols], 1, 0).astype(BF16)
    lane = lax.broadcasted_iota(jnp.int32, (span, 128), 1)
    real = lax.broadcasted_iota(jnp.int32, (span, span), 1) < seq
    for pair in range(width // 128):
        q, k, v = (
            qkv_ref[:, part * width + pair * 128 : part * width + (pair + 1) * 128]
            for part in range(3)
        )
        ctx = jnp.zeros((span, 128), F32)
        for side in range(2):
            mine = (lane >= 64) if side else (lane < 64)
            own_k = jnp.where(mine, k, jnp.zeros_like(k))
            own_v = jnp.where(mine, v, jnp.zeros_like(v))
            weights = softmax_rows(q, own_k, real)
            ctx = ctx + dot(weights.astype(BF16), own_v, 1, 0)
        ctx_ref[:, pair * 128 : (pair + 1) * 128] = ctx.astype(BF16)
    part_ref[...] = dot(ctx_ref[...], wo_ref[...], 1, 1).astype(BF16)


def attend(inputs, gain_at, packed, width, images, seq):
    rows, model = inputs.shape
    span = rows // images
    image = lambda last: pl.BlockSpec((span, last), lambda i: (i, 0))
    return pl.pallas_call(
        functools.partial(attend_kernel, seq, gain_at),
        grid=(images,),
        in_specs=[
            image(model),
            pl.BlockSpec((model, 128), lambda i: (0, 4 * width // 128)),
            pl.BlockSpec((model, 3 * width), lambda i: (0, 0)),
            pl.BlockSpec((model, width), lambda i: (0, 3)),
        ],
        out_specs=[image(model), image(3 * width), image(width)],
        scratch_shapes=[pltpu.VMEM((1, model), F32)],
        out_shape=[
            shaped((rows, model), BF16), shaped((rows, 3 * width), BF16), shaped((rows, width), BF16)
        ],
        compiler_params=params(),
        cost_estimate=cost(10 * rows * model * width, 8 * rows * model, rows * span * width // 64),
        name="attend",
    )(inputs, packed, packed, packed)


def attend_back_kernel(
    seq, gain_at, depth,
    core_ref, x_ref, gain_ref, datt_ref, qkv_ref, ctx_ref, wqkv_ref, wo_ref, side_ref,
    dnorm_ref, stats_ref, keep_ref, send_ref, dproj_ref, dgain_ref, dwqkv_ref, dwo_ref, dside_ref,
):
    width = wo_ref.shape[1]
    span, model = x_ref.shape
    step = pl.program_id(0)

    @pl.when(step == 0)
    def _():
        dgain_ref[...] = jnp.zeros_like(dgain_ref)
        dwqkv_ref[...] = jnp.zeros_like(dwqkv_ref)
        dwo_ref[...] = jnp.zeros_like(dwo_ref)

    datt = datt_ref[...]
    dwo_ref[...] += dot(datt, ctx_ref[...], 0, 0)
    dctx_all = dot(datt, wo_ref[...], 1, 0).astype(BF16)
    lane = lax.broadcasted_iota(jnp.int32, (span, 128), 1)
    real = lax.broadcasted_iota(jnp.int32, (span, span), 1) < seq
    for pair in range(width // 128):
        q, k, v = (
            qkv_ref[:, part * width + pair * 128 : part * width + (pair + 1) * 128]
            for part in range(3)
        )
        dctx = dctx_all[:, pair * 128 : (pair + 1) * 128]
        dq = jnp.zeros((span, 128), F32)
        dk = jnp.zeros((span, 128), F32)
        dv = jnp.zeros((span, 128), F32)
        for side in range(2):
            mine = (lane >= 64) if side else (lane < 64)
            own = lambda t: jnp.where(mine, t, jnp.zeros_like(t))
            own_k, own_v = own(k), own(v)
            weights = softmax_rows(q, own_k, real)
            dweights = dot(dctx, own_v, 1, 1)
            inner = jnp.sum(dweights * weights, axis=-1, keepdims=True)
            dscores = (weights * (dweights - inner)).astype(BF16)
            dq = dq + dot(dscores, own_k, 1, 0)
            dk = dk + dot(dscores, own(q), 0, 0)
            dv = dv + dot(weights.astype(BF16), own(dctx), 0, 0)
        for part, value in enumerate((dq * HEAD_DIM**-0.5, dk * HEAD_DIM**-0.5, dv)):
            start = part * width + pair * 128
            dproj_ref[:, start : start + 128] = value.astype(BF16)
    dproj = dproj_ref[...]
    gain = gain_ref[...]
    unit, _ = norm_parts(x_ref[...].astype(F32))
    normed = (unit * gain).astype(BF16)
    dwqkv_ref[...] += dot(normed, dproj, 0, 0)
    dnormed = dot(dproj, wqkv_ref[...], 1, 1)
    halves, _, half = dnorm_ref.shape
    for h in range(halves):
        dnorm_ref[h] = dnormed[:, h * half : (h + 1) * half].astype(BF16)
    along = dnormed * unit
    dgain_ref[...] += jnp.sum(along, axis=0, keepdims=True)
    first = jnp.sum(dnormed * gain, axis=-1, keepdims=True)
    second = jnp.sum(along * gain, axis=-1, keepdims=True)
    stats_ref[...] = jnp.where(lane == 0, first, jnp.where(lane == 1, second, 0.0))

    @pl.when(step == pl.num_programs(0) - 1)
    def _():
        line = lax.broadcasted_iota(jnp.int32, (128, model), 0)
        dside_ref[...] = side_ref[...] + jnp.where(line == gain_at, dgain_ref[...], 0.0).T
        part = model // (depth * CORES)
        for out_ref, which in ((keep_ref, core_ref[0]), (send_ref, 1 - core_ref[0])):
            for z in range(depth):
                rows = pl.ds(pl.multiple_of((z * CORES + which) * part, 16), part)
                here = slice(z * part, (z + 1) * part)
                out_ref[here, : 3 * width] = dwqkv_ref[rows, :].astype(BF16)
                out_ref[here, 3 * width : 4 * width] = dwo_ref[rows, :].astype(BF16)
                out_ref[here, 4 * width :] = dside_ref[rows, :].astype(BF16)


def attend_back(inputs, gain, datt, qkv, ctx, packed, dside, gain_at, width, images, seq, halves, core, depth):
    rows, model = inputs.shape
    span = rows // images
    image = lambda last: pl.BlockSpec((span, last), lambda i, s: (i, 0))
    fixed = lambda *size: pl.BlockSpec(size, lambda i, s: (0, 0))
    return pl.pallas_call(
        functools.partial(attend_back_kernel, seq, gain_at, depth),
        grid_spec=pltpu.PrefetchScalarGridSpec(
            num_scalar_prefetch=1,
            grid=(images,),
            in_specs=[
            image(model), fixed(1, model), image(model), image(3 * width), image(width),
            fixed(model, 3 * width), pl.BlockSpec((model, width), lambda i, s: (0, 3)),
            fixed(model, 128),
        ],
        out_specs=[
            pl.BlockSpec((halves, span, model // halves), lambda i, s: (0, i, 0)),
            image(128),
            fixed(model // CORES, packed.shape[1]),
            fixed(model // CORES, packed.shape[1]),
        ],
        scratch_shapes=[
            pltpu.VMEM((span, 3 * width), BF16),
            pltpu.VMEM((1, model), F32),
            pltpu.VMEM((model, 3 * width), F32),
            pltpu.VMEM((model, width), F32),
            pltpu.VMEM((model, 128), F32),
        ],
        ),
        out_shape=[
            shaped((halves, rows, model // halves), BF16),
            shaped((rows, 128), F32),
            shaped((model // CORES, packed.shape[1]), BF16),
            shaped((model // CORES, packed.shape[1]), BF16),
        ],
        compiler_params=params(),
        cost_estimate=cost(28 * rows * model * width, 12 * rows * model, rows * span * width // 64),
        name="attend_back",
    )(core, inputs, gain, datt, qkv, ctx, packed, packed, dside)


def slot_kernel(slots, place_ref, ids_ref, rows_ref, cols_ref):
    local, tokens = rows_ref.shape[1:]
    ids = ids_ref[0]
    line = lax.broadcasted_iota(jnp.int32, (8, tokens), 0)
    chosen = jnp.zeros((8, tokens), F32)
    for e in range(local):
        named = jnp.max(jnp.where(ids == place_ref[1] + e, 1.0, 0.0), axis=0, keepdims=True)
        chosen = jnp.where(line == e, named, chosen)
    first = lax.broadcasted_iota(jnp.int32, (tokens, tokens), 0)
    second = lax.broadcasted_iota(jnp.int32, (tokens, tokens), 1)
    before = jnp.where(first < second, 1.0, 0.0).astype(BF16)
    same = jnp.where(first == second, 1.0, 0.0).astype(BF16)
    marks = chosen.astype(BF16)
    rank = dot(marks, before, 1, 0)
    rows_ref[0] = jnp.where(chosen > 0.5, rank, -1.0)[:local].astype(jnp.int32)
    column = lax.broadcasted_iota(jnp.int32, (tokens, 8), 1).astype(F32) * slots
    found = jnp.where(dot(same, marks, 1, 1) > 0.5, dot(before, marks, 0, 1) + column, -1.0)
    cols_ref[0] = found[:, :local].astype(jnp.int32)


def find_slots(place, ids, local, slots):
    blocks, _, tokens = ids.shape
    block = lambda *size: pl.BlockSpec((1,) + size, lambda b, s: (b, 0, 0))
    return pl.pallas_call(
        functools.partial(slot_kernel, slots),
        grid_spec=pltpu.PrefetchScalarGridSpec(
            num_scalar_prefetch=1,
            grid=(blocks,),
            in_specs=[block(2, tokens)],
            out_specs=[block(local, tokens), block(tokens, local)],
        ),
        out_shape=[
            shaped((blocks, local, tokens), jnp.int32), shaped((blocks, tokens, local), jnp.int32)
        ],
        compiler_params=params(),
        cost_estimate=cost(64 * blocks * tokens * tokens, 64 * blocks * tokens),
        name="find_slots",
    )(place, ids)


def expert_kernel(index, depth, blocks, place_ref, slot_ref, router_ref, *refs):
    x_refs, refs = refs[:blocks], refs[blocks:]
    grad_refs, refs = refs[:blocks], refs[blocks:]
    win_refs, refs = refs[:depth], refs[depth:]
    wout_refs, refs = refs[:depth], refs[depth:]
    (
        rows_ref, mids_ref, dchosen_ref, drows_ref, yrows_ref, probs_ref, win_all, wout_all,
    ) = refs
    slots, model = rows_ref.shape[2:]
    tokens = x_refs[0].shape[0]
    part_rows, width = win_refs[0].shape[1:]
    step = pl.program_id(0)

    @pl.when(step == 0)
    def _():
        for k in range(depth):
            owner = lax.rem(place_ref[0] - k + depth, depth)
            at = pl.ds(pl.multiple_of(owner * part_rows, 16), part_rows)
            win_all[at, :] = win_refs[k][0]
            wout_all[at, :] = wout_refs[k][0]

    mask = lax.broadcasted_iota(jnp.int32, (slots, tokens), 0) == slot_ref[0, index : index + 1, :]
    pick = jnp.where(mask, 1.0, 0.0).astype(BF16)
    for b in range(blocks):

        @pl.when(step == b)
        def _(b=b):
            rows_ref[0, 0] = dot(pick, grad_refs[b][...], 1, 0).astype(BF16)
            rows_ref[1, 0] = dot(pick, x_refs[b][...], 1, 0).astype(BF16)
            logits = dot(router_ref[...], x_refs[b][...], 1, 1)
            powers = jnp.exp(logits - jnp.max(logits, axis=0, keepdims=True))
            probs_ref[0] = powers / jnp.sum(powers, axis=0, keepdims=True)

    probs = probs_ref[0]
    line = lax.broadcasted_iota(jnp.int32, probs.shape, 0)
    own = jnp.sum(jnp.where(line == place_ref[1], probs, 0.0), axis=0, keepdims=True)
    gate = jnp.sum(jnp.where(mask, own, 0.0), axis=1, keepdims=True)
    grows, rows = rows_ref[0, 0], rows_ref[1, 0]
    dgate = jnp.zeros((slots, 1), F32)
    tile = 512 if width % 512 == 0 else width
    curve = 0.7978845608028654

    def products(start):
        cols = slice(start, start + tile)
        return dot(rows, win_all[:, cols], 1, 0), dot(grows, wout_all[:, cols], 1, 0)

    ahead = products(0)
    for start in range(0, width, tile):
        cols = slice(start, start + tile)
        hidden, pulled = ahead
        if start + tile < width:
            ahead = products(start + tile)
        square = hidden * hidden
        bend = jnp.tanh(hidden * (curve + curve * 0.044715 * square))
        half = 0.5 + 0.5 * bend
        active = hidden * half
        slope = half + 0.5 * hidden * (1.0 - bend * bend) * (
            curve + 3.0 * curve * 0.044715 * square
        )
        dgate = dgate + jnp.sum(active * pulled, axis=1, keepdims=True)
        gact = (gate * active).astype(BF16)
        dhid = (gate * pulled * slope).astype(BF16)
        mids_ref[0, 0, :, cols] = gact
        mids_ref[1, 0, :, cols] = dhid
    dchosen_ref[0] = jnp.sum(jnp.where(mask, dgate, 0.0), axis=0, keepdims=True)
    drows_ref[0] = dot(mids_ref[1, 0], win_all[...], 1, 1).astype(BF16)
    yrows_ref[0] = dot(mids_ref[0, 0], wout_all[...], 1, 1).astype(BF16)


def run_expert(index, place, slot_of, router_rows, xs, grads, pieces, slots):
    blocks, depth = len(xs), len(pieces)
    tokens, model = xs[0].shape
    _, part_rows, width = pieces[0].shape
    experts = router_rows.shape[0]
    fixed = lambda *size: pl.BlockSpec(
        size, lambda b, s: (0,) * len(size), pipeline_mode=pl.Buffered(1)
    )
    block = lambda *size: pl.BlockSpec((1,) + size, lambda b, s: (b, 0, 0))
    both = lambda last: pl.BlockSpec((2, 1, slots, last), lambda b, s: (0, b, 0, 0))
    weight = lambda which: pl.BlockSpec(
        (1, part_rows, width), lambda b, s: (which, 0, 0), pipeline_mode=pl.Buffered(1)
    )
    return pl.pallas_call(
        functools.partial(expert_kernel, index, depth, blocks),
        grid_spec=pltpu.PrefetchScalarGridSpec(
            num_scalar_prefetch=1,
            grid=(blocks,),
            in_specs=[block(slot_of.shape[1], tokens), fixed(experts, model)]
            + [fixed(tokens, model)] * (2 * blocks)
            + [weight(1)] * depth
            + [weight(0)] * depth,
            out_specs=[
                both(model), both(width), block(1, tokens), block(slots, model),
                block(slots, model), block(experts, tokens),
            ],
            scratch_shapes=[pltpu.VMEM((model, width), BF16)] * 2,
        ),
        out_shape=[
            shaped((2, blocks, slots, model), BF16), shaped((2, blocks, slots, width), BF16),
            shaped((blocks, 1, tokens), F32), shaped((blocks, slots, model), BF16),
            shaped((blocks, slots, model), BF16), shaped((blocks, experts, tokens), F32),
        ],
        compiler_params=params(),
        cost_estimate=cost(
            8 * blocks * slots * model * width + 4 * blocks * slots * model * tokens,
            16 * blocks * slots * model,
            blocks * slots * width,
        ),
        name="expert",
    )(place, slot_of, router_rows, *xs, *grads, *pieces, *pieces)


def weight_grad_kernel(depth, place_ref, rows_ref, cols_ref, *refs):
    out_refs, total_ref = refs[:depth], refs[depth]
    _, blocks, slots, model = rows_ref.shape
    width = cols_ref.shape[3]
    part_rows = model // depth
    left = rows_ref[0].reshape(blocks * slots, model)
    right = cols_ref[0].reshape(blocks * slots, width)
    total_ref[...] = dot(left, right, 0, 0)
    for k in range(depth):
        owner = lax.rem(place_ref[0] - k + depth, depth)
        at = pl.ds(pl.multiple_of(owner * part_rows, 16), part_rows)
        out_refs[k][0] = total_ref[at, :].astype(BF16)


def weight_grad(place, rows, cols, depth):
    _, blocks, slots, model = rows.shape
    width = cols.shape[3]
    both = lambda last: pl.BlockSpec((1, blocks, slots, last), lambda i, s: (i, 0, 0, 0))
    return pl.pallas_call(
        functools.partial(weight_grad_kernel, depth),
        grid_spec=pltpu.PrefetchScalarGridSpec(
            num_scalar_prefetch=1,
            grid=(2,),
            in_specs=[both(model), both(width)],
            out_specs=[pl.BlockSpec((1, model // depth, width), lambda i, s: (i, 0, 0))] * depth,
            scratch_shapes=[pltpu.VMEM((model, width), F32)],
        ),
        out_shape=[shaped((2, model // depth, width), BF16)] * depth,
        compiler_params=params(),
        cost_estimate=cost(
            4 * blocks * slots * model * width,
            4 * (blocks * slots * (model + width) + model * width),
        ),
        name="weight_grad",
    )(place, rows, cols)


def gathered(local, slot_ref, rows_refs, all_ref):
    slots, tokens = rows_refs[0].shape[1], slot_ref.shape[1]
    at = lax.broadcasted_iota(jnp.int32, (tokens, local * slots), 1)
    mask = at == slot_ref[0, :, 0:1]
    all_ref[0:slots, :] = rows_refs[0][0]
    for e in range(1, local):
        mask = mask | (at == slot_ref[0, :, e : e + 1])
        all_ref[e * slots : (e + 1) * slots, :] = rows_refs[e][0]
    return dot(jnp.where(mask, 1.0, 0.0).astype(BF16), all_ref[...], 1, 0)


def combine_kernel(local, added, slot_ref, *refs):
    rows_refs, refs = refs[:local], refs[local:]
    out_ref, all_ref = refs[-2:]
    total = gathered(local, slot_ref, rows_refs, all_ref)
    if added:
        total = total + refs[0][...].astype(F32)
    out_ref[...] = total.astype(BF16)


def combine(slot_cols, rows, b, add=None):
    _, tokens, local = slot_cols.shape
    slots, model = rows[0].shape[1:]
    whole = pl.BlockSpec((tokens, model), lambda i: (0, 0))
    return pl.pallas_call(
        functools.partial(combine_kernel, local, add is not None),
        grid=(1,),
        in_specs=[pl.BlockSpec((1, tokens, local), lambda i: (b, 0, 0))]
        + [pl.BlockSpec((1, slots, model), lambda i: (b, 0, 0))] * local
        + [whole] * (add is not None),
        out_specs=whole,
        out_shape=shaped((tokens, model), BF16),
        scratch_shapes=[pltpu.VMEM((local * slots, model), BF16)],
        compiler_params=params(),
        cost_estimate=cost(
            2 * local * slots * model * tokens, 2 * model * (local * slots + 2 * tokens)
        ),
        name="combine",
    )(slot_cols, *rows, *(() if add is None else (add,)))


def combine_back_kernel(local, added, place_ref, slot_ref, *refs):
    rows_refs, refs = refs[:local], refs[local:]
    dchosen_refs, refs = refs[:local], refs[local:]
    probs_ref, router_ref, x_ref = refs[:3]
    out_refs, (drouter_ref, all_ref) = refs[-2 - PARTS : -2], refs[-2:]
    probs = probs_ref[0]
    line = lax.broadcasted_iota(jnp.int32, probs.shape, 0)
    dprobs = jnp.zeros_like(probs)
    for e in range(local):
        dprobs = jnp.where(line == place_ref[1] + e, dchosen_refs[e][0], dprobs)
    inner = jnp.sum(dprobs * probs, axis=0, keepdims=True)
    dlogits = (probs * (dprobs - inner)).astype(BF16)
    drouter_ref[...] = dot(dlogits, x_ref[...], 1, 0)
    total = gathered(local, slot_ref, rows_refs, all_ref) + dot(dlogits, router_ref[...], 0, 0)
    part = out_refs[0].shape[1]
    for p in range(PARTS):
        piece = total[:, p * part : (p + 1) * part]
        if added:
            piece = piece + refs[3 + p][...].astype(F32)
        out_refs[p][...] = piece.astype(BF16)


def combine_back(place, slot_cols, rows, dchosen, probs, router_rows, x, b, add=None):
    _, tokens, local = slot_cols.shape
    slots, model = rows[0].shape[1:]
    experts = router_rows.shape[0]
    whole = pl.BlockSpec((tokens, model), lambda i, s: (0, 0))
    part = pl.BlockSpec((tokens, model // PARTS), lambda i, s: (0, 0))
    block = lambda *size: pl.BlockSpec((1,) + size, lambda i, s: (b, 0, 0))
    small = pl.BlockSpec((experts, model), lambda i, s: (0, 0))
    return pl.pallas_call(
        functools.partial(combine_back_kernel, local, add is not None),
        grid_spec=pltpu.PrefetchScalarGridSpec(
            num_scalar_prefetch=1,
            grid=(1,),
            in_specs=[block(tokens, local)]
            + [block(slots, model)] * local
            + [block(1, tokens)] * local
            + [block(experts, tokens), small, whole]
            + [part] * (PARTS * (add is not None)),
            out_specs=[part] * PARTS + [small],
            scratch_shapes=[pltpu.VMEM((local * slots, model), BF16)],
        ),
        out_shape=[shaped((tokens, model // PARTS), BF16)] * PARTS
        + [shaped((experts, model), F32)],
        compiler_params=params(),
        cost_estimate=cost(
            2 * local * slots * model * tokens, 2 * model * (local * slots + 3 * tokens)
        ),
        name="combine_back",
    )(place, slot_cols, *rows, *dchosen, probs, router_rows, x, *(() if add is None else add))


def per_device(
    block_in, cotangent, route_ids, gain_attn, w_qkv, w_out_attn, gain_moe, router, w_in, w_out
):
    n_dp, n_heads, n_exp = (lax.axis_size(name) for name in ("dp", "heads", "expert"))
    n_z = n_dp // CORES
    dp, head, exp = (lax.axis_index(name) for name in ("dp", "heads", "expert"))
    z, core = dp // CORES, dp % CORES
    low = core == 0
    images, seq, half_width = block_in.shape
    span = -(-seq // 16) * 16
    rows = images * span
    model = half_width * n_heads
    width = w_qkv.shape[2]
    shard = w_qkv.shape[0]
    expert_count = router.shape[1]
    group = w_in.shape[1]
    local = group // CORES
    part_rows, _, hidden_width = w_in.shape
    capacity = 20 * images * seq // (7 * expert_count)
    slots = -(-capacity // 16) * 16
    blocks = n_exp * CORES
    rest = 128

    def shift(value, axis, step):
        size = lax.axis_size(axis)
        return lax.ppermute(value, axis, [(i, (i + step) % size) for i in range(size)])

    def shift_z(value, step):
        pairs = [
            (a * CORES + c, ((a + step) % n_z) * CORES + c) for a in range(n_z) for c in range(CORES)
        ]
        return lax.ppermute(value, "dp", pairs)

    def swap_core(value):
        return lax.ppermute(value, "dp", [(i, i ^ 1) for i in range(n_dp)])

    def place_at(pieces, index, count):
        if count == 2:
            first = index == 0
            return jnp.stack(
                [jnp.where(first, pieces[0], pieces[1]), jnp.where(first, pieces[1], pieces[0])]
            )
        out = jnp.zeros((count,) + pieces[0].shape, pieces[0].dtype)
        for k, piece in enumerate(pieces):
            out = lax.dynamic_update_index_in_dim(out, piece, (index - k) % count, 0)
        return out

    def spread(value, axis):
        return [value] + [shift(value, axis, k) for k in range(1, lax.axis_size(axis))]

    def take(value, index, dim=0):
        return lax.dynamic_index_in_dim(value, index, dim, keepdims=False)

    def expert_shards():
        both = jnp.stack([w_out, w_in]).reshape(2, part_rows, CORES, local, hidden_width)
        by_core = both.transpose(2, 3, 0, 1, 4)
        other = swap_core(take(by_core, 1 - core))
        mine = take(by_core, core)
        return jnp.concatenate(
            [jnp.where(low, mine, other), jnp.where(low, other, mine)], axis=2
        )

    ways_up = n_z // 2
    ways_down = n_z - 1 - ways_up

    def ring(piece):
        pieces = [piece] + [None] * (n_z - 1)
        for k in range(1, ways_up + 1):
            pieces[k] = shift_z(pieces[k - 1], 1)
        for k in range(1, ways_down + 1):
            pieces[n_z - k] = shift_z(pieces[(n_z - k + 1) % n_z], -1)
        return pieces

    def blocks_of(value, hold=()):
        along = spread(value, "expert")
        if hold:
            along[0] = after(along[0], *hold)
        return along + [swap_core(part) for part in along]

    def full_rows(value):
        padded = jnp.pad(value, ((0, 0), (0, span - seq), (0, 0))).reshape(rows, half_width)
        parts = place_at(spread(padded, "heads"), head, n_heads)
        return jnp.concatenate([parts[i] for i in range(n_heads)], axis=-1)

    inputs = full_rows(block_in)
    grad_full = full_rows(cotangent)

    tail = jnp.concatenate(
        [router, gain_attn[:, None], gain_moe[:, None],
         jnp.zeros((shard, rest - expert_count - 2), BF16)], axis=1
    )
    own_pack = jnp.concatenate([w_qkv.reshape(shard, 3 * width), w_out_attn, tail], axis=1)
    columns = own_pack.shape[1]
    shards = expert_shards()
    ids = jnp.pad(route_ids, ((0, 0), (0, span - seq), (0, 0)), constant_values=-1)
    ids_all = jnp.stack(blocks_of(ids.reshape(rows, 2).T))
    pack_z = place_at(
        [own_pack] + [after(shift_z(own_pack, k), shards) for k in range(1, n_z)], z, n_z
    )
    pieces = []
    for e in range(local):
        pieces.append(ring(after(shards[e], pieces[-1][1]) if e else shards[e]))
    last = local - 1
    pack = place_at(spread(after(pack_z, ids_all), "expert"), exp, n_exp)

    pack = after(pack, pieces[0][1], inputs, grad_full)
    other_pack = swap_core(pack)
    pack = jnp.stack([jnp.where(low, pack, other_pack), jnp.where(low, other_pack, pack)])
    pack = pack.transpose(2, 0, 1, 3, 4).reshape(model, columns)
    side = pack[:, 4 * width :].T
    router_rows = side[:expert_count]
    gain_one = side[expert_count : expert_count + 1].astype(F32)
    gain_two = side[expert_count + 1 : expert_count + 2].astype(F32)

    first_expert = exp * group + core * local
    place = [jnp.stack([z, first_expert + e]).astype(jnp.int32) for e in range(local)]
    slot_of, slot_cols = find_slots(place[0], ids_all, local, slots)

    grads_all = blocks_of(grad_full)
    inputs_ready = inputs
    part, qkv, ctx = attend(inputs_ready, expert_count, pack, width, images, seq)
    part = after(part, pieces[0][-1])
    part_other = shift(part, "heads", 1)
    for k in range(2, n_heads):
        part_other = part_other + shift(part, "heads", k)
    part_other = after(part_other, pieces[0][ways_up], slot_cols)
    middle = inputs.astype(F32) + (part.astype(F32) + part_other.astype(F32))
    unit_two, scale_two = norm_parts(middle)
    normed_two = (unit_two * gain_two).astype(BF16)
    tokens_all = blocks_of(normed_two, (pieces[last][1],))

    done = []

    def begin_rings(e, *hold):
        rows_e, mids_e = done[e][:2]
        rings.append(weight_grad(place[e], after(rows_e, *hold), mids_e, n_z))

    def ring_first(e):
        return shift_z(rings[e][-ways_up % n_z], 1)

    def ring_down(e, *hold):
        chunks = rings[e]
        downward = after(chunks[ways_down], *hold)
        for k in range(ways_down - 1, 0, -1):
            downward = (shift_z(downward, -1).astype(F32) + chunks[k].astype(F32)).astype(BF16)
        return shift_z(downward, -1)

    def ring_middle(e, upward, *hold):
        chunks = rings[e]
        for k in range(ways_up - 1, 0, -1):
            own = after(chunks[n_z - k], *hold)
            upward = (upward.astype(F32) + own.astype(F32)).astype(BF16)
            if k > 1:
                upward = shift_z(upward, 1)
        return upward

    def ring_end(e, upward, downward, *hold):
        own = after(rings[e][0], *hold).astype(F32)
        return own + shift_z(upward, 1).astype(F32) + downward.astype(F32)

    rings = []
    for e in range(local):
        here = list(pieces[e])
        if e:
            here[0] = after(here[0], rings[-1][0])
        done.append(
            run_expert(
                e, place[e], slot_of, router_rows, tokens_all, grads_all, here, slots
            )
        )
        if e < local - 1:
            begin_rings(e)
    drows, yrows, dchosen = ([r[i] for r in done] for i in (3, 4, 2))
    probs = done[0][5]

    arrived_zero, down_zero = ring_first(0), ring_down(0)
    drows[0] = after(drows[0], arrived_zero)

    def back_of(b, add=None):
        *parts, more = combine_back(
            place[0], slot_cols, drows, dchosen, probs, router_rows, tokens_all[b], b, add
        )
        return parts, more

    drouter = jnp.zeros((expert_count, model), F32)
    arrived = [None] * n_exp
    for k in reversed(range(n_exp)):
        sent, more = back_of(n_exp + k)
        arrived[k] = [swap_core(part) for part in sent]
        drouter = drouter + more
    from_exp = []
    for k in reversed(range(n_exp)):
        arrived[k][0] = after(arrived[k][0], total[0] if k < n_exp - 1 else down_zero)
        total, more = back_of(k, arrived[k])
        drouter = drouter + more
        if k:
            from_exp.append([shift(part, "expert", -k) for part in total])
        if k == 1:
            early = ring_middle(0, arrived_zero, total[0])
    ends = [ring_end(0, early, down_zero)]
    dsum, dsum_other = [], []
    for p in range(PARTS):
        if p == 1:
            begin_rings(last, dsum[0])
        value = (after(total[p], rings[last][0]) if p else total[p]).astype(F32)
        for came in from_exp:
            value = value + came[p].astype(F32)
        dsum.append(value.astype(BF16))
        other = shift(dsum[p], "heads", 1)
        for k in range(2, n_heads):
            other = other + shift(dsum[p], "heads", k)
        dsum_other.append(other)
    arrived_last, down_last = ring_first(last), ring_down(last)
    dsum_other[0] = after(dsum_other[0], ends[0])

    yrows[0] = after(yrows[0], dsum[0])
    y_came = [swap_core(combine(slot_cols, yrows, n_exp + k)) for k in range(n_exp)]
    y_from = [
        shift(combine(slot_cols, yrows, k, after(y_came[k], dsum[-1])), "expert", -k)
        for k in range(1, n_exp)
    ]
    dnormed_two = jnp.concatenate(
        [own.astype(F32) + other.astype(F32) for own, other in zip(dsum, dsum_other)], axis=1
    )
    scaled = dnormed_two * gain_two
    grad_gain_two = jnp.sum(dnormed_two * unit_two, axis=0)
    dmiddle = grad_full.astype(F32) + scale_two * (
        scaled
        - jnp.mean(scaled, axis=-1, keepdims=True)
        - unit_two * jnp.mean(scaled * unit_two, axis=-1, keepdims=True)
    )
    late = ring_middle(last, arrived_last, dsum_other[-1])
    datt = after(dmiddle.astype(BF16), *y_came)

    dside = jnp.concatenate(
        [drouter, jnp.zeros((1, model), F32), grad_gain_two[None, :],
         jnp.zeros((rest - expert_count - 2, model), F32)], axis=0
    ).T
    dnorm, stats, dkeep, dsend = attend_back(
        inputs, gain_one, datt, qkv, ctx, pack, dside, expert_count, width, images, seq, n_heads,
        core.astype(jnp.int32)[None], n_z,
    )
    dsend = after(dsend, *y_from, down_last)

    dcame = swap_core(dsend)
    dpack = (dkeep.astype(F32) + dcame.astype(F32)).astype(BF16)
    dpack = dpack.reshape(n_z, n_exp, shard, columns)
    y_own = combine(slot_cols, yrows, 0, after(y_came[0], dcame)).astype(F32)
    for value in y_from:
        y_own = y_own + value.astype(F32)
    y_own = y_own.astype(BF16)

    dtotal = take(dpack, exp, 1).astype(F32)
    for k in range(1, n_exp):
        came = shift(take(dpack, (exp + k) % n_exp, 1), "expert", k)
        dtotal = dtotal + came.astype(F32)
    dpack = dtotal.astype(BF16)

    came = [shift_z(take(dpack, (z + k) % n_z), k) for k in range(1, n_z)]
    dtotal = take(dpack, z).astype(F32)
    for value in came:
        dtotal = dtotal + value.astype(F32)

    ends.append(ring_end(last, late, down_last, dpack))
    stacked = jnp.stack(ends).reshape(local, 2, CORES, part_rows, hidden_width)
    other = swap_core(take(stacked, 1 - core, 2).astype(BF16)).astype(F32)
    own = take(stacked, core, 2)
    joined = jnp.concatenate([jnp.where(low, own, other), jnp.where(low, other, own)], axis=0)
    grads = joined.transpose(1, 2, 0, 3)
    dside = dtotal[:, 4 * width :]
    over_heads = dside[:, : expert_count + 1].T
    grad_w_out, grad_w_in, over_heads = lax.optimization_barrier((grads[0], grads[1], over_heads))
    summed = over_heads
    for k in range(1, n_heads):
        summed = summed + shift(over_heads, "heads", k)

    def own_half(value):
        return lax.dynamic_slice_in_dim(value, head * half_width, half_width, 1)

    def cut(value):
        return value.astype(BF16).reshape(images, span, half_width)[:, :seq]

    dnorm, stats = lax.optimization_barrier((dnorm, stats, dcame))[:2]
    dn_own = take(dnorm, head).astype(F32)
    sums = stats[:, :2].T
    sums_total = sums
    for k in range(1, n_heads):
        there = shift(take(dnorm, (head + k) % n_heads), "heads", k)
        dn_own = dn_own + after(there, came[0]).astype(F32)
        sums_total = sums_total + after(shift(sums, "heads", k), came[0])
    unit_one, scale_one = norm_parts(inputs.astype(F32))
    grad_in = own_half(dmiddle) + scale_one * (
        dn_own * own_half(gain_one)
        - sums_total[0][:, None] / model
        - own_half(unit_one) * (sums_total[1][:, None] / model)
    )

    y_total = own_half(y_own).astype(F32)
    for k in range(1, n_heads):
        there = (head + k) % n_heads
        part_y = lax.dynamic_slice_in_dim(y_own, there * half_width, half_width, 1)
        y_total = y_total + after(shift(part_y, "heads", k), came[0]).astype(F32)
    block_out = own_half(middle) + y_total

    return (
        cut(block_out),
        cut(grad_in),
        summed[expert_count],
        dtotal[:, : 3 * width].reshape(shard, 3, width),
        dtotal[:, 3 * width : 4 * width],
        dside[:, expert_count + 1],
        summed[:expert_count].T,
        grad_w_in,
        grad_w_out,
    )


def solution(mesh):
    return jax.shard_map(
        per_device,
        mesh=mesh,
        in_specs=(
            P(("dp", "expert"), None, "heads"),
            P(("dp", "expert"), None, "heads"),
            P(("dp", "expert"), None, None),
            P(("dp", "expert")),
            P(("dp", "expert"), None, "heads"),
            P(("dp", "expert"), "heads"),
            P(("dp", "expert")),
            P(("dp", "expert"), None),
            P("dp", "expert", "heads"),
            P("dp", "expert", "heads"),
        ),
        out_specs=(
            P(("dp", "expert"), None, "heads"),
            P(("dp", "expert"), None, "heads"),
            P(("dp", "expert")),
            P(("dp", "expert"), None, "heads"),
            P(("dp", "expert"), "heads"),
            P(("dp", "expert")),
            P(("dp", "expert"), None),
            P("dp", "expert", "heads"),
            P("dp", "expert", "heads"),
        ),
        check_vma=False,
    )
```
